256 devices in a mesh: ctx: 8 (over z_hi, core), dp: 32 (over x, y, z_lo).
Axes of the slice: x: 4, y: 4, z: 8 (z_hi: 4, z_lo: 2; z = z_hi * 2 + z_lo), core: 2. Of those that a mesh axis runs over, the one named last changes fastest.
Arguments:
- hidden_in: bfloat16 [32, 2048, 768], P('dp', 'ctx'), may hold values from -48 to 48
- w_qkv: bfloat16 [768, 2304], replicated
- w_out: bfloat16 [768, 768], replicated, may hold values from -1.75 to 1.75
- b_out: float32 [768], replicated, may hold values from -3 to 3
- ln_gain: float32 [768], replicated, may hold values from 0.5 to 1.5
- ln_bias: float32 [768], replicated, may hold values from -0.6 to 0.6
- doc_lengths: int32 [32, 4], P('dp'), may hold values from 1 to 1024, 2048 in all within a row
- pair_of: int32 [32, 4], P('dp'), may hold values from 0 to 127, as said below
Outputs:
- encoded: bfloat16 [32, 2048, 768], P('dp', 'ctx')
- grad_out: float32 [768, 768], P('dp')
The draws below stay inside these ranges and needn't reach their ends.
Inputs may be any that keep to these rules, and one draw needn't show every extreme that they name: pair_of[pair_of[i]] = i and pair_of[i] != i.
All inputs are finite; a program needn't handle non-finite values.
Results may differ from the reference program's by a relative error of at most 0.011.
Values may be sent and summed in bfloat16 or wider, within the bound.
No kernel may reach another device: no remote copies, remote signals or barrier semaphores. Data moves between devices by JAX's collectives and lax.ppermute only.
A program may use at most 64 MiB of HBM per device.

```python
import math
import jax
import jax.numpy as jnp
import numpy as np
from jax import lax

D = 768
HEADS = 12
HEAD_DIM = 64
DOCS = 4
SEQ = 2048
DOCUMENT_LIMIT = 1024
PACKS = 32
NDOC = 128


def draw_hidden_in(key, part):
    key = jax.random.fold_in(key, 1)
    base = jax.random.truncated_normal(jax.random.fold_in(key, 10), -6.0, 6.0, (PACKS, SEQ, D), jnp.float32)
    return base.astype(jnp.bfloat16)


def draw_w_qkv(key, part):
    key = jax.random.fold_in(key, 2)
    base = jax.random.truncated_normal(key, -6.0, 6.0, (D, 3 * D), jnp.float32) * D ** (-0.5)
    return base.astype(jnp.bfloat16)


def draw_pair_of(key, part):
    key = jax.random.fold_in(key, 3)
    shuffled = jax.random.permutation(key, PACKS * DOCS).astype(jnp.int32)
    position_of = jnp.argsort(shuffled, stable=True).astype(jnp.int32)
    partner = shuffled[position_of + 1 - 2 * (position_of % 2)]
    return partner.reshape(PACKS, DOCS).astype(jnp.int32)


def profile(number_of, total, bound, slope):
    weights = [(1 << 20) // math.isqrt(rank ** slope) + 1 for rank in range(2, number_of + 1)]
    surplus, holding = total - bound - (number_of - 1), [1] * (number_of - 1)
    while surplus > 0:
        movable = [i for i in range(number_of - 1) if holding[i] < bound]
        whole, left = sum([weights[i] for i in movable]), surplus
        for i in movable:
            more = min(bound - holding[i], max(1, left * weights[i] // whole), surplus)
            holding[i] = holding[i] + more
            surplus = surplus - more
    return np.array([bound] + holding)


def uneven_parts(own_key, amount, total, reach, lean):
    if amount == 2:
        one = jax.random.randint(own_key, (), max(1, total - reach), min(reach, total - 1) + 1)
        return jnp.stack([one, total - one])
    sizes = jnp.asarray(profile(amount, total, reach, lean), jnp.int32)
    couples = (amount - 1) // 2
    giver, receiver = sizes[1:1 + 2 * couples:2], sizes[2:2 + 2 * couples:2]
    slack = jnp.minimum(giver - 1, reach - receiver)
    shifted = jax.random.randint(jax.random.fold_in(own_key, 1), (couples,), 0, 1 << 20) % (slack + 1)
    sizes = sizes.at[1:1 + 2 * couples:2].set(giver - shifted).at[2:2 + 2 * couples:2].set(receiver + shifted)
    return sizes[jax.random.permutation(jax.random.fold_in(own_key, 2), amount)]


def normal_values(rng, dims, scale, most, kind=jnp.bfloat16):
    values = scale * jax.random.normal(rng, dims, jnp.float32)
    return jnp.clip(values, min=-most, max=most).astype(kind)


def setup_inputs(seed: int = 0) -> dict:
    key_list = jax.random.split(jax.random.key(seed), 9)
    return {
        "hidden_in": draw_hidden_in(jax.random.fold_in(key_list[8], 71), 0),
        "w_qkv": draw_w_qkv(jax.random.fold_in(key_list[8], 71), 0),
        "w_out": normal_values(key_list[2], (D, D), (max(D // 64, 1)) ** -0.5, 1.75),
        "b_out": normal_values(key_list[3], (D,), 0.5, 3.0, jnp.float32),
        "ln_gain": jnp.clip(1.0 + 0.1 * jax.random.normal(key_list[4], (D,), jnp.float32), 0.5, 1.5),
        "ln_bias": normal_values(key_list[5], (D,), 0.1, 0.6, jnp.float32),
        "doc_lengths": jax.vmap(lambda own: uneven_parts(own, DOCS, SEQ, DOCUMENT_LIMIT, 2))(jax.random.split(key_list[6], PACKS)).reshape((PACKS, DOCS)).astype(jnp.int32),
        "pair_of": draw_pair_of(jax.random.fold_in(key_list[8], 71), 0),
    }


SOFTMAX_TEMPER = 0.05
NORM_EPSILON = 1e-05
EMBED_EPSILON = 1e-06

def doc_index(lengths, positions):
    doc_ends = jnp.cumsum(lengths)
    return lax.optimization_barrier(jnp.sum((positions[:, None] >= doc_ends[None, :]).astype(jnp.int32), axis=1))

def split_heads(matrix):
    return matrix.reshape(matrix.shape[0], HEADS, HEAD_DIM).transpose(1, 0, 2)

def contract_rows(left, right):
    return lax.dot_general(left, right, (((0,), (0,)), ((), ())), preferred_element_type=jnp.float32)

def attend(queries, keys, values, allowed):

    def one_head(pieces):
        query_head, key_head, value_head = pieces
        scores = jnp.dot(query_head, key_head.T, preferred_element_type=jnp.float32) * HEAD_DIM ** (-0.5)
        scores = jnp.where(allowed, scores, -1e+30)
        highest = lax.optimization_barrier(jnp.max(scores, axis=1, keepdims=True))
        weights = jnp.exp(scores - highest)
        probabilities = (weights / lax.optimization_barrier(jnp.sum(weights, axis=1, keepdims=True))).astype(jnp.bfloat16)
        return jnp.dot(probabilities, value_head, preferred_element_type=jnp.float32).astype(jnp.bfloat16)
    head_outs = lax.map(one_head, (queries, keys, values))
    return head_outs.transpose(1, 0, 2).reshape(queries.shape[1], HEADS * HEAD_DIM)

def normalize(summed):
    centered = summed - lax.optimization_barrier(jnp.mean(summed, axis=1, keepdims=True))
    inverse = lax.rsqrt(lax.optimization_barrier(jnp.mean(centered * centered, axis=1, keepdims=True)) + NORM_EPSILON)
    return (centered * inverse, inverse)

def normalize_back(layer_grad, normal, inverse, ln_gain):
    scaled = layer_grad * ln_gain
    result = inverse * (scaled - lax.optimization_barrier(jnp.mean(scaled, axis=1, keepdims=True)) - normal * lax.optimization_barrier(jnp.mean(scaled * normal, axis=1, keepdims=True)))
    return result.astype(jnp.bfloat16)

def reference(hidden_in, w_qkv, w_out, b_out, ln_gain, ln_bias, doc_lengths, pair_of):
    positions = jnp.arange(SEQ, dtype=jnp.int32)
    doc_slots = jnp.arange(DOCS, dtype=jnp.int32)

    def encode(pieces):
        tokens, lengths = pieces
        doc_ids = doc_index(lengths, positions)
        projected = jnp.dot(tokens, w_qkv, preferred_element_type=jnp.float32).astype(jnp.bfloat16)
        allowed = doc_ids[:, None] == doc_ids[None, :]
        mixed_heads = attend(split_heads(projected[:, :D]), split_heads(projected[:, D:2 * D]), split_heads(projected[:, 2 * D:]), allowed)
        summed = jnp.dot(mixed_heads, w_out, preferred_element_type=jnp.float32) + b_out + tokens.astype(jnp.float32)
        normal, inverse = normalize(summed)
        layer_out = normal * ln_gain + ln_bias
        member = (doc_ids[None, :] == doc_slots[:, None]).astype(jnp.float32)
        pooled_sum = jnp.dot(member, layer_out, precision=lax.Precision.HIGHEST)
        return (layer_out.astype(jnp.bfloat16), mixed_heads, normal, inverse, pooled_sum)
    encoded, mixed_all, normal_all, inverse_all, pooled_sum = lax.map(encode, (hidden_in, doc_lengths))
    counts = doc_lengths.astype(jnp.float32)
    pooled = (pooled_sum / counts[:, :, None]).reshape(NDOC, D)
    emb_norm = jnp.sqrt(lax.optimization_barrier(jnp.sum(pooled * pooled, axis=1)) + EMBED_EPSILON)
    embedded_tokens = pooled / emb_norm[:, None]
    similarity_scores = jnp.dot(embedded_tokens, embedded_tokens.T, precision=lax.Precision.HIGHEST) / SOFTMAX_TEMPER
    columns = jnp.arange(NDOC, dtype=jnp.int32)
    is_self = columns[None, :] == columns[:, None]
    exp_sims = jnp.where(is_self, jnp.zeros_like(similarity_scores), jnp.exp(similarity_scores))
    totals = lax.optimization_barrier(jnp.sum(exp_sims, axis=1))
    target = (columns[None, :] == pair_of.reshape(NDOC)[:, None]).astype(jnp.float32)
    row_gradient = exp_sims / totals[:, None] - target
    embedding_gradient = jnp.dot(row_gradient + row_gradient.T, embedded_tokens, precision=lax.Precision.HIGHEST) / SOFTMAX_TEMPER
    pooled_grad = (embedding_gradient - embedded_tokens * lax.optimization_barrier(jnp.sum(embedded_tokens * embedding_gradient, axis=1, keepdims=True))) / emb_norm[:, None]
    per_token = pooled_grad.reshape(PACKS, DOCS, D) / counts[:, :, None]

    def accumulate(running, pieces):
        lengths, spread, mixed_pack, normal_pack, inverse_pack = pieces
        doc_ids = doc_index(lengths, positions)
        member = (doc_ids[None, :] == doc_slots[:, None]).astype(jnp.float32)
        layer_grad = jnp.dot(member.T, spread, precision=lax.Precision.HIGHEST)
        summed_grad = normalize_back(layer_grad, normal_pack, inverse_pack, ln_gain)
        return (running + contract_rows(mixed_pack, summed_grad), jnp.zeros((), jnp.float32))
    grad_out, unused = lax.scan(accumulate, jnp.zeros((D, D), jnp.float32), (doc_lengths, per_token, mixed_all, normal_all, inverse_all))
    return (encoded, grad_out)
```

```python
import functools

import jax
import jax.numpy as jnp
from jax import lax
from jax.experimental import pallas as pl
from jax.experimental.pallas import tpu as pltpu
from jax.sharding import PartitionSpec as P

D = 768
HEADS = 12
HEAD_DIM = 64
PAIRS = HEADS // 2
DOCS = 4
NDOC = 128
ROWS = 256
CTX = 8
DP = 32
AUG = 80

SOFTMAX_TEMPER = 0.05
NORM_EPSILON = 1e-05
EMBED_EPSILON = 1e-06
PENALTY = -1e30

VMEM_LIMIT = 48 * 1024 * 1024

CORE_SWAP = [(c, c ^ 1) for c in range(CTX)]
Z_UP = [(c, (c + 2) % CTX) for c in range(CTX)]
Z_DOWN = [(c, (c - 2) % CTX) for c in range(CTX)]


def doc_ends(lengths_ref):
    e0 = lengths_ref[0, 0]
    e1 = e0 + lengths_ref[0, 1]
    e2 = e1 + lengths_ref[0, 2]
    e3 = e2 + lengths_ref[0, 3]
    return e0, e1, e2, e3


def doc_of(ends, positions):
    e0, e1, e2, e3 = ends
    one = jnp.int32(1)
    zero = jnp.int32(0)
    return sum(jnp.where(positions >= e, one, zero) for e in (e0, e1, e2, e3))


def needed_span(ends, first):
    e0, e1, e2, e3 = ends
    last = first + ROWS - 1
    low = jnp.where(first >= e2, e2, jnp.where(first >= e1, e1, jnp.where(first >= e0, e0, 0)))
    high = jnp.where(last < e0, e0, jnp.where(last < e1, e1, jnp.where(last < e2, e2, e3)))
    return low, high


def fill_queries(ends, first, qt_ref, qbd):
    positions = first + lax.broadcasted_iota(jnp.int32, (HEAD_DIM * 2, ROWS), 1)
    slots = lax.broadcasted_iota(jnp.int32, (HEAD_DIM * 2, ROWS), 0)
    same = (doc_of(ends, positions) == slots) | (slots >= DOCS)
    penalty = jnp.where(same, 0.0, PENALTY).astype(jnp.bfloat16)
    penalties = jnp.concatenate([penalty, penalty], axis=1)
    zero = jnp.zeros((HEAD_DIM, ROWS), jnp.bfloat16)
    for j in range(PAIRS):
        qbd[j, :64, :ROWS] = qt_ref[128 * j : 128 * j + 64, :]
        qbd[j, :64, ROWS:] = zero
        qbd[j, 64:128, :ROWS] = zero
        qbd[j, 64:128, ROWS:] = qt_ref[128 * j + 64 : 128 * j + 128, :]
        qbd[j, 128:, :] = penalties


def attend_block(ends, base, hidden, wk_ref, wvt_ref, qbd, vt, m_ref, acc_ref):
    keys = jnp.dot(hidden, wk_ref[...], preferred_element_type=jnp.float32).astype(jnp.bfloat16)
    values = lax.dot_general(
        wvt_ref[...], hidden, (((1,), (1,)), ((), ())), preferred_element_type=jnp.float32
    ).astype(jnp.bfloat16)
    vt[:, :HEAD_DIM, :] = values.reshape(HEADS, HEAD_DIM, ROWS)
    key_doc = doc_of(ends, base + lax.broadcasted_iota(jnp.int32, (ROWS, 128), 0))
    lanes = lax.broadcasted_iota(jnp.int32, (ROWS, 128), 1)
    onehot = jnp.where(key_doc == lanes, 1.0, 0.0).astype(jnp.bfloat16)
    for j in range(PAIRS):
        pair_keys = jnp.concatenate([keys[:, 128 * j : 128 * j + 128], onehot], axis=1)
        scores = jnp.dot(pair_keys, qbd[j], preferred_element_type=jnp.float32)
        old = m_ref[j : j + 1, :]
        new = jnp.maximum(old, jnp.max(scores, axis=0, keepdims=True))
        m_ref[j : j + 1, :] = new
        shrink = jnp.exp(old - new)
        weights = jnp.exp(scores - new).astype(jnp.bfloat16)
        for h in range(2):
            part = slice(ROWS * h, ROWS * h + ROWS)
            mixed = jnp.dot(vt[2 * j + h], weights[:, part], preferred_element_type=jnp.float32)
            acc_ref[2 * j + h] = acc_ref[2 * j + h] * shrink[:, part] + mixed


def fill_ones(vt):
    row = lax.broadcasted_iota(jnp.int32, (HEADS, AUG - HEAD_DIM, ROWS), 1)
    vt[:, HEAD_DIM:, :] = jnp.where(row == 0, 1.0, 0.0).astype(jnp.bfloat16)


def attend_blocks(ends, first, bases, blocks, wk_ref, wvt_ref, qbd, vt, m_ref, acc_ref):
    low, high = needed_span(ends, first)
    for base, block in zip(bases, blocks):

        @pl.when((base < high) & (base + ROWS > low))
        def _():
            attend_block(ends, base, block[...], wk_ref, wvt_ref, qbd, vt, m_ref, acc_ref)


def first_kernel(
    lengths_ref, place_ref, own_ref, other_ref, wq_ref, wk_ref, wvt_ref, qt_ref, m_ref, acc_ref, qbd, vt
):
    place = place_ref[0]
    ends = doc_ends(lengths_ref)
    first = place * ROWS
    queries = jnp.dot(own_ref[...], wq_ref[...], preferred_element_type=jnp.float32)
    queries = queries.astype(jnp.bfloat16).astype(jnp.float32) * HEAD_DIM**-0.5
    qt_ref[...] = queries.T.astype(jnp.bfloat16)
    fill_queries(ends, first, qt_ref, qbd)
    fill_ones(vt)
    m_ref[...] = jnp.full(m_ref.shape, PENALTY, jnp.float32)
    acc_ref[...] = jnp.zeros(acc_ref.shape, jnp.float32)
    bases = [first, (place ^ 1) * ROWS]
    attend_blocks(ends, first, bases, [own_ref, other_ref], wk_ref, wvt_ref, qbd, vt, m_ref, acc_ref)


def middle_kernel(
    lengths_ref, place_ref, up_ref, down_ref, up_other_ref, down_other_ref, wk_ref, wvt_ref, qt_ref,
    m_in, acc_in, m_ref, acc_ref, qbd, vt
):
    place = place_ref[0]
    ends = doc_ends(lengths_ref)
    first = place * ROWS
    fill_queries(ends, first, qt_ref, qbd)
    fill_ones(vt)
    m_ref[...] = m_in[...]
    acc_ref[...] = acc_in[...]
    up = lax.rem(place + 6, 8)
    down = lax.rem(place + 2, 8)
    bases = [up * ROWS, down * ROWS, (up ^ 1) * ROWS, (down ^ 1) * ROWS]
    blocks = [up_ref, down_ref, up_other_ref, down_other_ref]
    attend_blocks(ends, first, bases, blocks, wk_ref, wvt_ref, qbd, vt, m_ref, acc_ref)


def last_kernel(
    lengths_ref, place_ref, far_ref, far_other_ref, wk_ref, wvt_ref, qt_ref, m_in, acc_in, own_ref, wout_ref,
    bias_ref, gain_ref, shift_ref, encoded_ref, mixed_ref, normal_ref, inverse_ref, pooled_ref,
    qbd, vt, m_ref, acc_ref
):
    place = place_ref[0]
    ends = doc_ends(lengths_ref)
    first = place * ROWS
    fill_queries(ends, first, qt_ref, qbd)
    fill_ones(vt)
    m_ref[...] = m_in[...]
    acc_ref[...] = acc_in[...]
    far = lax.rem(place + 4, 8)
    bases = [far * ROWS, (far ^ 1) * ROWS]
    attend_blocks(ends, first, bases, [far_ref, far_other_ref], wk_ref, wvt_ref, qbd, vt, m_ref, acc_ref)
    acc = acc_ref[...]
    mixed = acc[:, :HEAD_DIM, :] / acc[:, HEAD_DIM : HEAD_DIM + 1, :]
    mixed = mixed.reshape(D, ROWS)
    mixed_ref[...] = mixed.astype(jnp.bfloat16)
    summed = jnp.dot(mixed.T.astype(jnp.bfloat16), wout_ref[...], preferred_element_type=jnp.float32)
    summed = summed + bias_ref[...] + own_ref[...].astype(jnp.float32)
    centered = summed - jnp.mean(summed, axis=1, keepdims=True)
    inverse = lax.rsqrt(jnp.mean(centered * centered, axis=1, keepdims=True) + NORM_EPSILON)
    normal = centered * inverse
    normal_ref[...] = normal
    inverse_ref[...] = inverse
    layer = normal * gain_ref[...] + shift_ref[...]
    encoded_ref[...] = layer.astype(jnp.bfloat16)
    row_doc = doc_of(ends, first + lax.broadcasted_iota(jnp.int32, (ROWS, 1), 0))
    for d in range(DOCS):
        pooled_ref[d : d + 1, :] = jnp.sum(
            jnp.where(row_doc == d, layer, 0.0), axis=0, keepdims=True
        )


def back_kernel(
    lengths_ref, place_ref, pair_ref, pooled_ref, own_pooled_ref, mixed_ref, normal_ref, inverse_ref, gain_ref,
    out_ref
):
    place = place_ref[0]
    data_place = place_ref[1]
    ends = doc_ends(lengths_ref)
    first = place * ROWS
    pooled = pooled_ref[...]
    emb = pooled / jnp.sqrt(jnp.sum(pooled * pooled, axis=1, keepdims=True) + EMBED_EPSILON)
    nt = (((1,), (1,)), ((), ()))
    sims = (
        lax.dot_general(emb, emb, nt, precision=lax.Precision.HIGHEST, preferred_element_type=jnp.float32)
        / SOFTMAX_TEMPER
    )
    columns = lax.broadcasted_iota(jnp.int32, (NDOC, NDOC), 1)
    rows = lax.broadcasted_iota(jnp.int32, (NDOC, NDOC), 0)
    expo = jnp.where(rows == columns, 0.0, jnp.exp(sims))
    totals = 1.0 / jnp.sum(expo, axis=0, keepdims=True)
    own = own_pooled_ref[...]
    own_norm = jnp.sqrt(jnp.sum(own * own, axis=1, keepdims=True) + EMBED_EPSILON)
    own_emb = own / own_norm
    own_sims = (
        lax.dot_general(own_emb, emb, nt, precision=lax.Precision.HIGHEST, preferred_element_type=jnp.float32)
        / SOFTMAX_TEMPER
    )
    slots = lax.broadcasted_iota(jnp.int32, (8, NDOC), 0)
    lanes = lax.broadcasted_iota(jnp.int32, (8, NDOC), 1)
    own_expo = jnp.where(lanes == slots + data_place * DOCS, 0.0, jnp.exp(own_sims))
    own_totals = 1.0 / jnp.sum(own_expo, axis=1, keepdims=True)
    partner = jnp.where(
        slots == 0, pair_ref[0, 0],
        jnp.where(slots == 1, pair_ref[0, 1], jnp.where(slots == 2, pair_ref[0, 2], pair_ref[0, 3])),
    )
    both = own_expo * (own_totals + totals) - jnp.where(lanes == partner, 2.0, 0.0)
    emb_grad = (
        jnp.dot(both, emb, precision=lax.Precision.HIGHEST, preferred_element_type=jnp.float32) / SOFTMAX_TEMPER
    )
    pooled_grad = (emb_grad - own_emb * jnp.sum(own_emb * emb_grad, axis=1, keepdims=True)) / own_norm
    slot = lax.broadcasted_iota(jnp.int32, (8, 1), 0)
    length = jnp.where(
        slot == 0, lengths_ref[0, 0],
        jnp.where(slot == 1, lengths_ref[0, 1], jnp.where(slot == 2, lengths_ref[0, 2], lengths_ref[0, 3])),
    ).astype(jnp.float32)
    scaled = pooled_grad / length * gain_ref[...]
    row_doc = doc_of(ends, first + lax.broadcasted_iota(jnp.int32, (ROWS, 1), 0))
    spread = jnp.where(
        row_doc == 0, scaled[0:1],
        jnp.where(row_doc == 1, scaled[1:2], jnp.where(row_doc == 2, scaled[2:3], scaled[3:4])),
    )
    normal = normal_ref[...]
    grad = inverse_ref[...] * (
        spread
        - jnp.mean(spread, axis=1, keepdims=True)
        - normal * jnp.mean(spread * normal, axis=1, keepdims=True)
    )
    out_ref[...] = jnp.dot(
        mixed_ref[...], grad.astype(jnp.bfloat16), preferred_element_type=jnp.float32
    ).astype(jnp.bfloat16)


SMEM = pl.BlockSpec(memory_space=pltpu.SMEM)
VMEM = pl.BlockSpec(memory_space=pltpu.VMEM)


def call(kernel, name, smem, vmem, outs, scratch, flops):
    return pl.pallas_call(
        kernel,
        name=name,
        out_shape=[jax.ShapeDtypeStruct(s, t) for s, t in outs],
        in_specs=[SMEM] * len(smem) + [VMEM] * len(vmem),
        out_specs=[VMEM] * len(outs),
        scratch_shapes=[pltpu.VMEM(s, t) for s, t in scratch],
        cost_estimate=pl.CostEstimate(flops=flops, bytes_accessed=4 << 20, transcendentals=0),
        compiler_params=pltpu.CompilerParams(vmem_limit_bytes=VMEM_LIMIT),
    )(*smem, *vmem)


def copies(value, axis, count):
    return lax.all_to_all(jnp.broadcast_to(value[None], (count,) + value.shape), axis, 0, 0, tiled=True)


def per_device(hidden_in, w_qkv, w_out, b_out, ln_gain, ln_bias, doc_lengths, pair_of):
    f32, bf16 = jnp.float32, jnp.bfloat16
    own = hidden_in[0]
    places = jnp.stack([lax.axis_index("ctx"), lax.axis_index("dp")]).astype(jnp.int32)
    up = lax.ppermute(own, "ctx", Z_UP)
    down = lax.ppermute(own, "ctx", Z_DOWN)
    other = lax.ppermute(own, "ctx", CORE_SWAP)
    far_up = lax.ppermute(up[: ROWS // 2], "ctx", Z_UP)
    far_down = lax.ppermute(down[ROWS // 2 :], "ctx", Z_DOWN)
    up_other = lax.ppermute(up, "ctx", CORE_SWAP)
    down_other = lax.ppermute(down, "ctx", CORE_SWAP)
    far = jnp.concatenate([far_up, far_down], axis=0)
    far_other = lax.ppermute(far, "ctx", CORE_SWAP)

    wq = w_qkv[:, :D]
    wk = w_qkv[:, D : 2 * D]
    wvt = w_qkv[:, 2 * D :].T
    gain = ln_gain[None]
    smem = [doc_lengths, places]
    state = [((8, 2 * ROWS), f32), ((HEADS, AUG, ROWS), f32)]
    work = [((PAIRS, 256, 2 * ROWS), bf16), ((HEADS, AUG, ROWS), bf16)]
    qt, m, acc = call(
        first_kernel, "first", smem, [own, other, wq, wk, wvt], [((D, ROWS), bf16)] + state, work, 3 << 30
    )
    m, acc = call(
        middle_kernel, "middle", smem, [up, down, up_other, down_other, wk, wvt, qt, m, acc], state, work, 4 << 30
    )
    encoded, mixed, normal, inverse, partial = call(
        last_kernel,
        "last",
        smem,
        [far, far_other, wk, wvt, qt, m, acc, own, w_out, b_out[None], gain, ln_bias[None]],
        [((ROWS, D), bf16), ((D, ROWS), bf16), ((ROWS, D), f32), ((ROWS, 1), f32), ((DOCS, D), f32)],
        work + state,
        4 << 30,
    )
    pooled = jnp.sum(copies(partial, "ctx", CTX), axis=0) / doc_lengths[0].astype(f32)[:, None]
    every = copies(pooled, "dp", DP).reshape(NDOC, D)
    own_pooled = jnp.concatenate([pooled, jnp.ones_like(pooled)], axis=0)
    (term,) = call(
        back_kernel,
        "back",
        smem + [pair_of],
        [every, own_pooled, mixed, normal, inverse, gain],
        [((D, D), bf16)],
        [],
        1 << 30,
    )
    share = D // DP
    pieces = lax.all_to_all(term.reshape(DP, share, D), "dp", 0, 0, tiled=True)
    piece = jnp.sum(pieces.astype(f32), axis=0)
    grad_out = jnp.sum(copies(piece.astype(bf16), "ctx", CTX).astype(f32), axis=0)
    return (encoded[None], grad_out)


def solution(mesh):
    return jax.shard_map(
        per_device,
        mesh=mesh,
        in_specs=(P("dp", "ctx", None), P(), P(), P(), P(), P(), P("dp", None), P("dp", None)),
        out_specs=(P("dp", "ctx", None), P("dp", None)),
        check_vma=False,
    )
```

```python
import functools

import jax
import jax.numpy as jnp
from jax import lax
from jax.experimental import pallas as pl
from jax.experimental.pallas import tpu as pltpu
from jax.sharding import PartitionSpec as P

D = 768
HEADS = 12
HEAD_DIM = 64
PAIRS = HEADS // 2
DOCS = 4
NDOC = 128
ROWS = 256
CTX = 8
DP = 32
AUG = 80

SOFTMAX_TEMPER = 0.05
NORM_EPSILON = 1e-05
EMBED_EPSILON = 1e-06
PENALTY = -1e30

VMEM_LIMIT = 24 * 1024 * 1024

CORE_SWAP = [(c, c ^ 1) for c in range(CTX)]
AROUND = [(c, (c + 2) % CTX if c % 2 == 0 else (c - 2) % CTX) for c in range(CTX)]
BACK = [(b, a) for a, b in AROUND]


def came_from(place, hops):
    step = 2 * hops
    return lax.rem(jnp.where(lax.rem(place, 2) == 0, place - step, place + step) + 2 * CTX, CTX)


def doc_ends(lengths_ref):
    e0 = lengths_ref[0, 0]
    e1 = e0 + lengths_ref[0, 1]
    e2 = e1 + lengths_ref[0, 2]
    e3 = e2 + lengths_ref[0, 3]
    return e0, e1, e2, e3


def doc_of(ends, positions):
    e0, e1, e2, e3 = ends
    one = jnp.int32(1)
    zero = jnp.int32(0)
    return sum(jnp.where(positions >= e, one, zero) for e in (e0, e1, e2, e3))


def needed_span(ends, first):
    e0, e1, e2, e3 = ends
    last = first + ROWS - 1
    low = jnp.where(first >= e2, e2, jnp.where(first >= e1, e1, jnp.where(first >= e0, e0, 0)))
    high = jnp.where(last < e0, e0, jnp.where(last < e1, e1, jnp.where(last < e2, e2, e3)))
    return low, high


def fill_queries(ends, first, own, wqkv_ref, qbd):
    queries = lax.dot_general(
        wqkv_ref[:, :D], own, (((0,), (1,)), ((), ())), preferred_element_type=jnp.float32
    )
    queries = (queries.astype(jnp.bfloat16).astype(jnp.float32) * HEAD_DIM**-0.5).astype(jnp.bfloat16)
    positions = first + lax.broadcasted_iota(jnp.int32, (HEAD_DIM * 2, ROWS), 1)
    slots = lax.broadcasted_iota(jnp.int32, (HEAD_DIM * 2, ROWS), 0)
    same = (doc_of(ends, positions) == slots) | (slots >= DOCS)
    penalty = jnp.where(same, 0.0, PENALTY).astype(jnp.bfloat16)
    penalties = jnp.concatenate([penalty, penalty], axis=1)
    zero = jnp.zeros((HEAD_DIM, ROWS), jnp.bfloat16)
    for j in range(PAIRS):
        qbd[j, :64, :ROWS] = queries[128 * j : 128 * j + 64, :]
        qbd[j, :64, ROWS:] = zero
        qbd[j, 64:128, :ROWS] = zero
        qbd[j, 64:128, ROWS:] = queries[128 * j + 64 : 128 * j + 128, :]
        qbd[j, 128:, :] = penalties


def attend_block(ends, base, hidden, wqkv_ref, qbd, vt, m_ref, acc_ref):
    keys = jnp.dot(hidden, wqkv_ref[:, D : 2 * D], preferred_element_type=jnp.float32).astype(jnp.bfloat16)
    values = lax.dot_general(
        wqkv_ref[:, 2 * D :], hidden, (((0,), (1,)), ((), ())), preferred_element_type=jnp.float32
    ).astype(jnp.bfloat16)
    vt[:, :HEAD_DIM, :] = values.reshape(HEADS, HEAD_DIM, ROWS)
    key_doc = doc_of(ends, base + lax.broadcasted_iota(jnp.int32, (ROWS, 128), 0))
    lanes = lax.broadcasted_iota(jnp.int32, (ROWS, 128), 1)
    onehot = jnp.where(key_doc == lanes, 1.0, 0.0).astype(jnp.bfloat16)
    for j in range(PAIRS):
        pair_keys = jnp.concatenate([keys[:, 128 * j : 128 * j + 128], onehot], axis=1)
        scores = jnp.dot(pair_keys, qbd[j], preferred_element_type=jnp.float32)
        old = m_ref[j : j + 1, :]
        new = jnp.maximum(old, jnp.max(scores, axis=0, keepdims=True))
        m_ref[j : j + 1, :] = new
        shrink = jnp.exp(old - new)
        weights = jnp.exp(scores - new).astype(jnp.bfloat16)
        for h in range(2):
            part = slice(ROWS * h, ROWS * h + ROWS)
            mixed = jnp.dot(vt[2 * j + h], weights[:, part], preferred_element_type=jnp.float32)
            acc_ref[2 * j + h] = acc_ref[2 * j + h] * shrink[:, part] + mixed


def fill_ones(vt):
    row = lax.broadcasted_iota(jnp.int32, (HEADS, AUG - HEAD_DIM, ROWS), 1)
    vt[:, HEAD_DIM:, :] = jnp.where(row == 0, 1.0, 0.0).astype(jnp.bfloat16)


def attend_blocks(ends, first, places, blocks, wqkv_ref, qbd, vt, m_ref, acc_ref):
    low, high = needed_span(ends, first)
    for place, block in zip(places, blocks):
        base = place * ROWS

        @pl.when((base < high) & (base + ROWS > low))
        def _():
            attend_block(ends, base, block[...], wqkv_ref, qbd, vt, m_ref, acc_ref)


def first_kernel(lengths_ref, place_ref, own_ref, wqkv_ref, qbd, m_ref, acc_ref, vt):
    place = place_ref[0]
    ends = doc_ends(lengths_ref)
    first = place * ROWS
    fill_queries(ends, first, own_ref[...], wqkv_ref, qbd)
    fill_ones(vt)
    m_ref[...] = jnp.full(m_ref.shape, PENALTY, jnp.float32)
    acc_ref[...] = jnp.zeros(acc_ref.shape, jnp.float32)
    attend_blocks(ends, first, [place], [own_ref], wqkv_ref, qbd, vt, m_ref, acc_ref)


def fold_kernel(sources, lengths_ref, place_ref, wqkv_ref, qbd, m_in, acc_in, *refs):
    blocks, (m_ref, acc_ref, vt) = refs[: len(sources)], refs[len(sources) :]
    place = place_ref[0]
    ends = doc_ends(lengths_ref)
    fill_ones(vt)
    places = [came_from(place ^ flip, hops) for flip, hops in sources]
    attend_blocks(ends, place * ROWS, places, blocks, wqkv_ref, qbd, vt, m_ref, acc_ref)


def last_kernel(
    lengths_ref, place_ref, far_other_ref, wqkv_ref, qbd, m_in, acc_in, own_ref, wout_ref,
    bias_ref, gain_ref, shift_ref, m_ref, acc_ref, encoded_ref, mixed_ref, normal_ref, inverse_ref, pooled_ref,
    vt
):
    place = place_ref[0]
    ends = doc_ends(lengths_ref)
    first = place * ROWS
    fill_ones(vt)
    attend_blocks(ends, first, [came_from(place ^ 1, 2)], [far_other_ref], wqkv_ref, qbd, vt, m_ref, acc_ref)
    acc = acc_ref[...]
    mixed = acc[:, :HEAD_DIM, :] / acc[:, HEAD_DIM : HEAD_DIM + 1, :]
    mixed = mixed.reshape(D, ROWS)
    mixed_ref[...] = mixed.astype(jnp.bfloat16)
    summed = jnp.dot(mixed.T.astype(jnp.bfloat16), wout_ref[...], preferred_element_type=jnp.float32)
    summed = summed + bias_ref[...][None] + own_ref[...].astype(jnp.float32)
    centered = summed - jnp.mean(summed, axis=1, keepdims=True)
    inverse = lax.rsqrt(jnp.mean(centered * centered, axis=1, keepdims=True) + NORM_EPSILON)
    normal = centered * inverse
    normal_ref[...] = normal
    inverse_ref[...] = inverse
    layer = normal * gain_ref[...][None] + shift_ref[...][None]
    encoded_ref[...] = layer.astype(jnp.bfloat16)
    row_doc = doc_of(ends, first + lax.broadcasted_iota(jnp.int32, (ROWS, 1), 0))
    for d in range(DOCS):
        total = jnp.sum(jnp.where(row_doc == d, layer, 0.0), axis=0, keepdims=True)
        pooled_ref[:, d : d + 1, :] = jnp.broadcast_to(total[None], (CTX, 1, D))


def back_kernel(
    lengths_ref, place_ref, pair_ref, pooled_ref, mixed_ref, normal_ref, inverse_ref, gain_ref,
    out_ref
):
    place = place_ref[0]
    data_place = place_ref[1]
    ends = doc_ends(lengths_ref)
    first = place * ROWS
    pooled = pooled_ref[...]
    emb = pooled / jnp.sqrt(jnp.sum(pooled * pooled, axis=1, keepdims=True) + EMBED_EPSILON)
    nt = (((1,), (1,)), ((), ()))
    sims = (
        lax.dot_general(emb, emb, nt, precision=lax.Precision.HIGHEST, preferred_element_type=jnp.float32)
        / SOFTMAX_TEMPER
    )
    columns = lax.broadcasted_iota(jnp.int32, (NDOC, NDOC), 1)
    rows = lax.broadcasted_iota(jnp.int32, (NDOC, NDOC), 0)
    expo = jnp.where(rows == columns, 0.0, jnp.exp(sims))
    totals = 1.0 / jnp.sum(expo, axis=0, keepdims=True)
    half = lax.rem(data_place, 2)
    both_own = pooled_ref[pl.ds(pl.multiple_of((data_place - half) * DOCS, 8), 8), :]
    own = jnp.where(half == 0, both_own[:DOCS], both_own[DOCS:])
    own_norm = jnp.sqrt(jnp.sum(own * own, axis=1, keepdims=True) + EMBED_EPSILON)
    own_emb = own / own_norm
    own_sims = (
        lax.dot_general(own_emb, emb, nt, precision=lax.Precision.HIGHEST, preferred_element_type=jnp.float32)
        / SOFTMAX_TEMPER
    )
    slots = lax.broadcasted_iota(jnp.int32, (DOCS, NDOC), 0)
    lanes = lax.broadcasted_iota(jnp.int32, (DOCS, NDOC), 1)
    own_expo = jnp.where(lanes == slots + data_place * DOCS, 0.0, jnp.exp(own_sims))
    own_totals = 1.0 / jnp.sum(own_expo, axis=1, keepdims=True)
    partner = jnp.where(
        slots == 0, pair_ref[0, 0],
        jnp.where(slots == 1, pair_ref[0, 1], jnp.where(slots == 2, pair_ref[0, 2], pair_ref[0, 3])),
    )
    both = own_expo * (own_totals + totals) - jnp.where(lanes == partner, 2.0, 0.0)
    emb_grad = (
        jnp.dot(both, emb, precision=lax.Precision.HIGHEST, preferred_element_type=jnp.float32) / SOFTMAX_TEMPER
    )
    pooled_grad = (emb_grad - own_emb * jnp.sum(own_emb * emb_grad, axis=1, keepdims=True)) / own_norm
    slot = lax.broadcasted_iota(jnp.int32, (DOCS, 1), 0)
    length = jnp.where(
        slot == 0, lengths_ref[0, 0],
        jnp.where(slot == 1, lengths_ref[0, 1], jnp.where(slot == 2, lengths_ref[0, 2], lengths_ref[0, 3])),
    ).astype(jnp.float32)
    scaled = pooled_grad / length * gain_ref[...][None]
    row_doc = doc_of(ends, first + lax.broadcasted_iota(jnp.int32, (ROWS, 1), 0))
    spread = jnp.where(
        row_doc == 0, scaled[0:1],
        jnp.where(row_doc == 1, scaled[1:2], jnp.where(row_doc == 2, scaled[2:3], scaled[3:4])),
    )
    normal = normal_ref[...]
    grad = inverse_ref[...] * (
        spread
        - jnp.mean(spread, axis=1, keepdims=True)
        - normal * jnp.mean(spread * normal, axis=1, keepdims=True)
    )
    out_ref[...] = jnp.dot(
        mixed_ref[...], grad.astype(jnp.bfloat16), preferred_element_type=jnp.float32
    ).astype(jnp.bfloat16)


SMEM = pl.BlockSpec(memory_space=pltpu.SMEM)
VMEM = pl.BlockSpec(memory_space=pltpu.VMEM)


def call(kernel, name, smem, vmem, outs, scratch, flops, aliases={}):
    return pl.pallas_call(
        kernel,
        name=name,
        out_shape=[jax.ShapeDtypeStruct(s, t) for s, t in outs],
        in_specs=[SMEM] * len(smem) + [VMEM] * len(vmem),
        out_specs=[VMEM] * len(outs),
        scratch_shapes=[pltpu.VMEM(s, t) for s, t in scratch],
        input_output_aliases=aliases,
        cost_estimate=pl.CostEstimate(flops=flops, bytes_accessed=1 << 26, transcendentals=0),
        compiler_params=pltpu.CompilerParams(vmem_limit_bytes=VMEM_LIMIT),
    )(*smem, *vmem)


def copies(value, axis, count):
    return lax.all_to_all(jnp.broadcast_to(value[None], (count,) + value.shape), axis, 0, 0, tiled=True)


def per_device(hidden_in, w_qkv, w_out, b_out, ln_gain, ln_bias, doc_lengths, pair_of):
    f32, bf16 = jnp.float32, jnp.bfloat16
    own = hidden_in[0]
    places = jnp.stack([lax.axis_index("ctx"), lax.axis_index("dp")]).astype(jnp.int32)
    smem = [doc_lengths, places]
    state = [((8, 2 * ROWS), f32), ((HEADS, AUG, ROWS), f32)]
    work = [((HEADS, AUG, ROWS), bf16)]
    held = ((PAIRS, 256, 2 * ROWS), bf16)

    def fold(name, sources, blocks, m, acc):
        return call(
            functools.partial(fold_kernel, sources), name, smem, [w_qkv, qbd, m, acc, *blocks], state, work,
            1 << 34, {4: 0, 5: 1},
        )

    near = lax.ppermute(own, "ctx", AROUND)
    other = lax.ppermute(own, "ctx", CORE_SWAP)
    qbd, m, acc = call(first_kernel, "first", smem, [own, w_qkv], [held] + state, work, 1 << 34)
    own_later, m = lax.optimization_barrier((own, m))
    behind = lax.ppermute(own_later, "ctx", BACK)
    m, acc = fold("other", [(1, 0)], [other], m, acc)
    near, m = lax.optimization_barrier((near, m))
    far = lax.ppermute(near, "ctx", AROUND)
    near_other = lax.ppermute(near, "ctx", CORE_SWAP)
    m, acc = fold("near", [(0, 1)], [near], m, acc)
    near_other, m = lax.optimization_barrier((near_other, m))
    m, acc = fold("near_other", [(1, 1)], [near_other], m, acc)
    behind, m = lax.optimization_barrier((behind, m))
    behind_other = lax.ppermute(behind, "ctx", CORE_SWAP)
    m, acc = fold("behind", [(0, -1)], [behind], m, acc)
    behind_other, m = lax.optimization_barrier((behind_other, m))
    m, acc = fold("behind_other", [(1, -1)], [behind_other], m, acc)
    far, m = lax.optimization_barrier((far, m))
    far_other = lax.ppermute(far, "ctx", CORE_SWAP)
    m, acc = fold("far", [(0, 2)], [far], m, acc)
    far_other, m = lax.optimization_barrier((far_other, m))
    _, _, encoded, mixed, normal, inverse, partials = call(
        last_kernel,
        "last",
        smem,
        [far_other, w_qkv, qbd, m, acc, own, w_out, b_out, ln_gain, ln_bias],
        state
        + [((ROWS, D), bf16), ((D, ROWS), bf16), ((ROWS, D), f32), ((ROWS, 1), f32), ((CTX, DOCS, D), f32)],
        work,
        1 << 34,
        {5: 0, 6: 1},
    )
    partials = lax.all_to_all(partials, "ctx", 0, 0, tiled=True)
    pooled = jnp.sum(partials, axis=0) / doc_lengths[0].astype(f32)[:, None]
    every = copies(pooled, "dp", DP).reshape(NDOC, D)
    (term,) = call(
        back_kernel,
        "back",
        smem + [pair_of],
        [every, mixed, normal, inverse, ln_gain],
        [((D, D), bf16)],
        [],
        1 << 34,
    )
    share = D // DP
    pieces = lax.all_to_all(term.reshape(DP, share, D), "dp", 0, 0, tiled=True)
    piece = jnp.sum(pieces.astype(f32), axis=0)
    grad_out = jnp.sum(copies(piece.astype(bf16), "ctx", CTX).astype(f32), axis=0)
    return (encoded[None], grad_out)


def solution(mesh):
    return jax.shard_map(
        per_device,
        mesh=mesh,
        in_specs=(P("dp", "ctx", None), P(), P(), P(), P(), P(), P("dp", None), P("dp", None)),
        out_specs=(P("dp", "ctx", None), P("dp", None)),
        check_vma=False,
    )
```

```python
import functools

import jax
import jax.numpy as jnp
from jax import lax
from jax.experimental import pallas as pl
from jax.experimental.pallas import tpu as pltpu
from jax.sharding import PartitionSpec as P

D = 768
HEADS = 12
HEAD_DIM = 64
PAIRS = HEADS // 2
DOCS = 4
NDOC = 128
ROWS = 256
CTX = 8
DP = 32
AUG = 80

SOFTMAX_TEMPER = 0.05
NORM_EPSILON = 1e-05
EMBED_EPSILON = 1e-06
PENALTY = -1e30

VMEM_LIMIT = 24 * 1024 * 1024

CORE_SWAP = [(c, c ^ 1) for c in range(CTX)]
AROUND = [(c, (c + 2) % CTX if c % 2 == 0 else (c - 2) % CTX) for c in range(CTX)]
BACK = [(b, a) for a, b in AROUND]


def came_from(place, hops):
    step = 2 * hops
    return lax.rem(jnp.where(lax.rem(place, 2) == 0, place - step, place + step) + 2 * CTX, CTX)


def doc_ends(lengths_ref):
    e0 = lengths_ref[0, 0]
    e1 = e0 + lengths_ref[0, 1]
    e2 = e1 + lengths_ref[0, 2]
    e3 = e2 + lengths_ref[0, 3]
    return e0, e1, e2, e3


def doc_of(ends, positions):
    e0, e1, e2, e3 = ends
    one = jnp.int32(1)
    zero = jnp.int32(0)
    return sum(jnp.where(positions >= e, one, zero) for e in (e0, e1, e2, e3))


def needed_span(ends, first):
    e0, e1, e2, e3 = ends
    last = first + ROWS - 1
    low = jnp.where(first >= e2, e2, jnp.where(first >= e1, e1, jnp.where(first >= e0, e0, 0)))
    high = jnp.where(last < e0, e0, jnp.where(last < e1, e1, jnp.where(last < e2, e2, e3)))
    return low, high


def fill_queries(ends, first, own, wqkv_ref, qbd):
    queries = lax.dot_general(
        wqkv_ref[:, :D], own, (((0,), (1,)), ((), ())), preferred_element_type=jnp.float32
    )
    queries = (queries.astype(jnp.bfloat16).astype(jnp.float32) * HEAD_DIM**-0.5).astype(jnp.bfloat16)
    positions = first + lax.broadcasted_iota(jnp.int32, (HEAD_DIM * 2, ROWS), 1)
    slots = lax.broadcasted_iota(jnp.int32, (HEAD_DIM * 2, ROWS), 0)
    same = (doc_of(ends, positions) == slots) | (slots >= DOCS)
    penalty = jnp.where(same, 0.0, PENALTY).astype(jnp.bfloat16)
    penalties = jnp.concatenate([penalty, penalty], axis=1)
    zero = jnp.zeros((HEAD_DIM, ROWS), jnp.bfloat16)
    for j in range(PAIRS):
        qbd[j, :64, :ROWS] = queries[128 * j : 128 * j + 64, :]
        qbd[j, :64, ROWS:] = zero
        qbd[j, 64:128, :ROWS] = zero
        qbd[j, 64:128, ROWS:] = queries[128 * j + 64 : 128 * j + 128, :]
        qbd[j, 128:, :] = penalties


def attend_block(ends, base, hidden, wqkv_ref, qbd, vt, m_ref, acc_ref):
    keys = jnp.dot(hidden, wqkv_ref[:, D : 2 * D], preferred_element_type=jnp.float32).astype(jnp.bfloat16)
    values = lax.dot_general(
        wqkv_ref[:, 2 * D :], hidden, (((0,), (1,)), ((), ())), preferred_element_type=jnp.float32
    ).astype(jnp.bfloat16)
    vt[:, :HEAD_DIM, :] = values.reshape(HEADS, HEAD_DIM, ROWS)
    key_doc = doc_of(ends, base + lax.broadcasted_iota(jnp.int32, (ROWS, 128), 0))
    lanes = lax.broadcasted_iota(jnp.int32, (ROWS, 128), 1)
    onehot = jnp.where(key_doc == lanes, 1.0, 0.0).astype(jnp.bfloat16)
    for j in range(PAIRS):
        pair_keys = jnp.concatenate([keys[:, 128 * j : 128 * j + 128], onehot], axis=1)
        scores = jnp.dot(pair_keys, qbd[j], preferred_element_type=jnp.float32)
        old = m_ref[j : j + 1, :]
        new = jnp.maximum(old, jnp.max(scores, axis=0, keepdims=True))
        m_ref[j : j + 1, :] = new
        shrink = jnp.exp(old - new)
        weights = jnp.exp(scores - new).astype(jnp.bfloat16)
        for h in range(2):
            part = slice(ROWS * h, ROWS * h + ROWS)
            mixed = jnp.dot(vt[2 * j + h], weights[:, part], preferred_element_type=jnp.float32)
            acc_ref[2 * j + h] = acc_ref[2 * j + h] * shrink[:, part] + mixed


def fill_ones(vt):
    row = lax.broadcasted_iota(jnp.int32, (HEADS, AUG - HEAD_DIM, ROWS), 1)
    vt[:, HEAD_DIM:, :] = jnp.where(row == 0, 1.0, 0.0).astype(jnp.bfloat16)


def attend_blocks(ends, first, places, blocks, wqkv_ref, qbd, vt, m_ref, acc_ref):
    low, high = needed_span(ends, first)
    for place, block in zip(places, blocks):
        base = place * ROWS

        @pl.when((base < high) & (base + ROWS > low))
        def _():
            attend_block(ends, base, block[...], wqkv_ref, qbd, vt, m_ref, acc_ref)


def first_kernel(lengths_ref, place_ref, own_ref, wqkv_ref, qbd, m_ref, acc_ref, vt):
    place = place_ref[0]
    ends = doc_ends(lengths_ref)
    first = place * ROWS
    fill_queries(ends, first, own_ref[...], wqkv_ref, qbd)
    fill_ones(vt)
    m_ref[...] = jnp.full(m_ref.shape, PENALTY, jnp.float32)
    acc_ref[...] = jnp.zeros(acc_ref.shape, jnp.float32)
    attend_blocks(ends, first, [place], [own_ref], wqkv_ref, qbd, vt, m_ref, acc_ref)


def fold_kernel(sources, lengths_ref, place_ref, wqkv_ref, qbd, m_in, acc_in, *refs):
    blocks, (m_ref, acc_ref, vt) = refs[: len(sources)], refs[len(sources) :]
    place = place_ref[0]
    ends = doc_ends(lengths_ref)
    fill_ones(vt)
    places = [came_from(place ^ flip, hops) for flip, hops in sources]
    attend_blocks(ends, place * ROWS, places, blocks, wqkv_ref, qbd, vt, m_ref, acc_ref)


def last_kernel(
    lengths_ref, place_ref, far_other_ref, wqkv_ref, qbd, m_in, acc_in, own_ref, wout_ref,
    bias_ref, gain_ref, shift_ref, m_ref, acc_ref, encoded_ref, mixed_ref, normal_ref, inverse_ref, pooled_ref,
    vt
):
    place = place_ref[0]
    ends = doc_ends(lengths_ref)
    first = place * ROWS
    fill_ones(vt)
    attend_blocks(ends, first, [came_from(place ^ 1, 2)], [far_other_ref], wqkv_ref, qbd, vt, m_ref, acc_ref)
    acc = acc_ref[...]
    mixed = acc[:, :HEAD_DIM, :] / acc[:, HEAD_DIM : HEAD_DIM + 1, :]
    mixed = mixed.reshape(D, ROWS)
    mixed_ref[...] = mixed.astype(jnp.bfloat16)
    summed = jnp.dot(mixed.T.astype(jnp.bfloat16), wout_ref[...], preferred_element_type=jnp.float32)
    summed = summed + bias_ref[...][None] + own_ref[...].astype(jnp.float32)
    centered = summed - jnp.mean(summed, axis=1, keepdims=True)
    inverse = lax.rsqrt(jnp.mean(centered * centered, axis=1, keepdims=True) + NORM_EPSILON)
    normal = centered * inverse
    normal_ref[...] = normal
    inverse_ref[...] = inverse
    layer = normal * gain_ref[...][None] + shift_ref[...][None]
    encoded_ref[...] = layer.astype(jnp.bfloat16)
    row_doc = doc_of(ends, first + lax.broadcasted_iota(jnp.int32, (ROWS, 1), 0))
    for d in range(DOCS):
        pooled_ref[d : d + 1, :] = jnp.sum(
            jnp.where(row_doc == d, layer, 0.0), axis=0, keepdims=True
        )


def back_kernel(
    lengths_ref, place_ref, pair_ref, pooled_ref, mixed_ref, normal_ref, inverse_ref, gain_ref,
    out_ref
):
    place = place_ref[0]
    data_place = place_ref[1]
    ends = doc_ends(lengths_ref)
    first = place * ROWS
    pooled = pooled_ref[...]
    emb = pooled / jnp.sqrt(jnp.sum(pooled * pooled, axis=1, keepdims=True) + EMBED_EPSILON)
    nt = (((1,), (1,)), ((), ()))
    sims = (
        lax.dot_general(emb, emb, nt, precision=lax.Precision.HIGHEST, preferred_element_type=jnp.float32)
        / SOFTMAX_TEMPER
    )
    columns = lax.broadcasted_iota(jnp.int32, (NDOC, NDOC), 1)
    rows = lax.broadcasted_iota(jnp.int32, (NDOC, NDOC), 0)
    expo = jnp.where(rows == columns, 0.0, jnp.exp(sims))
    totals = 1.0 / jnp.sum(expo, axis=0, keepdims=True)
    half = lax.rem(data_place, 2)
    both_own = pooled_ref[pl.ds(pl.multiple_of((data_place - half) * DOCS, 8), 8), :]
    own = jnp.where(half == 0, both_own[:DOCS], both_own[DOCS:])
    own_norm = jnp.sqrt(jnp.sum(own * own, axis=1, keepdims=True) + EMBED_EPSILON)
    own_emb = own / own_norm
    own_sims = (
        lax.dot_general(own_emb, emb, nt, precision=lax.Precision.HIGHEST, preferred_element_type=jnp.float32)
        / SOFTMAX_TEMPER
    )
    slots = lax.broadcasted_iota(jnp.int32, (DOCS, NDOC), 0)
    lanes = lax.broadcasted_iota(jnp.int32, (DOCS, NDOC), 1)
    own_expo = jnp.where(lanes == slots + data_place * DOCS, 0.0, jnp.exp(own_sims))
    own_totals = 1.0 / jnp.sum(own_expo, axis=1, keepdims=True)
    partner = jnp.where(
        slots == 0, pair_ref[0, 0],
        jnp.where(slots == 1, pair_ref[0, 1], jnp.where(slots == 2, pair_ref[0, 2], pair_ref[0, 3])),
    )
    both = own_expo * (own_totals + totals) - jnp.where(lanes == partner, 2.0, 0.0)
    emb_grad = (
        jnp.dot(both, emb, precision=lax.Precision.HIGHEST, preferred_element_type=jnp.float32) / SOFTMAX_TEMPER
    )
    pooled_grad = (emb_grad - own_emb * jnp.sum(own_emb * emb_grad, axis=1, keepdims=True)) / own_norm
    slot = lax.broadcasted_iota(jnp.int32, (DOCS, 1), 0)
    length = jnp.where(
        slot == 0, lengths_ref[0, 0],
        jnp.where(slot == 1, lengths_ref[0, 1], jnp.where(slot == 2, lengths_ref[0, 2], lengths_ref[0, 3])),
    ).astype(jnp.float32)
    scaled = pooled_grad / length * gain_ref[...][None]
    row_doc = doc_of(ends, first + lax.broadcasted_iota(jnp.int32, (ROWS, 1), 0))
    spread = jnp.where(
        row_doc == 0, scaled[0:1],
        jnp.where(row_doc == 1, scaled[1:2], jnp.where(row_doc == 2, scaled[2:3], scaled[3:4])),
    )
    normal = normal_ref[...]
    grad = inverse_ref[...] * (
        spread
        - jnp.mean(spread, axis=1, keepdims=True)
        - normal * jnp.mean(spread * normal, axis=1, keepdims=True)
    )
    out_ref[...] = jnp.dot(
        mixed_ref[...], grad.astype(jnp.bfloat16), preferred_element_type=jnp.float32
    ).astype(jnp.bfloat16)


SMEM = pl.BlockSpec(memory_space=pltpu.SMEM)
VMEM = pl.BlockSpec(memory_space=pltpu.VMEM)


def call(kernel, name, smem, vmem, outs, scratch, flops, aliases={}):
    return pl.pallas_call(
        kernel,
        name=name,
        out_shape=[jax.ShapeDtypeStruct(s, t) for s, t in outs],
        in_specs=[SMEM] * len(smem) + [VMEM] * len(vmem),
        out_specs=[VMEM] * len(outs),
        scratch_shapes=[pltpu.VMEM(s, t) for s, t in scratch],
        input_output_aliases=aliases,
        cost_estimate=pl.CostEstimate(flops=flops, bytes_accessed=1 << 26, transcendentals=0),
        compiler_params=pltpu.CompilerParams(vmem_limit_bytes=VMEM_LIMIT),
    )(*smem, *vmem)


def copies(value, axis, count):
    return lax.all_to_all(jnp.broadcast_to(value[None], (count,) + value.shape), axis, 0, 0, tiled=True)


def swap_add(value):
    return value + lax.ppermute(value, "ctx", CORE_SWAP)


def sum_over_chips(value):
    one, two, three = [
        lax.ppermute(value, "ctx", [(c, (c + 2 * hops) % CTX) for c in range(CTX)]).astype(jnp.float32)
        for hops in (1, 2, 3)
    ]
    return (value.astype(jnp.float32) + two) + (one + three)


def per_device(hidden_in, w_qkv, w_out, b_out, ln_gain, ln_bias, doc_lengths, pair_of):
    f32, bf16 = jnp.float32, jnp.bfloat16
    own = hidden_in[0]
    places = jnp.stack([lax.axis_index("ctx"), lax.axis_index("dp")]).astype(jnp.int32)
    smem = [doc_lengths, places]
    state = [((8, 2 * ROWS), f32), ((HEADS, AUG, ROWS), f32)]
    work = [((HEADS, AUG, ROWS), bf16)]
    held = ((PAIRS, 256, 2 * ROWS), bf16)

    def fold(name, sources, blocks, m, acc):
        return call(
            functools.partial(fold_kernel, sources), name, smem, [w_qkv, qbd, m, acc, *blocks], state, work,
            1 << 34, {4: 0, 5: 1},
        )

    near = lax.ppermute(own, "ctx", AROUND)
    other = lax.ppermute(own, "ctx", CORE_SWAP)
    own_later, other = lax.optimization_barrier((own, other))
    behind = lax.ppermute(own_later, "ctx", BACK)
    qbd, m, acc = call(first_kernel, "first", smem, [own_later, w_qkv], [held] + state, work, 1 << 34)
    m, acc = fold("other", [(1, 0)], [other], m, acc)
    near, m = lax.optimization_barrier((near, m))
    far = lax.ppermute(near, "ctx", AROUND)
    near_other = lax.ppermute(near, "ctx", CORE_SWAP)
    m, acc = fold("near", [(0, 1)], [near], m, acc)
    near_other, m = lax.optimization_barrier((near_other, m))
    m, acc = fold("near_other", [(1, 1)], [near_other], m, acc)
    behind, m = lax.optimization_barrier((behind, m))
    behind_other = lax.ppermute(behind, "ctx", CORE_SWAP)
    m, acc = fold("behind", [(0, -1)], [behind], m, acc)
    behind_other, m = lax.optimization_barrier((behind_other, m))
    m, acc = fold("behind_other", [(1, -1)], [behind_other], m, acc)
    far, m = lax.optimization_barrier((far, m))
    far_other = lax.ppermute(far, "ctx", CORE_SWAP)
    m, acc = fold("far", [(0, 2)], [far], m, acc)
    far_other, m = lax.optimization_barrier((far_other, m))
    _, _, encoded, mixed, normal, inverse, partial = call(
        last_kernel,
        "last",
        smem,
        [far_other, w_qkv, qbd, m, acc, own, w_out, b_out, ln_gain, ln_bias],
        state
        + [((ROWS, D), bf16), ((D, ROWS), bf16), ((ROWS, D), f32), ((ROWS, 1), f32), ((DOCS, D), f32)],
        work,
        1 << 34,
        {5: 0, 6: 1},
    )
    pooled = sum_over_chips(swap_add(partial)) / doc_lengths[0].astype(f32)[:, None]
    every = copies(pooled, "dp", DP).reshape(NDOC, D)
    (term,) = call(
        back_kernel,
        "back",
        smem + [pair_of],
        [every, mixed, normal, inverse, ln_gain],
        [((D, D), bf16)],
        [],
        1 << 34,
    )
    share = D // DP
    pieces = lax.all_to_all(term.reshape(DP, share, D), "dp", 0, 0, tiled=True)
    piece = jnp.sum(pieces.astype(f32), axis=0)
    grad_out = sum_over_chips(swap_add(piece).astype(bf16))
    return (encoded[None], grad_out)


def solution(mesh):
    return jax.shard_map(
        per_device,
        mesh=mesh,
        in_specs=(P("dp", "ctx", None), P(), P(), P(), P(), P(), P("dp", None), P("dp", None)),
        out_specs=(P("dp", "ctx", None), P("dp", None)),
        check_vma=False,
    )
```

```python
import functools

import jax
import jax.numpy as jnp
from jax import lax
from jax.experimental import pallas as pl
from jax.experimental.pallas import tpu as pltpu
from jax.sharding import PartitionSpec as P

D = 768
HEADS = 12
HEAD_DIM = 64
PAIRS = HEADS // 2
DOCS = 4
NDOC = 128
ROWS = 256
CTX = 8
DP = 32
AUG = 80

SOFTMAX_TEMPER = 0.05
NORM_EPSILON = 1e-05
EMBED_EPSILON = 1e-06
PENALTY = -1e30

VMEM_LIMIT = 24 * 1024 * 1024

CORE_SWAP = [(c, c ^ 1) for c in range(CTX)]
AROUND = [(c, (c + 2) % CTX if c % 2 == 0 else (c - 2) % CTX) for c in range(CTX)]
BACK = [(b, a) for a, b in AROUND]


def came_from(place, hops):
    step = 2 * hops
    return lax.rem(jnp.where(lax.rem(place, 2) == 0, place - step, place + step) + 2 * CTX, CTX)


def doc_ends(lengths_ref):
    e0 = lengths_ref[0, 0]
    e1 = e0 + lengths_ref[0, 1]
    e2 = e1 + lengths_ref[0, 2]
    e3 = e2 + lengths_ref[0, 3]
    return e0, e1, e2, e3


def doc_of(ends, positions):
    e0, e1, e2, e3 = ends
    one = jnp.int32(1)
    zero = jnp.int32(0)
    return sum(jnp.where(positions >= e, one, zero) for e in (e0, e1, e2, e3))


def needed_span(ends, first):
    e0, e1, e2, e3 = ends
    last = first + ROWS - 1
    low = jnp.where(first >= e2, e2, jnp.where(first >= e1, e1, jnp.where(first >= e0, e0, 0)))
    high = jnp.where(last < e0, e0, jnp.where(last < e1, e1, jnp.where(last < e2, e2, e3)))
    return low, high


def fill_queries(ends, first, own, wqkv_ref, qbd):
    queries = lax.dot_general(
        wqkv_ref[:, :D], own, (((0,), (1,)), ((), ())), preferred_element_type=jnp.float32
    )
    queries = (queries.astype(jnp.bfloat16).astype(jnp.float32) * HEAD_DIM**-0.5).astype(jnp.bfloat16)
    positions = first + lax.broadcasted_iota(jnp.int32, (HEAD_DIM * 2, ROWS), 1)
    slots = lax.broadcasted_iota(jnp.int32, (HEAD_DIM * 2, ROWS), 0)
    same = (doc_of(ends, positions) == slots) | (slots >= DOCS)
    penalty = jnp.where(same, 0.0, PENALTY).astype(jnp.bfloat16)
    penalties = jnp.concatenate([penalty, penalty], axis=1)
    zero = jnp.zeros((HEAD_DIM, ROWS), jnp.bfloat16)
    for j in range(PAIRS):
        qbd[j, :64, :ROWS] = queries[128 * j : 128 * j + 64, :]
        qbd[j, :64, ROWS:] = zero
        qbd[j, 64:128, :ROWS] = zero
        qbd[j, 64:128, ROWS:] = queries[128 * j + 64 : 128 * j + 128, :]
        qbd[j, 128:, :] = penalties


def attend_block(ends, base, hidden, wqkv_ref, qbd, vt, m_ref, acc_ref):
    keys = jnp.dot(hidden, wqkv_ref[:, D : 2 * D], preferred_element_type=jnp.float32).astype(jnp.bfloat16)
    values = lax.dot_general(
        wqkv_ref[:, 2 * D :], hidden, (((0,), (1,)), ((), ())), preferred_element_type=jnp.float32
    ).astype(jnp.bfloat16)
    vt[:, :HEAD_DIM, :] = values.reshape(HEADS, HEAD_DIM, ROWS)
    key_doc = doc_of(ends, base + lax.broadcasted_iota(jnp.int32, (ROWS, 128), 0))
    lanes = lax.broadcasted_iota(jnp.int32, (ROWS, 128), 1)
    onehot = jnp.where(key_doc == lanes, 1.0, 0.0).astype(jnp.bfloat16)
    for j in range(PAIRS):
        pair_keys = jnp.concatenate([keys[:, 128 * j : 128 * j + 128], onehot], axis=1)
        scores = jnp.dot(pair_keys, qbd[j], preferred_element_type=jnp.float32)
        old = m_ref[j : j + 1, :]
        new = jnp.maximum(old, jnp.max(scores, axis=0, keepdims=True))
        m_ref[j : j + 1, :] = new
        shrink = jnp.exp(old - new)
        weights = jnp.exp(scores - new).astype(jnp.bfloat16)
        for h in range(2):
            part = slice(ROWS * h, ROWS * h + ROWS)
            mixed = jnp.dot(vt[2 * j + h], weights[:, part], preferred_element_type=jnp.float32)
            acc_ref[2 * j + h] = acc_ref[2 * j + h] * shrink[:, part] + mixed


def fill_ones(vt):
    row = lax.broadcasted_iota(jnp.int32, (HEADS, AUG - HEAD_DIM, ROWS), 1)
    vt[:, HEAD_DIM:, :] = jnp.where(row == 0, 1.0, 0.0).astype(jnp.bfloat16)


def attend_blocks(ends, first, places, blocks, wqkv_ref, qbd, vt, m_ref, acc_ref):
    low, high = needed_span(ends, first)
    for place, block in zip(places, blocks):
        base = place * ROWS

        @pl.when((base < high) & (base + ROWS > low))
        def _():
            attend_block(ends, base, block[...], wqkv_ref, qbd, vt, m_ref, acc_ref)


def queries_kernel(lengths_ref, place_ref, own_ref, wqkv_ref, qbd, m_ref, acc_ref):
    ends = doc_ends(lengths_ref)
    fill_queries(ends, place_ref[0] * ROWS, own_ref[...], wqkv_ref, qbd)
    m_ref[...] = jnp.full(m_ref.shape, PENALTY, jnp.float32)
    acc_ref[...] = jnp.zeros(acc_ref.shape, jnp.float32)


def fold_kernel(sources, lengths_ref, place_ref, wqkv_ref, qbd, m_in, acc_in, *refs):
    blocks, (m_ref, acc_ref, vt) = refs[: len(sources)], refs[len(sources) :]
    place = place_ref[0]
    ends = doc_ends(lengths_ref)
    fill_ones(vt)
    places = [came_from(place ^ flip, hops) for flip, hops in sources]
    attend_blocks(ends, place * ROWS, places, blocks, wqkv_ref, qbd, vt, m_ref, acc_ref)


def last_kernel(
    lengths_ref, place_ref, far_other_ref, wqkv_ref, qbd, m_in, acc_in, own_ref, wout_ref,
    bias_ref, gain_ref, shift_ref, m_ref, acc_ref, encoded_ref, mixed_ref, normal_ref, inverse_ref, pooled_ref,
    vt
):
    place = place_ref[0]
    ends = doc_ends(lengths_ref)
    first = place * ROWS
    fill_ones(vt)
    attend_blocks(ends, first, [came_from(place ^ 1, 2)], [far_other_ref], wqkv_ref, qbd, vt, m_ref, acc_ref)
    acc = acc_ref[...]
    mixed = acc[:, :HEAD_DIM, :] / acc[:, HEAD_DIM : HEAD_DIM + 1, :]
    mixed = mixed.reshape(D, ROWS)
    mixed_ref[...] = mixed.astype(jnp.bfloat16)
    summed = jnp.dot(mixed.T.astype(jnp.bfloat16), wout_ref[...], preferred_element_type=jnp.float32)
    summed = summed + bias_ref[...][None] + own_ref[...].astype(jnp.float32)
    centered = summed - jnp.mean(summed, axis=1, keepdims=True)
    inverse = lax.rsqrt(jnp.mean(centered * centered, axis=1, keepdims=True) + NORM_EPSILON)
    normal = centered * inverse
    normal_ref[...] = normal
    inverse_ref[...] = inverse
    layer = normal * gain_ref[...][None] + shift_ref[...][None]
    encoded_ref[...] = layer.astype(jnp.bfloat16)
    row_doc = doc_of(ends, first + lax.broadcasted_iota(jnp.int32, (ROWS, 1), 0))
    for d in range(DOCS):
        pooled_ref[d : d + 1, :] = jnp.sum(
            jnp.where(row_doc == d, layer, 0.0), axis=0, keepdims=True
        )


def back_kernel(
    lengths_ref, place_ref, pair_ref, pooled_ref, mixed_ref, normal_ref, inverse_ref, gain_ref,
    out_ref
):
    place = place_ref[0]
    data_place = place_ref[1]
    ends = doc_ends(lengths_ref)
    first = place * ROWS
    pooled = pooled_ref[...]
    emb = pooled / jnp.sqrt(jnp.sum(pooled * pooled, axis=1, keepdims=True) + EMBED_EPSILON)
    nt = (((1,), (1,)), ((), ()))
    sims = (
        lax.dot_general(emb, emb, nt, precision=lax.Precision.HIGHEST, preferred_element_type=jnp.float32)
        / SOFTMAX_TEMPER
    )
    columns = lax.broadcasted_iota(jnp.int32, (NDOC, NDOC), 1)
    rows = lax.broadcasted_iota(jnp.int32, (NDOC, NDOC), 0)
    expo = jnp.where(rows == columns, 0.0, jnp.exp(sims))
    totals = 1.0 / jnp.sum(expo, axis=0, keepdims=True)
    half = lax.rem(data_place, 2)
    both_own = pooled_ref[pl.ds(pl.multiple_of((data_place - half) * DOCS, 8), 8), :]
    own = jnp.where(half == 0, both_own[:DOCS], both_own[DOCS:])
    own_norm = jnp.sqrt(jnp.sum(own * own, axis=1, keepdims=True) + EMBED_EPSILON)
    own_emb = own / own_norm
    own_sims = (
        lax.dot_general(own_emb, emb, nt, precision=lax.Precision.HIGHEST, preferred_element_type=jnp.float32)
        / SOFTMAX_TEMPER
    )
    slots = lax.broadcasted_iota(jnp.int32, (DOCS, NDOC), 0)
    lanes = lax.broadcasted_iota(jnp.int32, (DOCS, NDOC), 1)
    own_expo = jnp.where(lanes == slots + data_place * DOCS, 0.0, jnp.exp(own_sims))
    own_totals = 1.0 / jnp.sum(own_expo, axis=1, keepdims=True)
    partner = jnp.where(
        slots == 0, pair_ref[0, 0],
        jnp.where(slots == 1, pair_ref[0, 1], jnp.where(slots == 2, pair_ref[0, 2], pair_ref[0, 3])),
    )
    both = own_expo * (own_totals + totals) - jnp.where(lanes == partner, 2.0, 0.0)
    emb_grad = (
        jnp.dot(both, emb, precision=lax.Precision.HIGHEST, preferred_element_type=jnp.float32) / SOFTMAX_TEMPER
    )
    pooled_grad = (emb_grad - own_emb * jnp.sum(own_emb * emb_grad, axis=1, keepdims=True)) / own_norm
    slot = lax.broadcasted_iota(jnp.int32, (DOCS, 1), 0)
    length = jnp.where(
        slot == 0, lengths_ref[0, 0],
        jnp.where(slot == 1, lengths_ref[0, 1], jnp.where(slot == 2, lengths_ref[0, 2], lengths_ref[0, 3])),
    ).astype(jnp.float32)
    scaled = pooled_grad / length * gain_ref[...][None]
    row_doc = doc_of(ends, first + lax.broadcasted_iota(jnp.int32, (ROWS, 1), 0))
    spread = jnp.where(
        row_doc == 0, scaled[0:1],
        jnp.where(row_doc == 1, scaled[1:2], jnp.where(row_doc == 2, scaled[2:3], scaled[3:4])),
    )
    normal = normal_ref[...]
    grad = inverse_ref[...] * (
        spread
        - jnp.mean(spread, axis=1, keepdims=True)
        - normal * jnp.mean(spread * normal, axis=1, keepdims=True)
    )
    out_ref[...] = jnp.dot(
        mixed_ref[...], grad.astype(jnp.bfloat16), preferred_element_type=jnp.float32
    ).astype(jnp.bfloat16)


SMEM = pl.BlockSpec(memory_space=pltpu.SMEM)
VMEM = pl.BlockSpec(memory_space=pltpu.VMEM)


def call(kernel, name, smem, vmem, outs, scratch, flops, aliases={}):
    return pl.pallas_call(
        kernel,
        name=name,
        out_shape=[jax.ShapeDtypeStruct(s, t) for s, t in outs],
        in_specs=[SMEM] * len(smem) + [VMEM] * len(vmem),
        out_specs=[VMEM] * len(outs),
        scratch_shapes=[pltpu.VMEM(s, t) for s, t in scratch],
        input_output_aliases=aliases,
        cost_estimate=pl.CostEstimate(flops=flops, bytes_accessed=1 << 26, transcendentals=0),
        compiler_params=pltpu.CompilerParams(vmem_limit_bytes=VMEM_LIMIT),
    )(*smem, *vmem)


def copies(value, axis, count):
    return lax.all_to_all(jnp.broadcast_to(value[None], (count,) + value.shape), axis, 0, 0, tiled=True)


def swap_add(value):
    return value + lax.ppermute(value, "ctx", CORE_SWAP)


def sum_over_chips(value):
    one, two, three = [
        lax.ppermute(value, "ctx", [(c, (c + 2 * hops) % CTX) for c in range(CTX)]).astype(jnp.float32)
        for hops in (1, 2, 3)
    ]
    return (value.astype(jnp.float32) + two) + (one + three)


def per_device(hidden_in, w_qkv, w_out, b_out, ln_gain, ln_bias, doc_lengths, pair_of):
    f32, bf16 = jnp.float32, jnp.bfloat16
    own = hidden_in[0]
    places = jnp.stack([lax.axis_index("ctx"), lax.axis_index("dp")]).astype(jnp.int32)
    smem = [doc_lengths, places]
    state = [((8, 2 * ROWS), f32), ((HEADS, AUG, ROWS), f32)]
    work = [((HEADS, AUG, ROWS), bf16)]
    held = ((PAIRS, 256, 2 * ROWS), bf16)

    def fold(name, sources, blocks, m, acc):
        return call(
            functools.partial(fold_kernel, sources), name, smem, [w_qkv, qbd, m, acc, *blocks], state, work,
            1 << 34, {4: 0, 5: 1},
        )

    near = lax.ppermute(own, "ctx", AROUND)
    other = lax.ppermute(own, "ctx", CORE_SWAP)
    qbd, m, acc = call(queries_kernel, "queries", smem, [own, w_qkv], [held] + state, [], 1 << 34)
    own_later, m = lax.optimization_barrier((own, m))
    behind = lax.ppermute(own_later, "ctx", BACK)
    m, acc = fold("own", [(0, 0)], [own], m, acc)
    m, acc = fold("other", [(1, 0)], [other], m, acc)
    near, m = lax.optimization_barrier((near, m))
    far = lax.ppermute(near, "ctx", AROUND)
    near_other = lax.ppermute(near, "ctx", CORE_SWAP)
    m, acc = fold("near", [(0, 1)], [near], m, acc)
    near_other, m = lax.optimization_barrier((near_other, m))
    m, acc = fold("near_other", [(1, 1)], [near_other], m, acc)
    behind, m = lax.optimization_barrier((behind, m))
    behind_other = lax.ppermute(behind, "ctx", CORE_SWAP)
    m, acc = fold("behind", [(0, -1)], [behind], m, acc)
    behind_other, m = lax.optimization_barrier((behind_other, m))
    m, acc = fold("behind_other", [(1, -1)], [behind_other], m, acc)
    far, m = lax.optimization_barrier((far, m))
    far_other = lax.ppermute(far, "ctx", CORE_SWAP)
    m, acc = fold("far", [(0, 2)], [far], m, acc)
    far_other, m = lax.optimization_barrier((far_other, m))
    _, _, encoded, mixed, normal, inverse, partial = call(
        last_kernel,
        "last",
        smem,
        [far_other, w_qkv, qbd, m, acc, own, w_out, b_out, ln_gain, ln_bias],
        state
        + [((ROWS, D), bf16), ((D, ROWS), bf16), ((ROWS, D), f32), ((ROWS, 1), f32), ((DOCS, D), f32)],
        work,
        1 << 34,
        {5: 0, 6: 1},
    )
    pooled = sum_over_chips(swap_add(partial)) / doc_lengths[0].astype(f32)[:, None]
    every = copies(pooled, "dp", DP).reshape(NDOC, D)
    (term,) = call(
        back_kernel,
        "back",
        smem + [pair_of],
        [every, mixed, normal, inverse, ln_gain],
        [((D, D), bf16)],
        [],
        1 << 34,
    )
    share = D // DP
    pieces = lax.all_to_all(term.reshape(DP, share, D), "dp", 0, 0, tiled=True)
    piece = jnp.sum(pieces.astype(f32), axis=0)
    grad_out = sum_over_chips(swap_add(piece).astype(bf16))
    return (encoded[None], grad_out)


def solution(mesh):
    return jax.shard_map(
        per_device,
        mesh=mesh,
        in_specs=(P("dp", "ctx", None), P(), P(), P(), P(), P(), P("dp", None), P("dp", None)),
        out_specs=(P("dp", "ctx", None), P("dp", None)),
        check_vma=False,
    )
```

```python
import functools

import jax
import jax.numpy as jnp
from jax import lax
from jax.experimental import pallas as pl
from jax.experimental.pallas import tpu as pltpu
from jax.sharding import PartitionSpec as P

D = 768
HEADS = 12
HEAD_DIM = 64
PAIRS = HEADS // 2
DOCS = 4
NDOC = 128
ROWS = 256
CTX = 8
DP = 32
AUG = 80

SOFTMAX_TEMPER = 0.05
NORM_EPSILON = 1e-05
EMBED_EPSILON = 1e-06
PENALTY = -1e30

VMEM_LIMIT = 24 * 1024 * 1024

CORE_SWAP = [(c, c ^ 1) for c in range(CTX)]
AROUND = [(c, (c + 2) % CTX if c % 2 == 0 else (c - 2) % CTX) for c in range(CTX)]
BACK = [(b, a) for a, b in AROUND]


def came_from(place, hops):
    step = 2 * hops
    return lax.rem(jnp.where(lax.rem(place, 2) == 0, place - step, place + step) + 2 * CTX, CTX)


SOURCES = [(0, 0), (1, 0), (0, 1), (1, 1), (0, -1), (1, -1), (0, 2), (1, 2)]


def doc_ends(lengths_ref):
    e0 = lengths_ref[0, 0]
    e1 = e0 + lengths_ref[0, 1]
    e2 = e1 + lengths_ref[0, 2]
    e3 = e2 + lengths_ref[0, 3]
    return e0, e1, e2, e3


def doc_of(ends, positions):
    e0, e1, e2, e3 = ends
    one = jnp.int32(1)
    zero = jnp.int32(0)
    return sum(jnp.where(positions >= e, one, zero) for e in (e0, e1, e2, e3))


def needed_span(ends, first):
    e0, e1, e2, e3 = ends
    last = first + ROWS - 1
    low = jnp.where(first >= e2, e2, jnp.where(first >= e1, e1, jnp.where(first >= e0, e0, 0)))
    high = jnp.where(last < e0, e0, jnp.where(last < e1, e1, jnp.where(last < e2, e2, e3)))
    return low, high


def fill_queries(ends, first, own, wqkv_ref, qbd):
    queries = lax.dot_general(
        wqkv_ref[:, :D], own, (((0,), (1,)), ((), ())), preferred_element_type=jnp.float32
    )
    queries = (queries.astype(jnp.bfloat16).astype(jnp.float32) * HEAD_DIM**-0.5).astype(jnp.bfloat16)
    positions = first + lax.broadcasted_iota(jnp.int32, (HEAD_DIM * 2, ROWS), 1)
    slots = lax.broadcasted_iota(jnp.int32, (HEAD_DIM * 2, ROWS), 0)
    same = (doc_of(ends, positions) == slots) | (slots >= DOCS)
    penalty = jnp.where(same, 0.0, PENALTY).astype(jnp.bfloat16)
    penalties = jnp.concatenate([penalty, penalty], axis=1)
    zero = jnp.zeros((HEAD_DIM, ROWS), jnp.bfloat16)
    for j in range(PAIRS):
        qbd[j, :64, :ROWS] = queries[128 * j : 128 * j + 64, :]
        qbd[j, :64, ROWS:] = zero
        qbd[j, 64:128, :ROWS] = zero
        qbd[j, 64:128, ROWS:] = queries[128 * j + 64 : 128 * j + 128, :]
        qbd[j, 128:, :] = penalties


def project(ends, bases, blocks, wqkv_ref, vt):
    rows = ROWS * len(blocks)
    hidden = jnp.concatenate(blocks, axis=0) if len(blocks) > 1 else blocks[0]
    keys = jnp.dot(hidden, wqkv_ref[:, D : 2 * D], preferred_element_type=jnp.float32).astype(jnp.bfloat16)
    values = lax.dot_general(
        wqkv_ref[:, 2 * D :], hidden, (((0,), (1,)), ((), ())), preferred_element_type=jnp.float32
    ).astype(jnp.bfloat16)
    vt[:, :HEAD_DIM, :rows] = values.reshape(HEADS, HEAD_DIM, rows)
    offsets = lax.broadcasted_iota(jnp.int32, (ROWS, 128), 0)
    lanes = lax.broadcasted_iota(jnp.int32, (ROWS, 128), 1)
    onehots = [
        jnp.where(doc_of(ends, base + offsets) == lanes, 1.0, 0.0).astype(jnp.bfloat16) for base in bases
    ]
    return keys, jnp.concatenate(onehots, axis=0) if len(blocks) > 1 else onehots[0]


def pair_scores(keys, onehot, qbd, j):
    pair_keys = jnp.concatenate([keys[:, 128 * j : 128 * j + 128], onehot], axis=1)
    return jnp.dot(pair_keys, qbd[j], preferred_element_type=jnp.float32)


def attend_plain(ends, bases, blocks, wqkv_ref, qbd, vt, acc_ref):
    rows = ROWS * len(blocks)
    keys, onehot = project(ends, bases, blocks, wqkv_ref, vt)
    for j in range(PAIRS):
        weights = jnp.exp(pair_scores(keys, onehot, qbd, j)).astype(jnp.bfloat16)
        for h in range(2):
            part = slice(ROWS * h, ROWS * h + ROWS)
            acc_ref[2 * j + h] += jnp.dot(
                vt[2 * j + h, :, :rows], weights[:, part], preferred_element_type=jnp.float32
            )


def attend_shifted(ends, base, block, wqkv_ref, qbd, vt, m_ref, acc_ref):
    keys, onehot = project(ends, [base], [block], wqkv_ref, vt)
    for j in range(PAIRS):
        scores = pair_scores(keys, onehot, qbd, j)
        old = m_ref[j : j + 1, :]
        new = jnp.maximum(old, jnp.max(scores, axis=0, keepdims=True))
        m_ref[j : j + 1, :] = new
        shrink = jnp.exp(old - new)
        weights = jnp.exp(scores - new).astype(jnp.bfloat16)
        for h in range(2):
            part = slice(ROWS * h, ROWS * h + ROWS)
            mixed = jnp.dot(vt[2 * j + h, :, :ROWS], weights[:, part], preferred_element_type=jnp.float32)
            acc_ref[2 * j + h] = acc_ref[2 * j + h] * shrink[:, part] + mixed


def fill_ones(vt):
    row = lax.broadcasted_iota(jnp.int32, (HEADS, AUG - HEAD_DIM, vt.shape[2]), 1)
    vt[:, HEAD_DIM:, :] = jnp.where(row == 0, 1.0, 0.0).astype(jnp.bfloat16)


def attend_blocks(ends, first, places, blocks, wqkv_ref, qbd, vt, acc_ref):
    low, high = needed_span(ends, first)
    bases = [place * ROWS for place in places]
    wanted = [(base < high) & (base + ROWS > low) for base in bases]

    def attend(which):
        attend_plain(
            ends, [bases[i] for i in which], [blocks[i][...] for i in which], wqkv_ref, qbd, vt, acc_ref
        )

    if len(blocks) == 1:
        pl.when(wanted[0])(lambda: attend([0]))
    else:
        one, two = wanted
        pl.when(one & two)(lambda: attend([0, 1]))
        pl.when(one & jnp.logical_not(two))(lambda: attend([0]))
        pl.when(two & jnp.logical_not(one))(lambda: attend([1]))


def queries_kernel(lengths_ref, place_ref, own_ref, wqkv_ref, qbd, acc_ref):
    ends = doc_ends(lengths_ref)
    fill_queries(ends, place_ref[0] * ROWS, own_ref[...], wqkv_ref, qbd)
    acc_ref[...] = jnp.zeros(acc_ref.shape, jnp.float32)


def fold_kernel(sources, lengths_ref, place_ref, wqkv_ref, qbd, acc_in, *refs):
    blocks, (acc_ref, vt) = refs[: len(sources)], refs[len(sources) :]
    place = place_ref[0]
    ends = doc_ends(lengths_ref)
    fill_ones(vt)
    places = [came_from(place ^ flip, hops) for flip, hops in sources]
    attend_blocks(ends, place * ROWS, places, blocks, wqkv_ref, qbd, vt, acc_ref)


def in_range(acc):
    sums = acc[:, HEAD_DIM, :]
    good = jnp.where((sums >= 1e-12) & (sums <= 1e12), 1.0, 0.0)
    finite = jnp.where(jnp.abs(acc) <= 1e38, 1.0, 0.0)
    return jnp.minimum(jnp.min(good), jnp.min(finite)) > 0.5


def attend_again(ends, place, blocks, wqkv_ref, qbd, vt, acc_ref, m_ref, held):
    for i, (flip, hops) in enumerate(SOURCES):
        pltpu.sync_copy(blocks[i], held.at[i])
    m_ref[...] = jnp.full(m_ref.shape, PENALTY, jnp.float32)
    acc_ref[...] = jnp.zeros(acc_ref.shape, jnp.float32)
    low, high = needed_span(ends, place * ROWS)

    def step(i, carry):
        base = jnp.int32(0)
        for k, (flip, hops) in enumerate(SOURCES):
            base = jnp.where(i == k, came_from(place ^ flip, hops) * ROWS, base)

        @pl.when((base < high) & (base + ROWS > low))
        def _():
            attend_shifted(ends, base, held[i], wqkv_ref, qbd, vt, m_ref, acc_ref)

        return carry

    lax.fori_loop(0, len(SOURCES), step, 0)


def last_kernel(
    lengths_ref, place_ref, far_other_ref, wqkv_ref, qbd, acc_in, own_ref, wout_ref, bias_ref, gain_ref, shift_ref,
    *refs
):
    blocks, refs = refs[: len(SOURCES)], refs[len(SOURCES) :]
    acc_ref, encoded_ref, mixed_ref, normal_ref, inverse_ref, pooled_ref, vt, m_ref, held = refs
    place = place_ref[0]
    ends = doc_ends(lengths_ref)
    first = place * ROWS
    fill_ones(vt)
    flip, hops = SOURCES[-1]
    attend_blocks(ends, first, [came_from(place ^ flip, hops)], [far_other_ref], wqkv_ref, qbd, vt, acc_ref)

    @pl.when(jnp.logical_not(in_range(acc_ref[...])))
    def _():
        attend_again(ends, place, blocks, wqkv_ref, qbd, vt, acc_ref, m_ref, held)

    acc = acc_ref[...]
    mixed = acc[:, :HEAD_DIM, :] / acc[:, HEAD_DIM : HEAD_DIM + 1, :]
    mixed = mixed.reshape(D, ROWS)
    mixed_ref[...] = mixed.astype(jnp.bfloat16)
    summed = jnp.dot(mixed.T.astype(jnp.bfloat16), wout_ref[...], preferred_element_type=jnp.float32)
    summed = summed + bias_ref[...][None] + own_ref[...].astype(jnp.float32)
    centered = summed - jnp.mean(summed, axis=1, keepdims=True)
    inverse = lax.rsqrt(jnp.mean(centered * centered, axis=1, keepdims=True) + NORM_EPSILON)
    normal = centered * inverse
    normal_ref[...] = normal
    inverse_ref[...] = inverse
    layer = normal * gain_ref[...][None] + shift_ref[...][None]
    encoded_ref[...] = layer.astype(jnp.bfloat16)
    row_doc = doc_of(ends, first + lax.broadcasted_iota(jnp.int32, (ROWS, 1), 0))
    for d in range(DOCS):
        pooled_ref[d : d + 1, :] = jnp.sum(
            jnp.where(row_doc == d, layer, 0.0), axis=0, keepdims=True
        )


def back_kernel(
    lengths_ref, place_ref, pair_ref, pooled_ref, mixed_ref, normal_ref, inverse_ref, gain_ref,
    out_ref, expo_ref
):
    place = place_ref[0]
    data_place = place_ref[1]
    ends = doc_ends(lengths_ref)
    first = place * ROWS
    pooled = pooled_ref[...]
    emb = pooled / jnp.sqrt(jnp.sum(pooled * pooled, axis=1, keepdims=True) + EMBED_EPSILON)
    nt = (((1,), (1,)), ((), ()))
    sims = (
        lax.dot_general(emb, emb, nt, precision=lax.Precision.HIGHEST, preferred_element_type=jnp.float32)
        / SOFTMAX_TEMPER
    )
    columns = lax.broadcasted_iota(jnp.int32, (NDOC, NDOC), 1)
    rows = lax.broadcasted_iota(jnp.int32, (NDOC, NDOC), 0)
    expo = jnp.where(rows == columns, 0.0, jnp.exp(sims))
    totals = 1.0 / jnp.sum(expo, axis=0, keepdims=True)
    expo_ref[...] = expo
    half = lax.rem(data_place, 2)
    rows8 = pl.ds(pl.multiple_of((data_place - half) * DOCS, 8), 8)

    def own_rows(ref):
        rows = ref[rows8, :]
        return jnp.where(half == 0, rows[:DOCS], rows[DOCS:])

    own = own_rows(pooled_ref)
    own_norm = jnp.sqrt(jnp.sum(own * own, axis=1, keepdims=True) + EMBED_EPSILON)
    own_emb = own / own_norm
    own_expo = own_rows(expo_ref)
    own_totals = 1.0 / jnp.sum(own_expo, axis=1, keepdims=True)
    slots = lax.broadcasted_iota(jnp.int32, (DOCS, NDOC), 0)
    lanes = lax.broadcasted_iota(jnp.int32, (DOCS, NDOC), 1)
    partner = jnp.where(
        slots == 0, pair_ref[0, 0],
        jnp.where(slots == 1, pair_ref[0, 1], jnp.where(slots == 2, pair_ref[0, 2], pair_ref[0, 3])),
    )
    both = own_expo * (own_totals + totals) - jnp.where(lanes == partner, 2.0, 0.0)
    emb_grad = (
        jnp.dot(both, emb, precision=lax.Precision.HIGHEST, preferred_element_type=jnp.float32) / SOFTMAX_TEMPER
    )
    pooled_grad = (emb_grad - own_emb * jnp.sum(own_emb * emb_grad, axis=1, keepdims=True)) / own_norm
    slot = lax.broadcasted_iota(jnp.int32, (DOCS, 1), 0)
    length = jnp.where(
        slot == 0, lengths_ref[0, 0],
        jnp.where(slot == 1, lengths_ref[0, 1], jnp.where(slot == 2, lengths_ref[0, 2], lengths_ref[0, 3])),
    ).astype(jnp.float32)
    scaled = pooled_grad / length * gain_ref[...][None]
    row_doc = doc_of(ends, first + lax.broadcasted_iota(jnp.int32, (ROWS, 1), 0))
    spread = jnp.where(
        row_doc == 0, scaled[0:1],
        jnp.where(row_doc == 1, scaled[1:2], jnp.where(row_doc == 2, scaled[2:3], scaled[3:4])),
    )
    normal = normal_ref[...]
    grad = inverse_ref[...] * (
        spread
        - jnp.mean(spread, axis=1, keepdims=True)
        - normal * jnp.mean(spread * normal, axis=1, keepdims=True)
    )
    out_ref[...] = jnp.dot(
        mixed_ref[...], grad.astype(jnp.bfloat16), preferred_element_type=jnp.float32
    ).astype(jnp.bfloat16)


SMEM = pl.BlockSpec(memory_space=pltpu.SMEM)
VMEM = pl.BlockSpec(memory_space=pltpu.VMEM)
ANY = pl.BlockSpec(memory_space=pl.ANY)


def call(kernel, name, smem, vmem, outs, scratch, flops, aliases={}, whole=()):
    return pl.pallas_call(
        kernel,
        name=name,
        out_shape=[jax.ShapeDtypeStruct(s, t) for s, t in outs],
        in_specs=[SMEM] * len(smem) + [VMEM] * len(vmem) + [ANY] * len(whole),
        out_specs=[VMEM] * len(outs),
        scratch_shapes=[pltpu.VMEM(s, t) for s, t in scratch],
        input_output_aliases=aliases,
        cost_estimate=pl.CostEstimate(flops=flops, bytes_accessed=1 << 26, transcendentals=0),
        compiler_params=pltpu.CompilerParams(vmem_limit_bytes=VMEM_LIMIT),
    )(*smem, *vmem, *whole)


def copies(value, axis, count):
    return lax.all_to_all(jnp.broadcast_to(value[None], (count,) + value.shape), axis, 0, 0, tiled=True)


def swap_add(value):
    return value + lax.ppermute(value, "ctx", CORE_SWAP)


def sum_over_chips(value):
    one, two, three = [
        lax.ppermute(value, "ctx", [(c, (c + 2 * hops) % CTX) for c in range(CTX)]).astype(jnp.float32)
        for hops in (1, 2, 3)
    ]
    return (value.astype(jnp.float32) + two) + (one + three)


def per_device(hidden_in, w_qkv, w_out, b_out, ln_gain, ln_bias, doc_lengths, pair_of):
    f32, bf16 = jnp.float32, jnp.bfloat16
    own = hidden_in[0]
    places = jnp.stack([lax.axis_index("ctx"), lax.axis_index("dp")]).astype(jnp.int32)
    smem = [doc_lengths, places]
    state = [((HEADS, AUG, ROWS), f32)]
    work = [((HEADS, AUG, 2 * ROWS), bf16)]
    held = ((PAIRS, 256, 2 * ROWS), bf16)

    def fold(name, sources, blocks, acc):
        (acc,) = call(
            functools.partial(fold_kernel, sources), name, smem, [w_qkv, qbd, acc, *blocks], state, work,
            1 << 34, {4: 0},
        )
        return acc

    near = lax.ppermute(own, "ctx", AROUND)
    other = lax.ppermute(own, "ctx", CORE_SWAP)
    qbd, acc = call(queries_kernel, "queries", smem, [own, w_qkv], [held] + state, [], 1 << 34)
    own_later, acc = lax.optimization_barrier((own, acc))
    behind = lax.ppermute(own_later, "ctx", BACK)
    acc = fold("own", SOURCES[0:2], [own, other], acc)
    near, acc = lax.optimization_barrier((near, acc))
    far = lax.ppermute(near, "ctx", AROUND)
    near_other = lax.ppermute(near, "ctx", CORE_SWAP)
    acc = fold("near", SOURCES[2:3], [near], acc)
    near_other, acc = lax.optimization_barrier((near_other, acc))
    acc = fold("near_other", SOURCES[3:4], [near_other], acc)
    behind, acc = lax.optimization_barrier((behind, acc))
    behind_other = lax.ppermute(behind, "ctx", CORE_SWAP)
    acc = fold("behind", SOURCES[4:5], [behind], acc)
    behind_other, acc = lax.optimization_barrier((behind_other, acc))
    acc = fold("behind_other", SOURCES[5:6], [behind_other], acc)
    far, acc = lax.optimization_barrier((far, acc))
    far_other = lax.ppermute(far, "ctx", CORE_SWAP)
    acc = fold("far", SOURCES[6:7], [far], acc)
    far_other, acc = lax.optimization_barrier((far_other, acc))
    _, encoded, mixed, normal, inverse, partial = call(
        last_kernel,
        "last",
        smem,
        [far_other, w_qkv, qbd, acc, own, w_out, b_out, ln_gain, ln_bias],
        state
        + [((ROWS, D), bf16), ((D, ROWS), bf16), ((ROWS, D), f32), ((ROWS, 1), f32), ((DOCS, D), f32)],
        work + [((8, 2 * ROWS), f32), ((len(SOURCES), ROWS, D), bf16)],
        1 << 34,
        {5: 0},
        [own, other, near, near_other, behind, behind_other, far, far_other],
    )
    pooled = sum_over_chips(swap_add(partial)) / doc_lengths[0].astype(f32)[:, None]
    every = copies(pooled, "dp", DP).reshape(NDOC, D)
    (term,) = call(
        back_kernel,
        "back",
        smem + [pair_of],
        [every, mixed, normal, inverse, ln_gain],
        [((D, D), bf16)],
        [((NDOC, NDOC), f32)],
        1 << 34,
    )
    share = D // DP
    pieces = lax.all_to_all(term.reshape(DP, share, D), "dp", 0, 0, tiled=True)
    piece = jnp.sum(pieces.astype(f32), axis=0)
    grad_out = sum_over_chips(swap_add(piece).astype(bf16))
    return (encoded[None], grad_out)


def solution(mesh):
    return jax.shard_map(
        per_device,
        mesh=mesh,
        in_specs=(P("dp", "ctx", None), P(), P(), P(), P(), P(), P("dp", None), P("dp", None)),
        out_specs=(P("dp", "ctx", None), P("dp", None)),
        check_vma=False,
    )
```

```python
import functools

import jax
import jax.numpy as jnp
from jax import lax
from jax.experimental import pallas as pl
from jax.experimental.pallas import tpu as pltpu
from jax.sharding import PartitionSpec as P

D = 768
HEADS = 12
HEAD_DIM = 64
PAIRS = HEADS // 2
DOCS = 4
NDOC = 128
ROWS = 256
CTX = 8
DP = 32
AUG = 80

SOFTMAX_TEMPER = 0.05
NORM_EPSILON = 1e-05
EMBED_EPSILON = 1e-06
PENALTY = -1e30

VMEM_LIMIT = 24 * 1024 * 1024

CORE_SWAP = [(c, c ^ 1) for c in range(CTX)]
AROUND = [(c, (c + 2) % CTX if c % 2 == 0 else (c - 2) % CTX) for c in range(CTX)]
BACK = [(b, a) for a, b in AROUND]


def came_from(place, hops):
    step = 2 * hops
    return lax.rem(jnp.where(lax.rem(place, 2) == 0, place - step, place + step) + 2 * CTX, CTX)


SOURCES = [(0, 0), (1, 0), (0, 1), (1, 1), (0, -1), (1, -1), (0, 2), (1, 2)]


def doc_ends(lengths_ref):
    e0 = lengths_ref[0, 0]
    e1 = e0 + lengths_ref[0, 1]
    e2 = e1 + lengths_ref[0, 2]
    e3 = e2 + lengths_ref[0, 3]
    return e0, e1, e2, e3


def doc_of(ends, positions):
    e0, e1, e2, e3 = ends
    one = jnp.int32(1)
    zero = jnp.int32(0)
    return sum(jnp.where(positions >= e, one, zero) for e in (e0, e1, e2, e3))


def needed_span(ends, first):
    e0, e1, e2, e3 = ends
    last = first + ROWS - 1
    low = jnp.where(first >= e2, e2, jnp.where(first >= e1, e1, jnp.where(first >= e0, e0, 0)))
    high = jnp.where(last < e0, e0, jnp.where(last < e1, e1, jnp.where(last < e2, e2, e3)))
    return low, high


def fill_queries(ends, first, own, wqkv_ref, qbd):
    queries = lax.dot_general(
        wqkv_ref[:, :D], own, (((0,), (1,)), ((), ())), preferred_element_type=jnp.float32
    )
    queries = (queries.astype(jnp.bfloat16).astype(jnp.float32) * HEAD_DIM**-0.5).astype(jnp.bfloat16)
    positions = first + lax.broadcasted_iota(jnp.int32, (HEAD_DIM * 2, ROWS), 1)
    slots = lax.broadcasted_iota(jnp.int32, (HEAD_DIM * 2, ROWS), 0)
    same = (doc_of(ends, positions) == slots) | (slots >= DOCS)
    penalty = jnp.where(same, 0.0, PENALTY).astype(jnp.bfloat16)
    penalties = jnp.concatenate([penalty, penalty], axis=1)
    zero = jnp.zeros((HEAD_DIM, ROWS), jnp.bfloat16)
    for j in range(PAIRS):
        qbd[j, :64, :ROWS] = queries[128 * j : 128 * j + 64, :]
        qbd[j, :64, ROWS:] = zero
        qbd[j, 64:128, :ROWS] = zero
        qbd[j, 64:128, ROWS:] = queries[128 * j + 64 : 128 * j + 128, :]
        qbd[j, 128:, :] = penalties


def project(ends, bases, blocks, wqkv_ref, vt):
    rows = ROWS * len(blocks)
    hidden = jnp.concatenate(blocks, axis=0) if len(blocks) > 1 else blocks[0]
    keys = jnp.dot(hidden, wqkv_ref[:, D : 2 * D], preferred_element_type=jnp.float32).astype(jnp.bfloat16)
    values = lax.dot_general(
        wqkv_ref[:, 2 * D :], hidden, (((0,), (1,)), ((), ())), preferred_element_type=jnp.float32
    ).astype(jnp.bfloat16)
    vt[:, :HEAD_DIM, :rows] = values.reshape(HEADS, HEAD_DIM, rows)
    offsets = lax.broadcasted_iota(jnp.int32, (ROWS, 128), 0)
    lanes = lax.broadcasted_iota(jnp.int32, (ROWS, 128), 1)
    onehots = [
        jnp.where(doc_of(ends, base + offsets) == lanes, 1.0, 0.0).astype(jnp.bfloat16) for base in bases
    ]
    return keys, jnp.concatenate(onehots, axis=0) if len(blocks) > 1 else onehots[0]


def pair_scores(keys, onehot, qbd, j):
    pair_keys = jnp.concatenate([keys[:, 128 * j : 128 * j + 128], onehot], axis=1)
    return jnp.dot(pair_keys, qbd[j], preferred_element_type=jnp.float32)


def attend_plain(ends, bases, blocks, wqkv_ref, qbd, vt, acc_ref):
    rows = ROWS * len(blocks)
    keys, onehot = project(ends, bases, blocks, wqkv_ref, vt)
    for j in range(PAIRS):
        weights = jnp.exp(pair_scores(keys, onehot, qbd, j)).astype(jnp.bfloat16)
        for h in range(2):
            part = slice(ROWS * h, ROWS * h + ROWS)
            acc_ref[2 * j + h] += jnp.dot(
                vt[2 * j + h, :, :rows], weights[:, part], preferred_element_type=jnp.float32
            )


def attend_shifted(ends, base, block, wqkv_ref, qbd, vt, m_ref, acc_ref):
    keys, onehot = project(ends, [base], [block], wqkv_ref, vt)
    for j in range(PAIRS):
        scores = pair_scores(keys, onehot, qbd, j)
        old = m_ref[j : j + 1, :]
        new = jnp.maximum(old, jnp.max(scores, axis=0, keepdims=True))
        m_ref[j : j + 1, :] = new
        shrink = jnp.exp(old - new)
        weights = jnp.exp(scores - new).astype(jnp.bfloat16)
        for h in range(2):
            part = slice(ROWS * h, ROWS * h + ROWS)
            mixed = jnp.dot(vt[2 * j + h, :, :ROWS], weights[:, part], preferred_element_type=jnp.float32)
            acc_ref[2 * j + h] = acc_ref[2 * j + h] * shrink[:, part] + mixed


def fill_ones(vt):
    row = lax.broadcasted_iota(jnp.int32, (HEADS, AUG - HEAD_DIM, vt.shape[2]), 1)
    vt[:, HEAD_DIM:, :] = jnp.where(row == 0, 1.0, 0.0).astype(jnp.bfloat16)


def attend_blocks(ends, first, places, blocks, wqkv_ref, qbd, vt, acc_ref):
    low, high = needed_span(ends, first)
    bases = [place * ROWS for place in places]
    wanted = [(base < high) & (base + ROWS > low) for base in bases]

    def attend(which):
        attend_plain(
            ends, [bases[i] for i in which], [blocks[i][...] for i in which], wqkv_ref, qbd, vt, acc_ref
        )

    if len(blocks) == 1:
        pl.when(wanted[0])(lambda: attend([0]))
    else:
        one, two = wanted
        pl.when(one & two)(lambda: attend([0, 1]))
        pl.when(one & jnp.logical_not(two))(lambda: attend([0]))
        pl.when(two & jnp.logical_not(one))(lambda: attend([1]))


def queries_kernel(lengths_ref, place_ref, own_ref, wqkv_ref, qbd, acc_ref):
    ends = doc_ends(lengths_ref)
    fill_queries(ends, place_ref[0] * ROWS, own_ref[...], wqkv_ref, qbd)
    acc_ref[...] = jnp.zeros(acc_ref.shape, jnp.float32)


def fold_kernel(sources, lengths_ref, place_ref, wqkv_ref, qbd, acc_in, *refs):
    blocks, (acc_ref, vt) = refs[: len(sources)], refs[len(sources) :]
    place = place_ref[0]
    ends = doc_ends(lengths_ref)
    fill_ones(vt)
    places = [came_from(place ^ flip, hops) for flip, hops in sources]
    attend_blocks(ends, place * ROWS, places, blocks, wqkv_ref, qbd, vt, acc_ref)


def in_range(acc):
    sums = acc[:, HEAD_DIM, :]
    good = jnp.where((sums >= 1e-12) & (sums <= 1e12), 1.0, 0.0)
    finite = jnp.where(jnp.abs(acc) <= 1e38, 1.0, 0.0)
    return jnp.minimum(jnp.min(good), jnp.min(finite)) > 0.5


def attend_again(ends, place, blocks, wqkv_ref, qbd, vt, acc_ref, m_ref, held):
    for i, (flip, hops) in enumerate(SOURCES):
        pltpu.sync_copy(blocks[i], held.at[i])
    m_ref[...] = jnp.full(m_ref.shape, PENALTY, jnp.float32)
    acc_ref[...] = jnp.zeros(acc_ref.shape, jnp.float32)
    low, high = needed_span(ends, place * ROWS)

    def step(i, carry):
        base = jnp.int32(0)
        for k, (flip, hops) in enumerate(SOURCES):
            base = jnp.where(i == k, came_from(place ^ flip, hops) * ROWS, base)

        @pl.when((base < high) & (base + ROWS > low))
        def _():
            attend_shifted(ends, base, held[i], wqkv_ref, qbd, vt, m_ref, acc_ref)

        return carry

    lax.fori_loop(0, len(SOURCES), step, 0)


def last_kernel(
    lengths_ref, place_ref, far_other_ref, wqkv_ref, qbd, acc_in, own_ref, wout_ref, bias_ref, gain_ref, shift_ref,
    *refs
):
    blocks, refs = refs[: len(SOURCES)], refs[len(SOURCES) :]
    acc_ref, encoded_ref, mixed_ref, normal_ref, inverse_ref, pooled_ref, vt, m_ref, held = refs
    place = place_ref[0]
    ends = doc_ends(lengths_ref)
    first = place * ROWS
    fill_ones(vt)
    flip, hops = SOURCES[-1]
    attend_blocks(ends, first, [came_from(place ^ flip, hops)], [far_other_ref], wqkv_ref, qbd, vt, acc_ref)

    @pl.when(jnp.logical_not(in_range(acc_ref[...])))
    def _():
        attend_again(ends, place, blocks, wqkv_ref, qbd, vt, acc_ref, m_ref, held)

    acc = acc_ref[...]
    mixed = acc[:, :HEAD_DIM, :] / acc[:, HEAD_DIM : HEAD_DIM + 1, :]
    mixed = mixed.reshape(D, ROWS)
    mixed_ref[...] = mixed.astype(jnp.bfloat16)
    summed = jnp.dot(mixed.T.astype(jnp.bfloat16), wout_ref[...], preferred_element_type=jnp.float32)
    summed = summed + bias_ref[...][None] + own_ref[...].astype(jnp.float32)
    centered = summed - jnp.mean(summed, axis=1, keepdims=True)
    inverse = lax.rsqrt(jnp.mean(centered * centered, axis=1, keepdims=True) + NORM_EPSILON)
    normal = centered * inverse
    normal_ref[...] = normal
    inverse_ref[...] = inverse
    layer = normal * gain_ref[...][None] + shift_ref[...][None]
    encoded_ref[...] = layer.astype(jnp.bfloat16)
    row_doc = doc_of(ends, first + lax.broadcasted_iota(jnp.int32, (ROWS, 1), 0))
    for d in range(DOCS):
        pooled_ref[d : d + 1, :] = jnp.sum(
            jnp.where(row_doc == d, layer, 0.0), axis=0, keepdims=True
        )


def back_kernel(
    lengths_ref, place_ref, pair_ref, pooled_ref, mixed_ref, normal_ref, inverse_ref, gain_ref,
    out_ref, expo_ref
):
    place = place_ref[0]
    data_place = place_ref[1]
    ends = doc_ends(lengths_ref)
    first = place * ROWS
    pooled = pooled_ref[...]
    emb = pooled / jnp.sqrt(jnp.sum(pooled * pooled, axis=1, keepdims=True) + EMBED_EPSILON)
    nt = (((1,), (1,)), ((), ()))
    sims = (
        lax.dot_general(emb, emb, nt, precision=lax.Precision.HIGHEST, preferred_element_type=jnp.float32)
        / SOFTMAX_TEMPER
    )
    columns = lax.broadcasted_iota(jnp.int32, (NDOC, NDOC), 1)
    rows = lax.broadcasted_iota(jnp.int32, (NDOC, NDOC), 0)
    expo = jnp.where(rows == columns, 0.0, jnp.exp(sims))
    totals = 1.0 / jnp.sum(expo, axis=0, keepdims=True)
    expo_ref[...] = expo
    half = lax.rem(data_place, 2)
    rows8 = pl.ds(pl.multiple_of((data_place - half) * DOCS, 8), 8)

    def own_rows(ref):
        rows = ref[rows8, :]
        return jnp.where(half == 0, rows[:DOCS], rows[DOCS:])

    own = own_rows(pooled_ref)
    own_norm = jnp.sqrt(jnp.sum(own * own, axis=1, keepdims=True) + EMBED_EPSILON)
    own_emb = own / own_norm
    own_expo = own_rows(expo_ref)
    own_totals = 1.0 / jnp.sum(own_expo, axis=1, keepdims=True)
    slots = lax.broadcasted_iota(jnp.int32, (DOCS, NDOC), 0)
    lanes = lax.broadcasted_iota(jnp.int32, (DOCS, NDOC), 1)
    partner = jnp.where(
        slots == 0, pair_ref[0, 0],
        jnp.where(slots == 1, pair_ref[0, 1], jnp.where(slots == 2, pair_ref[0, 2], pair_ref[0, 3])),
    )
    both = own_expo * (own_totals + totals) - jnp.where(lanes == partner, 2.0, 0.0)
    emb_grad = (
        jnp.dot(both, emb, precision=lax.Precision.HIGHEST, preferred_element_type=jnp.float32) / SOFTMAX_TEMPER
    )
    pooled_grad = (emb_grad - own_emb * jnp.sum(own_emb * emb_grad, axis=1, keepdims=True)) / own_norm
    slot = lax.broadcasted_iota(jnp.int32, (DOCS, 1), 0)
    length = jnp.where(
        slot == 0, lengths_ref[0, 0],
        jnp.where(slot == 1, lengths_ref[0, 1], jnp.where(slot == 2, lengths_ref[0, 2], lengths_ref[0, 3])),
    ).astype(jnp.float32)
    scaled = pooled_grad / length * gain_ref[...][None]
    row_doc = doc_of(ends, first + lax.broadcasted_iota(jnp.int32, (ROWS, 1), 0))
    spread = jnp.where(
        row_doc == 0, scaled[0:1],
        jnp.where(row_doc == 1, scaled[1:2], jnp.where(row_doc == 2, scaled[2:3], scaled[3:4])),
    )
    normal = normal_ref[...]
    grad = inverse_ref[...] * (
        spread
        - jnp.mean(spread, axis=1, keepdims=True)
        - normal * jnp.mean(spread * normal, axis=1, keepdims=True)
    )
    out_ref[...] = jnp.dot(
        mixed_ref[...], grad.astype(jnp.bfloat16), preferred_element_type=jnp.float32
    ).astype(jnp.bfloat16)


SMEM = pl.BlockSpec(memory_space=pltpu.SMEM)
VMEM = pl.BlockSpec(memory_space=pltpu.VMEM)
ANY = pl.BlockSpec(memory_space=pl.ANY)


def call(kernel, name, smem, vmem, outs, scratch, flops, aliases={}, whole=()):
    return pl.pallas_call(
        kernel,
        name=name,
        out_shape=[jax.ShapeDtypeStruct(s, t) for s, t in outs],
        in_specs=[SMEM] * len(smem) + [VMEM] * len(vmem) + [ANY] * len(whole),
        out_specs=[VMEM] * len(outs),
        scratch_shapes=[pltpu.VMEM(s, t) for s, t in scratch],
        input_output_aliases=aliases,
        cost_estimate=pl.CostEstimate(flops=flops, bytes_accessed=1 << 26, transcendentals=0),
        compiler_params=pltpu.CompilerParams(vmem_limit_bytes=VMEM_LIMIT),
    )(*smem, *vmem, *whole)


def copies(value, axis, count):
    return lax.all_to_all(jnp.broadcast_to(value[None], (count,) + value.shape), axis, 0, 0, tiled=True)


def swap_add(value):
    return value + lax.ppermute(value, "ctx", CORE_SWAP)


def sum_over_chips(value):
    one, two, three = [
        lax.ppermute(value, "ctx", [(c, (c + 2 * hops) % CTX) for c in range(CTX)]).astype(jnp.float32)
        for hops in (1, 2, 3)
    ]
    return (value.astype(jnp.float32) + two) + (one + three)


def per_device(hidden_in, w_qkv, w_out, b_out, ln_gain, ln_bias, doc_lengths, pair_of):
    f32, bf16 = jnp.float32, jnp.bfloat16
    own = hidden_in[0]
    places = jnp.stack([lax.axis_index("ctx"), lax.axis_index("dp")]).astype(jnp.int32)
    smem = [doc_lengths, places]
    state = [((HEADS, AUG, ROWS), f32)]
    work = [((HEADS, AUG, 2 * ROWS), bf16)]
    held = ((PAIRS, 256, 2 * ROWS), bf16)

    def fold(name, sources, blocks, acc):
        (acc,) = call(
            functools.partial(fold_kernel, sources), name, smem, [w_qkv, qbd, acc, *blocks], state, work,
            1 << 34, {4: 0},
        )
        return acc

    near = lax.ppermute(own, "ctx", AROUND)
    other = lax.ppermute(own, "ctx", CORE_SWAP)
    qbd, acc = call(queries_kernel, "queries", smem, [own, w_qkv], [held] + state, [], 1 << 34)
    acc = fold("own", SOURCES[0:1], [own], acc)
    own_later, acc = lax.optimization_barrier((own, acc))
    behind = lax.ppermute(own_later, "ctx", BACK)
    acc = fold("other", SOURCES[1:2], [other], acc)
    near, acc = lax.optimization_barrier((near, acc))
    near_other = lax.ppermute(near, "ctx", CORE_SWAP)
    acc = fold("near", SOURCES[2:3], [near], acc)
    near_later, acc = lax.optimization_barrier((near, acc))
    far = lax.ppermute(near_later, "ctx", AROUND)
    near_other, acc = lax.optimization_barrier((near_other, acc))
    acc = fold("near_other", SOURCES[3:4], [near_other], acc)
    behind, acc = lax.optimization_barrier((behind, acc))
    behind_other = lax.ppermute(behind, "ctx", CORE_SWAP)
    acc = fold("behind", SOURCES[4:5], [behind], acc)
    behind_other, acc = lax.optimization_barrier((behind_other, acc))
    acc = fold("behind_other", SOURCES[5:6], [behind_other], acc)
    far, acc = lax.optimization_barrier((far, acc))
    far_other = lax.ppermute(far, "ctx", CORE_SWAP)
    acc = fold("far", SOURCES[6:7], [far], acc)
    far_other, acc = lax.optimization_barrier((far_other, acc))
    _, encoded, mixed, normal, inverse, partial = call(
        last_kernel,
        "last",
        smem,
        [far_other, w_qkv, qbd, acc, own, w_out, b_out, ln_gain, ln_bias],
        state
        + [((ROWS, D), bf16), ((D, ROWS), bf16), ((ROWS, D), f32), ((ROWS, 1), f32), ((DOCS, D), f32)],
        work + [((8, 2 * ROWS), f32), ((len(SOURCES), ROWS, D), bf16)],
        1 << 34,
        {5: 0},
        [own, other, near, near_other, behind, behind_other, far, far_other],
    )
    pooled = sum_over_chips(swap_add(partial)) / doc_lengths[0].astype(f32)[:, None]
    every = copies(pooled, "dp", DP).reshape(NDOC, D)
    (term,) = call(
        back_kernel,
        "back",
        smem + [pair_of],
        [every, mixed, normal, inverse, ln_gain],
        [((D, D), bf16)],
        [((NDOC, NDOC), f32)],
        1 << 34,
    )
    share = D // DP
    pieces = lax.all_to_all(term.reshape(DP, share, D), "dp", 0, 0, tiled=True)
    piece = jnp.sum(pieces.astype(f32), axis=0)
    grad_out = sum_over_chips(swap_add(piece).astype(bf16))
    return (encoded[None], grad_out)


def solution(mesh):
    return jax.shard_map(
        per_device,
        mesh=mesh,
        in_specs=(P("dp", "ctx", None), P(), P(), P(), P(), P(), P("dp", None), P("dp", None)),
        out_specs=(P("dp", "ctx", None), P("dp", None)),
        check_vma=False,
    )
```

```python
import functools

import jax
import jax.numpy as jnp
from jax import lax
from jax.experimental import pallas as pl
from jax.experimental.pallas import tpu as pltpu
from jax.sharding import PartitionSpec as P

D = 768
HEADS = 12
HEAD_DIM = 64
PAIRS = HEADS // 2
DOCS = 4
NDOC = 128
ROWS = 256
CTX = 8
DP = 32
AUG = 80

SOFTMAX_TEMPER = 0.05
NORM_EPSILON = 1e-05
EMBED_EPSILON = 1e-06
PENALTY = -1e30

VMEM_LIMIT = 24 * 1024 * 1024

CORE_SWAP = [(c, c ^ 1) for c in range(CTX)]
AROUND = [(c, (c + 2) % CTX if c % 2 == 0 else (c - 2) % CTX) for c in range(CTX)]
BACK = [(b, a) for a, b in AROUND]


def came_from(place, hops):
    step = 2 * hops
    return lax.rem(jnp.where(lax.rem(place, 2) == 0, place - step, place + step) + 2 * CTX, CTX)


SOURCES = [(0, 0), (1, 0), (0, 1), (1, 1), (0, -1), (1, -1), (0, 2), (1, 2)]


def doc_ends(lengths_ref):
    e0 = lengths_ref[0, 0]
    e1 = e0 + lengths_ref[0, 1]
    e2 = e1 + lengths_ref[0, 2]
    e3 = e2 + lengths_ref[0, 3]
    return e0, e1, e2, e3


def doc_of(ends, positions):
    e0, e1, e2, e3 = ends
    one = jnp.int32(1)
    zero = jnp.int32(0)
    return sum(jnp.where(positions >= e, one, zero) for e in (e0, e1, e2, e3))


def needed_span(ends, first):
    e0, e1, e2, e3 = ends
    last = first + ROWS - 1
    low = jnp.where(first >= e2, e2, jnp.where(first >= e1, e1, jnp.where(first >= e0, e0, 0)))
    high = jnp.where(last < e0, e0, jnp.where(last < e1, e1, jnp.where(last < e2, e2, e3)))
    return low, high


def fill_queries(ends, first, own, wqkv_ref, qbd):
    queries = lax.dot_general(
        wqkv_ref[:, :D], own, (((0,), (1,)), ((), ())), preferred_element_type=jnp.float32
    )
    queries = (queries.astype(jnp.bfloat16).astype(jnp.float32) * HEAD_DIM**-0.5).astype(jnp.bfloat16)
    positions = first + lax.broadcasted_iota(jnp.int32, (HEAD_DIM * 2, ROWS), 1)
    slots = lax.broadcasted_iota(jnp.int32, (HEAD_DIM * 2, ROWS), 0)
    same = (doc_of(ends, positions) == slots) | (slots >= DOCS)
    penalty = jnp.where(same, 0.0, PENALTY).astype(jnp.bfloat16)
    penalties = jnp.concatenate([penalty, penalty], axis=1)
    zero = jnp.zeros((HEAD_DIM, ROWS), jnp.bfloat16)
    for j in range(PAIRS):
        qbd[j, :64, :ROWS] = queries[128 * j : 128 * j + 64, :]
        qbd[j, :64, ROWS:] = zero
        qbd[j, 64:128, :ROWS] = zero
        qbd[j, 64:128, ROWS:] = queries[128 * j + 64 : 128 * j + 128, :]
        qbd[j, 128:, :] = penalties


def project(ends, bases, blocks, wqkv_ref, vt):
    rows = ROWS * len(blocks)
    hidden = jnp.concatenate(blocks, axis=0) if len(blocks) > 1 else blocks[0]
    keys = jnp.dot(hidden, wqkv_ref[:, D : 2 * D], preferred_element_type=jnp.float32).astype(jnp.bfloat16)
    values = lax.dot_general(
        wqkv_ref[:, 2 * D :], hidden, (((0,), (1,)), ((), ())), preferred_element_type=jnp.float32
    ).astype(jnp.bfloat16)
    vt[:, :HEAD_DIM, :rows] = values.reshape(HEADS, HEAD_DIM, rows)
    offsets = lax.broadcasted_iota(jnp.int32, (ROWS, 128), 0)
    lanes = lax.broadcasted_iota(jnp.int32, (ROWS, 128), 1)
    onehots = [
        jnp.where(doc_of(ends, base + offsets) == lanes, 1.0, 0.0).astype(jnp.bfloat16) for base in bases
    ]
    return keys, jnp.concatenate(onehots, axis=0) if len(blocks) > 1 else onehots[0]


def pair_scores(keys, onehot, qbd, j):
    pair_keys = jnp.concatenate([keys[:, 128 * j : 128 * j + 128], onehot], axis=1)
    return jnp.dot(pair_keys, qbd[j], preferred_element_type=jnp.float32)


def attend_plain(ends, bases, blocks, wqkv_ref, qbd, vt, acc_ref):
    rows = ROWS * len(blocks)
    keys, onehot = project(ends, bases, blocks, wqkv_ref, vt)
    for j in range(PAIRS):
        weights = jnp.exp(pair_scores(keys, onehot, qbd, j)).astype(jnp.bfloat16)
        for h in range(2):
            part = slice(ROWS * h, ROWS * h + ROWS)
            acc_ref[2 * j + h] += jnp.dot(
                vt[2 * j + h, :, :rows], weights[:, part], preferred_element_type=jnp.float32
            )


def attend_shifted(ends, base, block, wqkv_ref, qbd, vt, m_ref, acc_ref):
    keys, onehot = project(ends, [base], [block], wqkv_ref, vt)
    for j in range(PAIRS):
        scores = pair_scores(keys, onehot, qbd, j)
        old = m_ref[j : j + 1, :]
        new = jnp.maximum(old, jnp.max(scores, axis=0, keepdims=True))
        m_ref[j : j + 1, :] = new
        shrink = jnp.exp(old - new)
        weights = jnp.exp(scores - new).astype(jnp.bfloat16)
        for h in range(2):
            part = slice(ROWS * h, ROWS * h + ROWS)
            mixed = jnp.dot(vt[2 * j + h, :, :ROWS], weights[:, part], preferred_element_type=jnp.float32)
            acc_ref[2 * j + h] = acc_ref[2 * j + h] * shrink[:, part] + mixed


def fill_ones(vt):
    row = lax.broadcasted_iota(jnp.int32, (HEADS, AUG - HEAD_DIM, vt.shape[2]), 1)
    vt[:, HEAD_DIM:, :] = jnp.where(row == 0, 1.0, 0.0).astype(jnp.bfloat16)


def attend_blocks(ends, first, places, blocks, wqkv_ref, qbd, vt, acc_ref):
    low, high = needed_span(ends, first)
    bases = [place * ROWS for place in places]
    wanted = [(base < high) & (base + ROWS > low) for base in bases]

    def attend(which):
        attend_plain(
            ends, [bases[i] for i in which], [blocks[i][...] for i in which], wqkv_ref, qbd, vt, acc_ref
        )

    if len(blocks) == 1:
        pl.when(wanted[0])(lambda: attend([0]))
    else:
        one, two = wanted
        pl.when(one & two)(lambda: attend([0, 1]))
        pl.when(one & jnp.logical_not(two))(lambda: attend([0]))
        pl.when(two & jnp.logical_not(one))(lambda: attend([1]))


def queries_kernel(lengths_ref, place_ref, own_ref, wqkv_ref, qbd, acc_ref):
    ends = doc_ends(lengths_ref)
    fill_queries(ends, place_ref[0] * ROWS, own_ref[...], wqkv_ref, qbd)
    acc_ref[...] = jnp.zeros(acc_ref.shape, jnp.float32)


def fold_kernel(sources, lengths_ref, place_ref, wqkv_ref, qbd, acc_in, *refs):
    blocks, (acc_ref, vt) = refs[: len(sources)], refs[len(sources) :]
    place = place_ref[0]
    ends = doc_ends(lengths_ref)
    fill_ones(vt)
    places = [came_from(place ^ flip, hops) for flip, hops in sources]
    attend_blocks(ends, place * ROWS, places, blocks, wqkv_ref, qbd, vt, acc_ref)


def in_range(acc):
    sums = acc[:, HEAD_DIM, :]
    good = jnp.where((sums >= 1e-12) & (sums <= 1e12), 1.0, 0.0)
    finite = jnp.where(jnp.abs(acc) <= 1e38, 1.0, 0.0)
    return jnp.minimum(jnp.min(good), jnp.min(finite)) > 0.5


def attend_again(ends, place, blocks, wqkv_ref, qbd, vt, acc_ref, m_ref, held):
    for i, (flip, hops) in enumerate(SOURCES):
        pltpu.sync_copy(blocks[i], held.at[i])
    m_ref[...] = jnp.full(m_ref.shape, PENALTY, jnp.float32)
    acc_ref[...] = jnp.zeros(acc_ref.shape, jnp.float32)
    low, high = needed_span(ends, place * ROWS)

    def step(i, carry):
        base = jnp.int32(0)
        for k, (flip, hops) in enumerate(SOURCES):
            base = jnp.where(i == k, came_from(place ^ flip, hops) * ROWS, base)

        @pl.when((base < high) & (base + ROWS > low))
        def _():
            attend_shifted(ends, base, held[i], wqkv_ref, qbd, vt, m_ref, acc_ref)

        return carry

    lax.fori_loop(0, len(SOURCES), step, 0)


def last_kernel(
    lengths_ref, place_ref, far_other_ref, wqkv_ref, qbd, acc_in, own_ref, wout_ref, bias_ref, gain_ref, shift_ref,
    *refs
):
    blocks, refs = refs[: len(SOURCES)], refs[len(SOURCES) :]
    acc_ref, encoded_ref, mixed_ref, normal_ref, inverse_ref, pooled_ref, vt, m_ref, held = refs
    place = place_ref[0]
    ends = doc_ends(lengths_ref)
    first = place * ROWS
    fill_ones(vt)
    flip, hops = SOURCES[-1]
    attend_blocks(ends, first, [came_from(place ^ flip, hops)], [far_other_ref], wqkv_ref, qbd, vt, acc_ref)

    @pl.when(jnp.logical_not(in_range(acc_ref[...])))
    def _():
        attend_again(ends, place, blocks, wqkv_ref, qbd, vt, acc_ref, m_ref, held)

    acc = acc_ref[...]
    mixed = acc[:, :HEAD_DIM, :] / acc[:, HEAD_DIM : HEAD_DIM + 1, :]
    mixed = mixed.reshape(D, ROWS)
    mixed_ref[...] = mixed.astype(jnp.bfloat16)
    summed = jnp.dot(mixed.T.astype(jnp.bfloat16), wout_ref[...], preferred_element_type=jnp.float32)
    summed = summed + bias_ref[...][None] + own_ref[...].astype(jnp.float32)
    centered = summed - jnp.mean(summed, axis=1, keepdims=True)
    inverse = lax.rsqrt(jnp.mean(centered * centered, axis=1, keepdims=True) + NORM_EPSILON)
    normal = centered * inverse
    normal_ref[...] = normal
    inverse_ref[...] = inverse
    layer = normal * gain_ref[...][None] + shift_ref[...][None]
    encoded_ref[...] = layer.astype(jnp.bfloat16)
    row_doc = doc_of(ends, first + lax.broadcasted_iota(jnp.int32, (ROWS, 1), 0))
    for d in range(DOCS):
        pooled_ref[d : d + 1, :] = jnp.sum(
            jnp.where(row_doc == d, layer, 0.0), axis=0, keepdims=True
        ) / lengths_ref[0, d].astype(jnp.float32)


def back_kernel(
    lengths_ref, place_ref, pair_ref, pooled_ref, mixed_ref, normal_ref, inverse_ref, gain_ref,
    out_ref, expo_ref
):
    place = place_ref[0]
    data_place = place_ref[1]
    ends = doc_ends(lengths_ref)
    first = place * ROWS
    pooled = pooled_ref[...]
    emb = pooled / jnp.sqrt(jnp.sum(pooled * pooled, axis=1, keepdims=True) + EMBED_EPSILON)
    nt = (((1,), (1,)), ((), ()))
    sims = (
        lax.dot_general(emb, emb, nt, precision=lax.Precision.HIGHEST, preferred_element_type=jnp.float32)
        / SOFTMAX_TEMPER
    )
    columns = lax.broadcasted_iota(jnp.int32, (NDOC, NDOC), 1)
    rows = lax.broadcasted_iota(jnp.int32, (NDOC, NDOC), 0)
    expo = jnp.where(rows == columns, 0.0, jnp.exp(sims))
    totals = 1.0 / jnp.sum(expo, axis=0, keepdims=True)
    expo_ref[...] = expo
    half = lax.rem(data_place, 2)
    rows8 = pl.ds(pl.multiple_of((data_place - half) * DOCS, 8), 8)

    def own_rows(ref):
        rows = ref[rows8, :]
        return jnp.where(half == 0, rows[:DOCS], rows[DOCS:])

    own = own_rows(pooled_ref)
    own_norm = jnp.sqrt(jnp.sum(own * own, axis=1, keepdims=True) + EMBED_EPSILON)
    own_emb = own / own_norm
    own_expo = own_rows(expo_ref)
    own_totals = 1.0 / jnp.sum(own_expo, axis=1, keepdims=True)
    slots = lax.broadcasted_iota(jnp.int32, (DOCS, NDOC), 0)
    lanes = lax.broadcasted_iota(jnp.int32, (DOCS, NDOC), 1)
    partner = jnp.where(
        slots == 0, pair_ref[0, 0],
        jnp.where(slots == 1, pair_ref[0, 1], jnp.where(slots == 2, pair_ref[0, 2], pair_ref[0, 3])),
    )
    both = own_expo * (own_totals + totals) - jnp.where(lanes == partner, 2.0, 0.0)
    emb_grad = (
        jnp.dot(both, emb, precision=lax.Precision.HIGHEST, preferred_element_type=jnp.float32) / SOFTMAX_TEMPER
    )
    pooled_grad = (emb_grad - own_emb * jnp.sum(own_emb * emb_grad, axis=1, keepdims=True)) / own_norm
    slot = lax.broadcasted_iota(jnp.int32, (DOCS, 1), 0)
    length = jnp.where(
        slot == 0, lengths_ref[0, 0],
        jnp.where(slot == 1, lengths_ref[0, 1], jnp.where(slot == 2, lengths_ref[0, 2], lengths_ref[0, 3])),
    ).astype(jnp.float32)
    scaled = pooled_grad / length * gain_ref[...][None]
    row_doc = doc_of(ends, first + lax.broadcasted_iota(jnp.int32, (ROWS, 1), 0))
    spread = jnp.where(
        row_doc == 0, scaled[0:1],
        jnp.where(row_doc == 1, scaled[1:2], jnp.where(row_doc == 2, scaled[2:3], scaled[3:4])),
    )
    normal = normal_ref[...]
    grad = inverse_ref[...] * (
        spread
        - jnp.mean(spread, axis=1, keepdims=True)
        - normal * jnp.mean(spread * normal, axis=1, keepdims=True)
    )
    out_ref[...] = jnp.dot(
        mixed_ref[...], grad.astype(jnp.bfloat16), preferred_element_type=jnp.float32
    ).astype(jnp.bfloat16)


SMEM = pl.BlockSpec(memory_space=pltpu.SMEM)
VMEM = pl.BlockSpec(memory_space=pltpu.VMEM)
ANY = pl.BlockSpec(memory_space=pl.ANY)


def call(kernel, name, smem, vmem, outs, scratch, flops, aliases={}, whole=()):
    return pl.pallas_call(
        kernel,
        name=name,
        out_shape=[jax.ShapeDtypeStruct(s, t) for s, t in outs],
        in_specs=[SMEM] * len(smem) + [VMEM] * len(vmem) + [ANY] * len(whole),
        out_specs=[VMEM] * len(outs),
        scratch_shapes=[pltpu.VMEM(s, t) for s, t in scratch],
        input_output_aliases=aliases,
        cost_estimate=pl.CostEstimate(flops=flops, bytes_accessed=1 << 26, transcendentals=0),
        compiler_params=pltpu.CompilerParams(vmem_limit_bytes=VMEM_LIMIT),
    )(*smem, *vmem, *whole)


def copies(value, axis, count):
    return lax.all_to_all(jnp.broadcast_to(value[None], (count,) + value.shape), axis, 0, 0, tiled=True)


def swap_add(value):
    return value + lax.ppermute(value, "ctx", CORE_SWAP)


def sum_over_chips(value):
    for flip in (2, 4):
        partner = lax.ppermute(value, "ctx", [(c, c ^ flip) for c in range(CTX)])
        total = value.astype(jnp.float32) + partner.astype(jnp.float32)
        value = total.astype(value.dtype)
    return total


def per_device(hidden_in, w_qkv, w_out, b_out, ln_gain, ln_bias, doc_lengths, pair_of):
    f32, bf16 = jnp.float32, jnp.bfloat16
    own = hidden_in[0]
    places = jnp.stack([lax.axis_index("ctx"), lax.axis_index("dp")]).astype(jnp.int32)
    smem = [doc_lengths, places]
    state = [((HEADS, AUG, ROWS), f32)]
    work = [((HEADS, AUG, 2 * ROWS), bf16)]
    held = ((PAIRS, 256, 2 * ROWS), bf16)

    def fold(name, sources, blocks, acc):
        (acc,) = call(
            functools.partial(fold_kernel, sources), name, smem, [w_qkv, qbd, acc, *blocks], state, work,
            1 << 34, {4: 0},
        )
        return acc

    near = lax.ppermute(own, "ctx", AROUND)
    other = lax.ppermute(own, "ctx", CORE_SWAP)
    qbd, acc = call(queries_kernel, "queries", smem, [own, w_qkv], [held] + state, [], 1 << 34)
    own_later, acc = lax.optimization_barrier((own, acc))
    behind = lax.ppermute(own_later, "ctx", BACK)
    acc = fold("own", SOURCES[0:2], [own, other], acc)
    near, acc = lax.optimization_barrier((near, acc))
    far = lax.ppermute(near, "ctx", AROUND)
    near_other = lax.ppermute(near, "ctx", CORE_SWAP)
    acc = fold("near", SOURCES[2:3], [near], acc)
    near_other, acc = lax.optimization_barrier((near_other, acc))
    acc = fold("near_other", SOURCES[3:4], [near_other], acc)
    behind, acc = lax.optimization_barrier((behind, acc))
    behind_other = lax.ppermute(behind, "ctx", CORE_SWAP)
    acc = fold("behind", SOURCES[4:5], [behind], acc)
    behind_other, acc = lax.optimization_barrier((behind_other, acc))
    acc = fold("behind_other", SOURCES[5:6], [behind_other], acc)
    far, acc = lax.optimization_barrier((far, acc))
    far_other = lax.ppermute(far, "ctx", CORE_SWAP)
    acc = fold("far", SOURCES[6:7], [far], acc)
    far_other, acc = lax.optimization_barrier((far_other, acc))
    _, encoded, mixed, normal, inverse, partial = call(
        last_kernel,
        "last",
        smem,
        [far_other, w_qkv, qbd, acc, own, w_out, b_out, ln_gain, ln_bias],
        state
        + [((ROWS, D), bf16), ((D, ROWS), bf16), ((ROWS, D), f32), ((ROWS, 1), f32), ((DOCS, D), f32)],
        work + [((8, 2 * ROWS), f32), ((len(SOURCES), ROWS, D), bf16)],
        1 << 34,
        {5: 0},
        [own, other, near, near_other, behind, behind_other, far, far_other],
    )
    pooled = sum_over_chips(swap_add(partial))
    every = copies(pooled, "dp", DP).reshape(NDOC, D)
    (term,) = call(
        back_kernel,
        "back",
        smem + [pair_of],
        [every, mixed, normal, inverse, ln_gain],
        [((D, D), bf16)],
        [((NDOC, NDOC), f32)],
        1 << 34,
    )
    share = D // DP
    pieces = lax.all_to_all(term.reshape(DP, share, D), "dp", 0, 0, tiled=True)
    piece = jnp.sum(pieces.astype(f32), axis=0)
    grad_out = sum_over_chips(swap_add(piece).astype(bf16))
    return (encoded[None], grad_out)


def solution(mesh):
    return jax.shard_map(
        per_device,
        mesh=mesh,
        in_specs=(P("dp", "ctx", None), P(), P(), P(), P(), P(), P("dp", None), P("dp", None)),
        out_specs=(P("dp", "ctx", None), P("dp", None)),
        check_vma=False,
    )
```

```python
import functools

import jax
import jax.numpy as jnp
from jax import lax
from jax.experimental import pallas as pl
from jax.experimental.pallas import tpu as pltpu
from jax.sharding import PartitionSpec as P

D = 768
HEADS = 12
HEAD_DIM = 64
PAIRS = HEADS // 2
DOCS = 4
NDOC = 128
ROWS = 256
CTX = 8
DP = 32
AUG = 80

SOFTMAX_TEMPER = 0.05
NORM_EPSILON = 1e-05
EMBED_EPSILON = 1e-06
PENALTY = -1e30

VMEM_LIMIT = 24 * 1024 * 1024

CORE_SWAP = [(c, c ^ 1) for c in range(CTX)]
AROUND = [(c, (c + 2) % CTX if c % 2 == 0 else (c - 2) % CTX) for c in range(CTX)]
BACK = [(b, a) for a, b in AROUND]


def came_from(place, hops):
    step = 2 * hops
    return lax.rem(jnp.where(lax.rem(place, 2) == 0, place - step, place + step) + 2 * CTX, CTX)


SOURCES = [(0, 0), (1, 0), (0, 1), (1, 1), (0, -1), (1, -1), (0, 2), (1, 2)]


def doc_ends(lengths_ref):
    e0 = lengths_ref[0, 0]
    e1 = e0 + lengths_ref[0, 1]
    e2 = e1 + lengths_ref[0, 2]
    e3 = e2 + lengths_ref[0, 3]
    return e0, e1, e2, e3


def doc_of(ends, positions):
    e0, e1, e2, e3 = ends
    one = jnp.int32(1)
    zero = jnp.int32(0)
    return sum(jnp.where(positions >= e, one, zero) for e in (e0, e1, e2, e3))


def needed_span(ends, first):
    e0, e1, e2, e3 = ends
    last = first + ROWS - 1
    low = jnp.where(first >= e2, e2, jnp.where(first >= e1, e1, jnp.where(first >= e0, e0, 0)))
    high = jnp.where(last < e0, e0, jnp.where(last < e1, e1, jnp.where(last < e2, e2, e3)))
    return low, high


def fill_queries(ends, first, own, wqkv_ref, qbd):
    queries = lax.dot_general(
        wqkv_ref[:, :D], own, (((0,), (1,)), ((), ())), preferred_element_type=jnp.float32
    )
    queries = (queries.astype(jnp.bfloat16).astype(jnp.float32) * HEAD_DIM**-0.5).astype(jnp.bfloat16)
    positions = first + lax.broadcasted_iota(jnp.int32, (HEAD_DIM * 2, ROWS), 1)
    slots = lax.broadcasted_iota(jnp.int32, (HEAD_DIM * 2, ROWS), 0)
    same = (doc_of(ends, positions) == slots) | (slots >= DOCS)
    penalty = jnp.where(same, 0.0, PENALTY).astype(jnp.bfloat16)
    penalties = jnp.concatenate([penalty, penalty], axis=1)
    zero = jnp.zeros((HEAD_DIM, ROWS), jnp.bfloat16)
    for j in range(PAIRS):
        qbd[j, :64, :ROWS] = queries[128 * j : 128 * j + 64, :]
        qbd[j, :64, ROWS:] = zero
        qbd[j, 64:128, :ROWS] = zero
        qbd[j, 64:128, ROWS:] = queries[128 * j + 64 : 128 * j + 128, :]
        qbd[j, 128:, :] = penalties


def project(ends, bases, blocks, wqkv_ref, vt):
    rows = ROWS * len(blocks)
    hidden = jnp.concatenate(blocks, axis=0) if len(blocks) > 1 else blocks[0]
    keys = jnp.dot(hidden, wqkv_ref[:, D : 2 * D], preferred_element_type=jnp.float32).astype(jnp.bfloat16)
    values = lax.dot_general(
        wqkv_ref[:, 2 * D :], hidden, (((0,), (1,)), ((), ())), preferred_element_type=jnp.float32
    ).astype(jnp.bfloat16)
    vt[:, :HEAD_DIM, :rows] = values.reshape(HEADS, HEAD_DIM, rows)
    offsets = lax.broadcasted_iota(jnp.int32, (ROWS, 128), 0)
    lanes = lax.broadcasted_iota(jnp.int32, (ROWS, 128), 1)
    onehots = [
        jnp.where(doc_of(ends, base + offsets) == lanes, 1.0, 0.0).astype(jnp.bfloat16) for base in bases
    ]
    return keys, jnp.concatenate(onehots, axis=0) if len(blocks) > 1 else onehots[0]


def pair_scores(keys, onehot, qbd, j):
    pair_keys = jnp.concatenate([keys[:, 128 * j : 128 * j + 128], onehot], axis=1)
    return jnp.dot(pair_keys, qbd[j], preferred_element_type=jnp.float32)


def attend_plain(ends, bases, blocks, wqkv_ref, qbd, vt, acc_ref):
    rows = ROWS * len(blocks)
    keys, onehot = project(ends, bases, blocks, wqkv_ref, vt)
    for j in range(PAIRS):
        weights = jnp.exp(pair_scores(keys, onehot, qbd, j)).astype(jnp.bfloat16)
        for h in range(2):
            part = slice(ROWS * h, ROWS * h + ROWS)
            acc_ref[2 * j + h] += jnp.dot(
                vt[2 * j + h, :, :rows], weights[:, part], preferred_element_type=jnp.float32
            )


def attend_shifted(ends, base, block, wqkv_ref, qbd, vt, m_ref, acc_ref):
    keys, onehot = project(ends, [base], [block], wqkv_ref, vt)
    for j in range(PAIRS):
        scores = pair_scores(keys, onehot, qbd, j)
        old = m_ref[j : j + 1, :]
        new = jnp.maximum(old, jnp.max(scores, axis=0, keepdims=True))
        m_ref[j : j + 1, :] = new
        shrink = jnp.exp(old - new)
        weights = jnp.exp(scores - new).astype(jnp.bfloat16)
        for h in range(2):
            part = slice(ROWS * h, ROWS * h + ROWS)
            mixed = jnp.dot(vt[2 * j + h, :, :ROWS], weights[:, part], preferred_element_type=jnp.float32)
            acc_ref[2 * j + h] = acc_ref[2 * j + h] * shrink[:, part] + mixed


def fill_ones(vt):
    row = lax.broadcasted_iota(jnp.int32, (HEADS, AUG - HEAD_DIM, vt.shape[2]), 1)
    vt[:, HEAD_DIM:, :] = jnp.where(row == 0, 1.0, 0.0).astype(jnp.bfloat16)


def attend_blocks(ends, first, places, blocks, wqkv_ref, qbd, vt, acc_ref):
    low, high = needed_span(ends, first)
    bases = [place * ROWS for place in places]
    wanted = [(base < high) & (base + ROWS > low) for base in bases]

    def attend(which):
        attend_plain(
            ends, [bases[i] for i in which], [blocks[i][...] for i in which], wqkv_ref, qbd, vt, acc_ref
        )

    if len(blocks) == 1:
        pl.when(wanted[0])(lambda: attend([0]))
    else:
        one, two = wanted
        pl.when(one & two)(lambda: attend([0, 1]))
        pl.when(one & jnp.logical_not(two))(lambda: attend([0]))
        pl.when(two & jnp.logical_not(one))(lambda: attend([1]))


def queries_kernel(lengths_ref, place_ref, own_ref, wqkv_ref, qbd, acc_ref):
    ends = doc_ends(lengths_ref)
    fill_queries(ends, place_ref[0] * ROWS, own_ref[...], wqkv_ref, qbd)
    acc_ref[...] = jnp.zeros(acc_ref.shape, jnp.float32)


def fold_kernel(sources, lengths_ref, place_ref, wqkv_ref, qbd, acc_in, *refs):
    blocks, (acc_ref, vt) = refs[: len(sources)], refs[len(sources) :]
    place = place_ref[0]
    ends = doc_ends(lengths_ref)
    fill_ones(vt)
    places = [came_from(place ^ flip, hops) for flip, hops in sources]
    attend_blocks(ends, place * ROWS, places, blocks, wqkv_ref, qbd, vt, acc_ref)


def in_range(acc):
    sums = acc[:, HEAD_DIM, :]
    good = jnp.where((sums >= 1e-12) & (sums <= 1e12), 1.0, 0.0)
    finite = jnp.where(jnp.abs(acc) <= 1e38, 1.0, 0.0)
    return jnp.minimum(jnp.min(good), jnp.min(finite)) > 0.5


def attend_again(ends, place, blocks, wqkv_ref, qbd, vt, acc_ref, m_ref, held):
    for i, (flip, hops) in enumerate(SOURCES):
        pltpu.sync_copy(blocks[i], held.at[i])
    m_ref[...] = jnp.full(m_ref.shape, PENALTY, jnp.float32)
    acc_ref[...] = jnp.zeros(acc_ref.shape, jnp.float32)
    low, high = needed_span(ends, place * ROWS)

    def step(i, carry):
        base = jnp.int32(0)
        for k, (flip, hops) in enumerate(SOURCES):
            base = jnp.where(i == k, came_from(place ^ flip, hops) * ROWS, base)

        @pl.when((base < high) & (base + ROWS > low))
        def _():
            attend_shifted(ends, base, held[i], wqkv_ref, qbd, vt, m_ref, acc_ref)

        return carry

    lax.fori_loop(0, len(SOURCES), step, 0)


def last_kernel(
    lengths_ref, place_ref, far_other_ref, wqkv_ref, qbd, acc_in, own_ref, wout_ref, bias_ref, gain_ref, shift_ref,
    *refs
):
    blocks, refs = refs[: len(SOURCES)], refs[len(SOURCES) :]
    acc_ref, encoded_ref, mixed_ref, normal_ref, inverse_ref, pooled_ref, vt, m_ref, held = refs
    place = place_ref[0]
    ends = doc_ends(lengths_ref)
    first = place * ROWS
    fill_ones(vt)
    flip, hops = SOURCES[-1]
    attend_blocks(ends, first, [came_from(place ^ flip, hops)], [far_other_ref], wqkv_ref, qbd, vt, acc_ref)

    @pl.when(jnp.logical_not(in_range(acc_ref[...])))
    def _():
        attend_again(ends, place, blocks, wqkv_ref, qbd, vt, acc_ref, m_ref, held)

    acc = acc_ref[...]
    mixed = acc[:, :HEAD_DIM, :] * (1.0 / acc[:, HEAD_DIM : HEAD_DIM + 1, :])
    mixed = mixed.reshape(D, ROWS).astype(jnp.bfloat16)
    mixed_ref[...] = mixed
    summed = lax.dot_general(
        mixed, wout_ref[...], (((0,), (0,)), ((), ())), preferred_element_type=jnp.float32
    )
    summed = summed + bias_ref[...][None] + own_ref[...].astype(jnp.float32)
    centered = summed - jnp.mean(summed, axis=1, keepdims=True)
    inverse = lax.rsqrt(jnp.mean(centered * centered, axis=1, keepdims=True) + NORM_EPSILON)
    normal = centered * inverse
    normal_ref[...] = normal
    inverse_ref[...] = inverse
    layer = normal * gain_ref[...][None] + shift_ref[...][None]
    encoded_ref[...] = layer.astype(jnp.bfloat16)
    row_doc = doc_of(ends, first + lax.broadcasted_iota(jnp.int32, (ROWS, 1), 0))
    pooled_ref[...] = jnp.zeros(pooled_ref.shape, jnp.float32)
    starts = (jnp.int32(0), *ends[:-1])
    for d in range(DOCS):

        @pl.when((starts[d] < first + ROWS) & (ends[d] > first))
        def _():
            total = jnp.sum(jnp.where(row_doc == d, layer, 0.0), axis=0, keepdims=True)
            mean = total * (1.0 / lengths_ref[0, d].astype(jnp.float32))
            pooled_ref[:, d : d + 1, :] = jnp.broadcast_to(mean[None], (CTX, 1, D))


def back_kernel(
    lengths_ref, place_ref, pair_ref, pooled_ref, mixed_ref, normal_ref, inverse_ref, gain_ref,
    out_ref, expo_ref
):
    place = place_ref[0]
    data_place = place_ref[1]
    ends = doc_ends(lengths_ref)
    first = place * ROWS
    pooled = pooled_ref[...]
    emb = pooled * lax.rsqrt(jnp.sum(pooled * pooled, axis=1, keepdims=True) + EMBED_EPSILON)
    nt = (((1,), (1,)), ((), ()))
    sims = (
        lax.dot_general(emb, emb, nt, precision=lax.Precision.HIGHEST, preferred_element_type=jnp.float32)
        * (1.0 / SOFTMAX_TEMPER)
    )
    columns = lax.broadcasted_iota(jnp.int32, (NDOC, NDOC), 1)
    rows = lax.broadcasted_iota(jnp.int32, (NDOC, NDOC), 0)
    expo = jnp.where(rows == columns, 0.0, jnp.exp(sims))
    totals = 1.0 / jnp.sum(expo, axis=0, keepdims=True)
    expo_ref[...] = expo
    half = lax.rem(data_place, 2)
    rows8 = pl.ds(pl.multiple_of((data_place - half) * DOCS, 8), 8)

    def own_rows(ref):
        rows = ref[rows8, :]
        return jnp.where(half == 0, rows[:DOCS], rows[DOCS:])

    own = own_rows(pooled_ref)
    own_inverse = lax.rsqrt(jnp.sum(own * own, axis=1, keepdims=True) + EMBED_EPSILON)
    own_emb = own * own_inverse
    own_expo = own_rows(expo_ref)
    own_totals = 1.0 / jnp.sum(own_expo, axis=1, keepdims=True)
    slots = lax.broadcasted_iota(jnp.int32, (DOCS, NDOC), 0)
    lanes = lax.broadcasted_iota(jnp.int32, (DOCS, NDOC), 1)
    partner = jnp.where(
        slots == 0, pair_ref[0, 0],
        jnp.where(slots == 1, pair_ref[0, 1], jnp.where(slots == 2, pair_ref[0, 2], pair_ref[0, 3])),
    )
    both = own_expo * (own_totals + totals) - jnp.where(lanes == partner, 2.0, 0.0)
    emb_grad = (
        jnp.dot(both, emb, precision=lax.Precision.HIGHEST, preferred_element_type=jnp.float32) / SOFTMAX_TEMPER
    )
    pooled_grad = (emb_grad - own_emb * jnp.sum(own_emb * emb_grad, axis=1, keepdims=True)) * own_inverse
    slot = lax.broadcasted_iota(jnp.int32, (DOCS, 1), 0)
    length = jnp.where(
        slot == 0, lengths_ref[0, 0],
        jnp.where(slot == 1, lengths_ref[0, 1], jnp.where(slot == 2, lengths_ref[0, 2], lengths_ref[0, 3])),
    ).astype(jnp.float32)
    scaled = pooled_grad * (1.0 / length) * gain_ref[...][None]
    scaled_mean = jnp.mean(scaled, axis=1, keepdims=True)
    row_doc = doc_of(ends, first + lax.broadcasted_iota(jnp.int32, (ROWS, 1), 0))

    def spread(rows):
        return jnp.where(
            row_doc == 0, rows[0:1], jnp.where(row_doc == 1, rows[1:2], jnp.where(row_doc == 2, rows[2:3], rows[3:4]))
        )

    normal = normal_ref[...]
    token_grad = spread(scaled)
    along = jnp.mean(token_grad * normal, axis=1, keepdims=True)
    grad = inverse_ref[...] * (token_grad - spread(scaled_mean) - normal * along)
    out_ref[...] = jnp.dot(
        mixed_ref[...], grad.astype(jnp.bfloat16), preferred_element_type=jnp.float32
    ).astype(jnp.bfloat16)


SMEM = pl.BlockSpec(memory_space=pltpu.SMEM)
VMEM = pl.BlockSpec(memory_space=pltpu.VMEM)
ANY = pl.BlockSpec(memory_space=pl.ANY)


def call(kernel, name, smem, vmem, outs, scratch, flops, aliases={}, whole=()):
    return pl.pallas_call(
        kernel,
        name=name,
        out_shape=[jax.ShapeDtypeStruct(s, t) for s, t in outs],
        in_specs=[SMEM] * len(smem) + [VMEM] * len(vmem) + [ANY] * len(whole),
        out_specs=[VMEM] * len(outs),
        scratch_shapes=[pltpu.VMEM(s, t) for s, t in scratch],
        input_output_aliases=aliases,
        cost_estimate=pl.CostEstimate(flops=flops, bytes_accessed=1 << 26, transcendentals=0),
        compiler_params=pltpu.CompilerParams(vmem_limit_bytes=VMEM_LIMIT),
    )(*smem, *vmem, *whole)


def copies(value, axis, count):
    return lax.all_to_all(jnp.broadcast_to(value[None], (count,) + value.shape), axis, 0, 0, tiled=True)


def swap_add(value):
    return value + lax.ppermute(value, "ctx", CORE_SWAP)


def sum_over_chips(value):
    one, two, three = [
        lax.ppermute(value, "ctx", [(c, (c + 2 * hops) % CTX) for c in range(CTX)]).astype(jnp.float32)
        for hops in (1, 2, 3)
    ]
    return (value.astype(jnp.float32) + two) + (one + three)


def per_device(hidden_in, w_qkv, w_out, b_out, ln_gain, ln_bias, doc_lengths, pair_of):
    f32, bf16 = jnp.float32, jnp.bfloat16
    own = hidden_in[0]
    places = jnp.stack([lax.axis_index("ctx"), lax.axis_index("dp")]).astype(jnp.int32)
    smem = [doc_lengths, places]
    state = [((HEADS, AUG, ROWS), f32)]
    work = [((HEADS, AUG, 2 * ROWS), bf16)]
    held = ((PAIRS, 256, 2 * ROWS), bf16)

    def fold(name, sources, blocks, acc):
        (acc,) = call(
            functools.partial(fold_kernel, sources), name, smem, [w_qkv, qbd, acc, *blocks], state, work,
            1 << 34, {4: 0},
        )
        return acc

    def after(value, acc):
        return lax.optimization_barrier((value, acc))

    near = lax.ppermute(own, "ctx", AROUND)
    qbd, acc = call(queries_kernel, "queries", smem, [own, w_qkv], [held] + state, [], 1 << 34)
    later, acc = after(own, acc)
    behind = lax.ppermute(later, "ctx", BACK)
    other = lax.ppermute(later, "ctx", CORE_SWAP)
    acc = fold("own", SOURCES[0:1], [own], acc)
    near, acc = after(near, acc)
    far = lax.ppermute(near, "ctx", AROUND)
    acc = fold("near", SOURCES[2:3], [near], acc)
    later, acc = after(near, acc)
    near_other = lax.ppermute(later, "ctx", CORE_SWAP)
    acc = fold("other", SOURCES[1:2], [other], acc)
    behind, acc = after(behind, acc)
    acc = fold("behind", SOURCES[4:5], [behind], acc)
    later, acc = after(behind, acc)
    behind_other = lax.ppermute(later, "ctx", CORE_SWAP)
    acc = fold("near_other", SOURCES[3:4], [near_other], acc)
    behind_other, acc = after(behind_other, acc)
    acc = fold("behind_other", SOURCES[5:6], [behind_other], acc)
    far, acc = after(far, acc)
    far_other = lax.ppermute(far, "ctx", CORE_SWAP)
    acc = fold("far", SOURCES[6:7], [far], acc)
    far_other, acc = after(far_other, acc)
    _, encoded, mixed, normal, inverse, partials = call(
        last_kernel,
        "last",
        smem,
        [far_other, w_qkv, qbd, acc, own, w_out, b_out, ln_gain, ln_bias],
        state
        + [((ROWS, D), bf16), ((D, ROWS), bf16), ((ROWS, D), f32), ((ROWS, 1), f32), ((CTX, DOCS, D), f32)],
        work + [((8, 2 * ROWS), f32), ((len(SOURCES), ROWS, D), bf16)],
        1 << 34,
        {5: 0},
        [own, other, near, near_other, behind, behind_other, far, far_other],
    )
    pooled = jnp.sum(lax.all_to_all(partials, "ctx", 0, 0, tiled=True), axis=0)
    every = copies(pooled, "dp", DP).reshape(NDOC, D)
    (term,) = call(
        back_kernel,
        "back",
        smem + [pair_of],
        [every, mixed, normal, inverse, ln_gain],
        [((D, D), bf16)],
        [((NDOC, NDOC), f32)],
        1 << 34,
    )
    share = D // DP
    pieces = lax.all_to_all(term.reshape(DP, share, D), "dp", 0, 0, tiled=True)
    piece = jnp.sum(pieces.astype(f32), axis=0)
    grad_out = sum_over_chips(swap_add(piece).astype(bf16))
    return (encoded[None], grad_out)


def solution(mesh):
    return jax.shard_map(
        per_device,
        mesh=mesh,
        in_specs=(P("dp", "ctx", None), P(), P(), P(), P(), P(), P("dp", None), P("dp", None)),
        out_specs=(P("dp", "ctx", None), P("dp", None)),
        check_vma=False,
    )
```

```python
import functools

import jax
import jax.numpy as jnp
from jax import lax
from jax.experimental import pallas as pl
from jax.experimental.pallas import tpu as pltpu
from jax.sharding import PartitionSpec as P

D = 768
HEADS = 12
HEAD_DIM = 64
PAIRS = HEADS // 2
DOCS = 4
NDOC = 128
ROWS = 256
CTX = 8
DP = 32
HALF = D // 2
AUG = 80

SOFTMAX_TEMPER = 0.05
NORM_EPSILON = 1e-05
EMBED_EPSILON = 1e-06
PENALTY = -1e30

VMEM_LIMIT = 24 * 1024 * 1024

CORE_SWAP = [(c, c ^ 1) for c in range(CTX)]
AROUND = [(c, (c + 2) % CTX if c % 2 == 0 else (c - 2) % CTX) for c in range(CTX)]
BACK = [(b, a) for a, b in AROUND]


def came_from(place, hops):
    step = 2 * hops
    return lax.rem(jnp.where(lax.rem(place, 2) == 0, place - step, place + step) + 2 * CTX, CTX)


SOURCES = [(0, 0), (1, 0), (0, 1), (1, 1), (0, -1), (1, -1), (0, 2), (1, 2)]


def doc_ends(lengths_ref):
    e0 = lengths_ref[0, 0]
    e1 = e0 + lengths_ref[0, 1]
    e2 = e1 + lengths_ref[0, 2]
    e3 = e2 + lengths_ref[0, 3]
    return e0, e1, e2, e3


def doc_of(ends, positions):
    e0, e1, e2, e3 = ends
    one = jnp.int32(1)
    zero = jnp.int32(0)
    return sum(jnp.where(positions >= e, one, zero) for e in (e0, e1, e2, e3))


def needed_span(ends, first):
    e0, e1, e2, e3 = ends
    last = first + ROWS - 1
    low = jnp.where(first >= e2, e2, jnp.where(first >= e1, e1, jnp.where(first >= e0, e0, 0)))
    high = jnp.where(last < e0, e0, jnp.where(last < e1, e1, jnp.where(last < e2, e2, e3)))
    return low, high


def fill_queries(ends, first, own, wqkv_ref, qbd):
    queries = lax.dot_general(
        wqkv_ref[:, :D], own, (((0,), (1,)), ((), ())), preferred_element_type=jnp.float32
    )
    queries = (queries.astype(jnp.bfloat16).astype(jnp.float32) * HEAD_DIM**-0.5).astype(jnp.bfloat16)
    positions = first + lax.broadcasted_iota(jnp.int32, (HEAD_DIM * 2, ROWS), 1)
    slots = lax.broadcasted_iota(jnp.int32, (HEAD_DIM * 2, ROWS), 0)
    same = (doc_of(ends, positions) == slots) | (slots >= DOCS)
    penalty = jnp.where(same, 0.0, PENALTY).astype(jnp.bfloat16)
    penalties = jnp.concatenate([penalty, penalty], axis=1)
    zero = jnp.zeros((HEAD_DIM, ROWS), jnp.bfloat16)
    for j in range(PAIRS):
        qbd[j, :64, :ROWS] = queries[128 * j : 128 * j + 64, :]
        qbd[j, :64, ROWS:] = zero
        qbd[j, 64:128, :ROWS] = zero
        qbd[j, 64:128, ROWS:] = queries[128 * j + 64 : 128 * j + 128, :]
        qbd[j, 128:, :] = penalties


def project(ends, bases, blocks, wqkv_ref, vt):
    rows = ROWS * len(blocks)
    hidden = jnp.concatenate(blocks, axis=0) if len(blocks) > 1 else blocks[0]
    keys = jnp.dot(hidden, wqkv_ref[:, D : 2 * D], preferred_element_type=jnp.float32).astype(jnp.bfloat16)
    values = lax.dot_general(
        wqkv_ref[:, 2 * D :], hidden, (((0,), (1,)), ((), ())), preferred_element_type=jnp.float32
    ).astype(jnp.bfloat16)
    vt[:, :HEAD_DIM, :rows] = values.reshape(HEADS, HEAD_DIM, rows)
    offsets = lax.broadcasted_iota(jnp.int32, (ROWS, 128), 0)
    lanes = lax.broadcasted_iota(jnp.int32, (ROWS, 128), 1)
    onehots = [
        jnp.where(doc_of(ends, base + offsets) == lanes, 1.0, 0.0).astype(jnp.bfloat16) for base in bases
    ]
    return keys, jnp.concatenate(onehots, axis=0) if len(blocks) > 1 else onehots[0]


def pair_scores(keys, onehot, qbd, j):
    pair_keys = jnp.concatenate([keys[:, 128 * j : 128 * j + 128], onehot], axis=1)
    return jnp.dot(pair_keys, qbd[j], preferred_element_type=jnp.float32)


def attend_plain(ends, bases, blocks, wqkv_ref, qbd, vt, acc_ref):
    rows = ROWS * len(blocks)
    keys, onehot = project(ends, bases, blocks, wqkv_ref, vt)
    for j in range(PAIRS):
        weights = jnp.exp(pair_scores(keys, onehot, qbd, j)).astype(jnp.bfloat16)
        for h in range(2):
            part = slice(ROWS * h, ROWS * h + ROWS)
            acc_ref[2 * j + h] += jnp.dot(
                vt[2 * j + h, :, :rows], weights[:, part], preferred_element_type=jnp.float32
            )


def attend_shifted(ends, base, block, wqkv_ref, qbd, vt, m_ref, acc_ref):
    keys, onehot = project(ends, [base], [block], wqkv_ref, vt)
    for j in range(PAIRS):
        scores = pair_scores(keys, onehot, qbd, j)
        old = m_ref[j : j + 1, :]
        new = jnp.maximum(old, jnp.max(scores, axis=0, keepdims=True))
        m_ref[j : j + 1, :] = new
        shrink = jnp.exp(old - new)
        weights = jnp.exp(scores - new).astype(jnp.bfloat16)
        for h in range(2):
            part = slice(ROWS * h, ROWS * h + ROWS)
            mixed = jnp.dot(vt[2 * j + h, :, :ROWS], weights[:, part], preferred_element_type=jnp.float32)
            acc_ref[2 * j + h] = acc_ref[2 * j + h] * shrink[:, part] + mixed


def fill_ones(vt):
    row = lax.broadcasted_iota(jnp.int32, (HEADS, AUG - HEAD_DIM, vt.shape[2]), 1)
    vt[:, HEAD_DIM:, :] = jnp.where(row == 0, 1.0, 0.0).astype(jnp.bfloat16)


def attend_blocks(ends, first, places, blocks, wqkv_ref, qbd, vt, acc_ref):
    low, high = needed_span(ends, first)
    bases = [place * ROWS for place in places]
    wanted = [(base < high) & (base + ROWS > low) for base in bases]

    def attend(which):
        attend_plain(
            ends, [bases[i] for i in which], [blocks[i][...] for i in which], wqkv_ref, qbd, vt, acc_ref
        )

    if len(blocks) == 1:
        pl.when(wanted[0])(lambda: attend([0]))
    else:
        one, two = wanted
        pl.when(one & two)(lambda: attend([0, 1]))
        pl.when(one & jnp.logical_not(two))(lambda: attend([0]))
        pl.when(two & jnp.logical_not(one))(lambda: attend([1]))


def queries_kernel(lengths_ref, place_ref, own_ref, wqkv_ref, qbd, acc_ref):
    ends = doc_ends(lengths_ref)
    fill_queries(ends, place_ref[0] * ROWS, own_ref[...], wqkv_ref, qbd)
    acc_ref[...] = jnp.zeros(acc_ref.shape, jnp.float32)


def fold_kernel(sources, lengths_ref, place_ref, wqkv_ref, qbd, acc_in, *refs):
    blocks, (acc_ref, vt) = refs[: len(sources)], refs[len(sources) :]
    place = place_ref[0]
    ends = doc_ends(lengths_ref)
    fill_ones(vt)
    places = [came_from(place ^ flip, hops) for flip, hops in sources]
    attend_blocks(ends, place * ROWS, places, blocks, wqkv_ref, qbd, vt, acc_ref)


def in_range(acc):
    sums = acc[:, HEAD_DIM, :]
    good = jnp.where((sums >= 1e-12) & (sums <= 1e12), 1.0, 0.0)
    finite = jnp.where(jnp.abs(acc) <= 1e38, 1.0, 0.0)
    return jnp.minimum(jnp.min(good), jnp.min(finite)) > 0.5


def attend_again(ends, place, blocks, wqkv_ref, qbd, vt, acc_ref, m_ref, held):
    for i, (flip, hops) in enumerate(SOURCES):
        pltpu.sync_copy(blocks[i], held.at[i])
    m_ref[...] = jnp.full(m_ref.shape, PENALTY, jnp.float32)
    acc_ref[...] = jnp.zeros(acc_ref.shape, jnp.float32)
    low, high = needed_span(ends, place * ROWS)

    def step(i, carry):
        base = jnp.int32(0)
        for k, (flip, hops) in enumerate(SOURCES):
            base = jnp.where(i == k, came_from(place ^ flip, hops) * ROWS, base)

        @pl.when((base < high) & (base + ROWS > low))
        def _():
            attend_shifted(ends, base, held[i], wqkv_ref, qbd, vt, m_ref, acc_ref)

        return carry

    lax.fori_loop(0, len(SOURCES), step, 0)


def last_kernel(
    lengths_ref, place_ref, far_other_ref, wqkv_ref, qbd, acc_in, own_ref, wout_ref, bias_ref, gain_ref, shift_ref,
    *refs
):
    blocks, refs = refs[: len(SOURCES)], refs[len(SOURCES) :]
    acc_ref, mixed_ref, normal_ref, inverse_ref, rows_ref, pooled_ref, vt, m_ref, held = refs
    place = place_ref[0]
    ends = doc_ends(lengths_ref)
    first = place * ROWS
    fill_ones(vt)
    flip, hops = SOURCES[-1]
    attend_blocks(ends, first, [came_from(place ^ flip, hops)], [far_other_ref], wqkv_ref, qbd, vt, acc_ref)

    @pl.when(jnp.logical_not(in_range(acc_ref[...])))
    def _():
        attend_again(ends, place, blocks, wqkv_ref, qbd, vt, acc_ref, m_ref, held)

    acc = acc_ref[...]
    mixed = acc[:, :HEAD_DIM, :] * (1.0 / acc[:, HEAD_DIM : HEAD_DIM + 1, :])
    mixed = mixed.reshape(D, ROWS).astype(jnp.bfloat16)
    mixed_ref[...] = mixed
    summed = lax.dot_general(
        mixed, wout_ref[...], (((0,), (0,)), ((), ())), preferred_element_type=jnp.float32
    )
    summed = summed + bias_ref[...][None] + own_ref[...].astype(jnp.float32)
    centered = summed - jnp.mean(summed, axis=1, keepdims=True)
    inverse = lax.rsqrt(jnp.mean(centered * centered, axis=1, keepdims=True) + NORM_EPSILON)
    normal = centered * inverse
    normal_ref[...] = normal
    inverse_ref[...] = inverse
    layer = normal * gain_ref[...][None] + shift_ref[...][None]
    rows_ref[:, :D] = normal.astype(jnp.bfloat16)
    high = inverse.astype(jnp.bfloat16).astype(jnp.float32)
    lane = lax.broadcasted_iota(jnp.int32, (ROWS, 128), 1)
    rows_ref[:, D:] = jnp.where(lane == 0, high, inverse - high).astype(jnp.bfloat16)
    row_doc = doc_of(ends, first + lax.broadcasted_iota(jnp.int32, (ROWS, 1), 0))
    pooled_ref[...] = jnp.zeros(pooled_ref.shape, jnp.float32)
    starts = (jnp.int32(0), *ends[:-1])
    for d in range(DOCS):

        @pl.when((starts[d] < first + ROWS) & (ends[d] > first))
        def _():
            total = jnp.sum(jnp.where(row_doc == d, layer, 0.0), axis=0, keepdims=True)
            mean = total * (1.0 / lengths_ref[0, d].astype(jnp.float32))
            pooled_ref[:, d : d + 1, :] = jnp.broadcast_to(mean[None], (CTX, 1, D))


def back_kernel(
    lengths_ref, place_ref, pair_ref, pooled_ref, mixed_ref, normal_ref, inverse_ref, other_mixed_ref, other_rows_ref,
    gain_ref, shift_ref, out_ref, encoded_hbm, expo_ref, scaled_ref, encoded_ref, sem
):
    place = place_ref[0]
    data_place = place_ref[1]
    ends = doc_ends(lengths_ref)
    f32, bf16 = jnp.float32, jnp.bfloat16
    encoded_ref[...] = (normal_ref[...] * gain_ref[...][None] + shift_ref[...][None]).astype(bf16)
    write = pltpu.make_async_copy(encoded_ref, encoded_hbm, sem)
    write.start()

    pooled = pooled_ref[...]
    emb = pooled * lax.rsqrt(jnp.sum(pooled * pooled, axis=1, keepdims=True) + EMBED_EPSILON)
    high = emb.astype(bf16)
    low = (emb - high.astype(f32)).astype(bf16)

    def times(left, right):
        return lax.dot_general(left, right, (((1,), (1,)), ((), ())), preferred_element_type=f32)

    sims = (times(high, high) + (times(high, low) + times(low, high))) * (1.0 / SOFTMAX_TEMPER)
    columns = lax.broadcasted_iota(jnp.int32, (NDOC, NDOC), 1)
    rows = lax.broadcasted_iota(jnp.int32, (NDOC, NDOC), 0)
    expo = jnp.where(rows == columns, 0.0, jnp.exp(sims))
    expo_ref[...] = expo
    totals = 1.0 / jnp.sum(expo, axis=0, keepdims=True)
    half = lax.rem(data_place, 2)
    rows8 = pl.ds(pl.multiple_of((data_place - half) * DOCS, 8), 8)

    def own_rows(ref):
        found = ref[rows8, :]
        return jnp.where(half == 0, found[:DOCS], found[DOCS:])

    own = own_rows(pooled_ref)
    own_inverse = lax.rsqrt(jnp.sum(own * own, axis=1, keepdims=True) + EMBED_EPSILON)
    own_emb = own * own_inverse
    own_expo = own_rows(expo_ref)
    own_totals = 1.0 / jnp.sum(own_expo, axis=1, keepdims=True)
    slots = lax.broadcasted_iota(jnp.int32, (DOCS, NDOC), 0)
    lanes = lax.broadcasted_iota(jnp.int32, (DOCS, NDOC), 1)
    partner = jnp.where(
        slots == 0, pair_ref[0, 0],
        jnp.where(slots == 1, pair_ref[0, 1], jnp.where(slots == 2, pair_ref[0, 2], pair_ref[0, 3])),
    )
    both = own_expo * (own_totals + totals) - jnp.where(lanes == partner, 2.0, 0.0)
    weights = jnp.concatenate([both, both], axis=0).T
    emb_grad = jnp.concatenate(
        [jnp.sum(weights[:, d : d + 1] * emb, axis=0, keepdims=True) for d in range(DOCS)], axis=0
    ) * (1.0 / SOFTMAX_TEMPER)
    pooled_grad = (emb_grad - own_emb * jnp.sum(own_emb * emb_grad, axis=1, keepdims=True)) * own_inverse
    slot = lax.broadcasted_iota(jnp.int32, (DOCS, 1), 0)
    length = jnp.where(
        slot == 0, lengths_ref[0, 0],
        jnp.where(slot == 1, lengths_ref[0, 1], jnp.where(slot == 2, lengths_ref[0, 2], lengths_ref[0, 3])),
    ).astype(f32)
    scaled = pooled_grad * (1.0 / length) * gain_ref[...][None]
    centered = scaled - jnp.mean(scaled, axis=1, keepdims=True)
    scaled_ref[...] = centered
    share = pl.ds(pl.multiple_of(lax.rem(place, 2) * HALF, 128), HALF)

    def grad(first, normal, normal_share, inverse):
        row_doc = doc_of(ends, first + lax.broadcasted_iota(jnp.int32, (ROWS, 1), 0))

        def spread(values):
            pick = jnp.where(row_doc == 2, values[2:3], values[3:4])
            return jnp.where(row_doc == 0, values[0:1], jnp.where(row_doc == 1, values[1:2], pick))

        along = jnp.mean(spread(scaled) * normal, axis=1, keepdims=True)
        return (inverse * (spread(scaled_ref[:, share]) - normal_share * along)).astype(bf16)

    mine = grad(place * ROWS, normal_ref[...], normal_ref[:, share], inverse_ref[...])
    product = jnp.dot(mixed_ref[...], mine, preferred_element_type=f32)
    inverse = other_rows_ref[:, D:].astype(f32)
    theirs = grad(
        (place ^ 1) * ROWS,
        other_rows_ref[:, :D].astype(f32),
        other_rows_ref[:, share].astype(f32),
        inverse[:, 0:1] + inverse[:, 1:2],
    )
    product += jnp.dot(other_mixed_ref[...], theirs, preferred_element_type=f32)
    out_ref[...] = product.astype(bf16)
    write.wait()


SMEM = pl.BlockSpec(memory_space=pltpu.SMEM)
VMEM = pl.BlockSpec(memory_space=pltpu.VMEM)
ANY = pl.BlockSpec(memory_space=pl.ANY)


def call(kernel, name, smem, vmem, outs, scratch, flops, aliases={}, whole=(), hbm_outs=0, sems=()):
    return pl.pallas_call(
        kernel,
        name=name,
        out_shape=[jax.ShapeDtypeStruct(s, t) for s, t in outs],
        in_specs=[SMEM] * len(smem) + [VMEM] * len(vmem) + [ANY] * len(whole),
        out_specs=[VMEM] * (len(outs) - hbm_outs) + [ANY] * hbm_outs,
        scratch_shapes=[pltpu.VMEM(s, t) for s, t in scratch] + list(sems),
        input_output_aliases=aliases,
        cost_estimate=pl.CostEstimate(flops=flops, bytes_accessed=1 << 26, transcendentals=0),
        compiler_params=pltpu.CompilerParams(vmem_limit_bytes=VMEM_LIMIT),
    )(*smem, *vmem, *whole)


def copies(value, axis, count):
    return lax.all_to_all(jnp.broadcast_to(value[None], (count,) + value.shape), axis, 0, 0, tiled=True)


def sum_over_chips(value):
    one, two, three = [
        lax.ppermute(value, "ctx", [(c, (c + 2 * hops) % CTX) for c in range(CTX)]).astype(jnp.float32)
        for hops in (1, 2, 3)
    ]
    return (value.astype(jnp.float32) + two) + (one + three)


def per_device(hidden_in, w_qkv, w_out, b_out, ln_gain, ln_bias, doc_lengths, pair_of):
    f32, bf16 = jnp.float32, jnp.bfloat16
    own = hidden_in[0]
    places = jnp.stack([lax.axis_index("ctx"), lax.axis_index("dp")]).astype(jnp.int32)
    smem = [doc_lengths, places]
    state = [((HEADS, AUG, ROWS), f32)]
    work = [((HEADS, AUG, 2 * ROWS), bf16)]
    held = ((PAIRS, 256, 2 * ROWS), bf16)

    def fold(name, sources, blocks, acc):
        (acc,) = call(
            functools.partial(fold_kernel, sources), name, smem, [w_qkv, qbd, acc, *blocks], state, work,
            1 << 34, {4: 0},
        )
        return acc

    near = lax.ppermute(own, "ctx", AROUND)
    other = lax.ppermute(own, "ctx", CORE_SWAP)
    qbd, acc = call(queries_kernel, "queries", smem, [own, w_qkv], [held] + state, [], 1 << 34)
    own_later, acc = lax.optimization_barrier((own, acc))
    behind = lax.ppermute(own_later, "ctx", BACK)
    acc = fold("own", SOURCES[0:2], [own, other], acc)
    near, acc = lax.optimization_barrier((near, acc))
    far = lax.ppermute(near, "ctx", AROUND)
    near_other = lax.ppermute(near, "ctx", CORE_SWAP)
    acc = fold("near", SOURCES[2:3], [near], acc)
    near_other, acc = lax.optimization_barrier((near_other, acc))
    acc = fold("near_other", SOURCES[3:4], [near_other], acc)
    behind, acc = lax.optimization_barrier((behind, acc))
    behind_other = lax.ppermute(behind, "ctx", CORE_SWAP)
    acc = fold("behind", SOURCES[4:5], [behind], acc)
    behind_other, acc = lax.optimization_barrier((behind_other, acc))
    acc = fold("behind_other", SOURCES[5:6], [behind_other], acc)
    far, acc = lax.optimization_barrier((far, acc))
    far_other = lax.ppermute(far, "ctx", CORE_SWAP)
    acc = fold("far", SOURCES[6:7], [far], acc)
    far_other, acc = lax.optimization_barrier((far_other, acc))
    _, mixed, normal, inverse, rows, partials = call(
        last_kernel,
        "last",
        smem,
        [far_other, w_qkv, qbd, acc, own, w_out, b_out, ln_gain, ln_bias],
        state
        + [((D, ROWS), bf16), ((ROWS, D), f32), ((ROWS, 1), f32), ((ROWS, D + 128), bf16), ((CTX, DOCS, D), f32)],
        work + [((8, 2 * ROWS), f32), ((len(SOURCES), ROWS, D), bf16)],
        1 << 34,
        {5: 0},
        [own, other, near, near_other, behind, behind_other, far, far_other],
    )
    other_mixed = lax.ppermute(mixed, "ctx", CORE_SWAP)
    other_rows = lax.ppermute(rows, "ctx", CORE_SWAP)
    pooled = jnp.sum(lax.all_to_all(partials, "ctx", 0, 0, tiled=True), axis=0)
    every = copies(pooled, "dp", DP).reshape(NDOC, D)
    every, other_mixed, other_rows = lax.optimization_barrier((every, other_mixed, other_rows))
    term, encoded = call(
        back_kernel,
        "back",
        smem + [pair_of],
        [every, mixed, normal, inverse, other_mixed, other_rows, ln_gain, ln_bias],
        [((D, HALF), bf16), ((ROWS, D), bf16)],
        [((NDOC, NDOC), f32), ((DOCS, D), f32), ((ROWS, D), bf16)],
        1 << 20,
        hbm_outs=1,
        sems=[pltpu.SemaphoreType.DMA],
    )
    share = D // DP
    pieces = lax.all_to_all(term.reshape(DP, share, HALF), "dp", 0, 0, tiled=True)
    piece = sum_over_chips(jnp.sum(pieces.astype(f32), axis=0).astype(bf16))
    other_piece = lax.ppermute(piece, "ctx", CORE_SWAP)
    mine = (jnp.arange(D, dtype=jnp.int32) >= HALF).astype(jnp.int32) == lax.rem(places[0], 2)
    grad_out = jnp.where(
        mine[None],
        jnp.concatenate([piece, piece], axis=1),
        jnp.concatenate([other_piece, other_piece], axis=1),
    )
    return (encoded[None], grad_out)


def solution(mesh):
    return jax.shard_map(
        per_device,
        mesh=mesh,
        in_specs=(P("dp", "ctx", None), P(), P(), P(), P(), P(), P("dp", None), P("dp", None)),
        out_specs=(P("dp", "ctx", None), P("dp", None)),
        check_vma=False,
    )
```

```python
import functools

import jax
import jax.numpy as jnp
from jax import lax
from jax.experimental import pallas as pl
from jax.experimental.pallas import tpu as pltpu
from jax.sharding import PartitionSpec as P

D = 768
HEADS = 12
HEAD_DIM = 64
PAIRS = HEADS // 2
DOCS = 4
NDOC = 128
ROWS = 256
CTX = 8
DP = 32
HALF = D // 2
AUG = 80

SOFTMAX_TEMPER = 0.05
NORM_EPSILON = 1e-05
EMBED_EPSILON = 1e-06
PENALTY = -1e30

VMEM_LIMIT = 24 * 1024 * 1024

CORE_SWAP = [(c, c ^ 1) for c in range(CTX)]
AROUND = [(c, (c + 2) % CTX if c % 2 == 0 else (c - 2) % CTX) for c in range(CTX)]
BACK = [(b, a) for a, b in AROUND]


def came_from(place, hops):
    step = 2 * hops
    return lax.rem(jnp.where(lax.rem(place, 2) == 0, place - step, place + step) + 2 * CTX, CTX)


SOURCES = [(0, 0), (1, 0), (0, 1), (1, 1), (0, -1), (1, -1), (0, 2), (1, 2)]


def doc_ends(lengths_ref):
    e0 = lengths_ref[0, 0]
    e1 = e0 + lengths_ref[0, 1]
    e2 = e1 + lengths_ref[0, 2]
    e3 = e2 + lengths_ref[0, 3]
    return e0, e1, e2, e3


def doc_of(ends, positions):
    e0, e1, e2, e3 = ends
    one = jnp.int32(1)
    zero = jnp.int32(0)
    return sum(jnp.where(positions >= e, one, zero) for e in (e0, e1, e2, e3))


def needed_span(ends, first):
    e0, e1, e2, e3 = ends
    last = first + ROWS - 1
    low = jnp.where(first >= e2, e2, jnp.where(first >= e1, e1, jnp.where(first >= e0, e0, 0)))
    high = jnp.where(last < e0, e0, jnp.where(last < e1, e1, jnp.where(last < e2, e2, e3)))
    return low, high


def fill_queries(ends, first, own, wqkv_ref, qbd):
    queries = lax.dot_general(
        wqkv_ref[:, :D], own, (((0,), (1,)), ((), ())), preferred_element_type=jnp.float32
    )
    queries = (queries.astype(jnp.bfloat16).astype(jnp.float32) * HEAD_DIM**-0.5).astype(jnp.bfloat16)
    positions = first + lax.broadcasted_iota(jnp.int32, (HEAD_DIM * 2, ROWS), 1)
    slots = lax.broadcasted_iota(jnp.int32, (HEAD_DIM * 2, ROWS), 0)
    same = (doc_of(ends, positions) == slots) | (slots >= DOCS)
    penalty = jnp.where(same, 0.0, PENALTY).astype(jnp.bfloat16)
    penalties = jnp.concatenate([penalty, penalty], axis=1)
    zero = jnp.zeros((HEAD_DIM, ROWS), jnp.bfloat16)
    for j in range(PAIRS):
        qbd[j, :64, :ROWS] = queries[128 * j : 128 * j + 64, :]
        qbd[j, :64, ROWS:] = zero
        qbd[j, 64:128, :ROWS] = zero
        qbd[j, 64:128, ROWS:] = queries[128 * j + 64 : 128 * j + 128, :]
        qbd[j, 128:, :] = penalties


def project(ends, bases, blocks, wqkv_ref, vt):
    rows = ROWS * len(blocks)
    hidden = jnp.concatenate(blocks, axis=0) if len(blocks) > 1 else blocks[0]
    keys = jnp.dot(hidden, wqkv_ref[:, D : 2 * D], preferred_element_type=jnp.float32).astype(jnp.bfloat16)
    values = lax.dot_general(
        wqkv_ref[:, 2 * D :], hidden, (((0,), (1,)), ((), ())), preferred_element_type=jnp.float32
    ).astype(jnp.bfloat16)
    vt[:, :HEAD_DIM, :rows] = values.reshape(HEADS, HEAD_DIM, rows)
    offsets = lax.broadcasted_iota(jnp.int32, (ROWS, 128), 0)
    lanes = lax.broadcasted_iota(jnp.int32, (ROWS, 128), 1)
    onehots = [
        jnp.where(doc_of(ends, base + offsets) == lanes, 1.0, 0.0).astype(jnp.bfloat16) for base in bases
    ]
    return keys, jnp.concatenate(onehots, axis=0) if len(blocks) > 1 else onehots[0]


def pair_scores(keys, onehot, qbd, j):
    pair_keys = jnp.concatenate([keys[:, 128 * j : 128 * j + 128], onehot], axis=1)
    return jnp.dot(pair_keys, qbd[j], preferred_element_type=jnp.float32)


def attend_plain(ends, bases, blocks, wqkv_ref, qbd, vt, acc_ref):
    rows = ROWS * len(blocks)
    keys, onehot = project(ends, bases, blocks, wqkv_ref, vt)
    for j in range(PAIRS):
        weights = jnp.exp(pair_scores(keys, onehot, qbd, j)).astype(jnp.bfloat16)
        for h in range(2):
            part = slice(ROWS * h, ROWS * h + ROWS)
            acc_ref[2 * j + h] += jnp.dot(
                vt[2 * j + h, :, :rows], weights[:, part], preferred_element_type=jnp.float32
            )


def attend_shifted(ends, base, block, wqkv_ref, qbd, vt, m_ref, acc_ref):
    keys, onehot = project(ends, [base], [block], wqkv_ref, vt)
    for j in range(PAIRS):
        scores = pair_scores(keys, onehot, qbd, j)
        old = m_ref[j : j + 1, :]
        new = jnp.maximum(old, jnp.max(scores, axis=0, keepdims=True))
        m_ref[j : j + 1, :] = new
        shrink = jnp.exp(old - new)
        weights = jnp.exp(scores - new).astype(jnp.bfloat16)
        for h in range(2):
            part = slice(ROWS * h, ROWS * h + ROWS)
            mixed = jnp.dot(vt[2 * j + h, :, :ROWS], weights[:, part], preferred_element_type=jnp.float32)
            acc_ref[2 * j + h] = acc_ref[2 * j + h] * shrink[:, part] + mixed


def fill_ones(vt):
    row = lax.broadcasted_iota(jnp.int32, (HEADS, AUG - HEAD_DIM, vt.shape[2]), 1)
    vt[:, HEAD_DIM:, :] = jnp.where(row == 0, 1.0, 0.0).astype(jnp.bfloat16)


def attend_blocks(ends, first, places, blocks, wqkv_ref, qbd, vt, acc_ref):
    low, high = needed_span(ends, first)
    bases = [place * ROWS for place in places]
    wanted = [(base < high) & (base + ROWS > low) for base in bases]

    def attend(which):
        attend_plain(
            ends, [bases[i] for i in which], [blocks[i][...] for i in which], wqkv_ref, qbd, vt, acc_ref
        )

    if len(blocks) == 1:
        pl.when(wanted[0])(lambda: attend([0]))
    else:
        one, two = wanted
        pl.when(one & two)(lambda: attend([0, 1]))
        pl.when(one & jnp.logical_not(two))(lambda: attend([0]))
        pl.when(two & jnp.logical_not(one))(lambda: attend([1]))


def queries_kernel(lengths_ref, place_ref, own_ref, wqkv_ref, qbd, acc_ref):
    ends = doc_ends(lengths_ref)
    fill_queries(ends, place_ref[0] * ROWS, own_ref[...], wqkv_ref, qbd)
    acc_ref[...] = jnp.zeros(acc_ref.shape, jnp.float32)


def fold_kernel(sources, lengths_ref, place_ref, wqkv_ref, qbd, acc_in, *refs):
    blocks, (acc_ref, vt) = refs[: len(sources)], refs[len(sources) :]
    place = place_ref[0]
    ends = doc_ends(lengths_ref)
    fill_ones(vt)
    places = [came_from(place ^ flip, hops) for flip, hops in sources]
    attend_blocks(ends, place * ROWS, places, blocks, wqkv_ref, qbd, vt, acc_ref)


def in_range(acc):
    sums = acc[:, HEAD_DIM, :]
    good = jnp.where((sums >= 1e-12) & (sums <= 1e12), 1.0, 0.0)
    finite = jnp.where(jnp.abs(acc) <= 1e38, 1.0, 0.0)
    return jnp.minimum(jnp.min(good), jnp.min(finite)) > 0.5


def attend_again(ends, place, blocks, wqkv_ref, qbd, vt, acc_ref, m_ref, held):
    for i, (flip, hops) in enumerate(SOURCES):
        pltpu.sync_copy(blocks[i], held.at[i])
    m_ref[...] = jnp.full(m_ref.shape, PENALTY, jnp.float32)
    acc_ref[...] = jnp.zeros(acc_ref.shape, jnp.float32)
    low, high = needed_span(ends, place * ROWS)

    def step(i, carry):
        base = jnp.int32(0)
        for k, (flip, hops) in enumerate(SOURCES):
            base = jnp.where(i == k, came_from(place ^ flip, hops) * ROWS, base)

        @pl.when((base < high) & (base + ROWS > low))
        def _():
            attend_shifted(ends, base, held[i], wqkv_ref, qbd, vt, m_ref, acc_ref)

        return carry

    lax.fori_loop(0, len(SOURCES), step, 0)


def last_kernel(
    lengths_ref, place_ref, far_other_ref, wqkv_ref, qbd, acc_in, own_ref, wout_ref, bias_ref, gain_ref, shift_ref,
    *refs
):
    blocks, refs = refs[: len(SOURCES)], refs[len(SOURCES) :]
    acc_ref, mixed_ref, normal_ref, inverse_ref, rows_ref, pooled_ref, vt, m_ref, held = refs
    place = place_ref[0]
    ends = doc_ends(lengths_ref)
    first = place * ROWS
    fill_ones(vt)
    flip, hops = SOURCES[-1]
    attend_blocks(ends, first, [came_from(place ^ flip, hops)], [far_other_ref], wqkv_ref, qbd, vt, acc_ref)

    @pl.when(jnp.logical_not(in_range(acc_ref[...])))
    def _():
        attend_again(ends, place, blocks, wqkv_ref, qbd, vt, acc_ref, m_ref, held)

    acc = acc_ref[...]
    mixed = acc[:, :HEAD_DIM, :] * (1.0 / acc[:, HEAD_DIM : HEAD_DIM + 1, :])
    mixed = mixed.reshape(D, ROWS).astype(jnp.bfloat16)
    mixed_ref[...] = mixed
    summed = lax.dot_general(
        mixed, wout_ref[...], (((0,), (0,)), ((), ())), preferred_element_type=jnp.float32
    )
    summed = summed + bias_ref[...][None] + own_ref[...].astype(jnp.float32)
    centered = summed - jnp.mean(summed, axis=1, keepdims=True)
    inverse = lax.rsqrt(jnp.mean(centered * centered, axis=1, keepdims=True) + NORM_EPSILON)
    normal = centered * inverse
    normal_ref[...] = normal
    inverse_ref[...] = inverse
    layer = normal * gain_ref[...][None] + shift_ref[...][None]
    rows_ref[:, :D] = normal.astype(jnp.bfloat16)
    high = inverse.astype(jnp.bfloat16).astype(jnp.float32)
    lane = lax.broadcasted_iota(jnp.int32, (ROWS, 128), 1)
    rows_ref[:, D:] = jnp.where(lane == 0, high, inverse - high).astype(jnp.bfloat16)
    row_doc = doc_of(ends, first + lax.broadcasted_iota(jnp.int32, (ROWS, 1), 0))
    pooled_ref[...] = jnp.zeros(pooled_ref.shape, jnp.float32)
    starts = (jnp.int32(0), *ends[:-1])
    for d in range(DOCS):

        @pl.when((starts[d] < first + ROWS) & (ends[d] > first))
        def _():
            total = jnp.sum(jnp.where(row_doc == d, layer, 0.0), axis=0, keepdims=True)
            mean = total * (1.0 / lengths_ref[0, d].astype(jnp.float32))
            pooled_ref[:, d : d + 1, :] = jnp.broadcast_to(mean[None], (CTX, 1, D))


def back_kernel(
    lengths_ref, place_ref, pair_ref, pooled_ref, mixed_ref, normal_ref, inverse_ref, other_mixed_ref, other_rows_ref,
    gain_ref, shift_ref, out_ref, encoded_hbm, expo_ref, scaled_ref, encoded_ref, sem
):
    place = place_ref[0]
    data_place = place_ref[1]
    ends = doc_ends(lengths_ref)
    f32, bf16 = jnp.float32, jnp.bfloat16
    encoded_ref[...] = (normal_ref[...] * gain_ref[...][None] + shift_ref[...][None]).astype(bf16)
    write = pltpu.make_async_copy(encoded_ref, encoded_hbm, sem)
    write.start()

    pooled = pooled_ref[...]
    emb = pooled * lax.rsqrt(jnp.sum(pooled * pooled, axis=1, keepdims=True) + EMBED_EPSILON)
    high = emb.astype(bf16)
    low = (emb - high.astype(f32)).astype(bf16)

    def times(left, right):
        return lax.dot_general(left, right, (((1,), (1,)), ((), ())), preferred_element_type=f32)

    sims = (times(high, high) + (times(high, low) + times(low, high))) * (1.0 / SOFTMAX_TEMPER)
    columns = lax.broadcasted_iota(jnp.int32, (NDOC, NDOC), 1)
    rows = lax.broadcasted_iota(jnp.int32, (NDOC, NDOC), 0)
    expo = jnp.where(rows == columns, 0.0, jnp.exp(sims))
    expo_ref[...] = expo
    totals = 1.0 / jnp.sum(expo, axis=0, keepdims=True)
    half = lax.rem(data_place, 2)
    rows8 = pl.ds(pl.multiple_of((data_place - half) * DOCS, 8), 8)

    def own_rows(ref):
        found = ref[rows8, :]
        return jnp.where(half == 0, found[:DOCS], found[DOCS:])

    own = own_rows(pooled_ref)
    own_inverse = lax.rsqrt(jnp.sum(own * own, axis=1, keepdims=True) + EMBED_EPSILON)
    own_emb = own * own_inverse
    own_expo = own_rows(expo_ref)
    own_totals = 1.0 / jnp.sum(own_expo, axis=1, keepdims=True)
    slots = lax.broadcasted_iota(jnp.int32, (DOCS, NDOC), 0)
    lanes = lax.broadcasted_iota(jnp.int32, (DOCS, NDOC), 1)
    partner = jnp.where(
        slots == 0, pair_ref[0, 0],
        jnp.where(slots == 1, pair_ref[0, 1], jnp.where(slots == 2, pair_ref[0, 2], pair_ref[0, 3])),
    )
    both = own_expo * (own_totals + totals) - jnp.where(lanes == partner, 2.0, 0.0)
    weights = jnp.concatenate([both, both], axis=0).T
    emb_grad = jnp.concatenate(
        [jnp.sum(weights[:, d : d + 1] * emb, axis=0, keepdims=True) for d in range(DOCS)], axis=0
    ) * (1.0 / SOFTMAX_TEMPER)
    pooled_grad = (emb_grad - own_emb * jnp.sum(own_emb * emb_grad, axis=1, keepdims=True)) * own_inverse
    slot = lax.broadcasted_iota(jnp.int32, (DOCS, 1), 0)
    length = jnp.where(
        slot == 0, lengths_ref[0, 0],
        jnp.where(slot == 1, lengths_ref[0, 1], jnp.where(slot == 2, lengths_ref[0, 2], lengths_ref[0, 3])),
    ).astype(f32)
    scaled = pooled_grad * (1.0 / length) * gain_ref[...][None]
    centered = scaled - jnp.mean(scaled, axis=1, keepdims=True)
    scaled_ref[...] = centered
    share = pl.ds(pl.multiple_of(lax.rem(place, 2) * HALF, 128), HALF)

    def grad(first, normal, normal_share, inverse):
        row_doc = doc_of(ends, first + lax.broadcasted_iota(jnp.int32, (ROWS, 1), 0))

        def spread(values):
            pick = jnp.where(row_doc == 2, values[2:3], values[3:4])
            return jnp.where(row_doc == 0, values[0:1], jnp.where(row_doc == 1, values[1:2], pick))

        along = jnp.mean(spread(scaled) * normal, axis=1, keepdims=True)
        return (inverse * (spread(scaled_ref[:, share]) - normal_share * along)).astype(bf16)

    mine = grad(place * ROWS, normal_ref[...], normal_ref[:, share], inverse_ref[...])
    product = jnp.dot(mixed_ref[...], mine, preferred_element_type=f32)
    inverse = other_rows_ref[:, D:].astype(f32)
    theirs = grad(
        (place ^ 1) * ROWS,
        other_rows_ref[:, :D].astype(f32),
        other_rows_ref[:, share].astype(f32),
        inverse[:, 0:1] + inverse[:, 1:2],
    )
    product += jnp.dot(other_mixed_ref[...], theirs, preferred_element_type=f32)
    out_ref[...] = product.astype(bf16)
    write.wait()


def join_kernel(halves_ref, out_ref):
    for core in range(2):
        parts = [halves_ref[c].astype(jnp.float32) for c in range(core, CTX, 2)]
        out_ref[:, HALF * core : HALF * (core + 1)] = (parts[0] + parts[1]) + (parts[2] + parts[3])


SMEM = pl.BlockSpec(memory_space=pltpu.SMEM)
VMEM = pl.BlockSpec(memory_space=pltpu.VMEM)
ANY = pl.BlockSpec(memory_space=pl.ANY)


def call(kernel, name, smem, vmem, outs, scratch, flops, aliases={}, whole=(), hbm_outs=0, sems=()):
    return pl.pallas_call(
        kernel,
        name=name,
        out_shape=[jax.ShapeDtypeStruct(s, t) for s, t in outs],
        in_specs=[SMEM] * len(smem) + [VMEM] * len(vmem) + [ANY] * len(whole),
        out_specs=[VMEM] * (len(outs) - hbm_outs) + [ANY] * hbm_outs,
        scratch_shapes=[pltpu.VMEM(s, t) for s, t in scratch] + list(sems),
        input_output_aliases=aliases,
        cost_estimate=pl.CostEstimate(flops=flops, bytes_accessed=1 << 26, transcendentals=0),
        compiler_params=pltpu.CompilerParams(vmem_limit_bytes=VMEM_LIMIT),
    )(*smem, *vmem, *whole)


def copies(value, axis, count):
    return lax.all_to_all(jnp.broadcast_to(value[None], (count,) + value.shape), axis, 0, 0, tiled=True)


def per_device(hidden_in, w_qkv, w_out, b_out, ln_gain, ln_bias, doc_lengths, pair_of):
    f32, bf16 = jnp.float32, jnp.bfloat16
    own = hidden_in[0]
    places = jnp.stack([lax.axis_index("ctx"), lax.axis_index("dp")]).astype(jnp.int32)
    smem = [doc_lengths, places]
    state = [((HEADS, AUG, ROWS), f32)]
    work = [((HEADS, AUG, 2 * ROWS), bf16)]
    held = ((PAIRS, 256, 2 * ROWS), bf16)

    def fold(name, sources, blocks, acc):
        (acc,) = call(
            functools.partial(fold_kernel, sources), name, smem, [w_qkv, qbd, acc, *blocks], state, work,
            1 << 34, {4: 0},
        )
        return acc

    def after(value, acc):
        return lax.optimization_barrier((value, acc))

    near = lax.ppermute(own, "ctx", AROUND)
    qbd, acc = call(queries_kernel, "queries", smem, [own, w_qkv], [held] + state, [], 1 << 34)
    later, acc = after(own, acc)
    other = lax.ppermute(later, "ctx", CORE_SWAP)
    acc = fold("own", SOURCES[0:1], [own], acc)
    later, acc = after(own, acc)
    behind = lax.ppermute(later, "ctx", BACK)
    near, acc = after(near, acc)
    far = lax.ppermute(near, "ctx", AROUND)
    acc = fold("near", SOURCES[2:3], [near], acc)
    later, acc = after(near, acc)
    near_other = lax.ppermute(later, "ctx", CORE_SWAP)
    acc = fold("other", SOURCES[1:2], [other], acc)
    behind, acc = after(behind, acc)
    acc = fold("behind", SOURCES[4:5], [behind], acc)
    later, acc = after(behind, acc)
    behind_other = lax.ppermute(later, "ctx", CORE_SWAP)
    acc = fold("near_other", SOURCES[3:4], [near_other], acc)
    behind_other, acc = after(behind_other, acc)
    acc = fold("behind_other", SOURCES[5:6], [behind_other], acc)
    far, acc = after(far, acc)
    far_other = lax.ppermute(far, "ctx", CORE_SWAP)
    acc = fold("far", SOURCES[6:7], [far], acc)
    far_other, acc = after(far_other, acc)
    _, mixed, normal, inverse, rows, partials = call(
        last_kernel,
        "last",
        smem,
        [far_other, w_qkv, qbd, acc, own, w_out, b_out, ln_gain, ln_bias],
        state
        + [((D, ROWS), bf16), ((ROWS, D), f32), ((ROWS, 1), f32), ((ROWS, D + 128), bf16), ((CTX, DOCS, D), f32)],
        work + [((8, 2 * ROWS), f32), ((len(SOURCES), ROWS, D), bf16)],
        1 << 34,
        {5: 0},
        [own, other, near, near_other, behind, behind_other, far, far_other],
    )
    other_mixed = lax.ppermute(mixed, "ctx", CORE_SWAP)
    other_rows = lax.ppermute(rows, "ctx", CORE_SWAP)
    pooled = jnp.sum(lax.all_to_all(partials, "ctx", 0, 0, tiled=True), axis=0)
    every = copies(pooled, "dp", DP).reshape(NDOC, D)
    every, other_mixed, other_rows = lax.optimization_barrier((every, other_mixed, other_rows))
    term, encoded = call(
        back_kernel,
        "back",
        smem + [pair_of],
        [every, mixed, normal, inverse, other_mixed, other_rows, ln_gain, ln_bias],
        [((D, HALF), bf16), ((ROWS, D), bf16)],
        [((NDOC, NDOC), f32), ((DOCS, D), f32), ((ROWS, D), bf16)],
        1 << 20,
        hbm_outs=1,
        sems=[pltpu.SemaphoreType.DMA],
    )
    share = D // DP
    pieces = lax.all_to_all(term.reshape(DP, share, HALF), "dp", 0, 0, tiled=True)
    piece = jnp.sum(pieces.astype(f32), axis=0).astype(bf16)
    halves = copies(piece, "ctx", CTX)
    (grad_out,) = call(join_kernel, "join", [], [halves], [((share, D), f32)], [], 1 << 20)
    return (encoded[None], grad_out)


def solution(mesh):
    return jax.shard_map(
        per_device,
        mesh=mesh,
        in_specs=(P("dp", "ctx", None), P(), P(), P(), P(), P(), P("dp", None), P("dp", None)),
        out_specs=(P("dp", "ctx", None), P("dp", None)),
        check_vma=False,
    )
```

```python
import functools

import jax
import jax.numpy as jnp
from jax import lax
from jax.experimental import pallas as pl
from jax.experimental.pallas import tpu as pltpu
from jax.sharding import PartitionSpec as P

D = 768
HEADS = 12
HEAD_DIM = 64
PAIRS = HEADS // 2
DOCS = 4
NDOC = 128
ROWS = 256
CTX = 8
DP = 32
HALF = D // 2
AUG = 80

SOFTMAX_TEMPER = 0.05
NORM_EPSILON = 1e-05
EMBED_EPSILON = 1e-06
PENALTY = -1e30

VMEM_LIMIT = 24 * 1024 * 1024

CORE_SWAP = [(c, c ^ 1) for c in range(CTX)]
AROUND = [(c, (c + 2) % CTX if c % 2 == 0 else (c - 2) % CTX) for c in range(CTX)]
BACK = [(b, a) for a, b in AROUND]


def came_from(place, hops):
    step = 2 * hops
    return lax.rem(jnp.where(lax.rem(place, 2) == 0, place - step, place + step) + 2 * CTX, CTX)


SOURCES = [(0, 0), (1, 0), (0, 1), (1, 1), (0, -1), (1, -1), (0, 2), (1, 2)]


def doc_ends(lengths_ref):
    e0 = lengths_ref[0, 0]
    e1 = e0 + lengths_ref[0, 1]
    e2 = e1 + lengths_ref[0, 2]
    e3 = e2 + lengths_ref[0, 3]
    return e0, e1, e2, e3


def doc_of(ends, positions):
    e0, e1, e2, e3 = ends
    one = jnp.int32(1)
    zero = jnp.int32(0)
    return sum(jnp.where(positions >= e, one, zero) for e in (e0, e1, e2, e3))


def needed_span(ends, first):
    e0, e1, e2, e3 = ends
    last = first + ROWS - 1
    low = jnp.where(first >= e2, e2, jnp.where(first >= e1, e1, jnp.where(first >= e0, e0, 0)))
    high = jnp.where(last < e0, e0, jnp.where(last < e1, e1, jnp.where(last < e2, e2, e3)))
    return low, high


def fill_queries(ends, first, own, wqkv_ref, qbd):
    queries = lax.dot_general(
        wqkv_ref[:, :D], own, (((0,), (1,)), ((), ())), preferred_element_type=jnp.float32
    )
    queries = (queries.astype(jnp.bfloat16).astype(jnp.float32) * HEAD_DIM**-0.5).astype(jnp.bfloat16)
    positions = first + lax.broadcasted_iota(jnp.int32, (HEAD_DIM * 2, ROWS), 1)
    slots = lax.broadcasted_iota(jnp.int32, (HEAD_DIM * 2, ROWS), 0)
    same = (doc_of(ends, positions) == slots) | (slots >= DOCS)
    penalty = jnp.where(same, 0.0, PENALTY).astype(jnp.bfloat16)
    penalties = jnp.concatenate([penalty, penalty], axis=1)
    zero = jnp.zeros((HEAD_DIM, ROWS), jnp.bfloat16)
    for j in range(PAIRS):
        qbd[j, :64, :ROWS] = queries[128 * j : 128 * j + 64, :]
        qbd[j, :64, ROWS:] = zero
        qbd[j, 64:128, :ROWS] = zero
        qbd[j, 64:128, ROWS:] = queries[128 * j + 64 : 128 * j + 128, :]
        qbd[j, 128:, :] = penalties


def project(ends, bases, blocks, wqkv_ref, vt):
    rows = ROWS * len(blocks)
    hidden = jnp.concatenate(blocks, axis=0) if len(blocks) > 1 else blocks[0]
    keys = jnp.dot(hidden, wqkv_ref[:, D : 2 * D], preferred_element_type=jnp.float32).astype(jnp.bfloat16)
    values = lax.dot_general(
        wqkv_ref[:, 2 * D :], hidden, (((0,), (1,)), ((), ())), preferred_element_type=jnp.float32
    ).astype(jnp.bfloat16)
    vt[:, :HEAD_DIM, :rows] = values.reshape(HEADS, HEAD_DIM, rows)
    offsets = lax.broadcasted_iota(jnp.int32, (ROWS, 128), 0)
    lanes = lax.broadcasted_iota(jnp.int32, (ROWS, 128), 1)
    onehots = [
        jnp.where(doc_of(ends, base + offsets) == lanes, 1.0, 0.0).astype(jnp.bfloat16) for base in bases
    ]
    return keys, jnp.concatenate(onehots, axis=0) if len(blocks) > 1 else onehots[0]


def pair_scores(keys, onehot, qbd, j):
    pair_keys = jnp.concatenate([keys[:, 128 * j : 128 * j + 128], onehot], axis=1)
    return jnp.dot(pair_keys, qbd[j], preferred_element_type=jnp.float32)


def attend_plain(ends, bases, blocks, wqkv_ref, qbd, vt, acc_ref):
    rows = ROWS * len(blocks)
    keys, onehot = project(ends, bases, blocks, wqkv_ref, vt)
    for j in range(PAIRS):
        weights = jnp.exp(pair_scores(keys, onehot, qbd, j)).astype(jnp.bfloat16)
        for h in range(2):
            part = slice(ROWS * h, ROWS * h + ROWS)
            acc_ref[2 * j + h] += jnp.dot(
                vt[2 * j + h, :, :rows], weights[:, part], preferred_element_type=jnp.float32
            )


def attend_shifted(ends, base, block, wqkv_ref, qbd, vt, m_ref, acc_ref):
    keys, onehot = project(ends, [base], [block], wqkv_ref, vt)
    for j in range(PAIRS):
        scores = pair_scores(keys, onehot, qbd, j)
        old = m_ref[j : j + 1, :]
        new = jnp.maximum(old, jnp.max(scores, axis=0, keepdims=True))
        m_ref[j : j + 1, :] = new
        shrink = jnp.exp(old - new)
        weights = jnp.exp(scores - new).astype(jnp.bfloat16)
        for h in range(2):
            part = slice(ROWS * h, ROWS * h + ROWS)
            mixed = jnp.dot(vt[2 * j + h, :, :ROWS], weights[:, part], preferred_element_type=jnp.float32)
            acc_ref[2 * j + h] = acc_ref[2 * j + h] * shrink[:, part] + mixed


def fill_ones(vt):
    row = lax.broadcasted_iota(jnp.int32, (HEADS, AUG - HEAD_DIM, vt.shape[2]), 1)
    vt[:, HEAD_DIM:, :] = jnp.where(row == 0, 1.0, 0.0).astype(jnp.bfloat16)


def attend_blocks(ends, first, places, blocks, wqkv_ref, qbd, vt, acc_ref):
    low, high = needed_span(ends, first)
    bases = [place * ROWS for place in places]
    wanted = [(base < high) & (base + ROWS > low) for base in bases]

    def attend(which):
        attend_plain(
            ends, [bases[i] for i in which], [blocks[i][...] for i in which], wqkv_ref, qbd, vt, acc_ref
        )

    if len(blocks) == 1:
        pl.when(wanted[0])(lambda: attend([0]))
    else:
        one, two = wanted
        pl.when(one & two)(lambda: attend([0, 1]))
        pl.when(one & jnp.logical_not(two))(lambda: attend([0]))
        pl.when(two & jnp.logical_not(one))(lambda: attend([1]))


def queries_kernel(lengths_ref, place_ref, own_ref, wqkv_ref, qbd, acc_ref):
    ends = doc_ends(lengths_ref)
    fill_queries(ends, place_ref[0] * ROWS, own_ref[...], wqkv_ref, qbd)
    acc_ref[...] = jnp.zeros(acc_ref.shape, jnp.float32)


def fold_kernel(sources, lengths_ref, place_ref, wqkv_ref, qbd, acc_in, *refs):
    blocks, (acc_ref, vt) = refs[: len(sources)], refs[len(sources) :]
    place = place_ref[0]
    ends = doc_ends(lengths_ref)
    fill_ones(vt)
    places = [came_from(place ^ flip, hops) for flip, hops in sources]
    attend_blocks(ends, place * ROWS, places, blocks, wqkv_ref, qbd, vt, acc_ref)


def in_range(acc):
    sums = acc[:, HEAD_DIM, :]
    good = jnp.where((sums >= 1e-12) & (sums <= 1e12), 1.0, 0.0)
    finite = jnp.where(jnp.abs(acc) <= 1e38, 1.0, 0.0)
    return jnp.minimum(jnp.min(good), jnp.min(finite)) > 0.5


def attend_again(ends, place, blocks, wqkv_ref, qbd, vt, acc_ref, m_ref, held):
    for i, (flip, hops) in enumerate(SOURCES):
        pltpu.sync_copy(blocks[i], held.at[i])
    m_ref[...] = jnp.full(m_ref.shape, PENALTY, jnp.float32)
    acc_ref[...] = jnp.zeros(acc_ref.shape, jnp.float32)
    low, high = needed_span(ends, place * ROWS)

    def step(i, carry):
        base = jnp.int32(0)
        for k, (flip, hops) in enumerate(SOURCES):
            base = jnp.where(i == k, came_from(place ^ flip, hops) * ROWS, base)

        @pl.when((base < high) & (base + ROWS > low))
        def _():
            attend_shifted(ends, base, held[i], wqkv_ref, qbd, vt, m_ref, acc_ref)

        return carry

    lax.fori_loop(0, len(SOURCES), step, 0)


def last_kernel(
    lengths_ref, place_ref, far_other_ref, wqkv_ref, qbd, acc_in, own_ref, wout_ref, bias_ref, gain_ref, shift_ref,
    *refs
):
    blocks, refs = refs[: len(SOURCES)], refs[len(SOURCES) :]
    acc_ref, mixed_ref, normal_ref, inverse_ref, rows_ref, pooled_ref, vt, m_ref, held = refs
    place = place_ref[0]
    ends = doc_ends(lengths_ref)
    first = place * ROWS
    fill_ones(vt)
    flip, hops = SOURCES[-1]
    attend_blocks(ends, first, [came_from(place ^ flip, hops)], [far_other_ref], wqkv_ref, qbd, vt, acc_ref)

    @pl.when(jnp.logical_not(in_range(acc_ref[...])))
    def _():
        attend_again(ends, place, blocks, wqkv_ref, qbd, vt, acc_ref, m_ref, held)

    acc = acc_ref[...]
    mixed = acc[:, :HEAD_DIM, :] * (1.0 / acc[:, HEAD_DIM : HEAD_DIM + 1, :])
    mixed = mixed.reshape(D, ROWS).astype(jnp.bfloat16)
    mixed_ref[...] = mixed
    summed = lax.dot_general(
        mixed, wout_ref[...], (((0,), (0,)), ((), ())), preferred_element_type=jnp.float32
    )
    summed = summed + bias_ref[...][None] + own_ref[...].astype(jnp.float32)
    centered = summed - jnp.mean(summed, axis=1, keepdims=True)
    inverse = lax.rsqrt(jnp.mean(centered * centered, axis=1, keepdims=True) + NORM_EPSILON)
    normal = centered * inverse
    normal_ref[...] = normal
    inverse_ref[...] = inverse
    layer = normal * gain_ref[...][None] + shift_ref[...][None]
    rows_ref[:, :D] = normal.astype(jnp.bfloat16)
    high = inverse.astype(jnp.bfloat16).astype(jnp.float32)
    lane = lax.broadcasted_iota(jnp.int32, (ROWS, 128), 1)
    rows_ref[:, D:] = jnp.where(lane == 0, high, inverse - high).astype(jnp.bfloat16)
    row_doc = doc_of(ends, first + lax.broadcasted_iota(jnp.int32, (ROWS, 1), 0))
    pooled_ref[...] = jnp.zeros(pooled_ref.shape, jnp.float32)
    starts = (jnp.int32(0), *ends[:-1])
    for d in range(DOCS):

        @pl.when((starts[d] < first + ROWS) & (ends[d] > first))
        def _():
            total = jnp.sum(jnp.where(row_doc == d, layer, 0.0), axis=0, keepdims=True)
            mean = total * (1.0 / lengths_ref[0, d].astype(jnp.float32))
            pooled_ref[:, d : d + 1, :] = jnp.broadcast_to(mean[None], (CTX, 1, D))


def back_kernel(
    lengths_ref, place_ref, pair_ref, pooled_ref, mixed_ref, normal_ref, inverse_ref, other_mixed_ref, other_rows_ref,
    gain_ref, shift_ref, out_ref, encoded_hbm, expo_ref, scaled_ref, encoded_ref, sem
):
    place = place_ref[0]
    data_place = place_ref[1]
    ends = doc_ends(lengths_ref)
    f32, bf16 = jnp.float32, jnp.bfloat16
    encoded_ref[...] = (normal_ref[...] * gain_ref[...][None] + shift_ref[...][None]).astype(bf16)
    write = pltpu.make_async_copy(encoded_ref, encoded_hbm, sem)
    write.start()

    pooled = pooled_ref[...]
    emb = pooled * lax.rsqrt(jnp.sum(pooled * pooled, axis=1, keepdims=True) + EMBED_EPSILON)
    high = emb.astype(bf16)
    low = (emb - high.astype(f32)).astype(bf16)

    def times(left, right):
        return lax.dot_general(left, right, (((1,), (1,)), ((), ())), preferred_element_type=f32)

    sims = (times(high, high) + (times(high, low) + times(low, high))) * (1.0 / SOFTMAX_TEMPER)
    columns = lax.broadcasted_iota(jnp.int32, (NDOC, NDOC), 1)
    rows = lax.broadcasted_iota(jnp.int32, (NDOC, NDOC), 0)
    expo = jnp.where(rows == columns, 0.0, jnp.exp(sims))
    expo_ref[...] = expo
    totals = 1.0 / jnp.sum(expo, axis=0, keepdims=True)
    half = lax.rem(data_place, 2)
    rows8 = pl.ds(pl.multiple_of((data_place - half) * DOCS, 8), 8)

    def own_rows(ref):
        found = ref[rows8, :]
        return jnp.where(half == 0, found[:DOCS], found[DOCS:])

    own = own_rows(pooled_ref)
    own_inverse = lax.rsqrt(jnp.sum(own * own, axis=1, keepdims=True) + EMBED_EPSILON)
    own_emb = own * own_inverse
    own_expo = own_rows(expo_ref)
    own_totals = 1.0 / jnp.sum(own_expo, axis=1, keepdims=True)
    slots = lax.broadcasted_iota(jnp.int32, (DOCS, NDOC), 0)
    lanes = lax.broadcasted_iota(jnp.int32, (DOCS, NDOC), 1)
    partner = jnp.where(
        slots == 0, pair_ref[0, 0],
        jnp.where(slots == 1, pair_ref[0, 1], jnp.where(slots == 2, pair_ref[0, 2], pair_ref[0, 3])),
    )
    both = own_expo * (own_totals + totals) - jnp.where(lanes == partner, 2.0, 0.0)
    weights = jnp.concatenate([both, both], axis=0).T
    emb_grad = jnp.concatenate(
        [jnp.sum(weights[:, d : d + 1] * emb, axis=0, keepdims=True) for d in range(DOCS)], axis=0
    ) * (1.0 / SOFTMAX_TEMPER)
    pooled_grad = (emb_grad - own_emb * jnp.sum(own_emb * emb_grad, axis=1, keepdims=True)) * own_inverse
    slot = lax.broadcasted_iota(jnp.int32, (DOCS, 1), 0)
    length = jnp.where(
        slot == 0, lengths_ref[0, 0],
        jnp.where(slot == 1, lengths_ref[0, 1], jnp.where(slot == 2, lengths_ref[0, 2], lengths_ref[0, 3])),
    ).astype(f32)
    scaled = pooled_grad * (1.0 / length) * gain_ref[...][None]
    centered = scaled - jnp.mean(scaled, axis=1, keepdims=True)
    scaled_ref[...] = centered
    share = pl.ds(pl.multiple_of(lax.rem(place, 2) * HALF, 128), HALF)

    def grad(first, normal, normal_share, inverse):
        row_doc = doc_of(ends, first + lax.broadcasted_iota(jnp.int32, (ROWS, 1), 0))

        def spread(values):
            pick = jnp.where(row_doc == 2, values[2:3], values[3:4])
            return jnp.where(row_doc == 0, values[0:1], jnp.where(row_doc == 1, values[1:2], pick))

        along = jnp.mean(spread(scaled) * normal, axis=1, keepdims=True)
        return (inverse * (spread(scaled_ref[:, share]) - normal_share * along)).astype(bf16)

    mine = grad(place * ROWS, normal_ref[...], normal_ref[:, share], inverse_ref[...])
    product = jnp.dot(mixed_ref[...], mine, preferred_element_type=f32)
    inverse = other_rows_ref[:, D:].astype(f32)
    theirs = grad(
        (place ^ 1) * ROWS,
        other_rows_ref[:, :D].astype(f32),
        other_rows_ref[:, share].astype(f32),
        inverse[:, 0:1] + inverse[:, 1:2],
    )
    product += jnp.dot(other_mixed_ref[...], theirs, preferred_element_type=f32)
    out_ref[...] = product.astype(bf16)
    write.wait()


def join_kernel(halves_ref, out_ref):
    for core in range(2):
        parts = [halves_ref[c].astype(jnp.float32) for c in range(core, CTX, 2)]
        out_ref[:, HALF * core : HALF * (core + 1)] = (parts[0] + parts[1]) + (parts[2] + parts[3])


SMEM = pl.BlockSpec(memory_space=pltpu.SMEM)
VMEM = pl.BlockSpec(memory_space=pltpu.VMEM)
ANY = pl.BlockSpec(memory_space=pl.ANY)


def call(kernel, name, smem, vmem, outs, scratch, flops, aliases={}, whole=(), hbm_outs=0, sems=()):
    return pl.pallas_call(
        kernel,
        name=name,
        out_shape=[jax.ShapeDtypeStruct(s, t) for s, t in outs],
        in_specs=[SMEM] * len(smem) + [VMEM] * len(vmem) + [ANY] * len(whole),
        out_specs=[VMEM] * (len(outs) - hbm_outs) + [ANY] * hbm_outs,
        scratch_shapes=[pltpu.VMEM(s, t) for s, t in scratch] + list(sems),
        input_output_aliases=aliases,
        cost_estimate=pl.CostEstimate(flops=flops, bytes_accessed=1 << 26, transcendentals=0),
        compiler_params=pltpu.CompilerParams(vmem_limit_bytes=VMEM_LIMIT),
    )(*smem, *vmem, *whole)


def copies(value, axis, count):
    return lax.all_to_all(jnp.broadcast_to(value[None], (count,) + value.shape), axis, 0, 0, tiled=True)


def per_device(hidden_in, w_qkv, w_out, b_out, ln_gain, ln_bias, doc_lengths, pair_of):
    f32, bf16 = jnp.float32, jnp.bfloat16
    own = hidden_in[0]
    places = jnp.stack([lax.axis_index("ctx"), lax.axis_index("dp")]).astype(jnp.int32)
    smem = [doc_lengths, places]
    state = [((HEADS, AUG, ROWS), f32)]
    work = [((HEADS, AUG, 2 * ROWS), bf16)]
    held = ((PAIRS, 256, 2 * ROWS), bf16)

    def fold(name, sources, blocks, acc):
        (acc,) = call(
            functools.partial(fold_kernel, sources), name, smem, [w_qkv, qbd, acc, *blocks], state, work,
            1 << 34, {4: 0},
        )
        return acc

    near = lax.ppermute(own, "ctx", AROUND)
    other = lax.ppermute(own, "ctx", CORE_SWAP)
    qbd, acc = call(queries_kernel, "queries", smem, [own, w_qkv], [held] + state, [], 1 << 34)
    own_later, acc = lax.optimization_barrier((own, acc))
    behind = lax.ppermute(own_later, "ctx", BACK)
    acc = fold("own", SOURCES[0:2], [own, other], acc)
    near, acc = lax.optimization_barrier((near, acc))
    far = lax.ppermute(near, "ctx", AROUND)
    near_other = lax.ppermute(near, "ctx", CORE_SWAP)
    acc = fold("near", SOURCES[2:3], [near], acc)
    near_other, acc = lax.optimization_barrier((near_other, acc))
    acc = fold("near_other", SOURCES[3:4], [near_other], acc)
    behind, acc = lax.optimization_barrier((behind, acc))
    behind_other = lax.ppermute(behind, "ctx", CORE_SWAP)
    acc = fold("behind", SOURCES[4:5], [behind], acc)
    behind_other, acc = lax.optimization_barrier((behind_other, acc))
    acc = fold("behind_other", SOURCES[5:6], [behind_other], acc)
    far, acc = lax.optimization_barrier((far, acc))
    far_other = lax.ppermute(far, "ctx", CORE_SWAP)
    acc = fold("far", SOURCES[6:7], [far], acc)
    far_other, acc = lax.optimization_barrier((far_other, acc))
    _, mixed, normal, inverse, rows, partials = call(
        last_kernel,
        "last",
        smem,
        [far_other, w_qkv, qbd, acc, own, w_out, b_out, ln_gain, ln_bias],
        state
        + [((D, ROWS), bf16), ((ROWS, D), f32), ((ROWS, 1), f32), ((ROWS, D + 128), bf16), ((CTX, DOCS, D), f32)],
        work + [((8, 2 * ROWS), f32), ((len(SOURCES), ROWS, D), bf16)],
        1 << 34,
        {5: 0},
        [own, other, near, near_other, behind, behind_other, far, far_other],
    )
    other_mixed = lax.ppermute(mixed, "ctx", CORE_SWAP)
    other_rows = lax.ppermute(rows, "ctx", CORE_SWAP)
    pooled = jnp.sum(lax.all_to_all(partials, "ctx", 0, 0, tiled=True), axis=0)
    every = copies(pooled, "dp", DP).reshape(NDOC, D)
    every, other_mixed, other_rows = lax.optimization_barrier((every, other_mixed, other_rows))
    term, encoded = call(
        back_kernel,
        "back",
        smem + [pair_of],
        [every, mixed, normal, inverse, other_mixed, other_rows, ln_gain, ln_bias],
        [((D, HALF), bf16), ((ROWS, D), bf16)],
        [((NDOC, NDOC), f32), ((DOCS, D), f32), ((ROWS, D), bf16)],
        1 << 20,
        hbm_outs=1,
        sems=[pltpu.SemaphoreType.DMA],
    )
    share = D // DP
    pieces = lax.all_to_all(term.reshape(DP, share, HALF), "dp", 0, 0, tiled=True)
    piece = jnp.sum(pieces.astype(f32), axis=0).astype(bf16)
    halves = copies(piece, "ctx", CTX)
    (grad_out,) = call(join_kernel, "join", [], [halves], [((share, D), f32)], [], 1 << 20)
    return (encoded[None], grad_out)


def solution(mesh):
    return jax.shard_map(
        per_device,
        mesh=mesh,
        in_specs=(P("dp", "ctx", None), P(), P(), P(), P(), P(), P("dp", None), P("dp", None)),
        out_specs=(P("dp", "ctx", None), P("dp", None)),
        check_vma=False,
    )
```

```python
import functools

import jax
import jax.numpy as jnp
from jax import lax
from jax.experimental import pallas as pl
from jax.experimental.pallas import tpu as pltpu
from jax.sharding import PartitionSpec as P

D = 768
HEADS = 12
HEAD_DIM = 64
PAIRS = HEADS // 2
DOCS = 4
NDOC = 128
ROWS = 256
CTX = 8
DP = 32
HALF = D // 2
PACK = D + 128
AUG = 80

SOFTMAX_TEMPER = 0.05
NORM_EPSILON = 1e-05
EMBED_EPSILON = 1e-06
PENALTY = -1e30

VMEM_LIMIT = 24 * 1024 * 1024

CORE_SWAP = [(c, c ^ 1) for c in range(CTX)]
AROUND = [(c, (c + 2) % CTX if c % 2 == 0 else (c - 2) % CTX) for c in range(CTX)]
BACK = [(b, a) for a, b in AROUND]


def came_from(place, hops):
    step = 2 * hops
    return lax.rem(jnp.where(lax.rem(place, 2) == 0, place - step, place + step) + 2 * CTX, CTX)


SOURCES = [(0, 0), (1, 0), (0, 1), (1, 1), (0, -1), (1, -1), (0, 2), (1, 2)]


def doc_ends(lengths_ref):
    e0 = lengths_ref[0, 0]
    e1 = e0 + lengths_ref[0, 1]
    e2 = e1 + lengths_ref[0, 2]
    e3 = e2 + lengths_ref[0, 3]
    return e0, e1, e2, e3


def doc_of(ends, positions):
    e0, e1, e2, e3 = ends
    one = jnp.int32(1)
    zero = jnp.int32(0)
    return sum(jnp.where(positions >= e, one, zero) for e in (e0, e1, e2, e3))


def needed_span(ends, first):
    e0, e1, e2, e3 = ends
    last = first + ROWS - 1
    low = jnp.where(first >= e2, e2, jnp.where(first >= e1, e1, jnp.where(first >= e0, e0, 0)))
    high = jnp.where(last < e0, e0, jnp.where(last < e1, e1, jnp.where(last < e2, e2, e3)))
    return low, high


def fill_queries(ends, first, own, wqkv_ref, qbd):
    queries = lax.dot_general(
        wqkv_ref[:, :D], own, (((0,), (1,)), ((), ())), preferred_element_type=jnp.float32
    )
    queries = (queries.astype(jnp.bfloat16).astype(jnp.float32) * HEAD_DIM**-0.5).astype(jnp.bfloat16)
    positions = first + lax.broadcasted_iota(jnp.int32, (HEAD_DIM * 2, ROWS), 1)
    slots = lax.broadcasted_iota(jnp.int32, (HEAD_DIM * 2, ROWS), 0)
    same = (doc_of(ends, positions) == slots) | (slots >= DOCS)
    penalty = jnp.where(same, 0.0, PENALTY).astype(jnp.bfloat16)
    penalties = jnp.concatenate([penalty, penalty], axis=1)
    zero = jnp.zeros((HEAD_DIM, ROWS), jnp.bfloat16)
    for j in range(PAIRS):
        qbd[j, :64, :ROWS] = queries[128 * j : 128 * j + 64, :]
        qbd[j, :64, ROWS:] = zero
        qbd[j, 64:128, :ROWS] = zero
        qbd[j, 64:128, ROWS:] = queries[128 * j + 64 : 128 * j + 128, :]
        qbd[j, 128:, :] = penalties


def project(ends, bases, blocks, wqkv_ref, vt):
    rows = ROWS * len(blocks)
    hidden = jnp.concatenate(blocks, axis=0) if len(blocks) > 1 else blocks[0]
    keys = jnp.dot(hidden, wqkv_ref[:, D : 2 * D], preferred_element_type=jnp.float32).astype(jnp.bfloat16)
    values = lax.dot_general(
        wqkv_ref[:, 2 * D :], hidden, (((0,), (1,)), ((), ())), preferred_element_type=jnp.float32
    ).astype(jnp.bfloat16)
    vt[:, :HEAD_DIM, :rows] = values.reshape(HEADS, HEAD_DIM, rows)
    offsets = lax.broadcasted_iota(jnp.int32, (ROWS, 128), 0)
    lanes = lax.broadcasted_iota(jnp.int32, (ROWS, 128), 1)
    onehots = [
        jnp.where(doc_of(ends, base + offsets) == lanes, 1.0, 0.0).astype(jnp.bfloat16) for base in bases
    ]
    return keys, jnp.concatenate(onehots, axis=0) if len(blocks) > 1 else onehots[0]


def pair_scores(keys, onehot, qbd, j):
    pair_keys = jnp.concatenate([keys[:, 128 * j : 128 * j + 128], onehot], axis=1)
    return jnp.dot(pair_keys, qbd[j], preferred_element_type=jnp.float32)


def attend_plain(ends, bases, blocks, wqkv_ref, qbd, vt, acc_ref):
    rows = ROWS * len(blocks)
    keys, onehot = project(ends, bases, blocks, wqkv_ref, vt)
    for j in range(PAIRS):
        weights = jnp.exp(pair_scores(keys, onehot, qbd, j)).astype(jnp.bfloat16)
        for h in range(2):
            part = slice(ROWS * h, ROWS * h + ROWS)
            acc_ref[2 * j + h] += jnp.dot(
                vt[2 * j + h, :, :rows], weights[:, part], preferred_element_type=jnp.float32
            )


def attend_shifted(ends, base, block, wqkv_ref, qbd, vt, m_ref, acc_ref):
    keys, onehot = project(ends, [base], [block], wqkv_ref, vt)
    for j in range(PAIRS):
        scores = pair_scores(keys, onehot, qbd, j)
        old = m_ref[j : j + 1, :]
        new = jnp.maximum(old, jnp.max(scores, axis=0, keepdims=True))
        m_ref[j : j + 1, :] = new
        shrink = jnp.exp(old - new)
        weights = jnp.exp(scores - new).astype(jnp.bfloat16)
        for h in range(2):
            part = slice(ROWS * h, ROWS * h + ROWS)
            mixed = jnp.dot(vt[2 * j + h, :, :ROWS], weights[:, part], preferred_element_type=jnp.float32)
            acc_ref[2 * j + h] = acc_ref[2 * j + h] * shrink[:, part] + mixed


def fill_ones(vt):
    row = lax.broadcasted_iota(jnp.int32, (HEADS, AUG - HEAD_DIM, vt.shape[2]), 1)
    vt[:, HEAD_DIM:, :] = jnp.where(row == 0, 1.0, 0.0).astype(jnp.bfloat16)


def attend_blocks(ends, first, places, blocks, wqkv_ref, qbd, vt, acc_ref):
    low, high = needed_span(ends, first)
    bases = [place * ROWS for place in places]
    wanted = [(base < high) & (base + ROWS > low) for base in bases]

    def attend(which):
        attend_plain(
            ends, [bases[i] for i in which], [blocks[i][...] for i in which], wqkv_ref, qbd, vt, acc_ref
        )

    if len(blocks) == 1:
        pl.when(wanted[0])(lambda: attend([0]))
    else:
        one, two = wanted
        pl.when(one & two)(lambda: attend([0, 1]))
        pl.when(one & jnp.logical_not(two))(lambda: attend([0]))
        pl.when(two & jnp.logical_not(one))(lambda: attend([1]))


def queries_kernel(lengths_ref, place_ref, own_ref, wqkv_ref, qbd, acc_ref):
    ends = doc_ends(lengths_ref)
    fill_queries(ends, place_ref[0] * ROWS, own_ref[...], wqkv_ref, qbd)
    acc_ref[...] = jnp.zeros(acc_ref.shape, jnp.float32)


def fold_kernel(sources, lengths_ref, place_ref, wqkv_ref, qbd, acc_in, *refs):
    blocks, (acc_ref, vt) = refs[: len(sources)], refs[len(sources) :]
    place = place_ref[0]
    ends = doc_ends(lengths_ref)
    fill_ones(vt)
    places = [came_from(place ^ flip, hops) for flip, hops in sources]
    attend_blocks(ends, place * ROWS, places, blocks, wqkv_ref, qbd, vt, acc_ref)


def in_range(acc):
    sums = acc[:, HEAD_DIM, :]
    good = jnp.where((sums >= 1e-12) & (sums <= 1e12), 1.0, 0.0)
    finite = jnp.where(jnp.abs(acc) <= 1e38, 1.0, 0.0)
    return jnp.minimum(jnp.min(good), jnp.min(finite)) > 0.5


def attend_again(ends, place, blocks, wqkv_ref, qbd, vt, acc_ref, m_ref, held):
    for i, (flip, hops) in enumerate(SOURCES):
        pltpu.sync_copy(blocks[i], held.at[i])
    m_ref[...] = jnp.full(m_ref.shape, PENALTY, jnp.float32)
    acc_ref[...] = jnp.zeros(acc_ref.shape, jnp.float32)
    low, high = needed_span(ends, place * ROWS)

    def step(i, carry):
        base = jnp.int32(0)
        for k, (flip, hops) in enumerate(SOURCES):
            base = jnp.where(i == k, came_from(place ^ flip, hops) * ROWS, base)

        @pl.when((base < high) & (base + ROWS > low))
        def _():
            attend_shifted(ends, base, held[i], wqkv_ref, qbd, vt, m_ref, acc_ref)

        return carry

    lax.fori_loop(0, len(SOURCES), step, 0)


def last_kernel(
    lengths_ref, place_ref, far_other_ref, wqkv_ref, qbd, acc_in, own_ref, wout_ref, bias_ref, gain_ref, shift_ref,
    *refs
):
    blocks, refs = refs[: len(SOURCES)], refs[len(SOURCES) :]
    acc_ref, mixed_ref, normal_ref, inverse_ref, rows_ref, pooled_ref, vt, m_ref, held = refs
    place = place_ref[0]
    ends = doc_ends(lengths_ref)
    first = place * ROWS
    fill_ones(vt)
    flip, hops = SOURCES[-1]
    attend_blocks(ends, first, [came_from(place ^ flip, hops)], [far_other_ref], wqkv_ref, qbd, vt, acc_ref)

    @pl.when(jnp.logical_not(in_range(acc_ref[...])))
    def _():
        attend_again(ends, place, blocks, wqkv_ref, qbd, vt, acc_ref, m_ref, held)

    acc = acc_ref[...]
    mixed = acc[:, :HEAD_DIM, :] * (1.0 / acc[:, HEAD_DIM : HEAD_DIM + 1, :])
    mixed = mixed.reshape(D, ROWS).astype(jnp.bfloat16)
    mixed_ref[...] = mixed
    summed = lax.dot_general(
        mixed, wout_ref[...], (((0,), (0,)), ((), ())), preferred_element_type=jnp.float32
    )
    summed = summed + bias_ref[...][None] + own_ref[...].astype(jnp.float32)
    centered = summed - jnp.mean(summed, axis=1, keepdims=True)
    inverse = lax.rsqrt(jnp.mean(centered * centered, axis=1, keepdims=True) + NORM_EPSILON)
    normal = centered * inverse
    normal_ref[...] = normal
    inverse_ref[...] = inverse
    layer = normal * gain_ref[...][None] + shift_ref[...][None]
    for i in range(D // ROWS):
        rows_ref[:, PACK + ROWS * i : PACK + ROWS * (i + 1)] = mixed[ROWS * i : ROWS * (i + 1)]
    rows_ref[:, :D] = normal.astype(jnp.bfloat16)
    high = inverse.astype(jnp.bfloat16).astype(jnp.float32)
    lane = lax.broadcasted_iota(jnp.int32, (ROWS, 128), 1)
    rows_ref[:, D:PACK] = jnp.where(lane == 0, high, inverse - high).astype(jnp.bfloat16)
    row_doc = doc_of(ends, first + lax.broadcasted_iota(jnp.int32, (ROWS, 1), 0))
    pooled_ref[...] = jnp.zeros(pooled_ref.shape, jnp.float32)
    starts = (jnp.int32(0), *ends[:-1])
    for d in range(DOCS):

        @pl.when((starts[d] < first + ROWS) & (ends[d] > first))
        def _():
            total = jnp.sum(jnp.where(row_doc == d, layer, 0.0), axis=0, keepdims=True)
            mean = total * (1.0 / lengths_ref[0, d].astype(jnp.float32))
            pooled_ref[:, d : d + 1, :] = jnp.broadcast_to(mean[None], (CTX, 1, D))


def back_kernel(
    lengths_ref, place_ref, pair_ref, pooled_ref, mixed_ref, normal_ref, inverse_ref, other_rows_ref,
    gain_ref, shift_ref, out_ref, encoded_hbm, expo_ref, scaled_ref, encoded_ref, sem
):
    place = place_ref[0]
    data_place = place_ref[1]
    ends = doc_ends(lengths_ref)
    f32, bf16 = jnp.float32, jnp.bfloat16
    encoded_ref[...] = (normal_ref[...] * gain_ref[...][None] + shift_ref[...][None]).astype(bf16)
    write = pltpu.make_async_copy(encoded_ref, encoded_hbm, sem)
    write.start()

    pooled = pooled_ref[...]
    emb = pooled * lax.rsqrt(jnp.sum(pooled * pooled, axis=1, keepdims=True) + EMBED_EPSILON)
    high = emb.astype(bf16)
    low = (emb - high.astype(f32)).astype(bf16)

    def times(left, right):
        return lax.dot_general(left, right, (((1,), (1,)), ((), ())), preferred_element_type=f32)

    sims = (times(high, high) + (times(high, low) + times(low, high))) * (1.0 / SOFTMAX_TEMPER)
    columns = lax.broadcasted_iota(jnp.int32, (NDOC, NDOC), 1)
    rows = lax.broadcasted_iota(jnp.int32, (NDOC, NDOC), 0)
    expo = jnp.where(rows == columns, 0.0, jnp.exp(sims))
    expo_ref[...] = expo
    totals = 1.0 / jnp.sum(expo, axis=0, keepdims=True)
    half = lax.rem(data_place, 2)
    rows8 = pl.ds(pl.multiple_of((data_place - half) * DOCS, 8), 8)

    def own_rows(ref):
        found = ref[rows8, :]
        return jnp.where(half == 0, found[:DOCS], found[DOCS:])

    own = own_rows(pooled_ref)
    own_inverse = lax.rsqrt(jnp.sum(own * own, axis=1, keepdims=True) + EMBED_EPSILON)
    own_emb = own * own_inverse
    own_expo = own_rows(expo_ref)
    own_totals = 1.0 / jnp.sum(own_expo, axis=1, keepdims=True)
    slots = lax.broadcasted_iota(jnp.int32, (DOCS, NDOC), 0)
    lanes = lax.broadcasted_iota(jnp.int32, (DOCS, NDOC), 1)
    partner = jnp.where(
        slots == 0, pair_ref[0, 0],
        jnp.where(slots == 1, pair_ref[0, 1], jnp.where(slots == 2, pair_ref[0, 2], pair_ref[0, 3])),
    )
    both = own_expo * (own_totals + totals) - jnp.where(lanes == partner, 2.0, 0.0)
    weights = jnp.concatenate([both, both], axis=0).T
    emb_grad = jnp.concatenate(
        [jnp.sum(weights[:, d : d + 1] * emb, axis=0, keepdims=True) for d in range(DOCS)], axis=0
    ) * (1.0 / SOFTMAX_TEMPER)
    pooled_grad = (emb_grad - own_emb * jnp.sum(own_emb * emb_grad, axis=1, keepdims=True)) * own_inverse
    slot = lax.broadcasted_iota(jnp.int32, (DOCS, 1), 0)
    length = jnp.where(
        slot == 0, lengths_ref[0, 0],
        jnp.where(slot == 1, lengths_ref[0, 1], jnp.where(slot == 2, lengths_ref[0, 2], lengths_ref[0, 3])),
    ).astype(f32)
    scaled = pooled_grad * (1.0 / length) * gain_ref[...][None]
    centered = scaled - jnp.mean(scaled, axis=1, keepdims=True)
    scaled_ref[...] = centered
    share = pl.ds(pl.multiple_of(lax.rem(place, 2) * HALF, 128), HALF)

    def grad(first, normal, normal_share, inverse):
        row_doc = doc_of(ends, first + lax.broadcasted_iota(jnp.int32, (ROWS, 1), 0))

        def spread(values):
            pick = jnp.where(row_doc == 2, values[2:3], values[3:4])
            return jnp.where(row_doc == 0, values[0:1], jnp.where(row_doc == 1, values[1:2], pick))

        along = jnp.mean(spread(scaled) * normal, axis=1, keepdims=True)
        return (inverse * (spread(scaled_ref[:, share]) - normal_share * along)).astype(bf16)

    mine = grad(place * ROWS, normal_ref[...], normal_ref[:, share], inverse_ref[...])
    inverse = other_rows_ref[:, D:PACK].astype(f32)
    theirs = grad(
        (place ^ 1) * ROWS,
        other_rows_ref[:, :D].astype(f32),
        other_rows_ref[:, share].astype(f32),
        inverse[:, 0:1] + inverse[:, 1:2],
    )
    for i in range(D // ROWS):
        part = slice(ROWS * i, ROWS * (i + 1))
        other_mixed = other_rows_ref[:, PACK + ROWS * i : PACK + ROWS * (i + 1)]
        product = jnp.dot(mixed_ref[part, :], mine, preferred_element_type=f32)
        product += jnp.dot(other_mixed, theirs, preferred_element_type=f32)
        out_ref[part, :] = product.astype(bf16)
    write.wait()


def join_kernel(halves_ref, out_ref):
    for core in range(2):
        parts = [halves_ref[c].astype(jnp.float32) for c in range(core, CTX, 2)]
        out_ref[:, HALF * core : HALF * (core + 1)] = (parts[0] + parts[1]) + (parts[2] + parts[3])


SMEM = pl.BlockSpec(memory_space=pltpu.SMEM)
VMEM = pl.BlockSpec(memory_space=pltpu.VMEM)
ANY = pl.BlockSpec(memory_space=pl.ANY)


def call(kernel, name, smem, vmem, outs, scratch, flops, aliases={}, whole=(), hbm_outs=0, sems=()):
    return pl.pallas_call(
        kernel,
        name=name,
        out_shape=[jax.ShapeDtypeStruct(s, t) for s, t in outs],
        in_specs=[SMEM] * len(smem) + [VMEM] * len(vmem) + [ANY] * len(whole),
        out_specs=[VMEM] * (len(outs) - hbm_outs) + [ANY] * hbm_outs,
        scratch_shapes=[pltpu.VMEM(s, t) for s, t in scratch] + list(sems),
        input_output_aliases=aliases,
        cost_estimate=pl.CostEstimate(flops=flops, bytes_accessed=1 << 26, transcendentals=0),
        compiler_params=pltpu.CompilerParams(vmem_limit_bytes=VMEM_LIMIT),
    )(*smem, *vmem, *whole)


def copies(value, axis, count):
    return lax.all_to_all(jnp.broadcast_to(value[None], (count,) + value.shape), axis, 0, 0, tiled=True)


def per_device(hidden_in, w_qkv, w_out, b_out, ln_gain, ln_bias, doc_lengths, pair_of):
    f32, bf16 = jnp.float32, jnp.bfloat16
    own = hidden_in[0]
    places = jnp.stack([lax.axis_index("ctx"), lax.axis_index("dp")]).astype(jnp.int32)
    smem = [doc_lengths, places]
    state = [((HEADS, AUG, ROWS), f32)]
    work = [((HEADS, AUG, 2 * ROWS), bf16)]
    held = ((PAIRS, 256, 2 * ROWS), bf16)

    def fold(name, sources, blocks, acc):
        (acc,) = call(
            functools.partial(fold_kernel, sources), name, smem, [w_qkv, qbd, acc, *blocks], state, work,
            1 << 34, {4: 0},
        )
        return acc

    near = lax.ppermute(own, "ctx", AROUND)
    other = lax.ppermute(own, "ctx", CORE_SWAP)
    qbd, acc = call(queries_kernel, "queries", smem, [own, w_qkv], [held] + state, [], 1 << 34)
    acc = fold("own", SOURCES[0:1], [own], acc)
    own_later, acc = lax.optimization_barrier((own, acc))
    behind = lax.ppermute(own_later, "ctx", BACK)
    acc = fold("other", SOURCES[1:2], [other], acc)
    near, acc = lax.optimization_barrier((near, acc))
    far = lax.ppermute(near, "ctx", AROUND)
    near_other = lax.ppermute(near, "ctx", CORE_SWAP)
    acc = fold("near", SOURCES[2:3], [near], acc)
    near_other, acc = lax.optimization_barrier((near_other, acc))
    acc = fold("near_other", SOURCES[3:4], [near_other], acc)
    behind, acc = lax.optimization_barrier((behind, acc))
    behind_other = lax.ppermute(behind, "ctx", CORE_SWAP)
    acc = fold("behind", SOURCES[4:5], [behind], acc)
    behind_other, acc = lax.optimization_barrier((behind_other, acc))
    acc = fold("behind_other", SOURCES[5:6], [behind_other], acc)
    far, acc = lax.optimization_barrier((far, acc))
    far_other = lax.ppermute(far, "ctx", CORE_SWAP)
    acc = fold("far", SOURCES[6:7], [far], acc)
    far_other, acc = lax.optimization_barrier((far_other, acc))
    _, mixed, normal, inverse, rows, partials = call(
        last_kernel,
        "last",
        smem,
        [far_other, w_qkv, qbd, acc, own, w_out, b_out, ln_gain, ln_bias],
        state
        + [((D, ROWS), bf16), ((ROWS, D), f32), ((ROWS, 1), f32), ((ROWS, PACK + D), bf16), ((CTX, DOCS, D), f32)],
        work + [((8, 2 * ROWS), f32), ((len(SOURCES), ROWS, D), bf16)],
        1 << 34,
        {5: 0},
        [own, other, near, near_other, behind, behind_other, far, far_other],
    )
    other_rows = lax.ppermute(rows, "ctx", CORE_SWAP)
    pooled = jnp.sum(lax.all_to_all(partials, "ctx", 0, 0, tiled=True), axis=0)
    every = copies(pooled, "dp", DP).reshape(NDOC, D)
    every, other_rows = lax.optimization_barrier((every, other_rows))
    term, encoded = call(
        back_kernel,
        "back",
        smem + [pair_of],
        [every, mixed, normal, inverse, other_rows, ln_gain, ln_bias],
        [((D, HALF), bf16), ((ROWS, D), bf16)],
        [((NDOC, NDOC), f32), ((DOCS, D), f32), ((ROWS, D), bf16)],
        1 << 20,
        hbm_outs=1,
        sems=[pltpu.SemaphoreType.DMA],
    )
    share = D // DP
    pieces = lax.all_to_all(term.reshape(DP, share, HALF), "dp", 0, 0, tiled=True)
    piece = jnp.sum(pieces.astype(f32), axis=0).astype(bf16)
    halves = copies(piece, "ctx", CTX)
    (grad_out,) = call(join_kernel, "join", [], [halves], [((share, D), f32)], [], 1 << 20)
    return (encoded[None], grad_out)


def solution(mesh):
    return jax.shard_map(
        per_device,
        mesh=mesh,
        in_specs=(P("dp", "ctx", None), P(), P(), P(), P(), P(), P("dp", None), P("dp", None)),
        out_specs=(P("dp", "ctx", None), P("dp", None)),
        check_vma=False,
    )
```

```python
import functools

import jax
import jax.numpy as jnp
from jax import lax
from jax.experimental import pallas as pl
from jax.experimental.pallas import tpu as pltpu
from jax.sharding import PartitionSpec as P

D = 768
HEADS = 12
HEAD_DIM = 64
PAIRS = HEADS // 2
DOCS = 4
NDOC = 128
ROWS = 256
CTX = 8
DP = 32
HALF = D // 2
PACK = D + 128
AUG = 80

SOFTMAX_TEMPER = 0.05
NORM_EPSILON = 1e-05
EMBED_EPSILON = 1e-06
PENALTY = -1e30

VMEM_LIMIT = 24 * 1024 * 1024

CORE_SWAP = [(c, c ^ 1) for c in range(CTX)]
AROUND = [(c, (c + 2) % CTX if c % 2 == 0 else (c - 2) % CTX) for c in range(CTX)]
BACK = [(b, a) for a, b in AROUND]


def came_from(place, hops):
    step = 2 * hops
    return lax.rem(jnp.where(lax.rem(place, 2) == 0, place - step, place + step) + 2 * CTX, CTX)


SOURCES = [(0, 0), (1, 0), (0, 1), (1, 1), (0, -1), (1, -1), (0, 2), (1, 2)]


def doc_ends(lengths_ref):
    e0 = lengths_ref[0, 0]
    e1 = e0 + lengths_ref[0, 1]
    e2 = e1 + lengths_ref[0, 2]
    e3 = e2 + lengths_ref[0, 3]
    return e0, e1, e2, e3


def doc_of(ends, positions):
    e0, e1, e2, e3 = ends
    one = jnp.int32(1)
    zero = jnp.int32(0)
    return sum(jnp.where(positions >= e, one, zero) for e in (e0, e1, e2, e3))


def needed_span(ends, first):
    e0, e1, e2, e3 = ends
    last = first + ROWS - 1
    low = jnp.where(first >= e2, e2, jnp.where(first >= e1, e1, jnp.where(first >= e0, e0, 0)))
    high = jnp.where(last < e0, e0, jnp.where(last < e1, e1, jnp.where(last < e2, e2, e3)))
    return low, high


def fill_queries(ends, first, own, wqkv_ref, qbd):
    queries = lax.dot_general(
        wqkv_ref[:, :D], own, (((0,), (1,)), ((), ())), preferred_element_type=jnp.float32
    )
    queries = (queries.astype(jnp.bfloat16).astype(jnp.float32) * HEAD_DIM**-0.5).astype(jnp.bfloat16)
    positions = first + lax.broadcasted_iota(jnp.int32, (HEAD_DIM * 2, ROWS), 1)
    slots = lax.broadcasted_iota(jnp.int32, (HEAD_DIM * 2, ROWS), 0)
    same = (doc_of(ends, positions) == slots) | (slots >= DOCS)
    penalty = jnp.where(same, 0.0, PENALTY).astype(jnp.bfloat16)
    penalties = jnp.concatenate([penalty, penalty], axis=1)
    zero = jnp.zeros((HEAD_DIM, ROWS), jnp.bfloat16)
    for j in range(PAIRS):
        qbd[j, :64, :ROWS] = queries[128 * j : 128 * j + 64, :]
        qbd[j, :64, ROWS:] = zero
        qbd[j, 64:128, :ROWS] = zero
        qbd[j, 64:128, ROWS:] = queries[128 * j + 64 : 128 * j + 128, :]
        qbd[j, 128:, :] = penalties


def project(ends, bases, blocks, wqkv_ref, vt):
    rows = ROWS * len(blocks)
    hidden = jnp.concatenate(blocks, axis=0) if len(blocks) > 1 else blocks[0]
    keys = jnp.dot(hidden, wqkv_ref[:, D : 2 * D], preferred_element_type=jnp.float32).astype(jnp.bfloat16)
    values = lax.dot_general(
        wqkv_ref[:, 2 * D :], hidden, (((0,), (1,)), ((), ())), preferred_element_type=jnp.float32
    ).astype(jnp.bfloat16)
    vt[:, :HEAD_DIM, :rows] = values.reshape(HEADS, HEAD_DIM, rows)
    offsets = lax.broadcasted_iota(jnp.int32, (ROWS, 128), 0)
    lanes = lax.broadcasted_iota(jnp.int32, (ROWS, 128), 1)
    onehots = [
        jnp.where(doc_of(ends, base + offsets) == lanes, 1.0, 0.0).astype(jnp.bfloat16) for base in bases
    ]
    return keys, jnp.concatenate(onehots, axis=0) if len(blocks) > 1 else onehots[0]


def pair_scores(keys, onehot, qbd, j):
    pair_keys = jnp.concatenate([keys[:, 128 * j : 128 * j + 128], onehot], axis=1)
    return jnp.dot(pair_keys, qbd[j], preferred_element_type=jnp.float32)


def attend_plain(ends, bases, blocks, wqkv_ref, qbd, vt, acc_ref):
    rows = ROWS * len(blocks)
    keys, onehot = project(ends, bases, blocks, wqkv_ref, vt)
    for j in range(PAIRS):
        weights = jnp.exp(pair_scores(keys, onehot, qbd, j)).astype(jnp.bfloat16)
        for h in range(2):
            part = slice(ROWS * h, ROWS * h + ROWS)
            acc_ref[2 * j + h] += jnp.dot(
                vt[2 * j + h, :, :rows], weights[:, part], preferred_element_type=jnp.float32
            )


def attend_shifted(ends, base, block, wqkv_ref, qbd, vt, m_ref, acc_ref):
    keys, onehot = project(ends, [base], [block], wqkv_ref, vt)
    for j in range(PAIRS):
        scores = pair_scores(keys, onehot, qbd, j)
        old = m_ref[j : j + 1, :]
        new = jnp.maximum(old, jnp.max(scores, axis=0, keepdims=True))
        m_ref[j : j + 1, :] = new
        shrink = jnp.exp(old - new)
        weights = jnp.exp(scores - new).astype(jnp.bfloat16)
        for h in range(2):
            part = slice(ROWS * h, ROWS * h + ROWS)
            mixed = jnp.dot(vt[2 * j + h, :, :ROWS], weights[:, part], preferred_element_type=jnp.float32)
            acc_ref[2 * j + h] = acc_ref[2 * j + h] * shrink[:, part] + mixed


def fill_ones(vt):
    row = lax.broadcasted_iota(jnp.int32, (HEADS, AUG - HEAD_DIM, vt.shape[2]), 1)
    vt[:, HEAD_DIM:, :] = jnp.where(row == 0, 1.0, 0.0).astype(jnp.bfloat16)


def attend_blocks(ends, first, places, blocks, wqkv_ref, qbd, vt, acc_ref):
    low, high = needed_span(ends, first)
    bases = [place * ROWS for place in places]
    wanted = [(base < high) & (base + ROWS > low) for base in bases]

    def attend(which):
        attend_plain(
            ends, [bases[i] for i in which], [blocks[i][...] for i in which], wqkv_ref, qbd, vt, acc_ref
        )

    if len(blocks) == 1:
        pl.when(wanted[0])(lambda: attend([0]))
    else:
        one, two = wanted
        pl.when(one & two)(lambda: attend([0, 1]))
        pl.when(one & jnp.logical_not(two))(lambda: attend([0]))
        pl.when(two & jnp.logical_not(one))(lambda: attend([1]))


def queries_kernel(lengths_ref, place_ref, own_ref, wqkv_ref, qbd, acc_ref):
    ends = doc_ends(lengths_ref)
    fill_queries(ends, place_ref[0] * ROWS, own_ref[...], wqkv_ref, qbd)
    acc_ref[...] = jnp.zeros(acc_ref.shape, jnp.float32)


def fold_kernel(sources, lengths_ref, place_ref, wqkv_ref, qbd, acc_in, *refs):
    blocks, (acc_ref, vt) = refs[: len(sources)], refs[len(sources) :]
    place = place_ref[0]
    ends = doc_ends(lengths_ref)
    fill_ones(vt)
    places = [came_from(place ^ flip, hops) for flip, hops in sources]
    attend_blocks(ends, place * ROWS, places, blocks, wqkv_ref, qbd, vt, acc_ref)


def in_range(acc):
    sums = acc[:, HEAD_DIM, :]
    good = jnp.where((sums >= 1e-12) & (sums <= 1e12), 1.0, 0.0)
    finite = jnp.where(jnp.abs(acc) <= 1e38, 1.0, 0.0)
    return jnp.minimum(jnp.min(good), jnp.min(finite)) > 0.5


def attend_again(ends, place, blocks, wqkv_ref, qbd, vt, acc_ref, m_ref, held):
    for i, (flip, hops) in enumerate(SOURCES):
        pltpu.sync_copy(blocks[i], held.at[i])
    m_ref[...] = jnp.full(m_ref.shape, PENALTY, jnp.float32)
    acc_ref[...] = jnp.zeros(acc_ref.shape, jnp.float32)
    low, high = needed_span(ends, place * ROWS)

    def step(i, carry):
        base = jnp.int32(0)
        for k, (flip, hops) in enumerate(SOURCES):
            base = jnp.where(i == k, came_from(place ^ flip, hops) * ROWS, base)

        @pl.when((base < high) & (base + ROWS > low))
        def _():
            attend_shifted(ends, base, held[i], wqkv_ref, qbd, vt, m_ref, acc_ref)

        return carry

    lax.fori_loop(0, len(SOURCES), step, 0)


def last_kernel(
    lengths_ref, place_ref, far_other_ref, wqkv_ref, qbd, acc_in, own_ref, wout_ref, bias_ref, gain_ref, shift_ref,
    *refs
):
    blocks, refs = refs[: len(SOURCES)], refs[len(SOURCES) :]
    acc_ref, mixed_ref, normal_ref, inverse_ref, rows_ref, pooled_ref, vt, m_ref, held = refs
    place = place_ref[0]
    ends = doc_ends(lengths_ref)
    first = place * ROWS
    fill_ones(vt)
    flip, hops = SOURCES[-1]
    attend_blocks(ends, first, [came_from(place ^ flip, hops)], [far_other_ref], wqkv_ref, qbd, vt, acc_ref)

    @pl.when(jnp.logical_not(in_range(acc_ref[...])))
    def _():
        attend_again(ends, place, blocks, wqkv_ref, qbd, vt, acc_ref, m_ref, held)

    acc = acc_ref[...]
    mixed = acc[:, :HEAD_DIM, :] * (1.0 / acc[:, HEAD_DIM : HEAD_DIM + 1, :])
    mixed = mixed.reshape(D, ROWS).astype(jnp.bfloat16)
    mixed_ref[...] = mixed
    summed = lax.dot_general(
        mixed, wout_ref[...], (((0,), (0,)), ((), ())), preferred_element_type=jnp.float32
    )
    summed = summed + bias_ref[...][None] + own_ref[...].astype(jnp.float32)
    centered = summed - jnp.mean(summed, axis=1, keepdims=True)
    inverse = lax.rsqrt(jnp.mean(centered * centered, axis=1, keepdims=True) + NORM_EPSILON)
    normal = centered * inverse
    normal_ref[...] = normal
    inverse_ref[...] = inverse
    layer = normal * gain_ref[...][None] + shift_ref[...][None]
    for i in range(D // ROWS):
        rows_ref[:, PACK + ROWS * i : PACK + ROWS * (i + 1)] = mixed[ROWS * i : ROWS * (i + 1)]
    rows_ref[:, :D] = normal.astype(jnp.bfloat16)
    high = inverse.astype(jnp.bfloat16).astype(jnp.float32)
    lane = lax.broadcasted_iota(jnp.int32, (ROWS, 128), 1)
    rows_ref[:, D:PACK] = jnp.where(lane == 0, high, inverse - high).astype(jnp.bfloat16)
    row_doc = doc_of(ends, first + lax.broadcasted_iota(jnp.int32, (ROWS, 1), 0))
    pooled_ref[...] = jnp.zeros(pooled_ref.shape, jnp.float32)
    starts = (jnp.int32(0), *ends[:-1])
    for d in range(DOCS):

        @pl.when((starts[d] < first + ROWS) & (ends[d] > first))
        def _():
            total = jnp.sum(jnp.where(row_doc == d, layer, 0.0), axis=0, keepdims=True)
            mean = total * (1.0 / lengths_ref[0, d].astype(jnp.float32))
            pooled_ref[:, d : d + 1, :] = jnp.broadcast_to(mean[None], (CTX, 1, D))


def back_kernel(
    lengths_ref, place_ref, pair_ref, pooled_ref, mixed_ref, normal_ref, inverse_ref, other_rows_ref,
    gain_ref, shift_ref, out_ref, encoded_hbm, expo_ref, scaled_ref, encoded_ref, sem
):
    place = place_ref[0]
    data_place = place_ref[1]
    ends = doc_ends(lengths_ref)
    f32, bf16 = jnp.float32, jnp.bfloat16
    encoded_ref[...] = (normal_ref[...] * gain_ref[...][None] + shift_ref[...][None]).astype(bf16)
    write = pltpu.make_async_copy(encoded_ref, encoded_hbm, sem)
    write.start()

    pooled = pooled_ref[...].reshape(NDOC, D)
    emb = pooled * lax.rsqrt(jnp.sum(pooled * pooled, axis=1, keepdims=True) + EMBED_EPSILON)
    high = emb.astype(bf16)
    low = (emb - high.astype(f32)).astype(bf16)

    def times(left, right):
        return lax.dot_general(left, right, (((1,), (1,)), ((), ())), preferred_element_type=f32)

    sims = (times(high, high) + (times(high, low) + times(low, high))) * (1.0 / SOFTMAX_TEMPER)
    columns = lax.broadcasted_iota(jnp.int32, (NDOC, NDOC), 1)
    rows = lax.broadcasted_iota(jnp.int32, (NDOC, NDOC), 0)
    expo = jnp.where(rows == columns, 0.0, jnp.exp(sims))
    expo_ref[...] = expo
    totals = 1.0 / jnp.sum(expo, axis=0, keepdims=True)
    half = lax.rem(data_place, 2)
    rows8 = expo_ref[pl.ds(pl.multiple_of((data_place - half) * DOCS, 8), 8), :]
    own_expo = jnp.where(half == 0, rows8[:DOCS], rows8[DOCS:])
    own = pooled_ref[data_place]
    own_inverse = lax.rsqrt(jnp.sum(own * own, axis=1, keepdims=True) + EMBED_EPSILON)
    own_emb = own * own_inverse
    own_totals = 1.0 / jnp.sum(own_expo, axis=1, keepdims=True)
    slots = lax.broadcasted_iota(jnp.int32, (DOCS, NDOC), 0)
    lanes = lax.broadcasted_iota(jnp.int32, (DOCS, NDOC), 1)
    partner = jnp.where(
        slots == 0, pair_ref[0, 0],
        jnp.where(slots == 1, pair_ref[0, 1], jnp.where(slots == 2, pair_ref[0, 2], pair_ref[0, 3])),
    )
    both = own_expo * (own_totals + totals) - jnp.where(lanes == partner, 2.0, 0.0)
    weights = jnp.concatenate([both, both], axis=0).T
    emb_grad = jnp.concatenate(
        [jnp.sum(weights[:, d : d + 1] * emb, axis=0, keepdims=True) for d in range(DOCS)], axis=0
    ) * (1.0 / SOFTMAX_TEMPER)
    pooled_grad = (emb_grad - own_emb * jnp.sum(own_emb * emb_grad, axis=1, keepdims=True)) * own_inverse
    slot = lax.broadcasted_iota(jnp.int32, (DOCS, 1), 0)
    length = jnp.where(
        slot == 0, lengths_ref[0, 0],
        jnp.where(slot == 1, lengths_ref[0, 1], jnp.where(slot == 2, lengths_ref[0, 2], lengths_ref[0, 3])),
    ).astype(f32)
    scaled = pooled_grad * (1.0 / length) * gain_ref[...][None]
    centered = scaled - jnp.mean(scaled, axis=1, keepdims=True)
    scaled_ref[...] = centered
    share = pl.ds(pl.multiple_of(lax.rem(place, 2) * HALF, 128), HALF)

    def grad(first, normal, normal_share, inverse):
        row_doc = doc_of(ends, first + lax.broadcasted_iota(jnp.int32, (ROWS, 1), 0))

        def spread(values):
            pick = jnp.where(row_doc == 2, values[2:3], values[3:4])
            return jnp.where(row_doc == 0, values[0:1], jnp.where(row_doc == 1, values[1:2], pick))

        along = jnp.mean(spread(scaled) * normal, axis=1, keepdims=True)
        return (inverse * (spread(scaled_ref[:, share]) - normal_share * along)).astype(bf16)

    mine = grad(place * ROWS, normal_ref[...], normal_ref[:, share], inverse_ref[...])
    inverse = other_rows_ref[:, D:PACK].astype(f32)
    theirs = grad(
        (place ^ 1) * ROWS,
        other_rows_ref[:, :D].astype(f32),
        other_rows_ref[:, share].astype(f32),
        inverse[:, 0:1] + inverse[:, 1:2],
    )
    for i in range(D // ROWS):
        part = slice(ROWS * i, ROWS * (i + 1))
        other_mixed = other_rows_ref[:, PACK + ROWS * i : PACK + ROWS * (i + 1)]
        product = jnp.dot(mixed_ref[part, :], mine, preferred_element_type=f32)
        product += jnp.dot(other_mixed, theirs, preferred_element_type=f32)
        out_ref[part, :] = product.astype(bf16)
    write.wait()


def join_kernel(halves_ref, out_ref):
    for core in range(2):
        parts = [halves_ref[c].astype(jnp.float32) for c in range(core, CTX, 2)]
        out_ref[:, HALF * core : HALF * (core + 1)] = (parts[0] + parts[1]) + (parts[2] + parts[3])


SMEM = pl.BlockSpec(memory_space=pltpu.SMEM)
VMEM = pl.BlockSpec(memory_space=pltpu.VMEM)
ANY = pl.BlockSpec(memory_space=pl.ANY)


def call(kernel, name, smem, vmem, outs, scratch, flops, aliases={}, whole=(), hbm_outs=0, sems=()):
    return pl.pallas_call(
        kernel,
        name=name,
        out_shape=[jax.ShapeDtypeStruct(s, t) for s, t in outs],
        in_specs=[SMEM] * len(smem) + [VMEM] * len(vmem) + [ANY] * len(whole),
        out_specs=[VMEM] * (len(outs) - hbm_outs) + [ANY] * hbm_outs,
        scratch_shapes=[pltpu.VMEM(s, t) for s, t in scratch] + list(sems),
        input_output_aliases=aliases,
        cost_estimate=pl.CostEstimate(flops=flops, bytes_accessed=1 << 26, transcendentals=0),
        compiler_params=pltpu.CompilerParams(vmem_limit_bytes=VMEM_LIMIT),
    )(*smem, *vmem, *whole)


def copies(value, axis, count):
    return lax.all_to_all(jnp.broadcast_to(value[None], (count,) + value.shape), axis, 0, 0, tiled=True)


def per_device(hidden_in, w_qkv, w_out, b_out, ln_gain, ln_bias, doc_lengths, pair_of):
    f32, bf16 = jnp.float32, jnp.bfloat16
    own = hidden_in[0]
    places = jnp.stack([lax.axis_index("ctx"), lax.axis_index("dp")]).astype(jnp.int32)
    smem = [doc_lengths, places]
    state = [((HEADS, AUG, ROWS), f32)]
    work = [((HEADS, AUG, 2 * ROWS), bf16)]
    held = ((PAIRS, 256, 2 * ROWS), bf16)

    def fold(name, sources, blocks, acc):
        (acc,) = call(
            functools.partial(fold_kernel, sources), name, smem, [w_qkv, qbd, acc, *blocks], state, work,
            1 << 34, {4: 0},
        )
        return acc

    near = lax.ppermute(own, "ctx", AROUND)
    other = lax.ppermute(own, "ctx", CORE_SWAP)
    qbd, acc = call(queries_kernel, "queries", smem, [own, w_qkv], [held] + state, [], 1 << 34)
    own_later, acc = lax.optimization_barrier((own, acc))
    behind = lax.ppermute(own_later, "ctx", BACK)
    acc = fold("own", SOURCES[0:2], [own, other], acc)
    near, acc = lax.optimization_barrier((near, acc))
    far = lax.ppermute(near, "ctx", AROUND)
    near_other = lax.ppermute(near, "ctx", CORE_SWAP)
    acc = fold("near", SOURCES[2:3], [near], acc)
    near_other, acc = lax.optimization_barrier((near_other, acc))
    acc = fold("near_other", SOURCES[3:4], [near_other], acc)
    behind, acc = lax.optimization_barrier((behind, acc))
    behind_other = lax.ppermute(behind, "ctx", CORE_SWAP)
    acc = fold("behind", SOURCES[4:5], [behind], acc)
    behind_other, acc = lax.optimization_barrier((behind_other, acc))
    acc = fold("behind_other", SOURCES[5:6], [behind_other], acc)
    far, acc = lax.optimization_barrier((far, acc))
    far_other = lax.ppermute(far, "ctx", CORE_SWAP)
    acc = fold("far", SOURCES[6:7], [far], acc)
    far_other, acc = lax.optimization_barrier((far_other, acc))
    _, mixed, normal, inverse, rows, partials = call(
        last_kernel,
        "last",
        smem,
        [far_other, w_qkv, qbd, acc, own, w_out, b_out, ln_gain, ln_bias],
        state
        + [((D, ROWS), bf16), ((ROWS, D), f32), ((ROWS, 1), f32), ((ROWS, PACK + D), bf16), ((CTX, DOCS, D), f32)],
        work + [((8, 2 * ROWS), f32), ((len(SOURCES), ROWS, D), bf16)],
        1 << 34,
        {5: 0},
        [own, other, near, near_other, behind, behind_other, far, far_other],
    )
    other_rows = lax.ppermute(rows, "ctx", CORE_SWAP)
    pooled = jnp.sum(lax.all_to_all(partials, "ctx", 0, 0, tiled=True), axis=0)
    every = copies(pooled, "dp", DP)
    every, other_rows = lax.optimization_barrier((every, other_rows))
    term, encoded = call(
        back_kernel,
        "back",
        smem + [pair_of],
        [every, mixed, normal, inverse, other_rows, ln_gain, ln_bias],
        [((D, HALF), bf16), ((ROWS, D), bf16)],
        [((NDOC, NDOC), f32), ((DOCS, D), f32), ((ROWS, D), bf16)],
        1 << 20,
        hbm_outs=1,
        sems=[pltpu.SemaphoreType.DMA],
    )
    share = D // DP
    pieces = lax.all_to_all(term.reshape(DP, share, HALF), "dp", 0, 0, tiled=True)
    piece = jnp.sum(pieces.astype(f32), axis=0).astype(bf16)
    halves = copies(piece, "ctx", CTX)
    (grad_out,) = call(join_kernel, "join", [], [halves], [((share, D), f32)], [], 1 << 20)
    return (encoded[None], grad_out)


def solution(mesh):
    return jax.shard_map(
        per_device,
        mesh=mesh,
        in_specs=(P("dp", "ctx", None), P(), P(), P(), P(), P(), P("dp", None), P("dp", None)),
        out_specs=(P("dp", "ctx", None), P("dp", None)),
        check_vma=False,
    )
```

```python
import functools

import jax
import jax.numpy as jnp
from jax import lax
from jax.experimental import pallas as pl
from jax.experimental.pallas import tpu as pltpu
from jax.sharding import PartitionSpec as P

D = 768
HEADS = 12
HEAD_DIM = 64
PAIRS = HEADS // 2
DOCS = 4
NDOC = 128
ROWS = 256
CTX = 8
DP = 32
HALF = D // 2
PACK = D + 128
AUG = 80

SOFTMAX_TEMPER = 0.05
NORM_EPSILON = 1e-05
EMBED_EPSILON = 1e-06
PENALTY = -1e30

VMEM_LIMIT = 24 * 1024 * 1024

CORE_SWAP = [(c, c ^ 1) for c in range(CTX)]
AROUND = [(c, (c + 2) % CTX if c % 2 == 0 else (c - 2) % CTX) for c in range(CTX)]
BACK = [(b, a) for a, b in AROUND]


def came_from(place, hops):
    step = 2 * hops
    return lax.rem(jnp.where(lax.rem(place, 2) == 0, place - step, place + step) + 2 * CTX, CTX)


SOURCES = [(0, 0), (1, 0), (0, 1), (1, 1), (0, -1), (1, -1), (0, 2), (1, 2)]


def doc_ends(lengths_ref):
    e0 = lengths_ref[0, 0]
    e1 = e0 + lengths_ref[0, 1]
    e2 = e1 + lengths_ref[0, 2]
    e3 = e2 + lengths_ref[0, 3]
    return e0, e1, e2, e3


def doc_of(ends, positions):
    e0, e1, e2, e3 = ends
    one = jnp.int32(1)
    zero = jnp.int32(0)
    return sum(jnp.where(positions >= e, one, zero) for e in (e0, e1, e2, e3))


def needed_span(ends, first):
    e0, e1, e2, e3 = ends
    last = first + ROWS - 1
    low = jnp.where(first >= e2, e2, jnp.where(first >= e1, e1, jnp.where(first >= e0, e0, 0)))
    high = jnp.where(last < e0, e0, jnp.where(last < e1, e1, jnp.where(last < e2, e2, e3)))
    return low, high


def fill_queries(ends, first, own, wqkv_ref, qbd):
    queries = lax.dot_general(
        wqkv_ref[:, :D], own, (((0,), (1,)), ((), ())), preferred_element_type=jnp.float32
    )
    queries = (queries.astype(jnp.bfloat16).astype(jnp.float32) * HEAD_DIM**-0.5).astype(jnp.bfloat16)
    positions = first + lax.broadcasted_iota(jnp.int32, (HEAD_DIM * 2, ROWS), 1)
    slots = lax.broadcasted_iota(jnp.int32, (HEAD_DIM * 2, ROWS), 0)
    same = (doc_of(ends, positions) == slots) | (slots >= DOCS)
    penalty = jnp.where(same, 0.0, PENALTY).astype(jnp.bfloat16)
    penalties = jnp.concatenate([penalty, penalty], axis=1)
    zero = jnp.zeros((HEAD_DIM, ROWS), jnp.bfloat16)
    for j in range(PAIRS):
        qbd[j, :64, :ROWS] = queries[128 * j : 128 * j + 64, :]
        qbd[j, :64, ROWS:] = zero
        qbd[j, 64:128, :ROWS] = zero
        qbd[j, 64:128, ROWS:] = queries[128 * j + 64 : 128 * j + 128, :]
        qbd[j, 128:, :] = penalties


def project(ends, bases, blocks, wqkv_ref, vt):
    rows = ROWS * len(blocks)
    hidden = jnp.concatenate(blocks, axis=0) if len(blocks) > 1 else blocks[0]
    keys = jnp.dot(hidden, wqkv_ref[:, D : 2 * D], preferred_element_type=jnp.float32).astype(jnp.bfloat16)
    values = lax.dot_general(
        wqkv_ref[:, 2 * D :], hidden, (((0,), (1,)), ((), ())), preferred_element_type=jnp.float32
    ).astype(jnp.bfloat16)
    vt[:, :HEAD_DIM, :rows] = values.reshape(HEADS, HEAD_DIM, rows)
    offsets = lax.broadcasted_iota(jnp.int32, (ROWS, 128), 0)
    lanes = lax.broadcasted_iota(jnp.int32, (ROWS, 128), 1)
    onehots = [
        jnp.where(doc_of(ends, base + offsets) == lanes, 1.0, 0.0).astype(jnp.bfloat16) for base in bases
    ]
    return keys, jnp.concatenate(onehots, axis=0) if len(blocks) > 1 else onehots[0]


def pair_scores(keys, onehot, qbd, j):
    pair_keys = jnp.concatenate([keys[:, 128 * j : 128 * j + 128], onehot], axis=1)
    return jnp.dot(pair_keys, qbd[j], preferred_element_type=jnp.float32)


def attend_plain(ends, bases, blocks, wqkv_ref, qbd, vt, acc_ref):
    rows = ROWS * len(blocks)
    keys, onehot = project(ends, bases, blocks, wqkv_ref, vt)
    for j in range(PAIRS):
        weights = jnp.exp(pair_scores(keys, onehot, qbd, j)).astype(jnp.bfloat16)
        for h in range(2):
            part = slice(ROWS * h, ROWS * h + ROWS)
            acc_ref[2 * j + h] += jnp.dot(
                vt[2 * j + h, :, :rows], weights[:, part], preferred_element_type=jnp.float32
            )


def attend_shifted(ends, base, block, wqkv_ref, qbd, vt, m_ref, acc_ref):
    keys, onehot = project(ends, [base], [block], wqkv_ref, vt)
    for j in range(PAIRS):
        scores = pair_scores(keys, onehot, qbd, j)
        old = m_ref[j : j + 1, :]
        new = jnp.maximum(old, jnp.max(scores, axis=0, keepdims=True))
        m_ref[j : j + 1, :] = new
        shrink = jnp.exp(old - new)
        weights = jnp.exp(scores - new).astype(jnp.bfloat16)
        for h in range(2):
            part = slice(ROWS * h, ROWS * h + ROWS)
            mixed = jnp.dot(vt[2 * j + h, :, :ROWS], weights[:, part], preferred_element_type=jnp.float32)
            acc_ref[2 * j + h] = acc_ref[2 * j + h] * shrink[:, part] + mixed


def fill_ones(vt):
    row = lax.broadcasted_iota(jnp.int32, (HEADS, AUG - HEAD_DIM, vt.shape[2]), 1)
    vt[:, HEAD_DIM:, :] = jnp.where(row == 0, 1.0, 0.0).astype(jnp.bfloat16)


def attend_blocks(ends, first, places, blocks, wqkv_ref, qbd, vt, acc_ref):
    low, high = needed_span(ends, first)
    bases = [place * ROWS for place in places]
    wanted = [(base < high) & (base + ROWS > low) for base in bases]

    def attend(which):
        attend_plain(
            ends, [bases[i] for i in which], [blocks[i][...] for i in which], wqkv_ref, qbd, vt, acc_ref
        )

    if len(blocks) == 1:
        pl.when(wanted[0])(lambda: attend([0]))
    else:
        one, two = wanted
        pl.when(one & two)(lambda: attend([0, 1]))
        pl.when(one & jnp.logical_not(two))(lambda: attend([0]))
        pl.when(two & jnp.logical_not(one))(lambda: attend([1]))


def queries_kernel(lengths_ref, place_ref, own_ref, wqkv_ref, qbd, acc_ref):
    ends = doc_ends(lengths_ref)
    fill_queries(ends, place_ref[0] * ROWS, own_ref[...], wqkv_ref, qbd)
    acc_ref[...] = jnp.zeros(acc_ref.shape, jnp.float32)


def fold_kernel(sources, lengths_ref, place_ref, wqkv_ref, qbd, acc_in, *refs):
    blocks, (acc_ref, vt) = refs[: len(sources)], refs[len(sources) :]
    place = place_ref[0]
    ends = doc_ends(lengths_ref)
    fill_ones(vt)
    places = [came_from(place ^ flip, hops) for flip, hops in sources]
    attend_blocks(ends, place * ROWS, places, blocks, wqkv_ref, qbd, vt, acc_ref)


def in_range(acc):
    sums = acc[:, HEAD_DIM, :]
    good = jnp.where((sums >= 1e-12) & (sums <= 1e12), 1.0, 0.0)
    finite = jnp.where(jnp.abs(acc) <= 1e38, 1.0, 0.0)
    return jnp.minimum(jnp.min(good), jnp.min(finite)) > 0.5


def attend_again(ends, place, blocks, wqkv_ref, qbd, vt, acc_ref, m_ref, held):
    for i, (flip, hops) in enumerate(SOURCES):
        pltpu.sync_copy(blocks[i], held.at[i])
    m_ref[...] = jnp.full(m_ref.shape, PENALTY, jnp.float32)
    acc_ref[...] = jnp.zeros(acc_ref.shape, jnp.float32)
    low, high = needed_span(ends, place * ROWS)

    def step(i, carry):
        base = jnp.int32(0)
        for k, (flip, hops) in enumerate(SOURCES):
            base = jnp.where(i == k, came_from(place ^ flip, hops) * ROWS, base)

        @pl.when((base < high) & (base + ROWS > low))
        def _():
            attend_shifted(ends, base, held[i], wqkv_ref, qbd, vt, m_ref, acc_ref)

        return carry

    lax.fori_loop(0, len(SOURCES), step, 0)


def last_kernel(
    lengths_ref, place_ref, far_other_ref, wqkv_ref, qbd, acc_in, own_ref, wout_ref, bias_ref, gain_ref, shift_ref,
    *refs
):
    blocks, refs = refs[: len(SOURCES)], refs[len(SOURCES) :]
    acc_ref, mixed_ref, normal_ref, inverse_ref, rows_ref, pooled_ref, vt, m_ref, held = refs
    place = place_ref[0]
    ends = doc_ends(lengths_ref)
    first = place * ROWS
    fill_ones(vt)
    flip, hops = SOURCES[-1]
    attend_blocks(ends, first, [came_from(place ^ flip, hops)], [far_other_ref], wqkv_ref, qbd, vt, acc_ref)

    @pl.when(jnp.logical_not(in_range(acc_ref[...])))
    def _():
        attend_again(ends, place, blocks, wqkv_ref, qbd, vt, acc_ref, m_ref, held)

    acc = acc_ref[...]
    mixed = acc[:, :HEAD_DIM, :] * (1.0 / acc[:, HEAD_DIM : HEAD_DIM + 1, :])
    mixed = mixed.reshape(D, ROWS).astype(jnp.bfloat16)
    mixed_ref[...] = mixed
    summed = lax.dot_general(
        mixed, wout_ref[...], (((0,), (0,)), ((), ())), preferred_element_type=jnp.float32
    )
    summed = summed + bias_ref[...][None] + own_ref[...].astype(jnp.float32)
    centered = summed - jnp.mean(summed, axis=1, keepdims=True)
    inverse = lax.rsqrt(jnp.mean(centered * centered, axis=1, keepdims=True) + NORM_EPSILON)
    normal = centered * inverse
    normal_ref[...] = normal
    inverse_ref[...] = inverse
    layer = normal * gain_ref[...][None] + shift_ref[...][None]
    for i in range(D // ROWS):
        rows_ref[:, PACK + ROWS * i : PACK + ROWS * (i + 1)] = mixed[ROWS * i : ROWS * (i + 1)]
    rows_ref[:, :D] = normal.astype(jnp.bfloat16)
    high = inverse.astype(jnp.bfloat16).astype(jnp.float32)
    lane = lax.broadcasted_iota(jnp.int32, (ROWS, 128), 1)
    rows_ref[:, D:PACK] = jnp.where(lane == 0, high, inverse - high).astype(jnp.bfloat16)
    row_doc = doc_of(ends, first + lax.broadcasted_iota(jnp.int32, (ROWS, 1), 0))
    pooled_ref[...] = jnp.zeros(pooled_ref.shape, jnp.float32)
    starts = (jnp.int32(0), *ends[:-1])
    for d in range(DOCS):

        @pl.when((starts[d] < first + ROWS) & (ends[d] > first))
        def _():
            total = jnp.sum(jnp.where(row_doc == d, layer, 0.0), axis=0, keepdims=True)
            mean = total * (1.0 / lengths_ref[0, d].astype(jnp.float32))
            pooled_ref[d : d + 1, :] = mean


def back_kernel(
    lengths_ref, place_ref, pair_ref, pooled_ref, mixed_ref, normal_ref, inverse_ref, other_rows_ref,
    gain_ref, shift_ref, out_ref, encoded_hbm, expo_ref, scaled_ref, encoded_ref, sem
):
    place = place_ref[0]
    data_place = place_ref[1]
    ends = doc_ends(lengths_ref)
    f32, bf16 = jnp.float32, jnp.bfloat16
    encoded_ref[...] = (normal_ref[...] * gain_ref[...][None] + shift_ref[...][None]).astype(bf16)
    write = pltpu.make_async_copy(encoded_ref, encoded_hbm, sem)
    write.start()

    pooled = pooled_ref[...]
    emb = pooled * lax.rsqrt(jnp.sum(pooled * pooled, axis=1, keepdims=True) + EMBED_EPSILON)
    high = emb.astype(bf16)
    low = (emb - high.astype(f32)).astype(bf16)

    def times(left, right):
        return lax.dot_general(left, right, (((1,), (1,)), ((), ())), preferred_element_type=f32)

    sims = (times(high, high) + (times(high, low) + times(low, high))) * (1.0 / SOFTMAX_TEMPER)
    columns = lax.broadcasted_iota(jnp.int32, (NDOC, NDOC), 1)
    rows = lax.broadcasted_iota(jnp.int32, (NDOC, NDOC), 0)
    expo = jnp.where(rows == columns, 0.0, jnp.exp(sims))
    expo_ref[...] = expo
    totals = 1.0 / jnp.sum(expo, axis=0, keepdims=True)
    half = lax.rem(data_place, 2)
    rows8 = pl.ds(pl.multiple_of((data_place - half) * DOCS, 8), 8)

    def own_rows(ref):
        found = ref[rows8, :]
        return jnp.where(half == 0, found[:DOCS], found[DOCS:])

    own = own_rows(pooled_ref)
    own_inverse = lax.rsqrt(jnp.sum(own * own, axis=1, keepdims=True) + EMBED_EPSILON)
    own_emb = own * own_inverse
    own_expo = own_rows(expo_ref)
    own_totals = 1.0 / jnp.sum(own_expo, axis=1, keepdims=True)
    slots = lax.broadcasted_iota(jnp.int32, (DOCS, NDOC), 0)
    lanes = lax.broadcasted_iota(jnp.int32, (DOCS, NDOC), 1)
    partner = jnp.where(
        slots == 0, pair_ref[0, 0],
        jnp.where(slots == 1, pair_ref[0, 1], jnp.where(slots == 2, pair_ref[0, 2], pair_ref[0, 3])),
    )
    both = own_expo * (own_totals + totals) - jnp.where(lanes == partner, 2.0, 0.0)
    weights = jnp.concatenate([both, both], axis=0).T
    emb_grad = jnp.concatenate(
        [jnp.sum(weights[:, d : d + 1] * emb, axis=0, keepdims=True) for d in range(DOCS)], axis=0
    ) * (1.0 / SOFTMAX_TEMPER)
    pooled_grad = (emb_grad - own_emb * jnp.sum(own_emb * emb_grad, axis=1, keepdims=True)) * own_inverse
    slot = lax.broadcasted_iota(jnp.int32, (DOCS, 1), 0)
    length = jnp.where(
        slot == 0, lengths_ref[0, 0],
        jnp.where(slot == 1, lengths_ref[0, 1], jnp.where(slot == 2, lengths_ref[0, 2], lengths_ref[0, 3])),
    ).astype(f32)
    scaled = pooled_grad * (1.0 / length) * gain_ref[...][None]
    centered = scaled - jnp.mean(scaled, axis=1, keepdims=True)
    scaled_ref[...] = centered
    share = pl.ds(pl.multiple_of(lax.rem(place, 2) * HALF, 128), HALF)

    def grad(first, normal, normal_share, inverse):
        row_doc = doc_of(ends, first + lax.broadcasted_iota(jnp.int32, (ROWS, 1), 0))

        def spread(values):
            pick = jnp.where(row_doc == 2, values[2:3], values[3:4])
            return jnp.where(row_doc == 0, values[0:1], jnp.where(row_doc == 1, values[1:2], pick))

        along = jnp.mean(spread(scaled) * normal, axis=1, keepdims=True)
        return (inverse * (spread(scaled_ref[:, share]) - normal_share * along)).astype(bf16)

    mine = grad(place * ROWS, normal_ref[...], normal_ref[:, share], inverse_ref[...])
    inverse = other_rows_ref[:, D:PACK].astype(f32)
    theirs = grad(
        (place ^ 1) * ROWS,
        other_rows_ref[:, :D].astype(f32),
        other_rows_ref[:, share].astype(f32),
        inverse[:, 0:1] + inverse[:, 1:2],
    )
    for i in range(D // ROWS):
        part = slice(ROWS * i, ROWS * (i + 1))
        other_mixed = other_rows_ref[:, PACK + ROWS * i : PACK + ROWS * (i + 1)]
        product = jnp.dot(mixed_ref[part, :], mine, preferred_element_type=f32)
        product += jnp.dot(other_mixed, theirs, preferred_element_type=f32)
        out_ref[part, :] = product.astype(bf16)
    write.wait()


def join_kernel(halves_ref, out_ref):
    for core in range(2):
        parts = [halves_ref[c].astype(jnp.float32) for c in range(core, CTX, 2)]
        out_ref[:, HALF * core : HALF * (core + 1)] = (parts[0] + parts[1]) + (parts[2] + parts[3])


SMEM = pl.BlockSpec(memory_space=pltpu.SMEM)
VMEM = pl.BlockSpec(memory_space=pltpu.VMEM)
ANY = pl.BlockSpec(memory_space=pl.ANY)


def call(kernel, name, smem, vmem, outs, scratch, flops, aliases={}, whole=(), hbm_outs=0, sems=()):
    return pl.pallas_call(
        kernel,
        name=name,
        out_shape=[jax.ShapeDtypeStruct(s, t) for s, t in outs],
        in_specs=[SMEM] * len(smem) + [VMEM] * len(vmem) + [ANY] * len(whole),
        out_specs=[VMEM] * (len(outs) - hbm_outs) + [ANY] * hbm_outs,
        scratch_shapes=[pltpu.VMEM(s, t) for s, t in scratch] + list(sems),
        input_output_aliases=aliases,
        cost_estimate=pl.CostEstimate(flops=flops, bytes_accessed=1 << 26, transcendentals=0),
        compiler_params=pltpu.CompilerParams(vmem_limit_bytes=VMEM_LIMIT),
    )(*smem, *vmem, *whole)


def copies(value, axis, count):
    return lax.all_to_all(jnp.broadcast_to(value[None], (count,) + value.shape), axis, 0, 0, tiled=True)


def swap_add(value):
    return value + lax.ppermute(value, "ctx", CORE_SWAP)


def sum_over_chips(value):
    one, two, three = [
        lax.ppermute(value, "ctx", [(c, (c + 2 * hops) % CTX) for c in range(CTX)]).astype(jnp.float32)
        for hops in (1, 2, 3)
    ]
    return (value.astype(jnp.float32) + two) + (one + three)


def per_device(hidden_in, w_qkv, w_out, b_out, ln_gain, ln_bias, doc_lengths, pair_of):
    f32, bf16 = jnp.float32, jnp.bfloat16
    own = hidden_in[0]
    places = jnp.stack([lax.axis_index("ctx"), lax.axis_index("dp")]).astype(jnp.int32)
    smem = [doc_lengths, places]
    state = [((HEADS, AUG, ROWS), f32)]
    work = [((HEADS, AUG, 2 * ROWS), bf16)]
    held = ((PAIRS, 256, 2 * ROWS), bf16)

    def fold(name, sources, blocks, acc):
        (acc,) = call(
            functools.partial(fold_kernel, sources), name, smem, [w_qkv, qbd, acc, *blocks], state, work,
            1 << 34, {4: 0},
        )
        return acc

    near = lax.ppermute(own, "ctx", AROUND)
    other = lax.ppermute(own, "ctx", CORE_SWAP)
    qbd, acc = call(queries_kernel, "queries", smem, [own, w_qkv], [held] + state, [], 1 << 34)
    own_later, acc = lax.optimization_barrier((own, acc))
    behind = lax.ppermute(own_later, "ctx", BACK)
    acc = fold("own", SOURCES[0:2], [own, other], acc)
    near, acc = lax.optimization_barrier((near, acc))
    far = lax.ppermute(near, "ctx", AROUND)
    near_other = lax.ppermute(near, "ctx", CORE_SWAP)
    acc = fold("near", SOURCES[2:3], [near], acc)
    near_other, acc = lax.optimization_barrier((near_other, acc))
    acc = fold("near_other", SOURCES[3:4], [near_other], acc)
    behind, acc = lax.optimization_barrier((behind, acc))
    behind_other = lax.ppermute(behind, "ctx", CORE_SWAP)
    acc = fold("behind", SOURCES[4:5], [behind], acc)
    behind_other, acc = lax.optimization_barrier((behind_other, acc))
    acc = fold("behind_other", SOURCES[5:6], [behind_other], acc)
    far, acc = lax.optimization_barrier((far, acc))
    far_other = lax.ppermute(far, "ctx", CORE_SWAP)
    acc = fold("far", SOURCES[6:7], [far], acc)
    far_other, acc = lax.optimization_barrier((far_other, acc))
    _, mixed, normal, inverse, rows, partial = call(
        last_kernel,
        "last",
        smem,
        [far_other, w_qkv, qbd, acc, own, w_out, b_out, ln_gain, ln_bias],
        state
        + [((D, ROWS), bf16), ((ROWS, D), f32), ((ROWS, 1), f32), ((ROWS, PACK + D), bf16), ((DOCS, D), f32)],
        work + [((8, 2 * ROWS), f32), ((len(SOURCES), ROWS, D), bf16)],
        1 << 34,
        {5: 0},
        [own, other, near, near_other, behind, behind_other, far, far_other],
    )
    other_rows = lax.ppermute(rows, "ctx", CORE_SWAP)
    pooled = sum_over_chips(swap_add(partial))
    every = copies(pooled, "dp", DP).reshape(NDOC, D)
    every, other_rows = lax.optimization_barrier((every, other_rows))
    term, encoded = call(
        back_kernel,
        "back",
        smem + [pair_of],
        [every, mixed, normal, inverse, other_rows, ln_gain, ln_bias],
        [((D, HALF), bf16), ((ROWS, D), bf16)],
        [((NDOC, NDOC), f32), ((DOCS, D), f32), ((ROWS, D), bf16)],
        1 << 20,
        hbm_outs=1,
        sems=[pltpu.SemaphoreType.DMA],
    )
    share = D // DP
    pieces = lax.all_to_all(term.reshape(DP, share, HALF), "dp", 0, 0, tiled=True)
    piece = jnp.sum(pieces.astype(f32), axis=0).astype(bf16)
    halves = copies(piece, "ctx", CTX)
    (grad_out,) = call(join_kernel, "join", [], [halves], [((share, D), f32)], [], 1 << 20)
    return (encoded[None], grad_out)


def solution(mesh):
    return jax.shard_map(
        per_device,
        mesh=mesh,
        in_specs=(P("dp", "ctx", None), P(), P(), P(), P(), P(), P("dp", None), P("dp", None)),
        out_specs=(P("dp", "ctx", None), P("dp", None)),
        check_vma=False,
    )
```

```python
import functools

import jax
import jax.numpy as jnp
from jax import lax
from jax.experimental import pallas as pl
from jax.experimental.pallas import tpu as pltpu
from jax.sharding import PartitionSpec as P

D = 768
HEADS = 12
HEAD_DIM = 64
PAIRS = HEADS // 2
DOCS = 4
NDOC = 128
ROWS = 256
CTX = 8
DP = 32
HALF = D // 2
PACK = D + 128
AUG = 80

SOFTMAX_TEMPER = 0.05
NORM_EPSILON = 1e-05
EMBED_EPSILON = 1e-06
PENALTY = -1e30

VMEM_LIMIT = 24 * 1024 * 1024

CORE_SWAP = [(c, c ^ 1) for c in range(CTX)]
AROUND = [(c, (c + 2) % CTX if c % 2 == 0 else (c - 2) % CTX) for c in range(CTX)]
BACK = [(b, a) for a, b in AROUND]


def came_from(place, hops):
    step = 2 * hops
    return lax.rem(jnp.where(lax.rem(place, 2) == 0, place - step, place + step) + 2 * CTX, CTX)


SOURCES = [(0, 0), (1, 0), (0, 1), (1, 1), (0, -1), (1, -1), (0, 2), (1, 2)]


def doc_ends(lengths_ref):
    e0 = lengths_ref[0, 0]
    e1 = e0 + lengths_ref[0, 1]
    e2 = e1 + lengths_ref[0, 2]
    e3 = e2 + lengths_ref[0, 3]
    return e0, e1, e2, e3


def doc_of(ends, positions):
    e0, e1, e2, e3 = ends
    one = jnp.int32(1)
    zero = jnp.int32(0)
    return sum(jnp.where(positions >= e, one, zero) for e in (e0, e1, e2, e3))


def needed_span(ends, first):
    e0, e1, e2, e3 = ends
    last = first + ROWS - 1
    low = jnp.where(first >= e2, e2, jnp.where(first >= e1, e1, jnp.where(first >= e0, e0, 0)))
    high = jnp.where(last < e0, e0, jnp.where(last < e1, e1, jnp.where(last < e2, e2, e3)))
    return low, high


def fill_queries(ends, first, own, wqkv_ref, qbd):
    queries = lax.dot_general(
        wqkv_ref[:, :D], own, (((0,), (1,)), ((), ())), preferred_element_type=jnp.float32
    )
    queries = (queries.astype(jnp.bfloat16).astype(jnp.float32) * HEAD_DIM**-0.5).astype(jnp.bfloat16)
    positions = first + lax.broadcasted_iota(jnp.int32, (HEAD_DIM * 2, ROWS), 1)
    slots = lax.broadcasted_iota(jnp.int32, (HEAD_DIM * 2, ROWS), 0)
    same = (doc_of(ends, positions) == slots) | (slots >= DOCS)
    penalty = jnp.where(same, 0.0, PENALTY).astype(jnp.bfloat16)
    penalties = jnp.concatenate([penalty, penalty], axis=1)
    zero = jnp.zeros((HEAD_DIM, ROWS), jnp.bfloat16)
    for j in range(PAIRS):
        qbd[j, :64, :ROWS] = queries[128 * j : 128 * j + 64, :]
        qbd[j, :64, ROWS:] = zero
        qbd[j, 64:128, :ROWS] = zero
        qbd[j, 64:128, ROWS:] = queries[128 * j + 64 : 128 * j + 128, :]
        qbd[j, 128:, :] = penalties


def project(ends, bases, blocks, wqkv_ref, vt):
    rows = ROWS * len(blocks)
    hidden = jnp.concatenate(blocks, axis=0) if len(blocks) > 1 else blocks[0]
    keys = jnp.dot(hidden, wqkv_ref[:, D : 2 * D], preferred_element_type=jnp.float32).astype(jnp.bfloat16)
    values = lax.dot_general(
        wqkv_ref[:, 2 * D :], hidden, (((0,), (1,)), ((), ())), preferred_element_type=jnp.float32
    ).astype(jnp.bfloat16)
    vt[:, :HEAD_DIM, :rows] = values.reshape(HEADS, HEAD_DIM, rows)
    offsets = lax.broadcasted_iota(jnp.int32, (ROWS, 128), 0)
    lanes = lax.broadcasted_iota(jnp.int32, (ROWS, 128), 1)
    onehots = [
        jnp.where(doc_of(ends, base + offsets) == lanes, 1.0, 0.0).astype(jnp.bfloat16) for base in bases
    ]
    return keys, jnp.concatenate(onehots, axis=0) if len(blocks) > 1 else onehots[0]


def pair_scores(keys, onehot, qbd, j):
    pair_keys = jnp.concatenate([keys[:, 128 * j : 128 * j + 128], onehot], axis=1)
    return jnp.dot(pair_keys, qbd[j], preferred_element_type=jnp.float32)


def attend_plain(ends, bases, blocks, wqkv_ref, qbd, vt, acc_ref):
    rows = ROWS * len(blocks)
    keys, onehot = project(ends, bases, blocks, wqkv_ref, vt)
    for j in range(PAIRS):
        weights = jnp.exp(pair_scores(keys, onehot, qbd, j)).astype(jnp.bfloat16)
        for h in range(2):
            part = slice(ROWS * h, ROWS * h + ROWS)
            acc_ref[2 * j + h] += jnp.dot(
                vt[2 * j + h, :, :rows], weights[:, part], preferred_element_type=jnp.float32
            )


def attend_shifted(ends, base, block, wqkv_ref, qbd, vt, m_ref, acc_ref):
    keys, onehot = project(ends, [base], [block], wqkv_ref, vt)
    for j in range(PAIRS):
        scores = pair_scores(keys, onehot, qbd, j)
        old = m_ref[j : j + 1, :]
        new = jnp.maximum(old, jnp.max(scores, axis=0, keepdims=True))
        m_ref[j : j + 1, :] = new
        shrink = jnp.exp(old - new)
        weights = jnp.exp(scores - new).astype(jnp.bfloat16)
        for h in range(2):
            part = slice(ROWS * h, ROWS * h + ROWS)
            mixed = jnp.dot(vt[2 * j + h, :, :ROWS], weights[:, part], preferred_element_type=jnp.float32)
            acc_ref[2 * j + h] = acc_ref[2 * j + h] * shrink[:, part] + mixed


def fill_ones(vt):
    row = lax.broadcasted_iota(jnp.int32, (HEADS, AUG - HEAD_DIM, vt.shape[2]), 1)
    vt[:, HEAD_DIM:, :] = jnp.where(row == 0, 1.0, 0.0).astype(jnp.bfloat16)


def attend_blocks(ends, first, places, blocks, wqkv_ref, qbd, vt, acc_ref):
    low, high = needed_span(ends, first)
    bases = [place * ROWS for place in places]
    wanted = [(base < high) & (base + ROWS > low) for base in bases]

    def attend(which):
        attend_plain(
            ends, [bases[i] for i in which], [blocks[i][...] for i in which], wqkv_ref, qbd, vt, acc_ref
        )

    if len(blocks) == 1:
        pl.when(wanted[0])(lambda: attend([0]))
    else:
        one, two = wanted
        pl.when(one & two)(lambda: attend([0, 1]))
        pl.when(one & jnp.logical_not(two))(lambda: attend([0]))
        pl.when(two & jnp.logical_not(one))(lambda: attend([1]))


def queries_kernel(lengths_ref, place_ref, own_ref, wqkv_ref, qbd, acc_ref):
    ends = doc_ends(lengths_ref)
    fill_queries(ends, place_ref[0] * ROWS, own_ref[...], wqkv_ref, qbd)
    acc_ref[...] = jnp.zeros(acc_ref.shape, jnp.float32)


def fold_kernel(sources, lengths_ref, place_ref, wqkv_ref, qbd, acc_in, *refs):
    blocks, (acc_ref, vt) = refs[: len(sources)], refs[len(sources) :]
    place = place_ref[0]
    ends = doc_ends(lengths_ref)
    fill_ones(vt)
    places = [came_from(place ^ flip, hops) for flip, hops in sources]
    attend_blocks(ends, place * ROWS, places, blocks, wqkv_ref, qbd, vt, acc_ref)


def in_range(acc):
    sums = acc[:, HEAD_DIM, :]
    good = jnp.where((sums >= 1e-12) & (sums <= 1e12), 1.0, 0.0)
    finite = jnp.where(jnp.abs(acc) <= 1e38, 1.0, 0.0)
    return jnp.minimum(jnp.min(good), jnp.min(finite)) > 0.5


def attend_again(ends, place, blocks, wqkv_ref, qbd, vt, acc_ref, m_ref, held):
    for i, (flip, hops) in enumerate(SOURCES):
        pltpu.sync_copy(blocks[i], held.at[i])
    m_ref[...] = jnp.full(m_ref.shape, PENALTY, jnp.float32)
    acc_ref[...] = jnp.zeros(acc_ref.shape, jnp.float32)
    low, high = needed_span(ends, place * ROWS)

    def step(i, carry):
        base = jnp.int32(0)
        for k, (flip, hops) in enumerate(SOURCES):
            base = jnp.where(i == k, came_from(place ^ flip, hops) * ROWS, base)

        @pl.when((base < high) & (base + ROWS > low))
        def _():
            attend_shifted(ends, base, held[i], wqkv_ref, qbd, vt, m_ref, acc_ref)

        return carry

    lax.fori_loop(0, len(SOURCES), step, 0)


def last_kernel(
    lengths_ref, place_ref, far_other_ref, wqkv_ref, qbd, acc_in, own_ref, wout_ref, bias_ref, gain_ref, shift_ref,
    *refs
):
    blocks, refs = refs[: len(SOURCES)], refs[len(SOURCES) :]
    acc_ref, mixed_ref, normal_ref, inverse_ref, rows_ref, pooled_ref, vt, m_ref, held = refs
    place = place_ref[0]
    ends = doc_ends(lengths_ref)
    first = place * ROWS
    fill_ones(vt)
    flip, hops = SOURCES[-1]
    attend_blocks(ends, first, [came_from(place ^ flip, hops)], [far_other_ref], wqkv_ref, qbd, vt, acc_ref)

    @pl.when(jnp.logical_not(in_range(acc_ref[...])))
    def _():
        attend_again(ends, place, blocks, wqkv_ref, qbd, vt, acc_ref, m_ref, held)

    acc = acc_ref[...]
    mixed = acc[:, :HEAD_DIM, :] * (1.0 / acc[:, HEAD_DIM : HEAD_DIM + 1, :])
    mixed = mixed.reshape(D, ROWS).astype(jnp.bfloat16)
    mixed_ref[...] = mixed
    summed = lax.dot_general(
        mixed, wout_ref[...], (((0,), (0,)), ((), ())), preferred_element_type=jnp.float32
    )
    summed = summed + bias_ref[...][None] + own_ref[...].astype(jnp.float32)
    centered = summed - jnp.mean(summed, axis=1, keepdims=True)
    inverse = lax.rsqrt(jnp.mean(centered * centered, axis=1, keepdims=True) + NORM_EPSILON)
    normal = centered * inverse
    normal_ref[...] = normal
    inverse_ref[...] = inverse
    layer = normal * gain_ref[...][None] + shift_ref[...][None]
    for i in range(D // ROWS):
        rows_ref[:, PACK + ROWS * i : PACK + ROWS * (i + 1)] = mixed[ROWS * i : ROWS * (i + 1)]
    rows_ref[:, :D] = normal.astype(jnp.bfloat16)
    high = inverse.astype(jnp.bfloat16).astype(jnp.float32)
    lane = lax.broadcasted_iota(jnp.int32, (ROWS, 128), 1)
    rows_ref[:, D:PACK] = jnp.where(lane == 0, high, inverse - high).astype(jnp.bfloat16)
    row_doc = doc_of(ends, first + lax.broadcasted_iota(jnp.int32, (ROWS, 1), 0))
    pooled_ref[...] = jnp.zeros(pooled_ref.shape, jnp.float32)
    starts = (jnp.int32(0), *ends[:-1])
    for d in range(DOCS):

        @pl.when((starts[d] < first + ROWS) & (ends[d] > first))
        def _():
            total = jnp.sum(jnp.where(row_doc == d, layer, 0.0), axis=0, keepdims=True)
            mean = total * (1.0 / lengths_ref[0, d].astype(jnp.float32))
            pooled_ref[d : d + 1, :] = mean


def back_kernel(
    lengths_ref, place_ref, pair_ref, pooled_ref, own_ref, mixed_ref, normal_ref, inverse_ref, other_rows_ref,
    gain_ref, shift_ref, out_ref, encoded_hbm, expo_ref, scaled_ref, encoded_ref, sem
):
    place = place_ref[0]
    data_place = place_ref[1]
    ends = doc_ends(lengths_ref)
    f32, bf16 = jnp.float32, jnp.bfloat16
    encoded_ref[...] = (normal_ref[...] * gain_ref[...][None] + shift_ref[...][None]).astype(bf16)
    write = pltpu.make_async_copy(encoded_ref, encoded_hbm, sem)
    write.start()

    pooled = pooled_ref[...].reshape(NDOC, D)
    emb = pooled * lax.rsqrt(jnp.sum(pooled * pooled, axis=1, keepdims=True) + EMBED_EPSILON)
    high = emb.astype(bf16)
    low = (emb - high.astype(f32)).astype(bf16)

    def times(left, right):
        return lax.dot_general(left, right, (((1,), (1,)), ((), ())), preferred_element_type=f32)

    sims = (times(high, high) + (times(high, low) + times(low, high))) * (1.0 / SOFTMAX_TEMPER)
    columns = lax.broadcasted_iota(jnp.int32, (NDOC, NDOC), 1)
    rows = lax.broadcasted_iota(jnp.int32, (NDOC, NDOC), 0)
    expo = jnp.where(rows == columns, 0.0, jnp.exp(sims))
    expo_ref[...] = expo
    totals = 1.0 / jnp.sum(expo, axis=0, keepdims=True)
    half = lax.rem(data_place, 2)
    rows8 = expo_ref[pl.ds(pl.multiple_of((data_place - half) * DOCS, 8), 8), :]
    own_expo = jnp.where(half == 0, rows8[:DOCS], rows8[DOCS:])
    own = own_ref[0]
    own_inverse = lax.rsqrt(jnp.sum(own * own, axis=1, keepdims=True) + EMBED_EPSILON)
    own_emb = own * own_inverse
    own_totals = 1.0 / jnp.sum(own_expo, axis=1, keepdims=True)
    slots = lax.broadcasted_iota(jnp.int32, (DOCS, NDOC), 0)
    lanes = lax.broadcasted_iota(jnp.int32, (DOCS, NDOC), 1)
    partner = jnp.where(
        slots == 0, pair_ref[0, 0],
        jnp.where(slots == 1, pair_ref[0, 1], jnp.where(slots == 2, pair_ref[0, 2], pair_ref[0, 3])),
    )
    both = own_expo * (own_totals + totals) - jnp.where(lanes == partner, 2.0, 0.0)
    weights = jnp.concatenate([both, both], axis=0).T
    emb_grad = jnp.concatenate(
        [jnp.sum(weights[:, d : d + 1] * emb, axis=0, keepdims=True) for d in range(DOCS)], axis=0
    ) * (1.0 / SOFTMAX_TEMPER)
    pooled_grad = (emb_grad - own_emb * jnp.sum(own_emb * emb_grad, axis=1, keepdims=True)) * own_inverse
    slot = lax.broadcasted_iota(jnp.int32, (DOCS, 1), 0)
    length = jnp.where(
        slot == 0, lengths_ref[0, 0],
        jnp.where(slot == 1, lengths_ref[0, 1], jnp.where(slot == 2, lengths_ref[0, 2], lengths_ref[0, 3])),
    ).astype(f32)
    scaled = pooled_grad * (1.0 / length) * gain_ref[...][None]
    centered = scaled - jnp.mean(scaled, axis=1, keepdims=True)
    scaled_ref[...] = centered
    share = pl.ds(pl.multiple_of(lax.rem(place, 2) * HALF, 128), HALF)

    def grad(first, normal, normal_share, inverse):
        row_doc = doc_of(ends, first + lax.broadcasted_iota(jnp.int32, (ROWS, 1), 0))

        def spread(values):
            pick = jnp.where(row_doc == 2, values[2:3], values[3:4])
            return jnp.where(row_doc == 0, values[0:1], jnp.where(row_doc == 1, values[1:2], pick))

        along = jnp.mean(spread(scaled) * normal, axis=1, keepdims=True)
        return (inverse * (spread(scaled_ref[:, share]) - normal_share * along)).astype(bf16)

    mine = grad(place * ROWS, normal_ref[...], normal_ref[:, share], inverse_ref[...])
    inverse = other_rows_ref[:, D:PACK].astype(f32)
    theirs = grad(
        (place ^ 1) * ROWS,
        other_rows_ref[:, :D].astype(f32),
        other_rows_ref[:, share].astype(f32),
        inverse[:, 0:1] + inverse[:, 1:2],
    )
    for i in range(D // ROWS):
        part = slice(ROWS * i, ROWS * (i + 1))
        other_mixed = other_rows_ref[:, PACK + ROWS * i : PACK + ROWS * (i + 1)]
        product = jnp.dot(mixed_ref[part, :], mine, preferred_element_type=f32)
        product += jnp.dot(other_mixed, theirs, preferred_element_type=f32)
        out_ref[part, :] = product.astype(bf16)
    write.wait()


def join_kernel(halves_ref, out_ref):
    for core in range(2):
        parts = [halves_ref[c].astype(jnp.float32) for c in range(core, CTX, 2)]
        out_ref[:, HALF * core : HALF * (core + 1)] = (parts[0] + parts[1]) + (parts[2] + parts[3])


SMEM = pl.BlockSpec(memory_space=pltpu.SMEM)
VMEM = pl.BlockSpec(memory_space=pltpu.VMEM)
ANY = pl.BlockSpec(memory_space=pl.ANY)


def call(kernel, name, smem, vmem, outs, scratch, flops, aliases={}, whole=(), hbm_outs=0, sems=()):
    return pl.pallas_call(
        kernel,
        name=name,
        out_shape=[jax.ShapeDtypeStruct(s, t) for s, t in outs],
        in_specs=[SMEM] * len(smem) + [VMEM] * len(vmem) + [ANY] * len(whole),
        out_specs=[VMEM] * (len(outs) - hbm_outs) + [ANY] * hbm_outs,
        scratch_shapes=[pltpu.VMEM(s, t) for s, t in scratch] + list(sems),
        input_output_aliases=aliases,
        cost_estimate=pl.CostEstimate(flops=flops, bytes_accessed=1 << 26, transcendentals=0),
        compiler_params=pltpu.CompilerParams(vmem_limit_bytes=VMEM_LIMIT),
    )(*smem, *vmem, *whole)


def copies(value, axis, count):
    return lax.all_to_all(jnp.broadcast_to(value[None], (count,) + value.shape), axis, 0, 0, tiled=True)


def swap_add(value):
    return value + lax.ppermute(value, "ctx", CORE_SWAP)


def sum_over_chips(value):
    one, two, three = [
        lax.ppermute(value, "ctx", [(c, (c + 2 * hops) % CTX) for c in range(CTX)]).astype(jnp.float32)
        for hops in (1, 2, 3)
    ]
    return (value.astype(jnp.float32) + two) + (one + three)


def per_device(hidden_in, w_qkv, w_out, b_out, ln_gain, ln_bias, doc_lengths, pair_of):
    f32, bf16 = jnp.float32, jnp.bfloat16
    own = hidden_in[0]
    places = jnp.stack([lax.axis_index("ctx"), lax.axis_index("dp")]).astype(jnp.int32)
    smem = [doc_lengths, places]
    state = [((HEADS, AUG, ROWS), f32)]
    work = [((HEADS, AUG, 2 * ROWS), bf16)]
    held = ((PAIRS, 256, 2 * ROWS), bf16)

    def fold(name, sources, blocks, acc):
        (acc,) = call(
            functools.partial(fold_kernel, sources), name, smem, [w_qkv, qbd, acc, *blocks], state, work,
            1 << 34, {4: 0},
        )
        return acc

    near = lax.ppermute(own, "ctx", AROUND)
    qbd, acc = call(queries_kernel, "queries", smem, [own, w_qkv], [held] + state, [], 1 << 34)
    own_later, acc = lax.optimization_barrier((own, acc))
    behind = lax.ppermute(own_later, "ctx", BACK)
    other = lax.ppermute(own_later, "ctx", CORE_SWAP)
    acc = fold("own", SOURCES[0:1], [own], acc)
    acc = fold("other", SOURCES[1:2], [other], acc)
    near, acc = lax.optimization_barrier((near, acc))
    far = lax.ppermute(near, "ctx", AROUND)
    near_other = lax.ppermute(near, "ctx", CORE_SWAP)
    acc = fold("near", SOURCES[2:3], [near], acc)
    near_other, acc = lax.optimization_barrier((near_other, acc))
    acc = fold("near_other", SOURCES[3:4], [near_other], acc)
    behind, acc = lax.optimization_barrier((behind, acc))
    behind_other = lax.ppermute(behind, "ctx", CORE_SWAP)
    acc = fold("behind", SOURCES[4:5], [behind], acc)
    behind_other, acc = lax.optimization_barrier((behind_other, acc))
    acc = fold("behind_other", SOURCES[5:6], [behind_other], acc)
    far, acc = lax.optimization_barrier((far, acc))
    far_other = lax.ppermute(far, "ctx", CORE_SWAP)
    acc = fold("far", SOURCES[6:7], [far], acc)
    far_other, acc = lax.optimization_barrier((far_other, acc))
    _, mixed, normal, inverse, rows, partial = call(
        last_kernel,
        "last",
        smem,
        [far_other, w_qkv, qbd, acc, own, w_out, b_out, ln_gain, ln_bias],
        state
        + [((D, ROWS), bf16), ((ROWS, D), f32), ((ROWS, 1), f32), ((ROWS, PACK + D), bf16), ((DOCS, D), f32)],
        work + [((8, 2 * ROWS), f32), ((len(SOURCES), ROWS, D), bf16)],
        1 << 34,
        {5: 0},
        [own, other, near, near_other, behind, behind_other, far, far_other],
    )
    other_rows = lax.ppermute(rows, "ctx", CORE_SWAP)
    pooled = sum_over_chips(swap_add(partial))
    every = copies(pooled, "dp", DP)
    own_rows = lax.dynamic_slice_in_dim(every, places[1], 1, 0)
    own_rows, other_rows = lax.optimization_barrier((own_rows, other_rows))
    term, encoded = call(
        back_kernel,
        "back",
        smem + [pair_of],
        [every, own_rows, mixed, normal, inverse, other_rows, ln_gain, ln_bias],
        [((D, HALF), bf16), ((ROWS, D), bf16)],
        [((NDOC, NDOC), f32), ((DOCS, D), f32), ((ROWS, D), bf16)],
        1 << 20,
        hbm_outs=1,
        sems=[pltpu.SemaphoreType.DMA],
    )
    share = D // DP
    pieces = lax.all_to_all(term.reshape(DP, share, HALF), "dp", 0, 0, tiled=True)
    piece = jnp.sum(pieces.astype(f32), axis=0).astype(bf16)
    halves = copies(piece, "ctx", CTX)
    (grad_out,) = call(join_kernel, "join", [], [halves], [((share, D), f32)], [], 1 << 20)
    return (encoded[None], grad_out)


def solution(mesh):
    return jax.shard_map(
        per_device,
        mesh=mesh,
        in_specs=(P("dp", "ctx", None), P(), P(), P(), P(), P(), P("dp", None), P("dp", None)),
        out_specs=(P("dp", "ctx", None), P("dp", None)),
        check_vma=False,
    )
```

```python
import functools

import jax
import jax.numpy as jnp
from jax import lax
from jax.experimental import pallas as pl
from jax.experimental.pallas import tpu as pltpu
from jax.sharding import PartitionSpec as P

D = 768
HEADS = 12
HEAD_DIM = 64
PAIRS = HEADS // 2
DOCS = 4
NDOC = 128
ROWS = 256
CTX = 8
DP = 32
HALF = D // 2
PACK = D + 128
AUG = 80

SOFTMAX_TEMPER = 0.05
NORM_EPSILON = 1e-05
EMBED_EPSILON = 1e-06
PENALTY = -1e30

VMEM_LIMIT = 24 * 1024 * 1024

CORE_SWAP = [(c, c ^ 1) for c in range(CTX)]
AROUND = [(c, (c + 2) % CTX if c % 2 == 0 else (c - 2) % CTX) for c in range(CTX)]
BACK = [(b, a) for a, b in AROUND]


def came_from(place, hops):
    step = 2 * hops
    return lax.rem(jnp.where(lax.rem(place, 2) == 0, place - step, place + step) + 2 * CTX, CTX)


SOURCES = [(0, 0), (1, 0), (0, 1), (1, 1), (0, -1), (1, -1), (0, 2), (1, 2)]


def doc_ends(lengths_ref):
    e0 = lengths_ref[0, 0]
    e1 = e0 + lengths_ref[0, 1]
    e2 = e1 + lengths_ref[0, 2]
    e3 = e2 + lengths_ref[0, 3]
    return e0, e1, e2, e3


def doc_of(ends, positions):
    e0, e1, e2, e3 = ends
    one = jnp.int32(1)
    zero = jnp.int32(0)
    return sum(jnp.where(positions >= e, one, zero) for e in (e0, e1, e2, e3))


def needed_span(ends, first):
    e0, e1, e2, e3 = ends
    last = first + ROWS - 1
    low = jnp.where(first >= e2, e2, jnp.where(first >= e1, e1, jnp.where(first >= e0, e0, 0)))
    high = jnp.where(last < e0, e0, jnp.where(last < e1, e1, jnp.where(last < e2, e2, e3)))
    return low, high


def fill_queries(ends, first, own, wqkv_ref, qbd):
    queries = lax.dot_general(
        wqkv_ref[:, :D], own, (((0,), (1,)), ((), ())), preferred_element_type=jnp.float32
    )
    queries = (queries.astype(jnp.bfloat16).astype(jnp.float32) * HEAD_DIM**-0.5).astype(jnp.bfloat16)
    positions = first + lax.broadcasted_iota(jnp.int32, (HEAD_DIM * 2, ROWS), 1)
    slots = lax.broadcasted_iota(jnp.int32, (HEAD_DIM * 2, ROWS), 0)
    same = (doc_of(ends, positions) == slots) | (slots >= DOCS)
    penalty = jnp.where(same, 0.0, PENALTY).astype(jnp.bfloat16)
    penalties = jnp.concatenate([penalty, penalty], axis=1)
    zero = jnp.zeros((HEAD_DIM, ROWS), jnp.bfloat16)
    for j in range(PAIRS):
        qbd[j, :64, :ROWS] = queries[128 * j : 128 * j + 64, :]
        qbd[j, :64, ROWS:] = zero
        qbd[j, 64:128, :ROWS] = zero
        qbd[j, 64:128, ROWS:] = queries[128 * j + 64 : 128 * j + 128, :]
        qbd[j, 128:, :] = penalties


def project(ends, bases, blocks, wqkv_ref, vt):
    rows = ROWS * len(blocks)
    hidden = jnp.concatenate(blocks, axis=0) if len(blocks) > 1 else blocks[0]
    keys = jnp.dot(hidden, wqkv_ref[:, D : 2 * D], preferred_element_type=jnp.float32).astype(jnp.bfloat16)
    values = lax.dot_general(
        wqkv_ref[:, 2 * D :], hidden, (((0,), (1,)), ((), ())), preferred_element_type=jnp.float32
    ).astype(jnp.bfloat16)
    vt[:, :HEAD_DIM, :rows] = values.reshape(HEADS, HEAD_DIM, rows)
    offsets = lax.broadcasted_iota(jnp.int32, (ROWS, 128), 0)
    lanes = lax.broadcasted_iota(jnp.int32, (ROWS, 128), 1)
    onehots = [
        jnp.where(doc_of(ends, base + offsets) == lanes, 1.0, 0.0).astype(jnp.bfloat16) for base in bases
    ]
    return keys, jnp.concatenate(onehots, axis=0) if len(blocks) > 1 else onehots[0]


def pair_scores(keys, onehot, qbd, j):
    pair_keys = jnp.concatenate([keys[:, 128 * j : 128 * j + 128], onehot], axis=1)
    return jnp.dot(pair_keys, qbd[j], preferred_element_type=jnp.float32)


def attend_plain(ends, bases, blocks, wqkv_ref, qbd, vt, acc_ref):
    rows = ROWS * len(blocks)
    keys, onehot = project(ends, bases, blocks, wqkv_ref, vt)
    for j in range(PAIRS):
        weights = jnp.exp(pair_scores(keys, onehot, qbd, j)).astype(jnp.bfloat16)
        for h in range(2):
            part = slice(ROWS * h, ROWS * h + ROWS)
            acc_ref[2 * j + h] += jnp.dot(
                vt[2 * j + h, :, :rows], weights[:, part], preferred_element_type=jnp.float32
            )


def attend_shifted(ends, base, block, wqkv_ref, qbd, vt, m_ref, acc_ref):
    keys, onehot = project(ends, [base], [block], wqkv_ref, vt)
    for j in range(PAIRS):
        scores = pair_scores(keys, onehot, qbd, j)
        old = m_ref[j : j + 1, :]
        new = jnp.maximum(old, jnp.max(scores, axis=0, keepdims=True))
        m_ref[j : j + 1, :] = new
        shrink = jnp.exp(old - new)
        weights = jnp.exp(scores - new).astype(jnp.bfloat16)
        for h in range(2):
            part = slice(ROWS * h, ROWS * h + ROWS)
            mixed = jnp.dot(vt[2 * j + h, :, :ROWS], weights[:, part], preferred_element_type=jnp.float32)
            acc_ref[2 * j + h] = acc_ref[2 * j + h] * shrink[:, part] + mixed


def fill_ones(vt):
    row = lax.broadcasted_iota(jnp.int32, (HEADS, AUG - HEAD_DIM, vt.shape[2]), 1)
    vt[:, HEAD_DIM:, :] = jnp.where(row == 0, 1.0, 0.0).astype(jnp.bfloat16)


def attend_blocks(ends, first, places, blocks, wqkv_ref, qbd, vt, acc_ref):
    low, high = needed_span(ends, first)
    bases = [place * ROWS for place in places]
    wanted = [(base < high) & (base + ROWS > low) for base in bases]

    def attend(which):
        attend_plain(
            ends, [bases[i] for i in which], [blocks[i][...] for i in which], wqkv_ref, qbd, vt, acc_ref
        )

    if len(blocks) == 1:
        pl.when(wanted[0])(lambda: attend([0]))
    else:
        one, two = wanted
        pl.when(one & two)(lambda: attend([0, 1]))
        pl.when(one & jnp.logical_not(two))(lambda: attend([0]))
        pl.when(two & jnp.logical_not(one))(lambda: attend([1]))


def queries_kernel(lengths_ref, place_ref, own_ref, wqkv_ref, qbd, acc_ref):
    ends = doc_ends(lengths_ref)
    fill_queries(ends, place_ref[0] * ROWS, own_ref[...], wqkv_ref, qbd)
    acc_ref[...] = jnp.zeros(acc_ref.shape, jnp.float32)


def fold_kernel(sources, lengths_ref, place_ref, wqkv_ref, qbd, acc_in, *refs):
    blocks, (acc_ref, vt) = refs[: len(sources)], refs[len(sources) :]
    place = place_ref[0]
    ends = doc_ends(lengths_ref)
    fill_ones(vt)
    places = [came_from(place ^ flip, hops) for flip, hops in sources]
    attend_blocks(ends, place * ROWS, places, blocks, wqkv_ref, qbd, vt, acc_ref)


def in_range(acc):
    sums = acc[:, HEAD_DIM, :]
    good = jnp.where((sums >= 1e-12) & (sums <= 1e12), 1.0, 0.0)
    finite = jnp.where(jnp.abs(acc) <= 1e38, 1.0, 0.0)
    return jnp.minimum(jnp.min(good), jnp.min(finite)) > 0.5


def attend_again(ends, place, blocks, wqkv_ref, qbd, vt, acc_ref, m_ref, held):
    for i, (flip, hops) in enumerate(SOURCES):
        pltpu.sync_copy(blocks[i], held.at[i])
    m_ref[...] = jnp.full(m_ref.shape, PENALTY, jnp.float32)
    acc_ref[...] = jnp.zeros(acc_ref.shape, jnp.float32)
    low, high = needed_span(ends, place * ROWS)

    def step(i, carry):
        base = jnp.int32(0)
        for k, (flip, hops) in enumerate(SOURCES):
            base = jnp.where(i == k, came_from(place ^ flip, hops) * ROWS, base)

        @pl.when((base < high) & (base + ROWS > low))
        def _():
            attend_shifted(ends, base, held[i], wqkv_ref, qbd, vt, m_ref, acc_ref)

        return carry

    lax.fori_loop(0, len(SOURCES), step, 0)


def last_kernel(
    lengths_ref, place_ref, far_other_ref, wqkv_ref, qbd, acc_in, own_ref, wout_ref, bias_ref, gain_ref, shift_ref,
    *refs
):
    blocks, refs = refs[: len(SOURCES)], refs[len(SOURCES) :]
    acc_ref, mixed_ref, normal_ref, inverse_ref, rows_ref, pooled_ref, vt, m_ref, held = refs
    place = place_ref[0]
    ends = doc_ends(lengths_ref)
    first = place * ROWS
    fill_ones(vt)
    flip, hops = SOURCES[-1]
    attend_blocks(ends, first, [came_from(place ^ flip, hops)], [far_other_ref], wqkv_ref, qbd, vt, acc_ref)

    @pl.when(jnp.logical_not(in_range(acc_ref[...])))
    def _():
        attend_again(ends, place, blocks, wqkv_ref, qbd, vt, acc_ref, m_ref, held)

    acc = acc_ref[...]
    mixed = acc[:, :HEAD_DIM, :] * (1.0 / acc[:, HEAD_DIM : HEAD_DIM + 1, :])
    mixed = mixed.reshape(D, ROWS).astype(jnp.bfloat16)
    mixed_ref[...] = mixed
    summed = lax.dot_general(
        mixed, wout_ref[...], (((0,), (0,)), ((), ())), preferred_element_type=jnp.float32
    )
    summed = summed + bias_ref[...][None] + own_ref[...].astype(jnp.float32)
    centered = summed - jnp.mean(summed, axis=1, keepdims=True)
    inverse = lax.rsqrt(jnp.mean(centered * centered, axis=1, keepdims=True) + NORM_EPSILON)
    normal = centered * inverse
    normal_ref[...] = normal
    inverse_ref[...] = inverse
    layer = normal * gain_ref[...][None] + shift_ref[...][None]
    for i in range(D // ROWS):
        rows_ref[:, PACK + ROWS * i : PACK + ROWS * (i + 1)] = mixed[ROWS * i : ROWS * (i + 1)]
    rows_ref[:, :D] = normal.astype(jnp.bfloat16)
    high = inverse.astype(jnp.bfloat16).astype(jnp.float32)
    lane = lax.broadcasted_iota(jnp.int32, (ROWS, 128), 1)
    rows_ref[:, D:PACK] = jnp.where(lane == 0, high, inverse - high).astype(jnp.bfloat16)
    row_doc = doc_of(ends, first + lax.broadcasted_iota(jnp.int32, (ROWS, 1), 0))
    pooled_ref[...] = jnp.zeros(pooled_ref.shape, jnp.float32)
    starts = (jnp.int32(0), *ends[:-1])
    for d in range(DOCS):

        @pl.when((starts[d] < first + ROWS) & (ends[d] > first))
        def _():
            total = jnp.sum(jnp.where(row_doc == d, layer, 0.0), axis=0, keepdims=True)
            mean = total * (1.0 / lengths_ref[0, d].astype(jnp.float32))
            pooled_ref[d : d + 1, :] = mean


def back_kernel(
    lengths_ref, place_ref, pair_ref, pooled_ref, mixed_ref, normal_ref, inverse_ref, other_rows_ref,
    gain_ref, shift_ref, out_ref, encoded_hbm, expo_ref, scaled_ref, encoded_ref, sem
):
    place = place_ref[0]
    data_place = place_ref[1]
    ends = doc_ends(lengths_ref)
    f32, bf16 = jnp.float32, jnp.bfloat16
    encoded_ref[...] = (normal_ref[...] * gain_ref[...][None] + shift_ref[...][None]).astype(bf16)
    write = pltpu.make_async_copy(encoded_ref, encoded_hbm, sem)
    write.start()

    pooled = pooled_ref[...].reshape(NDOC, D)
    emb = pooled * lax.rsqrt(jnp.sum(pooled * pooled, axis=1, keepdims=True) + EMBED_EPSILON)
    high = emb.astype(bf16)
    low = (emb - high.astype(f32)).astype(bf16)

    def times(left, right):
        return lax.dot_general(left, right, (((1,), (1,)), ((), ())), preferred_element_type=f32)

    sims = (times(high, high) + (times(high, low) + times(low, high))) * (1.0 / SOFTMAX_TEMPER)
    columns = lax.broadcasted_iota(jnp.int32, (NDOC, NDOC), 1)
    rows = lax.broadcasted_iota(jnp.int32, (NDOC, NDOC), 0)
    expo = jnp.where(rows == columns, 0.0, jnp.exp(sims))
    expo_ref[...] = expo
    totals = 1.0 / jnp.sum(expo, axis=0, keepdims=True)
    half = lax.rem(data_place, 2)
    rows8 = expo_ref[pl.ds(pl.multiple_of((data_place - half) * DOCS, 8), 8), :]
    own_expo = jnp.where(half == 0, rows8[:DOCS], rows8[DOCS:])
    own = pooled_ref[data_place]
    own_inverse = lax.rsqrt(jnp.sum(own * own, axis=1, keepdims=True) + EMBED_EPSILON)
    own_emb = own * own_inverse
    own_totals = 1.0 / jnp.sum(own_expo, axis=1, keepdims=True)
    slots = lax.broadcasted_iota(jnp.int32, (DOCS, NDOC), 0)
    lanes = lax.broadcasted_iota(jnp.int32, (DOCS, NDOC), 1)
    partner = jnp.where(
        slots == 0, pair_ref[0, 0],
        jnp.where(slots == 1, pair_ref[0, 1], jnp.where(slots == 2, pair_ref[0, 2], pair_ref[0, 3])),
    )
    both = own_expo * (own_totals + totals) - jnp.where(lanes == partner, 2.0, 0.0)
    weights = jnp.concatenate([both, both], axis=0).T
    emb_grad = jnp.concatenate(
        [jnp.sum(weights[:, d : d + 1] * emb, axis=0, keepdims=True) for d in range(DOCS)], axis=0
    ) * (1.0 / SOFTMAX_TEMPER)
    pooled_grad = (emb_grad - own_emb * jnp.sum(own_emb * emb_grad, axis=1, keepdims=True)) * own_inverse
    slot = lax.broadcasted_iota(jnp.int32, (DOCS, 1), 0)
    length = jnp.where(
        slot == 0, lengths_ref[0, 0],
        jnp.where(slot == 1, lengths_ref[0, 1], jnp.where(slot == 2, lengths_ref[0, 2], lengths_ref[0, 3])),
    ).astype(f32)
    scaled = pooled_grad * (1.0 / length) * gain_ref[...][None]
    centered = scaled - jnp.mean(scaled, axis=1, keepdims=True)
    scaled_ref[...] = centered
    share = pl.ds(pl.multiple_of(lax.rem(place, 2) * HALF, 128), HALF)

    def grad(first, normal, normal_share, inverse):
        row_doc = doc_of(ends, first + lax.broadcasted_iota(jnp.int32, (ROWS, 1), 0))

        def spread(values):
            pick = jnp.where(row_doc == 2, values[2:3], values[3:4])
            return jnp.where(row_doc == 0, values[0:1], jnp.where(row_doc == 1, values[1:2], pick))

        along = jnp.mean(spread(scaled) * normal, axis=1, keepdims=True)
        return (inverse * (spread(scaled_ref[:, share]) - normal_share * along)).astype(bf16)

    mine = grad(place * ROWS, normal_ref[...], normal_ref[:, share], inverse_ref[...])
    inverse = other_rows_ref[:, D:PACK].astype(f32)
    theirs = grad(
        (place ^ 1) * ROWS,
        other_rows_ref[:, :D].astype(f32),
        other_rows_ref[:, share].astype(f32),
        inverse[:, 0:1] + inverse[:, 1:2],
    )
    for i in range(D // ROWS):
        part = slice(ROWS * i, ROWS * (i + 1))
        other_mixed = other_rows_ref[:, PACK + ROWS * i : PACK + ROWS * (i + 1)]
        product = jnp.dot(mixed_ref[part, :], mine, preferred_element_type=f32)
        product += jnp.dot(other_mixed, theirs, preferred_element_type=f32)
        out_ref[part, :] = product.astype(bf16)
    write.wait()


def join_kernel(halves_ref, out_ref):
    for core in range(2):
        parts = [halves_ref[c].astype(jnp.float32) for c in range(core, CTX, 2)]
        out_ref[:, HALF * core : HALF * (core + 1)] = (parts[0] + parts[1]) + (parts[2] + parts[3])


SMEM = pl.BlockSpec(memory_space=pltpu.SMEM)
VMEM = pl.BlockSpec(memory_space=pltpu.VMEM)
ANY = pl.BlockSpec(memory_space=pl.ANY)


def call(kernel, name, smem, vmem, outs, scratch, flops, aliases={}, whole=(), hbm_outs=0, sems=()):
    return pl.pallas_call(
        kernel,
        name=name,
        out_shape=[jax.ShapeDtypeStruct(s, t) for s, t in outs],
        in_specs=[SMEM] * len(smem) + [VMEM] * len(vmem) + [ANY] * len(whole),
        out_specs=[VMEM] * (len(outs) - hbm_outs) + [ANY] * hbm_outs,
        scratch_shapes=[pltpu.VMEM(s, t) for s, t in scratch] + list(sems),
        input_output_aliases=aliases,
        cost_estimate=pl.CostEstimate(flops=flops, bytes_accessed=1 << 26, transcendentals=0),
        compiler_params=pltpu.CompilerParams(vmem_limit_bytes=VMEM_LIMIT),
    )(*smem, *vmem, *whole)


def copies(value, axis, count):
    return lax.all_to_all(jnp.broadcast_to(value[None], (count,) + value.shape), axis, 0, 0, tiled=True)


def swap_add(value):
    return value + lax.ppermute(value, "ctx", CORE_SWAP)


def sum_over_chips(value):
    one, two, three = [
        lax.ppermute(value, "ctx", [(c, (c + 2 * hops) % CTX) for c in range(CTX)]).astype(jnp.float32)
        for hops in (1, 2, 3)
    ]
    return (value.astype(jnp.float32) + two) + (one + three)


def per_device(hidden_in, w_qkv, w_out, b_out, ln_gain, ln_bias, doc_lengths, pair_of):
    f32, bf16 = jnp.float32, jnp.bfloat16
    own = hidden_in[0]
    places = jnp.stack([lax.axis_index("ctx"), lax.axis_index("dp")]).astype(jnp.int32)
    smem = [doc_lengths, places]
    state = [((HEADS, AUG, ROWS), f32)]
    work = [((HEADS, AUG, 2 * ROWS), bf16)]
    held = ((PAIRS, 256, 2 * ROWS), bf16)

    def fold(name, sources, blocks, acc):
        (acc,) = call(
            functools.partial(fold_kernel, sources), name, smem, [w_qkv, qbd, acc, *blocks], state, work,
            1 << 34, {4: 0},
        )
        return acc

    near = lax.ppermute(own, "ctx", AROUND)
    qbd, acc = call(queries_kernel, "queries", smem, [own, w_qkv], [held] + state, [], 1 << 34)
    own_later, acc = lax.optimization_barrier((own, acc))
    behind = lax.ppermute(own_later, "ctx", BACK)
    other = lax.ppermute(own_later, "ctx", CORE_SWAP)
    acc = fold("own", SOURCES[0:1], [own], acc)
    acc = fold("other", SOURCES[1:2], [other], acc)
    near, acc = lax.optimization_barrier((near, acc))
    far = lax.ppermute(near, "ctx", AROUND)
    near_other = lax.ppermute(near, "ctx", CORE_SWAP)
    acc = fold("near", SOURCES[2:3], [near], acc)
    near_other, acc = lax.optimization_barrier((near_other, acc))
    acc = fold("near_other", SOURCES[3:4], [near_other], acc)
    behind, acc = lax.optimization_barrier((behind, acc))
    behind_other = lax.ppermute(behind, "ctx", CORE_SWAP)
    acc = fold("behind", SOURCES[4:5], [behind], acc)
    behind_other, acc = lax.optimization_barrier((behind_other, acc))
    acc = fold("behind_other", SOURCES[5:6], [behind_other], acc)
    far, acc = lax.optimization_barrier((far, acc))
    far_other = lax.ppermute(far, "ctx", CORE_SWAP)
    acc = fold("far", SOURCES[6:7], [far], acc)
    far_other, acc = lax.optimization_barrier((far_other, acc))
    _, mixed, normal, inverse, rows, partial = call(
        last_kernel,
        "last",
        smem,
        [far_other, w_qkv, qbd, acc, own, w_out, b_out, ln_gain, ln_bias],
        state
        + [((D, ROWS), bf16), ((ROWS, D), f32), ((ROWS, 1), f32), ((ROWS, PACK + D), bf16), ((DOCS, D), f32)],
        work + [((8, 2 * ROWS), f32), ((len(SOURCES), ROWS, D), bf16)],
        1 << 34,
        {5: 0},
        [own, other, near, near_other, behind, behind_other, far, far_other],
    )
    other_rows = lax.ppermute(rows, "ctx", CORE_SWAP)
    pooled = sum_over_chips(swap_add(partial))
    pooled, other_rows = lax.optimization_barrier((pooled, other_rows))
    every = copies(pooled, "dp", DP)
    term, encoded = call(
        back_kernel,
        "back",
        smem + [pair_of],
        [every, mixed, normal, inverse, other_rows, ln_gain, ln_bias],
        [((D, HALF), bf16), ((ROWS, D), bf16)],
        [((NDOC, NDOC), f32), ((DOCS, D), f32), ((ROWS, D), bf16)],
        1 << 20,
        hbm_outs=1,
        sems=[pltpu.SemaphoreType.DMA],
    )
    share = D // DP
    pieces = lax.all_to_all(term.reshape(DP, share, HALF), "dp", 0, 0, tiled=True)
    piece = jnp.sum(pieces.astype(f32), axis=0).astype(bf16)
    halves = copies(piece, "ctx", CTX)
    (grad_out,) = call(join_kernel, "join", [], [halves], [((share, D), f32)], [], 1 << 20)
    return (encoded[None], grad_out)


def solution(mesh):
    return jax.shard_map(
        per_device,
        mesh=mesh,
        in_specs=(P("dp", "ctx", None), P(), P(), P(), P(), P(), P("dp", None), P("dp", None)),
        out_specs=(P("dp", "ctx", None), P("dp", None)),
        check_vma=False,
    )
```

```python
import functools

import jax
import jax.numpy as jnp
from jax import lax
from jax.experimental import pallas as pl
from jax.experimental.pallas import tpu as pltpu
from jax.sharding import PartitionSpec as P

D = 768
HEADS = 12
HEAD_DIM = 64
PAIRS = HEADS // 2
DOCS = 4
NDOC = 128
ROWS = 256
CTX = 8
DP = 32
HALF = D // 2
PACK = D + 128
AUG = 80

SOFTMAX_TEMPER = 0.05
NORM_EPSILON = 1e-05
EMBED_EPSILON = 1e-06
PENALTY = -1e30

VMEM_LIMIT = 24 * 1024 * 1024

CORE_SWAP = [(c, c ^ 1) for c in range(CTX)]
AROUND = [(c, (c + 2) % CTX if c % 2 == 0 else (c - 2) % CTX) for c in range(CTX)]
BACK = [(b, a) for a, b in AROUND]


def came_from(place, hops):
    step = 2 * hops
    return lax.rem(jnp.where(lax.rem(place, 2) == 0, place - step, place + step) + 2 * CTX, CTX)


SOURCES = [(0, 0), (1, 0), (0, 1), (1, 1), (0, -1), (1, -1), (0, 2), (1, 2)]


def doc_ends(lengths_ref):
    e0 = lengths_ref[0, 0]
    e1 = e0 + lengths_ref[0, 1]
    e2 = e1 + lengths_ref[0, 2]
    e3 = e2 + lengths_ref[0, 3]
    return e0, e1, e2, e3


def doc_of(ends, positions):
    e0, e1, e2, e3 = ends
    one = jnp.int32(1)
    zero = jnp.int32(0)
    return sum(jnp.where(positions >= e, one, zero) for e in (e0, e1, e2, e3))


def needed_span(ends, first):
    e0, e1, e2, e3 = ends
    last = first + ROWS - 1
    low = jnp.where(first >= e2, e2, jnp.where(first >= e1, e1, jnp.where(first >= e0, e0, 0)))
    high = jnp.where(last < e0, e0, jnp.where(last < e1, e1, jnp.where(last < e2, e2, e3)))
    return low, high


def fill_queries(ends, first, own, wqkv_ref, qbd):
    queries = lax.dot_general(
        wqkv_ref[:, :D], own, (((0,), (1,)), ((), ())), preferred_element_type=jnp.float32
    )
    queries = (queries.astype(jnp.bfloat16).astype(jnp.float32) * HEAD_DIM**-0.5).astype(jnp.bfloat16)
    positions = first + lax.broadcasted_iota(jnp.int32, (HEAD_DIM * 2, ROWS), 1)
    slots = lax.broadcasted_iota(jnp.int32, (HEAD_DIM * 2, ROWS), 0)
    same = (doc_of(ends, positions) == slots) | (slots >= DOCS)
    penalty = jnp.where(same, 0.0, PENALTY).astype(jnp.bfloat16)
    penalties = jnp.concatenate([penalty, penalty], axis=1)
    zero = jnp.zeros((HEAD_DIM, ROWS), jnp.bfloat16)
    for j in range(PAIRS):
        qbd[j, :64, :ROWS] = queries[128 * j : 128 * j + 64, :]
        qbd[j, :64, ROWS:] = zero
        qbd[j, 64:128, :ROWS] = zero
        qbd[j, 64:128, ROWS:] = queries[128 * j + 64 : 128 * j + 128, :]
        qbd[j, 128:, :] = penalties


def project(ends, bases, blocks, wqkv_ref, vt):
    rows = ROWS * len(blocks)
    hidden = jnp.concatenate(blocks, axis=0) if len(blocks) > 1 else blocks[0]
    keys = jnp.dot(hidden, wqkv_ref[:, D : 2 * D], preferred_element_type=jnp.float32).astype(jnp.bfloat16)
    values = lax.dot_general(
        wqkv_ref[:, 2 * D :], hidden, (((0,), (1,)), ((), ())), preferred_element_type=jnp.float32
    ).astype(jnp.bfloat16)
    vt[:, :HEAD_DIM, :rows] = values.reshape(HEADS, HEAD_DIM, rows)
    offsets = lax.broadcasted_iota(jnp.int32, (ROWS, 128), 0)
    lanes = lax.broadcasted_iota(jnp.int32, (ROWS, 128), 1)
    onehots = [
        jnp.where(doc_of(ends, base + offsets) == lanes, 1.0, 0.0).astype(jnp.bfloat16) for base in bases
    ]
    return keys, jnp.concatenate(onehots, axis=0) if len(blocks) > 1 else onehots[0]


def pair_scores(keys, onehot, qbd, j):
    pair_keys = jnp.concatenate([keys[:, 128 * j : 128 * j + 128], onehot], axis=1)
    return jnp.dot(pair_keys, qbd[j], preferred_element_type=jnp.float32)


def attend_plain(ends, bases, blocks, wqkv_ref, qbd, vt, acc_ref):
    rows = ROWS * len(blocks)
    keys, onehot = project(ends, bases, blocks, wqkv_ref, vt)
    for j in range(PAIRS):
        weights = jnp.exp(pair_scores(keys, onehot, qbd, j)).astype(jnp.bfloat16)
        for h in range(2):
            part = slice(ROWS * h, ROWS * h + ROWS)
            acc_ref[2 * j + h] += jnp.dot(
                vt[2 * j + h, :, :rows], weights[:, part], preferred_element_type=jnp.float32
            )


def attend_shifted(ends, base, block, wqkv_ref, qbd, vt, m_ref, acc_ref):
    keys, onehot = project(ends, [base], [block], wqkv_ref, vt)
    for j in range(PAIRS):
        scores = pair_scores(keys, onehot, qbd, j)
        old = m_ref[j : j + 1, :]
        new = jnp.maximum(old, jnp.max(scores, axis=0, keepdims=True))
        m_ref[j : j + 1, :] = new
        shrink = jnp.exp(old - new)
        weights = jnp.exp(scores - new).astype(jnp.bfloat16)
        for h in range(2):
            part = slice(ROWS * h, ROWS * h + ROWS)
            mixed = jnp.dot(vt[2 * j + h, :, :ROWS], weights[:, part], preferred_element_type=jnp.float32)
            acc_ref[2 * j + h] = acc_ref[2 * j + h] * shrink[:, part] + mixed


def fill_ones(vt):
    row = lax.broadcasted_iota(jnp.int32, (HEADS, AUG - HEAD_DIM, vt.shape[2]), 1)
    vt[:, HEAD_DIM:, :] = jnp.where(row == 0, 1.0, 0.0).astype(jnp.bfloat16)


def attend_blocks(ends, first, places, blocks, wqkv_ref, qbd, vt, acc_ref):
    low, high = needed_span(ends, first)
    bases = [place * ROWS for place in places]
    wanted = [(base < high) & (base + ROWS > low) for base in bases]

    def attend(which):
        attend_plain(
            ends, [bases[i] for i in which], [blocks[i][...] for i in which], wqkv_ref, qbd, vt, acc_ref
        )

    if len(blocks) == 1:
        pl.when(wanted[0])(lambda: attend([0]))
    else:
        one, two = wanted
        pl.when(one & two)(lambda: attend([0, 1]))
        pl.when(one & jnp.logical_not(two))(lambda: attend([0]))
        pl.when(two & jnp.logical_not(one))(lambda: attend([1]))


def queries_kernel(lengths_ref, place_ref, own_ref, wqkv_ref, qbd, acc_ref):
    ends = doc_ends(lengths_ref)
    fill_queries(ends, place_ref[0] * ROWS, own_ref[...], wqkv_ref, qbd)
    acc_ref[...] = jnp.zeros(acc_ref.shape, jnp.float32)


def fold_kernel(sources, lengths_ref, place_ref, wqkv_ref, qbd, acc_in, *refs):
    blocks, (acc_ref, vt) = refs[: len(sources)], refs[len(sources) :]
    place = place_ref[0]
    ends = doc_ends(lengths_ref)
    fill_ones(vt)
    places = [came_from(place ^ flip, hops) for flip, hops in sources]
    attend_blocks(ends, place * ROWS, places, blocks, wqkv_ref, qbd, vt, acc_ref)


def in_range(acc):
    sums = acc[:, HEAD_DIM, :]
    good = jnp.where((sums >= 1e-12) & (sums <= 1e12), 1.0, 0.0)
    finite = jnp.where(jnp.abs(acc) <= 1e38, 1.0, 0.0)
    return jnp.minimum(jnp.min(good), jnp.min(finite)) > 0.5


def attend_again(ends, place, blocks, wqkv_ref, qbd, vt, acc_ref, m_ref, held):
    for i, (flip, hops) in enumerate(SOURCES):
        pltpu.sync_copy(blocks[i], held.at[i])
    m_ref[...] = jnp.full(m_ref.shape, PENALTY, jnp.float32)
    acc_ref[...] = jnp.zeros(acc_ref.shape, jnp.float32)
    low, high = needed_span(ends, place * ROWS)

    def step(i, carry):
        base = jnp.int32(0)
        for k, (flip, hops) in enumerate(SOURCES):
            base = jnp.where(i == k, came_from(place ^ flip, hops) * ROWS, base)

        @pl.when((base < high) & (base + ROWS > low))
        def _():
            attend_shifted(ends, base, held[i], wqkv_ref, qbd, vt, m_ref, acc_ref)

        return carry

    lax.fori_loop(0, len(SOURCES), step, 0)


def last_kernel(
    lengths_ref, place_ref, far_other_ref, wqkv_ref, qbd, acc_in, own_ref, wout_ref, bias_ref, gain_ref, shift_ref,
    *refs
):
    blocks, refs = refs[: len(SOURCES)], refs[len(SOURCES) :]
    acc_ref, mixed_ref, normal_ref, inverse_ref, rows_ref, pooled_ref, vt, m_ref, held = refs
    place = place_ref[0]
    ends = doc_ends(lengths_ref)
    first = place * ROWS
    fill_ones(vt)
    flip, hops = SOURCES[-1]
    attend_blocks(ends, first, [came_from(place ^ flip, hops)], [far_other_ref], wqkv_ref, qbd, vt, acc_ref)

    @pl.when(jnp.logical_not(in_range(acc_ref[...])))
    def _():
        attend_again(ends, place, blocks, wqkv_ref, qbd, vt, acc_ref, m_ref, held)

    acc = acc_ref[...]
    mixed = acc[:, :HEAD_DIM, :] * (1.0 / acc[:, HEAD_DIM : HEAD_DIM + 1, :])
    mixed = mixed.reshape(D, ROWS).astype(jnp.bfloat16)
    mixed_ref[...] = mixed
    summed = lax.dot_general(
        mixed, wout_ref[...], (((0,), (0,)), ((), ())), preferred_element_type=jnp.float32
    )
    summed = summed + bias_ref[...][None] + own_ref[...].astype(jnp.float32)
    centered = summed - jnp.mean(summed, axis=1, keepdims=True)
    inverse = lax.rsqrt(jnp.mean(centered * centered, axis=1, keepdims=True) + NORM_EPSILON)
    normal = centered * inverse
    normal_ref[...] = normal
    inverse_ref[...] = inverse
    layer = normal * gain_ref[...][None] + shift_ref[...][None]
    for i in range(D // ROWS):
        rows_ref[:, PACK + ROWS * i : PACK + ROWS * (i + 1)] = mixed[ROWS * i : ROWS * (i + 1)]
    rows_ref[:, :D] = normal.astype(jnp.bfloat16)
    high = inverse.astype(jnp.bfloat16).astype(jnp.float32)
    lane = lax.broadcasted_iota(jnp.int32, (ROWS, 128), 1)
    rows_ref[:, D:PACK] = jnp.where(lane == 0, high, inverse - high).astype(jnp.bfloat16)
    row_doc = doc_of(ends, first + lax.broadcasted_iota(jnp.int32, (ROWS, 1), 0))
    pooled_ref[...] = jnp.zeros(pooled_ref.shape, jnp.float32)
    starts = (jnp.int32(0), *ends[:-1])
    for d in range(DOCS):

        @pl.when((starts[d] < first + ROWS) & (ends[d] > first))
        def _():
            total = jnp.sum(jnp.where(row_doc == d, layer, 0.0), axis=0, keepdims=True)
            mean = total * (1.0 / lengths_ref[0, d].astype(jnp.float32))
            pooled_ref[d : d + 1, :] = mean


def back_kernel(
    lengths_ref, place_ref, pair_ref, pooled_ref, mixed_ref, normal_ref, inverse_ref, other_rows_ref,
    gain_ref, shift_ref, out_ref, encoded_hbm, expo_ref, scaled_ref, encoded_ref, sem
):
    place = place_ref[0]
    data_place = place_ref[1]
    ends = doc_ends(lengths_ref)
    f32, bf16 = jnp.float32, jnp.bfloat16
    encoded_ref[...] = (normal_ref[...] * gain_ref[...][None] + shift_ref[...][None]).astype(bf16)
    write = pltpu.make_async_copy(encoded_ref, encoded_hbm, sem)
    write.start()

    pooled = pooled_ref[...].reshape(NDOC, D)
    emb = pooled * lax.rsqrt(jnp.sum(pooled * pooled, axis=1, keepdims=True) + EMBED_EPSILON)
    high = emb.astype(bf16)
    low = (emb - high.astype(f32)).astype(bf16)

    def times(left, right):
        return lax.dot_general(left, right, (((1,), (1,)), ((), ())), preferred_element_type=f32)

    sims = (times(high, high) + (times(high, low) + times(low, high))) * (1.0 / SOFTMAX_TEMPER)
    columns = lax.broadcasted_iota(jnp.int32, (NDOC, NDOC), 1)
    rows = lax.broadcasted_iota(jnp.int32, (NDOC, NDOC), 0)
    expo = jnp.where(rows == columns, 0.0, jnp.exp(sims))
    expo_ref[...] = expo
    totals = 1.0 / jnp.sum(expo, axis=0, keepdims=True)
    half = lax.rem(data_place, 2)
    rows8 = expo_ref[pl.ds(pl.multiple_of((data_place - half) * DOCS, 8), 8), :]
    own_expo = jnp.where(half == 0, rows8[:DOCS], rows8[DOCS:])
    own = pooled_ref[data_place]
    own_inverse = lax.rsqrt(jnp.sum(own * own, axis=1, keepdims=True) + EMBED_EPSILON)
    own_emb = own * own_inverse
    own_totals = 1.0 / jnp.sum(own_expo, axis=1, keepdims=True)
    slots = lax.broadcasted_iota(jnp.int32, (DOCS, NDOC), 0)
    lanes = lax.broadcasted_iota(jnp.int32, (DOCS, NDOC), 1)
    partner = jnp.where(
        slots == 0, pair_ref[0, 0],
        jnp.where(slots == 1, pair_ref[0, 1], jnp.where(slots == 2, pair_ref[0, 2], pair_ref[0, 3])),
    )
    both = own_expo * (own_totals + totals) - jnp.where(lanes == partner, 2.0, 0.0)
    weights = jnp.concatenate([both, both], axis=0).T
    emb_grad = jnp.concatenate(
        [jnp.sum(weights[:, d : d + 1] * emb, axis=0, keepdims=True) for d in range(DOCS)], axis=0
    ) * (1.0 / SOFTMAX_TEMPER)
    pooled_grad = (emb_grad - own_emb * jnp.sum(own_emb * emb_grad, axis=1, keepdims=True)) * own_inverse
    slot = lax.broadcasted_iota(jnp.int32, (DOCS, 1), 0)
    length = jnp.where(
        slot == 0, lengths_ref[0, 0],
        jnp.where(slot == 1, lengths_ref[0, 1], jnp.where(slot == 2, lengths_ref[0, 2], lengths_ref[0, 3])),
    ).astype(f32)
    scaled = pooled_grad * (1.0 / length) * gain_ref[...][None]
    centered = scaled - jnp.mean(scaled, axis=1, keepdims=True)
    scaled_ref[...] = centered
    share = pl.ds(pl.multiple_of(lax.rem(place, 2) * HALF, 128), HALF)

    def grad(first, normal, normal_share, inverse):
        row_doc = doc_of(ends, first + lax.broadcasted_iota(jnp.int32, (ROWS, 1), 0))

        def spread(values):
            pick = jnp.where(row_doc == 2, values[2:3], values[3:4])
            return jnp.where(row_doc == 0, values[0:1], jnp.where(row_doc == 1, values[1:2], pick))

        along = jnp.mean(spread(scaled) * normal, axis=1, keepdims=True)
        return (inverse * (spread(scaled_ref[:, share]) - normal_share * along)).astype(bf16)

    mine = grad(place * ROWS, normal_ref[...], normal_ref[:, share], inverse_ref[...])
    inverse = other_rows_ref[:, D:PACK].astype(f32)
    theirs = grad(
        (place ^ 1) * ROWS,
        other_rows_ref[:, :D].astype(f32),
        other_rows_ref[:, share].astype(f32),
        inverse[:, 0:1] + inverse[:, 1:2],
    )
    for i in range(D // ROWS):
        part = slice(ROWS * i, ROWS * (i + 1))
        other_mixed = other_rows_ref[:, PACK + ROWS * i : PACK + ROWS * (i + 1)]
        product = jnp.dot(mixed_ref[part, :], mine, preferred_element_type=f32)
        product += jnp.dot(other_mixed, theirs, preferred_element_type=f32)
        out_ref[part, :] = product.astype(bf16)
    write.wait()


def join_kernel(halves_ref, out_ref):
    for core in range(2):
        parts = [halves_ref[c].astype(jnp.float32) for c in range(core, CTX, 2)]
        out_ref[:, HALF * core : HALF * (core + 1)] = (parts[0] + parts[1]) + (parts[2] + parts[3])


SMEM = pl.BlockSpec(memory_space=pltpu.SMEM)
VMEM = pl.BlockSpec(memory_space=pltpu.VMEM)
ANY = pl.BlockSpec(memory_space=pl.ANY)


def call(kernel, name, smem, vmem, outs, scratch, flops, aliases={}, whole=(), hbm_outs=0, sems=()):
    return pl.pallas_call(
        kernel,
        name=name,
        out_shape=[jax.ShapeDtypeStruct(s, t) for s, t in outs],
        in_specs=[SMEM] * len(smem) + [VMEM] * len(vmem) + [ANY] * len(whole),
        out_specs=[VMEM] * (len(outs) - hbm_outs) + [ANY] * hbm_outs,
        scratch_shapes=[pltpu.VMEM(s, t) for s, t in scratch] + list(sems),
        input_output_aliases=aliases,
        cost_estimate=pl.CostEstimate(flops=flops, bytes_accessed=1 << 26, transcendentals=0),
        compiler_params=pltpu.CompilerParams(vmem_limit_bytes=VMEM_LIMIT),
    )(*smem, *vmem, *whole)


def copies(value, axis, count):
    return lax.all_to_all(jnp.broadcast_to(value[None], (count,) + value.shape), axis, 0, 0, tiled=True)


def swap_add(value):
    return value + lax.ppermute(value, "ctx", CORE_SWAP)


def sum_over_chips(value):
    one, two, three = [
        lax.ppermute(value, "ctx", [(c, (c + 2 * hops) % CTX) for c in range(CTX)]).astype(jnp.float32)
        for hops in (1, 2, 3)
    ]
    return (value.astype(jnp.float32) + two) + (one + three)


def per_device(hidden_in, w_qkv, w_out, b_out, ln_gain, ln_bias, doc_lengths, pair_of):
    f32, bf16 = jnp.float32, jnp.bfloat16
    own = hidden_in[0]
    places = jnp.stack([lax.axis_index("ctx"), lax.axis_index("dp")]).astype(jnp.int32)
    smem = [doc_lengths, places]
    state = [((HEADS, AUG, ROWS), f32)]
    work = [((HEADS, AUG, 2 * ROWS), bf16)]
    held = ((PAIRS, 256, 2 * ROWS), bf16)

    def fold(name, sources, blocks, acc):
        (acc,) = call(
            functools.partial(fold_kernel, sources), name, smem, [w_qkv, qbd, acc, *blocks], state, work,
            1 << 34, {4: 0},
        )
        return acc

    near = lax.ppermute(own, "ctx", AROUND)
    qbd, acc = call(queries_kernel, "queries", smem, [own, w_qkv], [held] + state, [], 1 << 34)
    own_later, acc = lax.optimization_barrier((own, acc))
    behind = lax.ppermute(own_later, "ctx", BACK)
    other = lax.ppermute(own_later, "ctx", CORE_SWAP)
    acc = fold("own", SOURCES[0:1], [own], acc)
    acc = fold("other", SOURCES[1:2], [other], acc)
    near, acc = lax.optimization_barrier((near, acc))
    far = lax.ppermute(near, "ctx", AROUND)
    near_other = lax.ppermute(near, "ctx", CORE_SWAP)
    acc = fold("near", SOURCES[2:3], [near], acc)
    near_other, acc = lax.optimization_barrier((near_other, acc))
    acc = fold("near_other", SOURCES[3:4], [near_other], acc)
    behind, acc = lax.optimization_barrier((behind, acc))
    behind_other = lax.ppermute(behind, "ctx", CORE_SWAP)
    acc = fold("behind", SOURCES[4:5], [behind], acc)
    far, acc = lax.optimization_barrier((far, acc))
    far_other = lax.ppermute(far, "ctx", CORE_SWAP)
    acc = fold("far", SOURCES[5:7], [behind_other, far], acc)
    far_other, acc = lax.optimization_barrier((far_other, acc))
    _, mixed, normal, inverse, rows, partial = call(
        last_kernel,
        "last",
        smem,
        [far_other, w_qkv, qbd, acc, own, w_out, b_out, ln_gain, ln_bias],
        state
        + [((D, ROWS), bf16), ((ROWS, D), f32), ((ROWS, 1), f32), ((ROWS, PACK + D), bf16), ((DOCS, D), f32)],
        work + [((8, 2 * ROWS), f32), ((len(SOURCES), ROWS, D), bf16)],
        1 << 34,
        {5: 0},
        [own, other, near, near_other, behind, behind_other, far, far_other],
    )
    other_rows = lax.ppermute(rows, "ctx", CORE_SWAP)
    pooled = sum_over_chips(swap_add(partial))
    pooled, other_rows = lax.optimization_barrier((pooled, other_rows))
    every = copies(pooled, "dp", DP)
    term, encoded = call(
        back_kernel,
        "back",
        smem + [pair_of],
        [every, mixed, normal, inverse, other_rows, ln_gain, ln_bias],
        [((D, HALF), bf16), ((ROWS, D), bf16)],
        [((NDOC, NDOC), f32), ((DOCS, D), f32), ((ROWS, D), bf16)],
        1 << 20,
        hbm_outs=1,
        sems=[pltpu.SemaphoreType.DMA],
    )
    share = D // DP
    pieces = lax.all_to_all(term.reshape(DP, share, HALF), "dp", 0, 0, tiled=True)
    piece = jnp.sum(pieces.astype(f32), axis=0).astype(bf16)
    halves = copies(piece, "ctx", CTX)
    (grad_out,) = call(join_kernel, "join", [], [halves], [((share, D), f32)], [], 1 << 20)
    return (encoded[None], grad_out)


def solution(mesh):
    return jax.shard_map(
        per_device,
        mesh=mesh,
        in_specs=(P("dp", "ctx", None), P(), P(), P(), P(), P(), P("dp", None), P("dp", None)),
        out_specs=(P("dp", "ctx", None), P("dp", None)),
        check_vma=False,
    )
```

```python
import functools

import jax
import jax.numpy as jnp
from jax import lax
from jax.experimental import pallas as pl
from jax.experimental.pallas import tpu as pltpu
from jax.sharding import PartitionSpec as P

D = 768
HEADS = 12
HEAD_DIM = 64
PAIRS = HEADS // 2
DOCS = 4
NDOC = 128
ROWS = 256
CTX = 8
DP = 32
HALF = D // 2
PACK = D + 128
AUG = 80

SOFTMAX_TEMPER = 0.05
NORM_EPSILON = 1e-05
EMBED_EPSILON = 1e-06
PENALTY = -1e30

VMEM_LIMIT = 24 * 1024 * 1024

CORE_SWAP = [(c, c ^ 1) for c in range(CTX)]
AROUND = [(c, (c + 2) % CTX if c % 2 == 0 else (c - 2) % CTX) for c in range(CTX)]
BACK = [(b, a) for a, b in AROUND]


def came_from(place, hops):
    step = 2 * hops
    return lax.rem(jnp.where(lax.rem(place, 2) == 0, place - step, place + step) + 2 * CTX, CTX)


SOURCES = [(0, 0), (1, 0), (0, 1), (1, 1), (0, -1), (1, -1), (0, 2), (1, 2)]


def doc_ends(lengths_ref):
    e0 = lengths_ref[0, 0]
    e1 = e0 + lengths_ref[0, 1]
    e2 = e1 + lengths_ref[0, 2]
    e3 = e2 + lengths_ref[0, 3]
    return e0, e1, e2, e3


def doc_of(ends, positions):
    e0, e1, e2, e3 = ends
    one = jnp.int32(1)
    zero = jnp.int32(0)
    return sum(jnp.where(positions >= e, one, zero) for e in (e0, e1, e2, e3))


def needed_span(ends, first):
    e0, e1, e2, e3 = ends
    last = first + ROWS - 1
    low = jnp.where(first >= e2, e2, jnp.where(first >= e1, e1, jnp.where(first >= e0, e0, 0)))
    high = jnp.where(last < e0, e0, jnp.where(last < e1, e1, jnp.where(last < e2, e2, e3)))
    return low, high


def fill_queries(ends, first, own, wqkv_ref, qbd):
    queries = lax.dot_general(
        wqkv_ref[:, :D], own, (((0,), (1,)), ((), ())), preferred_element_type=jnp.float32
    )
    queries = (queries.astype(jnp.bfloat16).astype(jnp.float32) * HEAD_DIM**-0.5).astype(jnp.bfloat16)
    positions = first + lax.broadcasted_iota(jnp.int32, (HEAD_DIM * 2, ROWS), 1)
    slots = lax.broadcasted_iota(jnp.int32, (HEAD_DIM * 2, ROWS), 0)
    same = (doc_of(ends, positions) == slots) | (slots >= DOCS)
    penalty = jnp.where(same, 0.0, PENALTY).astype(jnp.bfloat16)
    penalties = jnp.concatenate([penalty, penalty], axis=1)
    zero = jnp.zeros((HEAD_DIM, ROWS), jnp.bfloat16)
    for j in range(PAIRS):
        qbd[j, :64, :ROWS] = queries[128 * j : 128 * j + 64, :]
        qbd[j, :64, ROWS:] = zero
        qbd[j, 64:128, :ROWS] = zero
        qbd[j, 64:128, ROWS:] = queries[128 * j + 64 : 128 * j + 128, :]
        qbd[j, 128:, :] = penalties


def project(ends, bases, blocks, wqkv_ref, vt):
    rows = ROWS * len(blocks)
    hidden = jnp.concatenate(blocks, axis=0) if len(blocks) > 1 else blocks[0]
    keys = jnp.dot(hidden, wqkv_ref[:, D : 2 * D], preferred_element_type=jnp.float32).astype(jnp.bfloat16)
    values = lax.dot_general(
        wqkv_ref[:, 2 * D :], hidden, (((0,), (1,)), ((), ())), preferred_element_type=jnp.float32
    ).astype(jnp.bfloat16)
    vt[:, :HEAD_DIM, :rows] = values.reshape(HEADS, HEAD_DIM, rows)
    offsets = lax.broadcasted_iota(jnp.int32, (ROWS, 128), 0)
    lanes = lax.broadcasted_iota(jnp.int32, (ROWS, 128), 1)
    onehots = [
        jnp.where(doc_of(ends, base + offsets) == lanes, 1.0, 0.0).astype(jnp.bfloat16) for base in bases
    ]
    return keys, jnp.concatenate(onehots, axis=0) if len(blocks) > 1 else onehots[0]


def pair_scores(keys, onehot, qbd, j):
    pair_keys = jnp.concatenate([keys[:, 128 * j : 128 * j + 128], onehot], axis=1)
    return jnp.dot(pair_keys, qbd[j], preferred_element_type=jnp.float32)


def attend_plain(ends, bases, blocks, wqkv_ref, qbd, vt, acc_ref):
    rows = ROWS * len(blocks)
    keys, onehot = project(ends, bases, blocks, wqkv_ref, vt)
    for j in range(PAIRS):
        weights = jnp.exp(pair_scores(keys, onehot, qbd, j)).astype(jnp.bfloat16)
        for h in range(2):
            part = slice(ROWS * h, ROWS * h + ROWS)
            acc_ref[2 * j + h] += jnp.dot(
                vt[2 * j + h, :, :rows], weights[:, part], preferred_element_type=jnp.float32
            )


def attend_shifted(ends, base, block, wqkv_ref, qbd, vt, m_ref, acc_ref):
    keys, onehot = project(ends, [base], [block], wqkv_ref, vt)
    for j in range(PAIRS):
        scores = pair_scores(keys, onehot, qbd, j)
        old = m_ref[j : j + 1, :]
        new = jnp.maximum(old, jnp.max(scores, axis=0, keepdims=True))
        m_ref[j : j + 1, :] = new
        shrink = jnp.exp(old - new)
        weights = jnp.exp(scores - new).astype(jnp.bfloat16)
        for h in range(2):
            part = slice(ROWS * h, ROWS * h + ROWS)
            mixed = jnp.dot(vt[2 * j + h, :, :ROWS], weights[:, part], preferred_element_type=jnp.float32)
            acc_ref[2 * j + h] = acc_ref[2 * j + h] * shrink[:, part] + mixed


def fill_ones(vt):
    row = lax.broadcasted_iota(jnp.int32, (HEADS, AUG - HEAD_DIM, vt.shape[2]), 1)
    vt[:, HEAD_DIM:, :] = jnp.where(row == 0, 1.0, 0.0).astype(jnp.bfloat16)


def attend_blocks(ends, first, places, blocks, wqkv_ref, qbd, vt, acc_ref):
    low, high = needed_span(ends, first)
    bases = [place * ROWS for place in places]
    wanted = [(base < high) & (base + ROWS > low) for base in bases]

    def attend(which):
        attend_plain(
            ends, [bases[i] for i in which], [blocks[i][...] for i in which], wqkv_ref, qbd, vt, acc_ref
        )

    if len(blocks) == 1:
        pl.when(wanted[0])(lambda: attend([0]))
    else:
        one, two = wanted
        pl.when(one & two)(lambda: attend([0, 1]))
        pl.when(one & jnp.logical_not(two))(lambda: attend([0]))
        pl.when(two & jnp.logical_not(one))(lambda: attend([1]))


def queries_kernel(lengths_ref, place_ref, own_ref, wqkv_ref, qbd, acc_ref):
    ends = doc_ends(lengths_ref)
    fill_queries(ends, place_ref[0] * ROWS, own_ref[...], wqkv_ref, qbd)
    acc_ref[...] = jnp.zeros(acc_ref.shape, jnp.float32)


def fold_kernel(sources, lengths_ref, place_ref, wqkv_ref, qbd, acc_in, *refs):
    blocks, (acc_ref, vt) = refs[: len(sources)], refs[len(sources) :]
    place = place_ref[0]
    ends = doc_ends(lengths_ref)
    fill_ones(vt)
    places = [came_from(place ^ flip, hops) for flip, hops in sources]
    attend_blocks(ends, place * ROWS, places, blocks, wqkv_ref, qbd, vt, acc_ref)


def in_range(acc):
    sums = acc[:, HEAD_DIM, :]
    good = jnp.where((sums >= 1e-12) & (sums <= 1e12), 1.0, 0.0)
    finite = jnp.where(jnp.abs(acc) <= 1e38, 1.0, 0.0)
    return jnp.minimum(jnp.min(good), jnp.min(finite)) > 0.5


def attend_again(ends, place, blocks, wqkv_ref, qbd, vt, acc_ref, m_ref, held):
    for i, (flip, hops) in enumerate(SOURCES):
        pltpu.sync_copy(blocks[i], held.at[i])
    m_ref[...] = jnp.full(m_ref.shape, PENALTY, jnp.float32)
    acc_ref[...] = jnp.zeros(acc_ref.shape, jnp.float32)
    low, high = needed_span(ends, place * ROWS)

    def step(i, carry):
        base = jnp.int32(0)
        for k, (flip, hops) in enumerate(SOURCES):
            base = jnp.where(i == k, came_from(place ^ flip, hops) * ROWS, base)

        @pl.when((base < high) & (base + ROWS > low))
        def _():
            attend_shifted(ends, base, held[i], wqkv_ref, qbd, vt, m_ref, acc_ref)

        return carry

    lax.fori_loop(0, len(SOURCES), step, 0)


def last_kernel(
    lengths_ref, place_ref, far_other_ref, wqkv_ref, qbd, acc_in, own_ref, wout_ref, bias_ref, gain_ref, shift_ref,
    *refs
):
    blocks, refs = refs[: len(SOURCES)], refs[len(SOURCES) :]
    acc_ref, mixed_ref, normal_ref, inverse_ref, rows_ref, pooled_ref, vt, m_ref, held = refs
    place = place_ref[0]
    ends = doc_ends(lengths_ref)
    first = place * ROWS
    fill_ones(vt)
    flip, hops = SOURCES[-1]
    attend_blocks(ends, first, [came_from(place ^ flip, hops)], [far_other_ref], wqkv_ref, qbd, vt, acc_ref)

    @pl.when(jnp.logical_not(in_range(acc_ref[...])))
    def _():
        attend_again(ends, place, blocks, wqkv_ref, qbd, vt, acc_ref, m_ref, held)

    acc = acc_ref[...]
    mixed = acc[:, :HEAD_DIM, :] * (1.0 / acc[:, HEAD_DIM : HEAD_DIM + 1, :])
    mixed = mixed.reshape(D, ROWS).astype(jnp.bfloat16)
    mixed_ref[...] = mixed
    summed = lax.dot_general(
        mixed, wout_ref[...], (((0,), (0,)), ((), ())), preferred_element_type=jnp.float32
    )
    summed = summed + bias_ref[...][None] + own_ref[...].astype(jnp.float32)
    centered = summed - jnp.mean(summed, axis=1, keepdims=True)
    inverse = lax.rsqrt(jnp.mean(centered * centered, axis=1, keepdims=True) + NORM_EPSILON)
    normal = centered * inverse
    normal_ref[...] = normal
    inverse_ref[...] = inverse
    layer = normal * gain_ref[...][None] + shift_ref[...][None]
    for i in range(D // ROWS):
        rows_ref[:, PACK + ROWS * i : PACK + ROWS * (i + 1)] = mixed[ROWS * i : ROWS * (i + 1)]
    rows_ref[:, :D] = normal.astype(jnp.bfloat16)
    high = inverse.astype(jnp.bfloat16).astype(jnp.float32)
    lane = lax.broadcasted_iota(jnp.int32, (ROWS, 128), 1)
    rows_ref[:, D:PACK] = jnp.where(lane == 0, high, inverse - high).astype(jnp.bfloat16)
    row_doc = doc_of(ends, first + lax.broadcasted_iota(jnp.int32, (ROWS, 1), 0))
    pooled_ref[...] = jnp.zeros(pooled_ref.shape, jnp.float32)
    starts = (jnp.int32(0), *ends[:-1])
    for d in range(DOCS):

        @pl.when((starts[d] < first + ROWS) & (ends[d] > first))
        def _():
            total = jnp.sum(jnp.where(row_doc == d, layer, 0.0), axis=0, keepdims=True)
            mean = total * (1.0 / lengths_ref[0, d].astype(jnp.float32))
            pooled_ref[:, d : d + 1, :] = jnp.broadcast_to(mean[None], (CTX, 1, D))


def back_kernel(
    lengths_ref, place_ref, pair_ref, pooled_ref, mixed_ref, normal_ref, inverse_ref, other_rows_ref,
    gain_ref, shift_ref, out_ref, encoded_hbm, expo_ref, scaled_ref, encoded_ref, sem
):
    place = place_ref[0]
    data_place = place_ref[1]
    ends = doc_ends(lengths_ref)
    f32, bf16 = jnp.float32, jnp.bfloat16
    encoded_ref[...] = (normal_ref[...] * gain_ref[...][None] + shift_ref[...][None]).astype(bf16)
    write = pltpu.make_async_copy(encoded_ref, encoded_hbm, sem)
    write.start()

    pooled = pooled_ref[...].reshape(NDOC, D)
    emb = pooled * lax.rsqrt(jnp.sum(pooled * pooled, axis=1, keepdims=True) + EMBED_EPSILON)
    high = emb.astype(bf16)
    low = (emb - high.astype(f32)).astype(bf16)

    def times(left, right):
        return lax.dot_general(left, right, (((1,), (1,)), ((), ())), preferred_element_type=f32)

    sims = (times(high, high) + (times(high, low) + times(low, high))) * (1.0 / SOFTMAX_TEMPER)
    columns = lax.broadcasted_iota(jnp.int32, (NDOC, NDOC), 1)
    rows = lax.broadcasted_iota(jnp.int32, (NDOC, NDOC), 0)
    expo = jnp.where(rows == columns, 0.0, jnp.exp(sims))
    expo_ref[...] = expo
    totals = 1.0 / jnp.sum(expo, axis=0, keepdims=True)
    half = lax.rem(data_place, 2)
    rows8 = expo_ref[pl.ds(pl.multiple_of((data_place - half) * DOCS, 8), 8), :]
    own_expo = jnp.where(half == 0, rows8[:DOCS], rows8[DOCS:])
    own = pooled_ref[data_place]
    own_inverse = lax.rsqrt(jnp.sum(own * own, axis=1, keepdims=True) + EMBED_EPSILON)
    own_emb = own * own_inverse
    own_totals = 1.0 / jnp.sum(own_expo, axis=1, keepdims=True)
    slots = lax.broadcasted_iota(jnp.int32, (DOCS, NDOC), 0)
    lanes = lax.broadcasted_iota(jnp.int32, (DOCS, NDOC), 1)
    partner = jnp.where(
        slots == 0, pair_ref[0, 0],
        jnp.where(slots == 1, pair_ref[0, 1], jnp.where(slots == 2, pair_ref[0, 2], pair_ref[0, 3])),
    )
    both = own_expo * (own_totals + totals) - jnp.where(lanes == partner, 2.0, 0.0)
    weights = jnp.concatenate([both, both], axis=0).T
    emb_grad = jnp.concatenate(
        [jnp.sum(weights[:, d : d + 1] * emb, axis=0, keepdims=True) for d in range(DOCS)], axis=0
    ) * (1.0 / SOFTMAX_TEMPER)
    pooled_grad = (emb_grad - own_emb * jnp.sum(own_emb * emb_grad, axis=1, keepdims=True)) * own_inverse
    slot = lax.broadcasted_iota(jnp.int32, (DOCS, 1), 0)
    length = jnp.where(
        slot == 0, lengths_ref[0, 0],
        jnp.where(slot == 1, lengths_ref[0, 1], jnp.where(slot == 2, lengths_ref[0, 2], lengths_ref[0, 3])),
    ).astype(f32)
    scaled = pooled_grad * (1.0 / length) * gain_ref[...][None]
    centered = scaled - jnp.mean(scaled, axis=1, keepdims=True)
    scaled_ref[...] = centered
    share = pl.ds(pl.multiple_of(lax.rem(place, 2) * HALF, 128), HALF)

    def grad(first, normal, normal_share, inverse):
        row_doc = doc_of(ends, first + lax.broadcasted_iota(jnp.int32, (ROWS, 1), 0))

        def spread(values):
            pick = jnp.where(row_doc == 2, values[2:3], values[3:4])
            return jnp.where(row_doc == 0, values[0:1], jnp.where(row_doc == 1, values[1:2], pick))

        along = jnp.mean(spread(scaled) * normal, axis=1, keepdims=True)
        return (inverse * (spread(scaled_ref[:, share]) - normal_share * along)).astype(bf16)

    mine = grad(place * ROWS, normal_ref[...], normal_ref[:, share], inverse_ref[...])
    inverse = other_rows_ref[:, D:PACK].astype(f32)
    theirs = grad(
        (place ^ 1) * ROWS,
        other_rows_ref[:, :D].astype(f32),
        other_rows_ref[:, share].astype(f32),
        inverse[:, 0:1] + inverse[:, 1:2],
    )
    for i in range(D // ROWS):
        part = slice(ROWS * i, ROWS * (i + 1))
        other_mixed = other_rows_ref[:, PACK + ROWS * i : PACK + ROWS * (i + 1)]
        product = jnp.dot(mixed_ref[part, :], mine, preferred_element_type=f32)
        product += jnp.dot(other_mixed, theirs, preferred_element_type=f32)
        out_ref[part, :] = product.astype(bf16)
    write.wait()


def join_kernel(halves_ref, out_ref):
    for core in range(2):
        parts = [halves_ref[c].astype(jnp.float32) for c in range(core, CTX, 2)]
        out_ref[:, HALF * core : HALF * (core + 1)] = (parts[0] + parts[1]) + (parts[2] + parts[3])


SMEM = pl.BlockSpec(memory_space=pltpu.SMEM)
VMEM = pl.BlockSpec(memory_space=pltpu.VMEM)
ANY = pl.BlockSpec(memory_space=pl.ANY)


def call(kernel, name, smem, vmem, outs, scratch, flops, aliases={}, whole=(), hbm_outs=0, sems=()):
    return pl.pallas_call(
        kernel,
        name=name,
        out_shape=[jax.ShapeDtypeStruct(s, t) for s, t in outs],
        in_specs=[SMEM] * len(smem) + [VMEM] * len(vmem) + [ANY] * len(whole),
        out_specs=[VMEM] * (len(outs) - hbm_outs) + [ANY] * hbm_outs,
        scratch_shapes=[pltpu.VMEM(s, t) for s, t in scratch] + list(sems),
        input_output_aliases=aliases,
        cost_estimate=pl.CostEstimate(flops=flops, bytes_accessed=1 << 26, transcendentals=0),
        compiler_params=pltpu.CompilerParams(vmem_limit_bytes=VMEM_LIMIT),
    )(*smem, *vmem, *whole)


def copies(value, axis, count):
    return lax.all_to_all(jnp.broadcast_to(value[None], (count,) + value.shape), axis, 0, 0, tiled=True)


def per_device(hidden_in, w_qkv, w_out, b_out, ln_gain, ln_bias, doc_lengths, pair_of):
    f32, bf16 = jnp.float32, jnp.bfloat16
    own = hidden_in[0]
    places = jnp.stack([lax.axis_index("ctx"), lax.axis_index("dp")]).astype(jnp.int32)
    smem = [doc_lengths, places]
    state = [((HEADS, AUG, ROWS), f32)]
    work = [((HEADS, AUG, 2 * ROWS), bf16)]
    held = ((PAIRS, 256, 2 * ROWS), bf16)

    def fold(name, sources, blocks, acc):
        (acc,) = call(
            functools.partial(fold_kernel, sources), name, smem, [w_qkv, qbd, acc, *blocks], state, work,
            1 << 34, {4: 0},
        )
        return acc

    near = lax.ppermute(own, "ctx", AROUND)
    qbd, acc = call(queries_kernel, "queries", smem, [own, w_qkv], [held] + state, [], 1 << 34)
    own_later, acc = lax.optimization_barrier((own, acc))
    behind = lax.ppermute(own_later, "ctx", BACK)
    other = lax.ppermute(own_later, "ctx", CORE_SWAP)
    acc = fold("own", SOURCES[0:1], [own], acc)
    acc = fold("other", SOURCES[1:2], [other], acc)
    near, acc = lax.optimization_barrier((near, acc))
    far = lax.ppermute(near, "ctx", AROUND)
    near_other = lax.ppermute(near, "ctx", CORE_SWAP)
    acc = fold("near", SOURCES[2:3], [near], acc)
    near_other, acc = lax.optimization_barrier((near_other, acc))
    acc = fold("near_other", SOURCES[3:4], [near_other], acc)
    behind, acc = lax.optimization_barrier((behind, acc))
    behind_other = lax.ppermute(behind, "ctx", CORE_SWAP)
    acc = fold("behind", SOURCES[4:5], [behind], acc)
    far, acc = lax.optimization_barrier((far, acc))
    far_other = lax.ppermute(far, "ctx", CORE_SWAP)
    acc = fold("far", SOURCES[5:7], [behind_other, far], acc)
    far_other, acc = lax.optimization_barrier((far_other, acc))
    _, mixed, normal, inverse, rows, partials = call(
        last_kernel,
        "last",
        smem,
        [far_other, w_qkv, qbd, acc, own, w_out, b_out, ln_gain, ln_bias],
        state
        + [((D, ROWS), bf16), ((ROWS, D), f32), ((ROWS, 1), f32), ((ROWS, PACK + D), bf16), ((CTX, DOCS, D), f32)],
        work + [((8, 2 * ROWS), f32), ((len(SOURCES), ROWS, D), bf16)],
        1 << 34,
        {5: 0},
        [own, other, near, near_other, behind, behind_other, far, far_other],
    )
    other_rows = lax.ppermute(rows, "ctx", CORE_SWAP)
    pooled = jnp.sum(lax.all_to_all(partials, "ctx", 0, 0, tiled=True), axis=0)
    pooled, other_rows = lax.optimization_barrier((pooled, other_rows))
    every = copies(pooled, "dp", DP)
    term, encoded = call(
        back_kernel,
        "back",
        smem + [pair_of],
        [every, mixed, normal, inverse, other_rows, ln_gain, ln_bias],
        [((D, HALF), bf16), ((ROWS, D), bf16)],
        [((NDOC, NDOC), f32), ((DOCS, D), f32), ((ROWS, D), bf16)],
        1 << 20,
        hbm_outs=1,
        sems=[pltpu.SemaphoreType.DMA],
    )
    share = D // DP
    pieces = lax.all_to_all(term.reshape(DP, share, HALF), "dp", 0, 0, tiled=True)
    piece = jnp.sum(pieces.astype(f32), axis=0).astype(bf16)
    halves = copies(piece, "ctx", CTX)
    (grad_out,) = call(join_kernel, "join", [], [halves], [((share, D), f32)], [], 1 << 20)
    return (encoded[None], grad_out)


def solution(mesh):
    return jax.shard_map(
        per_device,
        mesh=mesh,
        in_specs=(P("dp", "ctx", None), P(), P(), P(), P(), P(), P("dp", None), P("dp", None)),
        out_specs=(P("dp", "ctx", None), P("dp", None)),
        check_vma=False,
    )
```

```python
import functools

import jax
import jax.numpy as jnp
from jax import lax
from jax.experimental import pallas as pl
from jax.experimental.pallas import tpu as pltpu
from jax.sharding import PartitionSpec as P

D = 768
HEADS = 12
HEAD_DIM = 64
PAIRS = HEADS // 2
DOCS = 4
NDOC = 128
ROWS = 256
CTX = 8
DP = 32
HALF = D // 2
PACK = D + 128
AUG = 80

SOFTMAX_TEMPER = 0.05
NORM_EPSILON = 1e-05
EMBED_EPSILON = 1e-06
PENALTY = -1e30

VMEM_LIMIT = 24 * 1024 * 1024

CORE_SWAP = [(c, c ^ 1) for c in range(CTX)]
AROUND = [(c, (c + 2) % CTX if c % 2 == 0 else (c - 2) % CTX) for c in range(CTX)]
BACK = [(b, a) for a, b in AROUND]


def came_from(place, hops):
    step = 2 * hops
    return lax.rem(jnp.where(lax.rem(place, 2) == 0, place - step, place + step) + 2 * CTX, CTX)


SOURCES = [(0, 0), (1, 0), (0, 1), (1, 1), (0, -1), (1, -1), (0, 2), (1, 2)]


def doc_ends(lengths_ref):
    e0 = lengths_ref[0, 0]
    e1 = e0 + lengths_ref[0, 1]
    e2 = e1 + lengths_ref[0, 2]
    e3 = e2 + lengths_ref[0, 3]
    return e0, e1, e2, e3


def doc_of(ends, positions):
    e0, e1, e2, e3 = ends
    one = jnp.int32(1)
    zero = jnp.int32(0)
    return sum(jnp.where(positions >= e, one, zero) for e in (e0, e1, e2, e3))


def needed_span(ends, first):
    e0, e1, e2, e3 = ends
    last = first + ROWS - 1
    low = jnp.where(first >= e2, e2, jnp.where(first >= e1, e1, jnp.where(first >= e0, e0, 0)))
    high = jnp.where(last < e0, e0, jnp.where(last < e1, e1, jnp.where(last < e2, e2, e3)))
    return low, high


def fill_queries(ends, first, own, wqkv_ref, qbd):
    queries = lax.dot_general(
        wqkv_ref[:, :D], own, (((0,), (1,)), ((), ())), preferred_element_type=jnp.float32
    )
    queries = (queries.astype(jnp.bfloat16).astype(jnp.float32) * HEAD_DIM**-0.5).astype(jnp.bfloat16)
    positions = first + lax.broadcasted_iota(jnp.int32, (HEAD_DIM * 2, ROWS), 1)
    slots = lax.broadcasted_iota(jnp.int32, (HEAD_DIM * 2, ROWS), 0)
    same = (doc_of(ends, positions) == slots) | (slots >= DOCS)
    penalty = jnp.where(same, 0.0, PENALTY).astype(jnp.bfloat16)
    penalties = jnp.concatenate([penalty, penalty], axis=1)
    zero = jnp.zeros((HEAD_DIM, ROWS), jnp.bfloat16)
    for j in range(PAIRS):
        qbd[j, :64, :ROWS] = queries[128 * j : 128 * j + 64, :]
        qbd[j, :64, ROWS:] = zero
        qbd[j, 64:128, :ROWS] = zero
        qbd[j, 64:128, ROWS:] = queries[128 * j + 64 : 128 * j + 128, :]
        qbd[j, 128:, :] = penalties


def project(ends, bases, blocks, wqkv_ref, vt):
    rows = ROWS * len(blocks)
    hidden = jnp.concatenate(blocks, axis=0) if len(blocks) > 1 else blocks[0]
    keys = jnp.dot(hidden, wqkv_ref[:, D : 2 * D], preferred_element_type=jnp.float32).astype(jnp.bfloat16)
    values = lax.dot_general(
        wqkv_ref[:, 2 * D :], hidden, (((0,), (1,)), ((), ())), preferred_element_type=jnp.float32
    ).astype(jnp.bfloat16)
    vt[:, :HEAD_DIM, :rows] = values.reshape(HEADS, HEAD_DIM, rows)
    offsets = lax.broadcasted_iota(jnp.int32, (ROWS, 128), 0)
    lanes = lax.broadcasted_iota(jnp.int32, (ROWS, 128), 1)
    onehots = [
        jnp.where(doc_of(ends, base + offsets) == lanes, 1.0, 0.0).astype(jnp.bfloat16) for base in bases
    ]
    return keys, jnp.concatenate(onehots, axis=0) if len(blocks) > 1 else onehots[0]


def pair_scores(keys, onehot, qbd, j):
    pair_keys = jnp.concatenate([keys[:, 128 * j : 128 * j + 128], onehot], axis=1)
    return jnp.dot(pair_keys, qbd[j], preferred_element_type=jnp.float32)


def attend_plain(ends, bases, blocks, wqkv_ref, qbd, vt, acc_ref):
    rows = ROWS * len(blocks)
    keys, onehot = project(ends, bases, blocks, wqkv_ref, vt)
    for j in range(PAIRS):
        weights = jnp.exp(pair_scores(keys, onehot, qbd, j)).astype(jnp.bfloat16)
        for h in range(2):
            part = slice(ROWS * h, ROWS * h + ROWS)
            acc_ref[2 * j + h] += jnp.dot(
                vt[2 * j + h, :, :rows], weights[:, part], preferred_element_type=jnp.float32
            )


def attend_shifted(ends, base, block, wqkv_ref, qbd, vt, m_ref, acc_ref):
    keys, onehot = project(ends, [base], [block], wqkv_ref, vt)
    for j in range(PAIRS):
        scores = pair_scores(keys, onehot, qbd, j)
        old = m_ref[j : j + 1, :]
        new = jnp.maximum(old, jnp.max(scores, axis=0, keepdims=True))
        m_ref[j : j + 1, :] = new
        shrink = jnp.exp(old - new)
        weights = jnp.exp(scores - new).astype(jnp.bfloat16)
        for h in range(2):
            part = slice(ROWS * h, ROWS * h + ROWS)
            mixed = jnp.dot(vt[2 * j + h, :, :ROWS], weights[:, part], preferred_element_type=jnp.float32)
            acc_ref[2 * j + h] = acc_ref[2 * j + h] * shrink[:, part] + mixed


def fill_ones(vt):
    row = lax.broadcasted_iota(jnp.int32, (HEADS, AUG - HEAD_DIM, vt.shape[2]), 1)
    vt[:, HEAD_DIM:, :] = jnp.where(row == 0, 1.0, 0.0).astype(jnp.bfloat16)


def attend_blocks(ends, first, places, blocks, wqkv_ref, qbd, vt, acc_ref):
    low, high = needed_span(ends, first)
    bases = [place * ROWS for place in places]
    wanted = [(base < high) & (base + ROWS > low) for base in bases]

    def attend(which):
        attend_plain(
            ends, [bases[i] for i in which], [blocks[i][...] for i in which], wqkv_ref, qbd, vt, acc_ref
        )

    if len(blocks) == 1:
        pl.when(wanted[0])(lambda: attend([0]))
    else:
        one, two = wanted
        pl.when(one & two)(lambda: attend([0, 1]))
        pl.when(one & jnp.logical_not(two))(lambda: attend([0]))
        pl.when(two & jnp.logical_not(one))(lambda: attend([1]))


def queries_kernel(lengths_ref, place_ref, own_ref, wqkv_ref, qbd, acc_ref):
    ends = doc_ends(lengths_ref)
    fill_queries(ends, place_ref[0] * ROWS, own_ref[...], wqkv_ref, qbd)
    acc_ref[...] = jnp.zeros(acc_ref.shape, jnp.float32)


def fold_kernel(sources, lengths_ref, place_ref, wqkv_ref, qbd, acc_in, *refs):
    blocks, (acc_ref, vt) = refs[: len(sources)], refs[len(sources) :]
    place = place_ref[0]
    ends = doc_ends(lengths_ref)
    fill_ones(vt)
    places = [came_from(place ^ flip, hops) for flip, hops in sources]
    attend_blocks(ends, place * ROWS, places, blocks, wqkv_ref, qbd, vt, acc_ref)


def in_range(acc):
    sums = acc[:, HEAD_DIM, :]
    good = jnp.where((sums >= 1e-12) & (sums <= 1e12), 1.0, 0.0)
    finite = jnp.where(jnp.abs(acc) <= 1e38, 1.0, 0.0)
    return jnp.minimum(jnp.min(good), jnp.min(finite)) > 0.5


def attend_again(ends, place, blocks, wqkv_ref, qbd, vt, acc_ref, m_ref, held):
    for i, (flip, hops) in enumerate(SOURCES):
        pltpu.sync_copy(blocks[i], held.at[i])
    m_ref[...] = jnp.full(m_ref.shape, PENALTY, jnp.float32)
    acc_ref[...] = jnp.zeros(acc_ref.shape, jnp.float32)
    low, high = needed_span(ends, place * ROWS)

    def step(i, carry):
        base = jnp.int32(0)
        for k, (flip, hops) in enumerate(SOURCES):
            base = jnp.where(i == k, came_from(place ^ flip, hops) * ROWS, base)

        @pl.when((base < high) & (base + ROWS > low))
        def _():
            attend_shifted(ends, base, held[i], wqkv_ref, qbd, vt, m_ref, acc_ref)

        return carry

    lax.fori_loop(0, len(SOURCES), step, 0)


def last_kernel(
    lengths_ref, place_ref, far_other_ref, wqkv_ref, qbd, acc_in, own_ref, wout_ref, bias_ref, gain_ref, shift_ref,
    *refs
):
    blocks, refs = refs[: len(SOURCES)], refs[len(SOURCES) :]
    acc_ref, mixed_ref, normal_ref, inverse_ref, rows_ref, pooled_ref, vt, m_ref, held = refs
    place = place_ref[0]
    ends = doc_ends(lengths_ref)
    first = place * ROWS
    fill_ones(vt)
    flip, hops = SOURCES[-1]
    attend_blocks(ends, first, [came_from(place ^ flip, hops)], [far_other_ref], wqkv_ref, qbd, vt, acc_ref)

    @pl.when(jnp.logical_not(in_range(acc_ref[...])))
    def _():
        attend_again(ends, place, blocks, wqkv_ref, qbd, vt, acc_ref, m_ref, held)

    acc = acc_ref[...]
    mixed = acc[:, :HEAD_DIM, :] * (1.0 / acc[:, HEAD_DIM : HEAD_DIM + 1, :])
    mixed = mixed.reshape(D, ROWS).astype(jnp.bfloat16)
    mixed_ref[...] = mixed
    summed = lax.dot_general(
        mixed, wout_ref[...], (((0,), (0,)), ((), ())), preferred_element_type=jnp.float32
    )
    summed = summed + bias_ref[...][None] + own_ref[...].astype(jnp.float32)
    centered = summed - jnp.mean(summed, axis=1, keepdims=True)
    inverse = lax.rsqrt(jnp.mean(centered * centered, axis=1, keepdims=True) + NORM_EPSILON)
    normal = centered * inverse
    normal_ref[...] = normal
    inverse_ref[...] = inverse
    layer = normal * gain_ref[...][None] + shift_ref[...][None]
    for i in range(D // ROWS):
        rows_ref[:, PACK + ROWS * i : PACK + ROWS * (i + 1)] = mixed[ROWS * i : ROWS * (i + 1)]
    rows_ref[:, :D] = normal.astype(jnp.bfloat16)
    high = inverse.astype(jnp.bfloat16).astype(jnp.float32)
    lane = lax.broadcasted_iota(jnp.int32, (ROWS, 128), 1)
    rows_ref[:, D:PACK] = jnp.where(lane == 0, high, inverse - high).astype(jnp.bfloat16)
    row_doc = doc_of(ends, first + lax.broadcasted_iota(jnp.int32, (ROWS, 1), 0))
    pooled_ref[...] = jnp.zeros(pooled_ref.shape, jnp.float32)
    starts = (jnp.int32(0), *ends[:-1])
    for d in range(DOCS):

        @pl.when((starts[d] < first + ROWS) & (ends[d] > first))
        def _():
            total = jnp.sum(jnp.where(row_doc == d, layer, 0.0), axis=0, keepdims=True)
            mean = total * (1.0 / lengths_ref[0, d].astype(jnp.float32))
            pooled_ref[:, d : d + 1, :] = jnp.broadcast_to(mean[None], (CTX, 1, D))


def back_kernel(
    lengths_ref, place_ref, pair_ref, pooled_ref, mixed_ref, normal_ref, inverse_ref, other_rows_ref,
    gain_ref, shift_ref, out_ref, encoded_hbm, expo_ref, scaled_ref, encoded_ref, sem
):
    place = place_ref[0]
    data_place = place_ref[1]
    ends = doc_ends(lengths_ref)
    f32, bf16 = jnp.float32, jnp.bfloat16
    encoded_ref[...] = (normal_ref[...] * gain_ref[...][None] + shift_ref[...][None]).astype(bf16)
    write = pltpu.make_async_copy(encoded_ref, encoded_hbm, sem)
    write.start()

    pooled = pooled_ref[...].reshape(NDOC, D)
    emb = pooled * lax.rsqrt(jnp.sum(pooled * pooled, axis=1, keepdims=True) + EMBED_EPSILON)
    high = emb.astype(bf16)
    low = (emb - high.astype(f32)).astype(bf16)

    def times(left, right):
        return lax.dot_general(left, right, (((1,), (1,)), ((), ())), preferred_element_type=f32)

    sims = (times(high, high) + (times(high, low) + times(low, high))) * (1.0 / SOFTMAX_TEMPER)
    columns = lax.broadcasted_iota(jnp.int32, (NDOC, NDOC), 1)
    rows = lax.broadcasted_iota(jnp.int32, (NDOC, NDOC), 0)
    expo = jnp.where(rows == columns, 0.0, jnp.exp(sims))
    expo_ref[...] = expo
    totals = 1.0 / jnp.sum(expo, axis=0, keepdims=True)
    half = lax.rem(data_place, 2)
    rows8 = expo_ref[pl.ds(pl.multiple_of((data_place - half) * DOCS, 8), 8), :]
    own_expo = jnp.where(half == 0, rows8[:DOCS], rows8[DOCS:])
    own = pooled_ref[data_place]
    own_inverse = lax.rsqrt(jnp.sum(own * own, axis=1, keepdims=True) + EMBED_EPSILON)
    own_emb = own * own_inverse
    own_totals = 1.0 / jnp.sum(own_expo, axis=1, keepdims=True)
    slots = lax.broadcasted_iota(jnp.int32, (DOCS, NDOC), 0)
    lanes = lax.broadcasted_iota(jnp.int32, (DOCS, NDOC), 1)
    partner = jnp.where(
        slots == 0, pair_ref[0, 0],
        jnp.where(slots == 1, pair_ref[0, 1], jnp.where(slots == 2, pair_ref[0, 2], pair_ref[0, 3])),
    )
    both = own_expo * (own_totals + totals) - jnp.where(lanes == partner, 2.0, 0.0)
    weights = jnp.concatenate([both, both], axis=0).T
    emb_grad = jnp.concatenate(
        [jnp.sum(weights[:, d : d + 1] * emb, axis=0, keepdims=True) for d in range(DOCS)], axis=0
    ) * (1.0 / SOFTMAX_TEMPER)
    pooled_grad = (emb_grad - own_emb * jnp.sum(own_emb * emb_grad, axis=1, keepdims=True)) * own_inverse
    slot = lax.broadcasted_iota(jnp.int32, (DOCS, 1), 0)
    length = jnp.where(
        slot == 0, lengths_ref[0, 0],
        jnp.where(slot == 1, lengths_ref[0, 1], jnp.where(slot == 2, lengths_ref[0, 2], lengths_ref[0, 3])),
    ).astype(f32)
    scaled = pooled_grad * (1.0 / length) * gain_ref[...][None]
    centered = scaled - jnp.mean(scaled, axis=1, keepdims=True)
    scaled_ref[...] = centered
    share = pl.ds(pl.multiple_of(lax.rem(place, 2) * HALF, 128), HALF)

    def grad(first, normal, normal_share, inverse):
        row_doc = doc_of(ends, first + lax.broadcasted_iota(jnp.int32, (ROWS, 1), 0))

        def spread(values):
            pick = jnp.where(row_doc == 2, values[2:3], values[3:4])
            return jnp.where(row_doc == 0, values[0:1], jnp.where(row_doc == 1, values[1:2], pick))

        along = jnp.mean(spread(scaled) * normal, axis=1, keepdims=True)
        return (inverse * (spread(scaled_ref[:, share]) - normal_share * along)).astype(bf16)

    mine = grad(place * ROWS, normal_ref[...], normal_ref[:, share], inverse_ref[...])
    inverse = other_rows_ref[:, D:PACK].astype(f32)
    theirs = grad(
        (place ^ 1) * ROWS,
        other_rows_ref[:, :D].astype(f32),
        other_rows_ref[:, share].astype(f32),
        inverse[:, 0:1] + inverse[:, 1:2],
    )
    for i in range(D // ROWS):
        part = slice(ROWS * i, ROWS * (i + 1))
        other_mixed = other_rows_ref[:, PACK + ROWS * i : PACK + ROWS * (i + 1)]
        product = jnp.dot(mixed_ref[part, :], mine, preferred_element_type=f32)
        product += jnp.dot(other_mixed, theirs, preferred_element_type=f32)
        out_ref[part, :] = product.astype(bf16)
    write.wait()


def join_kernel(halves_ref, out_ref):
    for core in range(2):
        parts = [halves_ref[c].astype(jnp.float32) for c in range(core, CTX, 2)]
        out_ref[:, HALF * core : HALF * (core + 1)] = (parts[0] + parts[1]) + (parts[2] + parts[3])


SMEM = pl.BlockSpec(memory_space=pltpu.SMEM)
VMEM = pl.BlockSpec(memory_space=pltpu.VMEM)
ANY = pl.BlockSpec(memory_space=pl.ANY)


def call(kernel, name, smem, vmem, outs, scratch, flops, aliases={}, whole=(), hbm_outs=0, sems=()):
    return pl.pallas_call(
        kernel,
        name=name,
        out_shape=[jax.ShapeDtypeStruct(s, t) for s, t in outs],
        in_specs=[SMEM] * len(smem) + [VMEM] * len(vmem) + [ANY] * len(whole),
        out_specs=[VMEM] * (len(outs) - hbm_outs) + [ANY] * hbm_outs,
        scratch_shapes=[pltpu.VMEM(s, t) for s, t in scratch] + list(sems),
        input_output_aliases=aliases,
        cost_estimate=pl.CostEstimate(flops=flops, bytes_accessed=1 << 26, transcendentals=0),
        compiler_params=pltpu.CompilerParams(vmem_limit_bytes=VMEM_LIMIT),
    )(*smem, *vmem, *whole)


def copies(value, axis, count):
    return lax.all_to_all(jnp.broadcast_to(value[None], (count,) + value.shape), axis, 0, 0, tiled=True)


def per_device(hidden_in, w_qkv, w_out, b_out, ln_gain, ln_bias, doc_lengths, pair_of):
    f32, bf16 = jnp.float32, jnp.bfloat16
    own = hidden_in[0]
    places = jnp.stack([lax.axis_index("ctx"), lax.axis_index("dp")]).astype(jnp.int32)
    smem = [doc_lengths, places]
    state = [((HEADS, AUG, ROWS), f32)]
    work = [((HEADS, AUG, 2 * ROWS), bf16)]
    held = ((PAIRS, 256, 2 * ROWS), bf16)

    def fold(name, sources, blocks, acc):
        (acc,) = call(
            functools.partial(fold_kernel, sources), name, smem, [w_qkv, qbd, acc, *blocks], state, work,
            1 << 34, {4: 0},
        )
        return acc

    near = lax.ppermute(own, "ctx", AROUND)
    qbd, acc = call(queries_kernel, "queries", smem, [own, w_qkv], [held] + state, [], 1 << 34)
    own_later, acc = lax.optimization_barrier((own, acc))
    behind = lax.ppermute(own_later, "ctx", BACK)
    other = lax.ppermute(own_later, "ctx", CORE_SWAP)
    acc = fold("own", SOURCES[0:1], [own], acc)
    acc = fold("other", SOURCES[1:2], [other], acc)
    near, acc = lax.optimization_barrier((near, acc))
    far = lax.ppermute(near, "ctx", AROUND)
    near_other = lax.ppermute(near, "ctx", CORE_SWAP)
    acc = fold("near", SOURCES[2:3], [near], acc)
    near_other, acc = lax.optimization_barrier((near_other, acc))
    acc = fold("near_other", SOURCES[3:4], [near_other], acc)
    behind, acc = lax.optimization_barrier((behind, acc))
    behind_other = lax.ppermute(behind, "ctx", CORE_SWAP)
    acc = fold("behind", SOURCES[4:5], [behind], acc)
    behind_other, acc = lax.optimization_barrier((behind_other, acc))
    acc = fold("behind_other", SOURCES[5:6], [behind_other], acc)
    far, acc = lax.optimization_barrier((far, acc))
    far_other = lax.ppermute(far, "ctx", CORE_SWAP)
    acc = fold("far", SOURCES[6:7], [far], acc)
    far_other, acc = lax.optimization_barrier((far_other, acc))
    _, mixed, normal, inverse, rows, partials = call(
        last_kernel,
        "last",
        smem,
        [far_other, w_qkv, qbd, acc, own, w_out, b_out, ln_gain, ln_bias],
        state
        + [((D, ROWS), bf16), ((ROWS, D), f32), ((ROWS, 1), f32), ((ROWS, PACK + D), bf16), ((CTX, DOCS, D), f32)],
        work + [((8, 2 * ROWS), f32), ((len(SOURCES), ROWS, D), bf16)],
        1 << 34,
        {5: 0},
        [own, other, near, near_other, behind, behind_other, far, far_other],
    )
    other_rows = lax.ppermute(rows, "ctx", CORE_SWAP)
    pooled = jnp.sum(lax.all_to_all(partials, "ctx", 0, 0, tiled=True), axis=0)
    pooled, other_rows = lax.optimization_barrier((pooled, other_rows))
    every = copies(pooled, "dp", DP)
    term, encoded = call(
        back_kernel,
        "back",
        smem + [pair_of],
        [every, mixed, normal, inverse, other_rows, ln_gain, ln_bias],
        [((D, HALF), bf16), ((ROWS, D), bf16)],
        [((NDOC, NDOC), f32), ((DOCS, D), f32), ((ROWS, D), bf16)],
        1 << 20,
        hbm_outs=1,
        sems=[pltpu.SemaphoreType.DMA],
    )
    share = D // DP
    pieces = lax.all_to_all(term.reshape(DP, share, HALF), "dp", 0, 0, tiled=True)
    piece = jnp.sum(pieces.astype(f32), axis=0).astype(bf16)
    halves = copies(piece, "ctx", CTX)
    (grad_out,) = call(join_kernel, "join", [], [halves], [((share, D), f32)], [], 1 << 20)
    return (encoded[None], grad_out)


def solution(mesh):
    return jax.shard_map(
        per_device,
        mesh=mesh,
        in_specs=(P("dp", "ctx", None), P(), P(), P(), P(), P(), P("dp", None), P("dp", None)),
        out_specs=(P("dp", "ctx", None), P("dp", None)),
        check_vma=False,
    )
```

```python
import functools

import jax
import jax.numpy as jnp
from jax import lax
from jax.experimental import pallas as pl
from jax.experimental.pallas import tpu as pltpu
from jax.sharding import PartitionSpec as P

D = 768
HEADS = 12
HEAD_DIM = 64
PAIRS = HEADS // 2
DOCS = 4
NDOC = 128
ROWS = 256
CTX = 8
DP = 32
HALF = D // 2
PACK = D + 128
AUG = 80

SOFTMAX_TEMPER = 0.05
NORM_EPSILON = 1e-05
EMBED_EPSILON = 1e-06
PENALTY = -1e30

VMEM_LIMIT = 24 * 1024 * 1024

CORE_SWAP = [(c, c ^ 1) for c in range(CTX)]
AROUND = [(c, (c + 2) % CTX if c % 2 == 0 else (c - 2) % CTX) for c in range(CTX)]
BACK = [(b, a) for a, b in AROUND]


def came_from(place, hops):
    step = 2 * hops
    return lax.rem(jnp.where(lax.rem(place, 2) == 0, place - step, place + step) + 2 * CTX, CTX)


SOURCES = [(0, 0), (1, 0), (0, 1), (1, 1), (0, -1), (1, -1), (0, 2), (1, 2)]


def doc_ends(lengths_ref):
    e0 = lengths_ref[0, 0]
    e1 = e0 + lengths_ref[0, 1]
    e2 = e1 + lengths_ref[0, 2]
    e3 = e2 + lengths_ref[0, 3]
    return e0, e1, e2, e3


def doc_of(ends, positions):
    e0, e1, e2, e3 = ends
    one = jnp.int32(1)
    zero = jnp.int32(0)
    return sum(jnp.where(positions >= e, one, zero) for e in (e0, e1, e2, e3))


def needed_span(ends, first):
    e0, e1, e2, e3 = ends
    last = first + ROWS - 1
    low = jnp.where(first >= e2, e2, jnp.where(first >= e1, e1, jnp.where(first >= e0, e0, 0)))
    high = jnp.where(last < e0, e0, jnp.where(last < e1, e1, jnp.where(last < e2, e2, e3)))
    return low, high


def fill_queries(ends, first, own, wqkv_ref, qbd):
    queries = lax.dot_general(
        wqkv_ref[:, :D], own, (((0,), (1,)), ((), ())), preferred_element_type=jnp.float32
    )
    queries = (queries.astype(jnp.bfloat16).astype(jnp.float32) * HEAD_DIM**-0.5).astype(jnp.bfloat16)
    positions = first + lax.broadcasted_iota(jnp.int32, (HEAD_DIM * 2, ROWS), 1)
    slots = lax.broadcasted_iota(jnp.int32, (HEAD_DIM * 2, ROWS), 0)
    same = (doc_of(ends, positions) == slots) | (slots >= DOCS)
    penalty = jnp.where(same, 0.0, PENALTY).astype(jnp.bfloat16)
    penalties = jnp.concatenate([penalty, penalty], axis=1)
    zero = jnp.zeros((HEAD_DIM, ROWS), jnp.bfloat16)
    for j in range(PAIRS):
        qbd[j, :64, :ROWS] = queries[128 * j : 128 * j + 64, :]
        qbd[j, :64, ROWS:] = zero
        qbd[j, 64:128, :ROWS] = zero
        qbd[j, 64:128, ROWS:] = queries[128 * j + 64 : 128 * j + 128, :]
        qbd[j, 128:, :] = penalties


def project(ends, bases, blocks, wqkv_ref, vt):
    rows = ROWS * len(blocks)
    hidden = jnp.concatenate(blocks, axis=0) if len(blocks) > 1 else blocks[0]
    keys = jnp.dot(hidden, wqkv_ref[:, D : 2 * D], preferred_element_type=jnp.float32).astype(jnp.bfloat16)
    values = lax.dot_general(
        wqkv_ref[:, 2 * D :], hidden, (((0,), (1,)), ((), ())), preferred_element_type=jnp.float32
    ).astype(jnp.bfloat16)
    vt[:, :HEAD_DIM, :rows] = values.reshape(HEADS, HEAD_DIM, rows)
    offsets = lax.broadcasted_iota(jnp.int32, (ROWS, 128), 0)
    lanes = lax.broadcasted_iota(jnp.int32, (ROWS, 128), 1)
    onehots = [
        jnp.where(doc_of(ends, base + offsets) == lanes, 1.0, 0.0).astype(jnp.bfloat16) for base in bases
    ]
    return keys, jnp.concatenate(onehots, axis=0) if len(blocks) > 1 else onehots[0]


def pair_scores(keys, onehot, qbd, j):
    pair_keys = jnp.concatenate([keys[:, 128 * j : 128 * j + 128], onehot], axis=1)
    return jnp.dot(pair_keys, qbd[j], preferred_element_type=jnp.float32)


def attend_plain(ends, bases, blocks, wqkv_ref, qbd, vt, acc_ref):
    rows = ROWS * len(blocks)
    keys, onehot = project(ends, bases, blocks, wqkv_ref, vt)
    for j in range(PAIRS):
        weights = jnp.exp(pair_scores(keys, onehot, qbd, j)).astype(jnp.bfloat16)
        for h in range(2):
            part = slice(ROWS * h, ROWS * h + ROWS)
            acc_ref[2 * j + h] += jnp.dot(
                vt[2 * j + h, :, :rows], weights[:, part], preferred_element_type=jnp.float32
            )


def attend_shifted(ends, base, block, wqkv_ref, qbd, vt, m_ref, acc_ref):
    keys, onehot = project(ends, [base], [block], wqkv_ref, vt)
    for j in range(PAIRS):
        scores = pair_scores(keys, onehot, qbd, j)
        old = m_ref[j : j + 1, :]
        new = jnp.maximum(old, jnp.max(scores, axis=0, keepdims=True))
        m_ref[j : j + 1, :] = new
        shrink = jnp.exp(old - new)
        weights = jnp.exp(scores - new).astype(jnp.bfloat16)
        for h in range(2):
            part = slice(ROWS * h, ROWS * h + ROWS)
            mixed = jnp.dot(vt[2 * j + h, :, :ROWS], weights[:, part], preferred_element_type=jnp.float32)
            acc_ref[2 * j + h] = acc_ref[2 * j + h] * shrink[:, part] + mixed


def fill_ones(vt):
    row = lax.broadcasted_iota(jnp.int32, (HEADS, AUG - HEAD_DIM, vt.shape[2]), 1)
    vt[:, HEAD_DIM:, :] = jnp.where(row == 0, 1.0, 0.0).astype(jnp.bfloat16)


def attend_blocks(ends, first, places, blocks, wqkv_ref, qbd, vt, acc_ref):
    low, high = needed_span(ends, first)
    bases = [place * ROWS for place in places]
    wanted = [(base < high) & (base + ROWS > low) for base in bases]

    def attend(which):
        attend_plain(
            ends, [bases[i] for i in which], [blocks[i][...] for i in which], wqkv_ref, qbd, vt, acc_ref
        )

    if len(blocks) == 1:
        pl.when(wanted[0])(lambda: attend([0]))
    else:
        one, two = wanted
        pl.when(one & two)(lambda: attend([0, 1]))
        pl.when(one & jnp.logical_not(two))(lambda: attend([0]))
        pl.when(two & jnp.logical_not(one))(lambda: attend([1]))


def queries_kernel(lengths_ref, place_ref, own_ref, wqkv_ref, qbd, acc_ref):
    ends = doc_ends(lengths_ref)
    fill_queries(ends, place_ref[0] * ROWS, own_ref[...], wqkv_ref, qbd)
    acc_ref[...] = jnp.zeros(acc_ref.shape, jnp.float32)


def fold_kernel(sources, lengths_ref, place_ref, wqkv_ref, qbd, acc_in, *refs):
    blocks, (acc_ref, vt) = refs[: len(sources)], refs[len(sources) :]
    place = place_ref[0]
    ends = doc_ends(lengths_ref)
    fill_ones(vt)
    places = [came_from(place ^ flip, hops) for flip, hops in sources]
    attend_blocks(ends, place * ROWS, places, blocks, wqkv_ref, qbd, vt, acc_ref)


def in_range(acc):
    sums = acc[:, HEAD_DIM, :]
    good = jnp.where((sums >= 1e-12) & (sums <= 1e12), 1.0, 0.0)
    finite = jnp.where(jnp.abs(acc) <= 1e38, 1.0, 0.0)
    return jnp.minimum(jnp.min(good), jnp.min(finite)) > 0.5


def attend_again(ends, place, blocks, wqkv_ref, qbd, vt, acc_ref, m_ref, held):
    for i, (flip, hops) in enumerate(SOURCES):
        pltpu.sync_copy(blocks[i], held.at[i])
    m_ref[...] = jnp.full(m_ref.shape, PENALTY, jnp.float32)
    acc_ref[...] = jnp.zeros(acc_ref.shape, jnp.float32)
    low, high = needed_span(ends, place * ROWS)

    def step(i, carry):
        base = jnp.int32(0)
        for k, (flip, hops) in enumerate(SOURCES):
            base = jnp.where(i == k, came_from(place ^ flip, hops) * ROWS, base)

        @pl.when((base < high) & (base + ROWS > low))
        def _():
            attend_shifted(ends, base, held[i], wqkv_ref, qbd, vt, m_ref, acc_ref)

        return carry

    lax.fori_loop(0, len(SOURCES), step, 0)


def last_kernel(
    lengths_ref, place_ref, far_other_ref, wqkv_ref, qbd, acc_in, own_ref, wout_ref, bias_ref, gain_ref, shift_ref,
    *refs
):
    blocks, refs = refs[: len(SOURCES)], refs[len(SOURCES) :]
    acc_ref, mixed_ref, normal_ref, inverse_ref, rows_ref, pooled_ref, vt, m_ref, held = refs
    place = place_ref[0]
    ends = doc_ends(lengths_ref)
    first = place * ROWS
    fill_ones(vt)
    flip, hops = SOURCES[-1]
    attend_blocks(ends, first, [came_from(place ^ flip, hops)], [far_other_ref], wqkv_ref, qbd, vt, acc_ref)

    @pl.when(jnp.logical_not(in_range(acc_ref[...])))
    def _():
        attend_again(ends, place, blocks, wqkv_ref, qbd, vt, acc_ref, m_ref, held)

    acc = acc_ref[...]
    mixed = acc[:, :HEAD_DIM, :] * (1.0 / acc[:, HEAD_DIM : HEAD_DIM + 1, :])
    mixed = mixed.reshape(D, ROWS).astype(jnp.bfloat16)
    mixed_ref[...] = mixed
    summed = lax.dot_general(
        mixed, wout_ref[...], (((0,), (0,)), ((), ())), preferred_element_type=jnp.float32
    )
    summed = summed + bias_ref[...][None] + own_ref[...].astype(jnp.float32)
    centered = summed - jnp.mean(summed, axis=1, keepdims=True)
    inverse = lax.rsqrt(jnp.mean(centered * centered, axis=1, keepdims=True) + NORM_EPSILON)
    normal = centered * inverse
    normal_ref[...] = normal
    inverse_ref[...] = inverse
    layer = normal * gain_ref[...][None] + shift_ref[...][None]
    for i in range(D // ROWS):
        rows_ref[:, PACK + ROWS * i : PACK + ROWS * (i + 1)] = mixed[ROWS * i : ROWS * (i + 1)]
    rows_ref[:, :D] = normal.astype(jnp.bfloat16)
    high = inverse.astype(jnp.bfloat16).astype(jnp.float32)
    lane = lax.broadcasted_iota(jnp.int32, (ROWS, 128), 1)
    rows_ref[:, D:PACK] = jnp.where(lane == 0, high, inverse - high).astype(jnp.bfloat16)
    row_doc = doc_of(ends, first + lax.broadcasted_iota(jnp.int32, (ROWS, 1), 0))
    pooled_ref[...] = jnp.zeros(pooled_ref.shape, jnp.float32)
    starts = (jnp.int32(0), *ends[:-1])
    for d in range(DOCS):

        @pl.when((starts[d] < first + ROWS) & (ends[d] > first))
        def _():
            total = jnp.sum(jnp.where(row_doc == d, layer, 0.0), axis=0, keepdims=True)
            mean = total * (1.0 / lengths_ref[0, d].astype(jnp.float32))
            pooled_ref[:, d : d + 1, :] = jnp.broadcast_to(mean[None], (CTX, 1, D))


def back_kernel(
    lengths_ref, place_ref, pair_ref, pooled_ref, mixed_ref, normal_ref, inverse_ref, other_rows_ref,
    gain_ref, shift_ref, out_ref, encoded_hbm, expo_ref, scaled_ref, encoded_ref, sem
):
    place = place_ref[0]
    data_place = place_ref[1]
    ends = doc_ends(lengths_ref)
    f32, bf16 = jnp.float32, jnp.bfloat16

    pooled = pooled_ref[...].reshape(NDOC, D)
    emb = pooled * lax.rsqrt(jnp.sum(pooled * pooled, axis=1, keepdims=True) + EMBED_EPSILON)
    high = emb.astype(bf16)
    low = (emb - high.astype(f32)).astype(bf16)

    def times(left, right):
        return lax.dot_general(left, right, (((1,), (1,)), ((), ())), preferred_element_type=f32)

    sims = (times(high, high) + (times(high, low) + times(low, high))) * (1.0 / SOFTMAX_TEMPER)
    columns = lax.broadcasted_iota(jnp.int32, (NDOC, NDOC), 1)
    rows = lax.broadcasted_iota(jnp.int32, (NDOC, NDOC), 0)
    expo = jnp.where(rows == columns, 0.0, jnp.exp(sims))
    expo_ref[...] = expo
    totals = 1.0 / jnp.sum(expo, axis=0, keepdims=True)
    half = lax.rem(data_place, 2)
    rows8 = expo_ref[pl.ds(pl.multiple_of((data_place - half) * DOCS, 8), 8), :]
    own_expo = jnp.where(half == 0, rows8[:DOCS], rows8[DOCS:])
    own = pooled_ref[data_place]
    own_inverse = lax.rsqrt(jnp.sum(own * own, axis=1, keepdims=True) + EMBED_EPSILON)
    own_emb = own * own_inverse
    own_totals = 1.0 / jnp.sum(own_expo, axis=1, keepdims=True)
    slots = lax.broadcasted_iota(jnp.int32, (DOCS, NDOC), 0)
    lanes = lax.broadcasted_iota(jnp.int32, (DOCS, NDOC), 1)
    partner = jnp.where(
        slots == 0, pair_ref[0, 0],
        jnp.where(slots == 1, pair_ref[0, 1], jnp.where(slots == 2, pair_ref[0, 2], pair_ref[0, 3])),
    )
    both = own_expo * (own_totals + totals) - jnp.where(lanes == partner, 2.0, 0.0)
    weights = jnp.concatenate([both, both], axis=0).T
    emb_grad = jnp.concatenate(
        [jnp.sum(weights[:, d : d + 1] * emb, axis=0, keepdims=True) for d in range(DOCS)], axis=0
    ) * (1.0 / SOFTMAX_TEMPER)
    pooled_grad = (emb_grad - own_emb * jnp.sum(own_emb * emb_grad, axis=1, keepdims=True)) * own_inverse
    slot = lax.broadcasted_iota(jnp.int32, (DOCS, 1), 0)
    length = jnp.where(
        slot == 0, lengths_ref[0, 0],
        jnp.where(slot == 1, lengths_ref[0, 1], jnp.where(slot == 2, lengths_ref[0, 2], lengths_ref[0, 3])),
    ).astype(f32)
    scaled = pooled_grad * (1.0 / length) * gain_ref[...][None]
    centered = scaled - jnp.mean(scaled, axis=1, keepdims=True)
    scaled_ref[...] = centered
    share = pl.ds(pl.multiple_of(lax.rem(place, 2) * HALF, 128), HALF)

    def grad(first, normal, normal_share, inverse):
        row_doc = doc_of(ends, first + lax.broadcasted_iota(jnp.int32, (ROWS, 1), 0))

        def spread(values):
            pick = jnp.where(row_doc == 2, values[2:3], values[3:4])
            return jnp.where(row_doc == 0, values[0:1], jnp.where(row_doc == 1, values[1:2], pick))

        along = jnp.mean(spread(scaled) * normal, axis=1, keepdims=True)
        return (inverse * (spread(scaled_ref[:, share]) - normal_share * along)).astype(bf16)

    encoded_ref[...] = (normal_ref[...] * gain_ref[...][None] + shift_ref[...][None]).astype(bf16)
    write = pltpu.make_async_copy(encoded_ref, encoded_hbm, sem)
    write.start()
    mine = grad(place * ROWS, normal_ref[...], normal_ref[:, share], inverse_ref[...])
    inverse = other_rows_ref[:, D:PACK].astype(f32)
    theirs = grad(
        (place ^ 1) * ROWS,
        other_rows_ref[:, :D].astype(f32),
        other_rows_ref[:, share].astype(f32),
        inverse[:, 0:1] + inverse[:, 1:2],
    )
    for i in range(D // ROWS):
        part = slice(ROWS * i, ROWS * (i + 1))
        other_mixed = other_rows_ref[:, PACK + ROWS * i : PACK + ROWS * (i + 1)]
        product = jnp.dot(mixed_ref[part, :], mine, preferred_element_type=f32)
        product += jnp.dot(other_mixed, theirs, preferred_element_type=f32)
        out_ref[part, :] = product.astype(bf16)
    write.wait()


def join_kernel(halves_ref, out_ref):
    for core in range(2):
        parts = [halves_ref[c].astype(jnp.float32) for c in range(core, CTX, 2)]
        out_ref[:, HALF * core : HALF * (core + 1)] = (parts[0] + parts[1]) + (parts[2] + parts[3])


SMEM = pl.BlockSpec(memory_space=pltpu.SMEM)
VMEM = pl.BlockSpec(memory_space=pltpu.VMEM)
ANY = pl.BlockSpec(memory_space=pl.ANY)


def call(kernel, name, smem, vmem, outs, scratch, flops, aliases={}, whole=(), hbm_outs=0, sems=()):
    return pl.pallas_call(
        kernel,
        name=name,
        out_shape=[jax.ShapeDtypeStruct(s, t) for s, t in outs],
        in_specs=[SMEM] * len(smem) + [VMEM] * len(vmem) + [ANY] * len(whole),
        out_specs=[VMEM] * (len(outs) - hbm_outs) + [ANY] * hbm_outs,
        scratch_shapes=[pltpu.VMEM(s, t) for s, t in scratch] + list(sems),
        input_output_aliases=aliases,
        cost_estimate=pl.CostEstimate(flops=flops, bytes_accessed=1 << 26, transcendentals=0),
        compiler_params=pltpu.CompilerParams(vmem_limit_bytes=VMEM_LIMIT),
    )(*smem, *vmem, *whole)


def copies(value, axis, count):
    return lax.all_to_all(jnp.broadcast_to(value[None], (count,) + value.shape), axis, 0, 0, tiled=True)


def per_device(hidden_in, w_qkv, w_out, b_out, ln_gain, ln_bias, doc_lengths, pair_of):
    f32, bf16 = jnp.float32, jnp.bfloat16
    own = hidden_in[0]
    places = jnp.stack([lax.axis_index("ctx"), lax.axis_index("dp")]).astype(jnp.int32)
    smem = [doc_lengths, places]
    state = [((HEADS, AUG, ROWS), f32)]
    work = [((HEADS, AUG, 2 * ROWS), bf16)]
    held = ((PAIRS, 256, 2 * ROWS), bf16)

    def fold(name, sources, blocks, acc):
        (acc,) = call(
            functools.partial(fold_kernel, sources), name, smem, [w_qkv, qbd, acc, *blocks], state, work,
            1 << 34, {4: 0},
        )
        return acc

    near = lax.ppermute(own, "ctx", AROUND)
    qbd, acc = call(queries_kernel, "queries", smem, [own, w_qkv], [held] + state, [], 1 << 34)
    own_later, acc = lax.optimization_barrier((own, acc))
    behind = lax.ppermute(own_later, "ctx", BACK)
    other = lax.ppermute(own_later, "ctx", CORE_SWAP)
    acc = fold("own", SOURCES[0:1], [own], acc)
    acc = fold("other", SOURCES[1:2], [other], acc)
    near, acc = lax.optimization_barrier((near, acc))
    far = lax.ppermute(near, "ctx", AROUND)
    near_other = lax.ppermute(near, "ctx", CORE_SWAP)
    acc = fold("near", SOURCES[2:3], [near], acc)
    near_other, acc = lax.optimization_barrier((near_other, acc))
    acc = fold("near_other", SOURCES[3:4], [near_other], acc)
    behind, acc = lax.optimization_barrier((behind, acc))
    behind_other = lax.ppermute(behind, "ctx", CORE_SWAP)
    acc = fold("behind", SOURCES[4:5], [behind], acc)
    behind_other, acc = lax.optimization_barrier((behind_other, acc))
    acc = fold("behind_other", SOURCES[5:6], [behind_other], acc)
    far, acc = lax.optimization_barrier((far, acc))
    far_other = lax.ppermute(far, "ctx", CORE_SWAP)
    acc = fold("far", SOURCES[6:7], [far], acc)
    far_other, acc = lax.optimization_barrier((far_other, acc))
    _, mixed, normal, inverse, rows, partials = call(
        last_kernel,
        "last",
        smem,
        [far_other, w_qkv, qbd, acc, own, w_out, b_out, ln_gain, ln_bias],
        state
        + [((D, ROWS), bf16), ((ROWS, D), f32), ((ROWS, 1), f32), ((ROWS, PACK + D), bf16), ((CTX, DOCS, D), f32)],
        work + [((8, 2 * ROWS), f32), ((len(SOURCES), ROWS, D), bf16)],
        1 << 34,
        {5: 0},
        [own, other, near, near_other, behind, behind_other, far, far_other],
    )
    other_rows = lax.ppermute(rows, "ctx", CORE_SWAP)
    pooled = jnp.sum(lax.all_to_all(partials, "ctx", 0, 0, tiled=True), axis=0)
    pooled, other_rows = lax.optimization_barrier((pooled, other_rows))
    every = copies(pooled, "dp", DP)
    term, encoded = call(
        back_kernel,
        "back",
        smem + [pair_of],
        [every, mixed, normal, inverse, other_rows, ln_gain, ln_bias],
        [((D, HALF), bf16), ((ROWS, D), bf16)],
        [((NDOC, NDOC), f32), ((DOCS, D), f32), ((ROWS, D), bf16)],
        1 << 20,
        hbm_outs=1,
        sems=[pltpu.SemaphoreType.DMA],
    )
    share = D // DP
    pieces = lax.all_to_all(term.reshape(DP, share, HALF), "dp", 0, 0, tiled=True)
    piece = jnp.sum(pieces.astype(f32), axis=0).astype(bf16)
    halves = copies(piece, "ctx", CTX)
    (grad_out,) = call(join_kernel, "join", [], [halves], [((share, D), f32)], [], 1 << 20)
    return (encoded[None], grad_out)


def solution(mesh):
    return jax.shard_map(
        per_device,
        mesh=mesh,
        in_specs=(P("dp", "ctx", None), P(), P(), P(), P(), P(), P("dp", None), P("dp", None)),
        out_specs=(P("dp", "ctx", None), P("dp", None)),
        check_vma=False,
    )
```
